32 devices in a mesh: dp: 8 (over z, y), fsdp: 4 (over x, core).
Axes of the slice: x: 2, y: 2, z: 4, core: 2. Of those that a mesh axis runs over, the one named last changes fastest.
Arguments:
- tokens: bfloat16 [12288, 768], P(('dp', 'fsdp')), may hold values from -6 to 6
- qkv_weight: bfloat16 [768, 2304], P(('dp', 'fsdp')), may hold values from -0.21875 to 0.21875
- out_weight: bfloat16 [768, 768], P(('dp', 'fsdp')), may hold values from -0.875 to 0.875
- up_weight: bfloat16 [768, 3072], P(('dp', 'fsdp')), may hold values from -0.21875 to 0.21875
- down_weight: bfloat16 [3072, 768], P(('dp', 'fsdp')), may hold values from -0.109375 to 0.109375
- norm_gains: bfloat16 [768, 2], P(('dp', 'fsdp')), may hold values from 0.5 to 1.5
- up_bias: bfloat16 [3072], P(('dp', 'fsdp')), may hold values from -3 to 3
- pass_table: bfloat16 [768, 5], P(('dp', 'fsdp')), may hold values from -3 to 3
- pass_index: int32 [2], replicated, may hold values from 0 to 4
- lengths: int32 [8], P('dp'), may hold values from 1153 to 1536, as said below
- cotangent: bfloat16 [12288, 768], P(('dp', 'fsdp')), may hold values from -6 to 6
Outputs:
- block_out: bfloat16 [12288, 768], P(('dp', 'fsdp'))
- input_grad: float32 [12288, 768], P(('dp', 'fsdp'))
- qkv_grad: float32 [768, 2304], P(('dp', 'fsdp'))
- out_grad: float32 [768, 768], P(('dp', 'fsdp'))
- up_grad: float32 [768, 3072], P(('dp', 'fsdp'))
- down_grad: float32 [3072, 768], P(('dp', 'fsdp'))
- gain_grad: float32 [768, 2], P(('dp', 'fsdp'))
- bias_grad: float32 [3072], P(('dp', 'fsdp'))
- table_grad: float32 [768, 5], P(('dp', 'fsdp'))
The draws below stay inside these ranges and needn't reach their ends.
Inputs may be any that keep to these rules, and one draw needn't show every extreme that they name: `lengths`: every length is at least 1153, and some sequence has length exactly 1536.
All inputs are finite; a program needn't handle non-finite values.
Results may differ from the reference program's by a relative error of at most 0.013.
Values may be sent and summed in bfloat16 or wider, within the bound.
A program may use at most 192 MiB of HBM per device.

```python
import jax
import jax.numpy as jnp
from jax import lax

D = 768
HEADS = 12
FF = 3072
REPEATS = 5
TOK_DEV = 384
SEQ = 1536
SEQS = 8
TOKENS = 12288


def draw_lengths(key, part):
    key = jax.random.fold_in(key, 7)
    first_key, second_key = jax.random.split(key)
    drawn = jax.random.randint(first_key, (SEQS,), SEQ - TOK_DEV + 1, SEQ + 1, dtype=jnp.int32)
    chosen = jax.random.randint(second_key, (), 0, SEQS, dtype=jnp.int32)
    return jnp.where(jnp.arange(SEQS, dtype=jnp.int32) == chosen, SEQ, drawn).astype(jnp.int32)


def levels(stream_key, dims, pieces, smallest, high):
    def one(dim, blocks):
        steps = jax.random.uniform(jax.random.fold_in(jax.random.fold_in(stream_key, 6), dim), (blocks,), jnp.float32, smallest / len(pieces), high / len(pieces))
        return jnp.repeat(jnp.exp(steps), dims[dim] // blocks).reshape((-1,) + (1,) * (len(dims) - dim - 1))

    level = one(*pieces[0])
    for cut in pieces[1:]:
        level = level * one(*cut)
    return level


def centred(own_key, shape, width, reach, cuts=(), kind=jnp.bfloat16):
    factor_of = levels(own_key, shape, cuts, -0.22, 0.18) if cuts else 1.0
    values = jax.random.normal(own_key, shape, jnp.float32) * width * factor_of
    return jnp.minimum(jnp.maximum(values, -reach), reach).astype(kind)


def setup_inputs(seed: int = 0) -> dict:
    streams_of = jax.random.split(jax.random.key(seed), 12)
    return {
        "tokens": centred(streams_of[0], (TOKENS, D), 1.0, 6.0, ((0, 32),)),
        "qkv_weight": centred(streams_of[1], (D, 3 * D), D ** -0.5, 0.21875, ((0, 32),)),
        "out_weight": centred(streams_of[2], (D, D), (D // 16) ** -0.5, 0.875, ((0, 32),)),
        "up_weight": centred(streams_of[3], (D, FF), D ** -0.5, 0.21875, ((0, 32),)),
        "down_weight": centred(streams_of[4], (FF, D), FF ** -0.5, 0.109375, ((0, 32),)),
        "norm_gains": jnp.clip(1.0 + 0.1 * jax.random.normal(streams_of[5], (D, 2), jnp.float32), 0.5, 1.5).astype(jnp.bfloat16),
        "up_bias": centred(streams_of[6], (FF,), 0.5, 3.0, ((0, 32),)),
        "pass_table": centred(streams_of[7], (D, REPEATS), 0.5, 3.0, ((0, 32),)),
        "pass_index": jax.random.randint(streams_of[8], (2,), 0, REPEATS).astype(jnp.int32),
        "lengths": draw_lengths(jax.random.fold_in(streams_of[11], 71), 0),
        "cotangent": centred(streams_of[10], (TOKENS, D), 1.0, 6.0, ((0, 32),)),
    }


@jax.custom_vjp
def low(v):
    return lax.optimization_barrier(v.astype(jnp.bfloat16)).astype(jnp.float32)

@jax.custom_vjp
def low_back(v):
    return v

def low_keep(v):
    return (low(v), None)

def low_pass(kept, grad):
    return (grad,)

def back_keep(v):
    return (v, None)

def back_low(kept, grad):
    return (low(grad),)
low.defvjp(low_keep, low_pass)
low_back.defvjp(back_keep, back_low)

def both_low(value):
    return low(low_back(value))

def matmul(left, right):
    return jnp.dot(left, right, precision=lax.Precision.HIGHEST)

def layer_norm(values, gain_vec):
    center = values - lax.optimization_barrier(jnp.mean(values, axis=-1, keepdims=True))
    spread = lax.optimization_barrier(jnp.mean(center * center, axis=-1, keepdims=True))
    return center * lax.rsqrt(spread + 1e-05) * gain_vec

def sequence_attention(packed):
    qkv_rows, seq_limit = packed
    head_width = D // HEADS
    queries = qkv_rows[:, :D].reshape(SEQ, HEADS, head_width)
    key_rows = qkv_rows[:, D:2 * D].reshape(SEQ, HEADS, head_width)
    value_rows = qkv_rows[:, 2 * D:].reshape(SEQ, HEADS, head_width)
    block_rows = min(512, SEQ)
    key_pos = jnp.arange(SEQ, dtype=jnp.int32)

    def query_block(start_row):
        query_rows = lax.dynamic_slice_in_dim(queries, start_row, block_rows, 0)
        row_pos = start_row + jnp.arange(block_rows, dtype=jnp.int32)
        allowed = (key_pos[None, :] <= row_pos[:, None]) & (key_pos[None, :] < seq_limit)
        scores = jnp.einsum('qhd,khd->hqk', query_rows, key_rows, precision=lax.Precision.HIGHEST) * head_width ** (-0.5)
        scores = jnp.where(allowed[None], low_back(scores), -1e+30)
        attend = jax.nn.softmax(scores, axis=-1)
        mixed_rows = jnp.einsum('hqk,khd->qhd', low(attend), value_rows, precision=lax.Precision.HIGHEST)
        return mixed_rows.reshape(block_rows, D)
    starts = jnp.arange(SEQ // block_rows, dtype=jnp.int32) * block_rows
    return lax.map(jax.checkpoint(query_block), starts).reshape(SEQ, D)

def one_pass(stream, weights, embedding, lengths):
    qkv_weight, out_weight, up_weight, down_weight, norm_gains, up_bias = weights
    hidden = stream + embedding[None, :]
    first_norm = low(layer_norm(hidden, norm_gains[:, 0]))
    qkv_rows = both_low(matmul(first_norm, qkv_weight))
    mixed_rows = lax.map(jax.checkpoint(sequence_attention), (qkv_rows.reshape(SEQS, SEQ, 3 * D), lengths))
    mixed_rows = both_low(mixed_rows.reshape(TOKENS, D))
    after_attn = hidden + low_back(matmul(mixed_rows, out_weight))
    second_norm = low(layer_norm(after_attn, norm_gains[:, 1]))
    pre_gelu = low_back(matmul(second_norm, up_weight) + up_bias)
    active = low(jax.nn.gelu(pre_gelu, approximate=True))
    return after_attn + low_back(matmul(active, down_weight))

def reference(tokens, qkv_weight, out_weight, up_weight, down_weight, norm_gains, up_bias, pass_table, pass_index, lengths, cotangent):
    position = jnp.arange(TOKENS, dtype=jnp.int32)
    seq_limit = lengths[position // SEQ]
    valid_rows = (position % SEQ < seq_limit).astype(jnp.float32)[:, None]
    chooser = [(jnp.arange(REPEATS, dtype=jnp.int32) == pass_index[number]).astype(jnp.float32) for number in range(2)]

    def forward(start_rows, qkv_full, out_full, up_full, down_full, gain_full, bias_full, table_full):
        weights = (qkv_full, out_full, up_full, down_full, gain_full, bias_full)
        stream = start_rows
        for number in range(2):
            stream = one_pass(stream, weights, matmul(table_full, chooser[number]), lengths)
        return stream * valid_rows
    primals = tuple((array.astype(jnp.float32) for array in (tokens, qkv_weight, out_weight, up_weight, down_weight, norm_gains, up_bias, pass_table)))
    result, pullback = jax.vjp(forward, *primals)
    gradients = pullback(cotangent.astype(jnp.float32))
    return (result.astype(jnp.bfloat16), gradients[0], gradients[1], gradients[2], gradients[3], gradients[4], gradients[5], gradients[6], gradients[7])
```

```python
from functools import partial
import jax
import jax.numpy as jnp
from jax import lax
from jax.experimental import pallas as pl
from jax.experimental.pallas import tpu as pltpu
from jax.sharding import PartitionSpec as P
BF=jnp.bfloat16; F32=jnp.float32
MESH = pl.DeviceIdType.MESH
NEG = -1e30
QB = 512
VMEM_LIMIT = 58 * 2**20

def remote(src, dst, ssem, rsem, dev):
    return pltpu.make_async_remote_copy(src_ref=src, dst_ref=dst, send_sem=ssem, recv_sem=rsem, device_id=dev, device_id_type=MESH)

def rows_at(start, count, step=16):
    return pl.ds(pl.multiple_of(start, step), count)

def normed(values):
    center = values - jnp.mean(values, axis=-1, keepdims=True)
    spread = jnp.mean(center * center, axis=-1, keepdims=True)
    scale = lax.rsqrt(spread + 1e-05)
    return center * scale, scale

def norm_back(xhat, scale, grad_out, gain):
    eg = grad_out * gain
    first = jnp.mean(eg, axis=-1, keepdims=True)
    second = jnp.mean(eg * xhat, axis=-1, keepdims=True)
    return scale * (eg - first - xhat * second)

def nt(left, right):
    return lax.dot_general(left, right, (((1,), (1,)), ((), ())), preferred_element_type=F32)

def dot(left, right):
    return jnp.dot(left, right, preferred_element_type=F32)

def mask_scores(sT, i, limit):
    lo = i * QB
    free = min(lo, 1024)
    parts = []
    if free: parts.append(sT[:free])
    if lo > free:
        kpos = free + lax.broadcasted_iota(jnp.int32, (lo - free, QB), 0)
        parts.append(jnp.where(kpos < limit, sT[free:lo], NEG))
    kpos = lo + lax.broadcasted_iota(jnp.int32, (QB, QB), 0)
    ok = kpos <= lo + lax.broadcasted_iota(jnp.int32, (QB, QB), 1)
    if lo + QB > 1024: ok = ok & (kpos < limit)
    parts.append(jnp.where(ok, sT[lo:], NEG))
    return parts[0] if len(parts) == 1 else jnp.concatenate(parts, 0)

def pick(xT, h):
    r = lax.broadcasted_iota(jnp.int32, xT.shape, 0)
    return jnp.where((r // 64) == (h % 2), xT, jnp.zeros_like(xT))

def slot_of(h, base=0):
    return pl.ds(pl.multiple_of(base + (h // 2) * 128, 128), 128)

def fwd_block(i, qkv, limit, qT, vT, oT, lse):
    keys = (i + 1) * QB
    cols = pl.ds(i * QB, QB)
    def head(h, _):
        hr = pl.ds(pl.multiple_of(h * 64, 64), 64)
        sT = dot(qkv[0:keys, slot_of(h, 256)], pick(qT[slot_of(h), cols], h))
        sT = mask_scores(sT, i, limit)
        m = jnp.max(sT, axis=0, keepdims=True)
        p = jnp.exp(sT - m)
        l = jnp.sum(p, axis=0, keepdims=True)
        oT[hr, cols] = dot(vT[hr, 0:keys], p.astype(BF)) * (1.0 / l)
        lse[pl.ds(h, 1), cols] = m + jnp.log(l)
        return 0
    lax.fori_loop(0, 3, head, 0)

def bwd_block(i, qkv, do, lse, limit, qT, kT, doT, dqT, delta, dkv):
    keys = (i + 1) * QB
    cols = pl.ds(i * QB, QB)
    def head(h, _):
        hr = pl.ds(pl.multiple_of(h * 64, 64), 64)
        lm = (lax.broadcasted_iota(jnp.int32, (QB, 128), 1) // 64) == (h % 2)
        sT = dot(qkv[0:keys, slot_of(h, 256)], pick(qT[slot_of(h), cols], h))
        sT = mask_scores(sT, i, limit)
        p = jnp.exp(sT - lse[pl.ds(h, 1), cols])
        dp = dot(qkv[0:keys, slot_of(h, 512)], pick(doT[slot_of(h), cols], h))
        dsT = (p * (dp - delta[pl.ds(h, 1), cols])).astype(BF)
        dqT[hr, cols] = dot(kT[hr, 0:keys], dsT)
        qn = qkv[cols, slot_of(h)]
        dn = do[cols, slot_of(h)]
        dkv[0:keys, slot_of(h)] += dot(dsT, jnp.where(lm, qn, jnp.zeros_like(qn)))
        dkv[0:keys, slot_of(h, 256)] += dot(p.astype(BF), jnp.where(lm, dn, jnp.zeros_like(dn)))
        return 0
    lax.fori_loop(0, 3, head, 0)

def group_barrier(d, f):
    bar = pltpu.get_barrier_semaphore()
    for k in (1, 2, 3):
        pl.semaphore_signal(bar, inc=1, device_id=(d, f ^ k), device_id_type=MESH)
    pl.semaphore_wait(bar, 3)

T, D, FF, S = 384, 768, 3072, 1536
CH = 128

def fwd_kernel(lim, x, vec, bias, wq_h, wou_h, wd_h,
               xo_h, n1_h, qkv_h, o_h, lse_h, og_h, r_h, n2_h, gp_h, a_h,
               wq, wou, wd, n1, qkv, qT, vT, oT, o, lse, og, r, n2, gp, a, xo,
               lsem, osem, ssem, rsem):
    d = lax.axis_index("dp"); f = lax.axis_index("fsdp")
    loads = [pltpu.make_async_copy(s, t, lsem.at[i]) for i, (s, t) in enumerate([(wq_h, wq), (wou_h, wou), (wd_h, wd)])]
    for c in loads: c.start()
    group_barrier(d, f)
    stores = []
    def store(src, dst):
        c = pltpu.make_async_copy(src, dst, osem.at[len(stores)])
        c.start(); stores.append(c)
    limit = lim[0]
    g0, g1, emb = vec[0:1, :], vec[1:2, :], vec[2:3, :]
    sends = []
    def send(src, dst, k, dev):
        c = remote(src, dst, ssem.at[k], rsem.at[k], dev)
        c.start(); sends.append(c)
    def got(region, k):
        remote(region, region, ssem.at[k], rsem.at[k], (d, f ^ 1)).wait_recv()
    for j in range(T // CH):
        rows = pl.ds(j * CH, CH)
        xhat, _ = normed(x[rows, :].astype(F32) + emb)
        n1[f, rows, :] = (xhat * g0).astype(BF)
        reg = n1.at[f, rows, :]
        send(reg, reg, j, (d, f ^ 2))
        send(reg, reg, 3 + j, (d, f ^ 1))
    loads[0].wait()
    def project(k):
        def tile(j, _):
            rows = rows_at(j * 192, 192)
            qkv[rows_at(k * T + j * 192, 192), :] = dot(n1[k, rows, :], wq[...]).astype(BF)
            return 0
        lax.fori_loop(0, 2, tile, 0)
    project(f)
    for j in range(3): got(n1.at[f ^ 1, pl.ds(j * CH, CH), :], 3 + j)
    project(f ^ 1)
    for j in range(3):
        reg = n1.at[f ^ 2, pl.ds(j * CH, CH), :]
        got(reg, j)
        send(reg, reg, 6 + j, (d, f ^ 1))
    project(f ^ 2)
    for j in range(3): got(n1.at[f ^ 3, pl.ds(j * CH, CH), :], 6 + j)
    project(f ^ 3)
    store(n1, n1_h); store(qkv, qkv_h)
    qT[...] = (qkv[:, 0:256] * 0.125).astype(BF).T
    vT[...] = qkv[:, 512:768].T
    oT[192:256, :] = jnp.zeros((64, S), F32)
    lse[...] = jnp.zeros_like(lse)
    def finish(b):
        rows = pl.ds(b * T, T)
        o[rows, :] = oT[:, rows].astype(BF).T
        @pl.when(f == b)
        def _(): og[b] = o[rows, :]
        for k in (1, 2, 3):
            @pl.when((f ^ k) == b)
            def _(): remote(o.at[rows, :], og.at[f], ssem.at[8 + k], rsem.at[8 + k], (d, f ^ k)).start()
    for i in reversed(range(S // QB)):
        fwd_block(i, qkv, limit, qT, vT, oT, lse)
        for b in reversed(range(4)):
            if i * QB <= b * T and not (b * T >= (i + 1) * QB): finish(b)
    store(o, o_h); store(lse, lse_h)
    for k in (1, 2, 3): got(og.at[f ^ k], 8 + k)
    store(og, og_h)
    loads[1].wait()
    def out_rows(j, _):
        rows = rows_at(j * 192, 192)
        acc = x[rows, :].astype(F32) + emb
        for k in range(4):
            acc = acc + dot(og[k, rows, 0:192], wou[k * 192:(k + 1) * 192, 0:D])
        r[rows, :] = acc
        xhat, _ = normed(acc)
        n2[rows, :] = (xhat * g1).astype(BF)
        return 0
    lax.fori_loop(0, 2, out_rows, 0)
    store(r, r_h); store(n2, n2_h)
    W = 768
    def up_tile(j, _):
        cols = pl.ds(pl.multiple_of(j * W, 128), W)
        u = dot(n2[...], wou[:, pl.ds(pl.multiple_of(D + j * W, 128), W)]) + bias[:, cols]
        sq = u * u
        t = jnp.tanh(0.7978845608028654 * u * (1.0 + 0.044715 * sq))
        half = 0.5 * (1.0 + t)
        a[:, cols] = (u * half).astype(BF)
        gp[:, cols] = (half + 0.5 * u * (1.0 - t * t) * (0.7978845608028654 * (1.0 + 0.134145 * sq))).astype(BF)
        return 0
    lax.fori_loop(0, FF // W, up_tile, 0)
    store(gp, gp_h); store(a, a_h)
    loads[2].wait()
    def down_tile(j, _):
        cols = pl.ds(pl.multiple_of(j * 256, 128), 256)
        xo[:, cols] = r[:, cols] + dot(a[...], wd[:, cols])
        return 0
    lax.fori_loop(0, D // 256, down_tile, 0)
    store(xo, xo_h)
    for c in sends: c.wait_send()
    for k in (1, 2, 3): remote(o.at[pl.ds(0, T), :], og.at[f], ssem.at[8 + k], rsem.at[8 + k], (d, f ^ k)).wait_send()
    for c in stores: c.wait()

def fwd(lim, x, vec, bias, wq, wou, wd, cid):
    Z = jax.ShapeDtypeStruct
    hbm = pl.BlockSpec(memory_space=pltpu.HBM); vm = pl.BlockSpec(memory_space=pltpu.VMEM); sm = pl.BlockSpec(memory_space=pltpu.SMEM)
    V = pltpu.VMEM
    outs = [((T, D), F32), ((4, T, D), BF), ((S, D), BF), ((S, 256), BF), ((8, S), F32), ((4, T, 256), BF), ((T, D), F32), ((T, D), BF), ((T, FF), BF), ((T, FF), BF)]
    return pl.pallas_call(fwd_kernel, out_shape=[Z(*s) for s in outs],
        in_specs=[sm, vm, vm, vm, hbm, hbm, hbm], out_specs=[hbm] * len(outs),
        scratch_shapes=[V((D, D), BF), V((D, 3840), BF), V((FF, D), BF), V((4, T, D), BF), V((S, D), BF), V((256, S), BF), V((256, S), BF), V((256, S), F32),
            V((S, 256), BF), V((8, S), F32), V((4, T, 256), BF), V((T, D), F32), V((T, D), BF), V((T, FF), BF), V((T, FF), BF), V((T, D), F32),
            pltpu.SemaphoreType.DMA((3,)), pltpu.SemaphoreType.DMA((16,)), pltpu.SemaphoreType.DMA((12,)), pltpu.SemaphoreType.DMA((12,))],
        compiler_params=pltpu.CompilerParams(collective_id=cid, has_side_effects=True, vmem_limit_bytes=VMEM_LIMIT))(lim, x, vec, bias, wq, wou, wd)

def bwd_kernel(lim, g, x, vec, wq_h, wou_h, wd_h, qkv_h, o_h, lse_h, r_h, gp_h,
               go_h, dm_h, du_h, da_h, dqkv_h, sums, bsum,
               wq, wou, wd, qkv, o, lse, r, gp, dm, du, da, dr, dos, do, qT, kT, doT, dqT, delta, dkv, dqkv, mine, part, inc, go,
               lsem, osem, ssem, rsem):
    d = lax.axis_index("dp"); f = lax.axis_index("fsdp")
    loads = [pltpu.make_async_copy(s, t, lsem.at[i]) for i, (s, t) in enumerate(
        [(wd_h, wd), (gp_h, gp), (wou_h, wou), (r_h, r), (qkv_h, qkv), (o_h, o), (lse_h, lse), (wq_h, wq)])]
    for c in loads: c.start()
    group_barrier(d, f)
    stores = []
    def store(src, dst):
        c = pltpu.make_async_copy(src, dst, osem.at[len(stores)])
        c.start(); stores.append(c)
    limit = lim[0]
    g0, g1, emb = vec[0:1, :], vec[1:2, :], vec[2:3, :]
    sends = []
    def send(src, dst, k, dev):
        c = remote(src, dst, ssem.at[k], rsem.at[k], dev)
        c.start(); sends.append(c)
    def got(region, k):
        remote(region, region, ssem.at[k], rsem.at[k], (d, f ^ 1)).wait_recv()
    dm[...] = g[...].astype(BF)
    store(dm, dm_h)
    loads[0].wait(); loads[1].wait()
    W = 768
    def up_tile(j, _):
        cols = pl.ds(pl.multiple_of(j * W, 128), W)
        t = (nt(dm[...], wd[cols, :]) * gp[:, cols].astype(F32)).astype(BF)
        du[:, cols] = t
        bsum[:, cols] = jnp.sum(t.astype(F32), axis=0, keepdims=True)
        return 0
    lax.fori_loop(0, FF // W, up_tile, 0)
    store(du, du_h)
    loads[2].wait(); loads[3].wait()
    sums[...] = jnp.zeros_like(sums)
    def norm2(j, _):
        rows = rows_at(j * 128, 128)
        e = nt(du[rows, :], wou[:, D:])
        xhat, scale = normed(r[rows, :])
        sums[1:2, :] += jnp.sum(e * xhat, axis=0, keepdims=True)
        t = g[rows, :] + norm_back(xhat, scale, e, g1)
        dr[rows, :] = t
        da[rows, :] = t.astype(BF)
        return 0
    lax.fori_loop(0, T // 128, norm2, 0)
    store(da, da_h)
    for k in (3, 2, 1, 0):
        b = f ^ k
        dos[b, :, 0:192] = nt(da[...], wou[rows_at(b * 192, 192), 0:D]).astype(BF)
        dos[b, :, 192:256] = jnp.zeros((T, 64), BF)
        if k:
            send(dos.at[b], do.at[rows_at(f * T, T), :], k, (d, b))
        else:
            do[rows_at(f * T, T), :] = dos[b]
    for c in loads[4:]: c.wait()
    qT[...] = (qkv[:, 0:256] * 0.125).astype(BF).T
    kT[...] = qkv[:, 256:512].T
    dqT[192:256, :] = jnp.zeros((64, S), F32)
    dkv[...] = jnp.zeros_like(dkv)
    for k in (1, 2, 3): got(do.at[rows_at((f ^ k) * T, T), :], k)
    doT[...] = do[...].T
    prod = (do[...].astype(F32) * o[...].astype(F32)).T
    for h in range(3):
        delta[h:h + 1, :] = jnp.sum(prod[h * 64:h * 64 + 64], axis=0, keepdims=True)
    for i in range(S // QB):
        bwd_block(i, qkv, do, lse, limit, qT, kT, doT, dqT, delta, dkv)
    dqkv[:, 0:256] = (dqT[...] * 0.125).astype(BF).T
    dqkv[:, 256:512] = (dkv[:, 0:256] * 0.125).astype(BF)
    dqkv[:, 512:768] = dkv[:, 256:512].astype(BF)
    store(dqkv, dqkv_h)
    def partial_rows(b, j):
        return nt(dqkv[rows_at(b * T + j * CH, CH), :], wq[...])
    for j in range(3):
        rows = pl.ds(j * CH, CH)
        mine[0, rows, :] = partial_rows(f ^ 3, j).astype(BF)
        send(mine.at[0, rows, :], part.at[0, rows, :], 4 + j, (d, f ^ 1))
    for j in range(3):
        rows = pl.ds(j * CH, CH)
        t = partial_rows(f ^ 2, j)
        got(part.at[0, rows, :], 4 + j)
        inc[rows, :] = (t + part[0, rows, :].astype(F32)).astype(BF)
        send(inc.at[rows, :], part.at[2, rows, :], 7 + j, (d, f ^ 2))
    for j in range(3):
        rows = pl.ds(j * CH, CH)
        mine[1, rows, :] = partial_rows(f ^ 1, j).astype(BF)
        send(mine.at[1, rows, :], part.at[1, rows, :], 10 + j, (d, f ^ 1))
    for j in range(3):
        rows = pl.ds(j * CH, CH)
        go[rows, :] = partial_rows(f, j)
    for j in range(3):
        rows = pl.ds(j * CH, CH)
        got(part.at[1, rows, :], 10 + j)
        got(part.at[2, rows, :], 7 + j)
        e = go[rows, :] + part[1, rows, :].astype(F32) + part[2, rows, :].astype(F32)
        xhat, scale = normed(x[rows, :].astype(F32) + emb)
        sums[0:1, :] += jnp.sum(e * xhat, axis=0, keepdims=True)
        t = dr[rows, :] + norm_back(xhat, scale, e, g0)
        sums[2:3, :] += jnp.sum(t, axis=0, keepdims=True)
        go[rows, :] = t
    store(go, go_h)
    for c in sends: c.wait_send()
    for c in stores: c.wait()

def bwd(lim, g, x, vec, wq, wou, wd, qkv, o, lse, r, gp, cid):
    Z = jax.ShapeDtypeStruct
    hbm = pl.BlockSpec(memory_space=pltpu.HBM); vm = pl.BlockSpec(memory_space=pltpu.VMEM); sm = pl.BlockSpec(memory_space=pltpu.SMEM)
    V = pltpu.VMEM
    outs = [((T, D), F32), ((T, D), BF), ((T, FF), BF), ((T, D), BF), ((S, D), BF), ((8, D), F32), ((1, FF), F32)]
    return pl.pallas_call(bwd_kernel, out_shape=[Z(*s) for s in outs],
        in_specs=[sm, vm, vm, vm] + [hbm] * 8, out_specs=[hbm] * 5 + [vm] * 2,
        scratch_shapes=[V((D, D), BF), V((D, 3840), BF), V((FF, D), BF), V((S, D), BF), V((S, 256), BF), V((8, S), F32), V((T, D), F32), V((T, FF), BF),
            V((T, D), BF), V((T, FF), BF), V((T, D), BF), V((T, D), F32), V((4, T, 256), BF), V((S, 256), BF),
            V((256, S), BF), V((256, S), BF), V((256, S), BF), V((256, S), F32), V((8, S), F32), V((S, 512), F32), V((S, D), BF),
            V((2, T, D), BF), V((3, T, D), BF), V((T, D), BF), V((T, D), F32),
            pltpu.SemaphoreType.DMA((8,)), pltpu.SemaphoreType.DMA((8,)), pltpu.SemaphoreType.DMA((13,)), pltpu.SemaphoreType.DMA((13,))],
        compiler_params=pltpu.CompilerParams(collective_id=cid, has_side_effects=True, vmem_limit_bytes=VMEM_LIMIT))(lim, g, x, vec, wq, wou, wd, qkv, o, lse, r, gp)

def place():
    d = lax.axis_index("dp"); f = lax.axis_index("fsdp")
    return d, f, d // 2, d % 2, f // 2, f % 2

def gather_kernel(nz, q4, ou, dn, wq, wou, we, wd, rq, rou, blk, blkq, local, ssem, rsem):
    d, f, z, y, x, c = place()
    q = z * 4 + y * 2 + x
    up, down = (d + 2, f), (d - 2, f)
    yp, xp, sp = (d ^ 1, f), (d, f ^ 2), (d, f ^ 1)
    bar = pltpu.get_barrier_semaphore()
    for dev in (sp, xp, (d, f ^ 3), yp):
        pl.semaphore_signal(bar, inc=1, device_id=dev, device_id_type=MESH)
    @pl.when(z > 0)
    def _(): pl.semaphore_signal(bar, inc=1, device_id=down, device_id_type=MESH)
    @pl.when(z < nz - 1)
    def _(): pl.semaphore_signal(bar, inc=1, device_id=up, device_id_type=MESH)
    pl.semaphore_wait(bar, 4 + (z > 0).astype(jnp.int32) + (z < nz - 1).astype(jnp.int32))

    sends = []
    def go(copy, pred=None):
        if pred is None:
            copy.start()
        else:
            pl.when(pred)(copy.start)
        sends.append((pred, copy))
    def got(region, sem, pred=None):
        w = remote(region, region, ssem.at[0], sem, sp)
        if pred is None: w.wait_recv()
        else: pl.when(pred)(w.wait_recv)

    n = [0]
    def sem():
        n[0] += 1
        return ssem.at[n[0] - 1], rsem.at[n[0] - 1]
    s_ou = sem(); go(remote(ou, rou, *s_ou, sp))
    s_q = [sem() for _ in range(4)]
    for k in range(1, 4):
        dst = f ^ k
        go(remote(q4.at[dst], rq.at[f], s_q[k][0], rsem.at[n[0] - 4 + k], (d, dst)))
    own_dn = wd.at[pl.ds(pl.multiple_of((q * 2 + c) * 96, 16), 96), :]
    s_dn = sem(); go(remote(dn, own_dn, *s_dn, sp))
    loc = [pltpu.make_async_copy(dn, own_dn, local.at[0])]
    loc[0].start()
    rq[f] = q4[f]
    got(rou, s_ou[1])
    mine, other = ou[...].astype(F32), rou[...].astype(F32)
    blk[...] = jnp.concatenate([jnp.where(c == 0, mine, other), jnp.where(c == 0, other, mine)], axis=0).astype(BF)
    row = pl.ds(pl.multiple_of(q * 48, 16), 48)
    l1 = pltpu.make_async_copy(blk.at[:, pl.ds(0, 3840)], wou.at[row, :], local.at[1]); l1.start()
    l2 = pltpu.make_async_copy(blk.at[:, pl.ds(3840, 128)], we.at[row, :], local.at[2]); l2.start()
    for k in range(1, 4):
        got(rq.at[f ^ k], s_q[k][1])
    blkq[...] = jnp.concatenate([rq[k].astype(F32) for k in range(4)], axis=0).astype(BF)
    l3 = pltpu.make_async_copy(blkq, wq.at[pl.ds(pl.multiple_of(d * 96, 16), 96), :], local.at[3]); l3.start()
    l2.wait(); l3.wait(); l1.wait(); loc[0].wait()
    other_dn = wd.at[pl.ds(pl.multiple_of((q * 2 + 1 - c) * 96, 16), 96), :]
    got(other_dn, s_dn[1])

    c1 = pl.multiple_of(c * 1920, 128)
    NA = 1280
    parts = {
        "Q": dict(ref=wq, rows=96, col0=0, cols=768, order="zy", sib=False),
        "E": dict(ref=we, rows=48, col0=0, cols=128, order="xyz", sib=False),
        "O": dict(ref=wou, rows=48, col0=c1, cols=NA, order="zxy", sib=True),
        "D": dict(ref=wd, rows=192, col0=pl.multiple_of(c * 384, 128), cols=384, order="zyx", sib=True),
        "P": dict(ref=wou, rows=48, col0=pl.multiple_of(c1 + NA, 128), cols=1920 - NA, order="xyz", sib=True),
    }
    def reg(p, r0, cnt):
        p = parts[p]
        return p["ref"].at[pl.ds(pl.multiple_of(r0 * p["rows"], 16), cnt * p["rows"]), pl.ds(p["col0"], p["cols"])]
    def push(p, r0, cnt, dev, pred=None):
        s, r = sem()
        region = reg(p, r0, cnt)
        go(remote(region, region, s, r, dev), pred)
        return r
    def recv(p, r0, cnt, r, pred=None, sib=True):
        got(reg(p, r0, cnt), r, pred)
        if sib and parts[p]["sib"]:
            rs = push(p, r0, cnt, sp, pred)
            late.append((p, r0, cnt, rs, pred))
    late = []
    slots = [(0, 0)] + [(s, k) for s in range(1, nz) for k in (0, 1)]
    def slot_z(s, k):
        return z - s if k == 0 else z + s
    def slot_ok(s, k):
        if s == 0: return None
        return (z - s >= 0) if k == 0 else (z + s < nz)
    def both(a, b):
        if a is None: return b
        return a & b
    zr = {}
    def zblock(p, zz):
        o = parts[p]["order"]
        if o == "zy": return zz * 2 + y, 1
        if o[0] == "z": return zz * 4 + y * 2 + x, 1
        return zz * 4, 4
    def zsend(p, s):
        for k in (0, 1):
            okc = slot_ok(s - 1, k) if s > 1 else None
            edge = (z < nz - 1) if k == 0 else (z > 0)
            r0, cnt = zblock(p, slot_z(s - 1, k))
            zr[p, s, k] = push(p, r0, cnt, up if k == 0 else down, both(okc, edge))
    def zrecv(p, s, then):
        for k in (0, 1):
            r0, cnt = zblock(p, slot_z(s, k))
            recv(p, r0, cnt, zr[p, s, k], slot_ok(s, k))
            if then: then(p, s, k)
    second = {}; third = {}
    def step2(p, s, k):
        o = parts[p]["order"]; zz = slot_z(s, k)
        if o == "zy": second[p, s, k] = push(p, zz * 2 + y, 1, yp, slot_ok(s, k))
        elif o[1] == "x": second[p, s, k] = push(p, zz * 4 + y * 2 + x, 1, xp, slot_ok(s, k))
        else: second[p, s, k] = push(p, zz * 4 + y * 2 + x, 1, yp, slot_ok(s, k))
    def recv2(p, s, k):
        o = parts[p]["order"]; zz = slot_z(s, k); ok = slot_ok(s, k)
        if o == "zy":
            recv(p, zz * 2 + 1 - y, 1, second[p, s, k], ok)
        elif o[1] == "x":
            recv(p, zz * 4 + y * 2 + 1 - x, 1, second[p, s, k], ok)
            third[p, s, k] = [(zz * 4 + (1 - y) * 2, 2, push(p, zz * 4 + y * 2, 2, yp, ok))]
        else:
            recv(p, zz * 4 + (1 - y) * 2 + x, 1, second[p, s, k], ok)
            third[p, s, k] = [(zz * 4 + yy * 2 + 1 - x, 1, push(p, zz * 4 + yy * 2 + x, 1, xp, ok)) for yy in range(2)]
    def recv3(p, s, k):
        for r0, cnt, r in third[p, s, k]:
            recv(p, r0, cnt, r, slot_ok(s, k))
    zp = ("Q", "O", "D")
    for p in zp: zsend(p, 1)
    e1 = push("E", q, 1, xp); p1 = push("P", q, 1, xp)
    for p in zp: step2(p, 0, 0)
    recv("E", z * 4 + y * 2 + 1 - x, 1, e1); e2 = push("E", z * 4 + y * 2, 2, yp)
    recv("P", z * 4 + y * 2 + 1 - x, 1, p1); p2 = push("P", z * 4 + y * 2, 2, yp)
    recv("E", z * 4 + (1 - y) * 2, 2, e2); zsend("E", 1)
    for p in zp:
        zrecv(p, 1, step2)
        if nz > 2: zsend(p, 2)
    recv("P", z * 4 + (1 - y) * 2, 2, p2); zsend("P", 1)
    for p in zp: recv2(p, 0, 0)
    zrecv("E", 1, None)
    if nz > 2: zsend("E", 2)
    for s in range(2, nz):
        for p in zp:
            zrecv(p, s, step2)
            if s + 1 < nz: zsend(p, s + 1)
        zrecv("E", s, None)
        if s + 1 < nz: zsend("E", s + 1)
        for p in zp:
            for k in (0, 1): recv2(p, s - 1, k)
        zrecv("P", s - 1, None)
        zsend("P", s)
        for p in zp[1:]:
            for k in ((0,) if s == 2 else (0, 1)): recv3(p, s - 2, k)
    for p in zp:
        for k in (0, 1): recv2(p, nz - 1, k)
    for s in ([nz - 2, nz - 1]):
        for p in zp[1:]:
            for k in (0, 1): recv3(p, s, k)
    zrecv("P", nz - 1, None)
    for p, r0, cnt, rs, pred in late:
        pp = parts[p]
        other = dict(pp); base = {"O": 0, "P": NA, "D": 0}[p]
        half = 384 if p == "D" else 1920
        col = pl.multiple_of((1 - c) * half + base, 128)
        region = pp["ref"].at[pl.ds(pl.multiple_of(r0 * pp["rows"], 16), cnt * pp["rows"]), pl.ds(col, pp["cols"])]
        got(region, rs, pred)
    for pred, copy in sends:
        if pred is None: copy.wait_send()
        else: pl.when(pred)(copy.wait_send)

NSEM = 400
def gather(q4, ou, dn, nz):
    hbm = pl.BlockSpec(memory_space=pltpu.HBM); vm = pl.BlockSpec(memory_space=pltpu.VMEM)
    S = jax.ShapeDtypeStruct
    return pl.pallas_call(partial(gather_kernel, nz),
        out_shape=(S((768, 768), BF), S((768, 3840), BF), S((768, 128), BF), S((3072, 768), BF)),
        in_specs=[vm] * 3, out_specs=[hbm] * 4,
        scratch_shapes=[pltpu.VMEM((4, 24, 768), BF), pltpu.VMEM((24, 3968), BF), pltpu.VMEM((48, 3968), BF), pltpu.VMEM((96, 768), BF),
            pltpu.SemaphoreType.DMA((4,)), pltpu.SemaphoreType.DMA((NSEM,)), pltpu.SemaphoreType.DMA((NSEM,))],
        compiler_params=pltpu.CompilerParams(collective_id=0, has_side_effects=True, vmem_limit_bytes=32 * 2**20))(q4, ou, dn)


def gather_any(q4, ou, dn):
    both = ("dp", "fsdp")
    mine = lax.dynamic_index_in_dim(lax.all_gather(q4, both, axis=0), lax.axis_index("fsdp"), 1, keepdims=False)
    full = lax.all_gather(ou, both, axis=0, tiled=True)
    return mine.reshape(D, D), full[:, :3840], full[:, 3840:], lax.all_gather(dn, both, axis=0, tiled=True)

def body(tokens, qkv_weight, out_weight, up_weight, down_weight, norm_gains, up_bias, pass_table, pass_index, lengths, cotangent):
    rd = qkv_weight.shape[0]
    q4 = jnp.pad(qkv_weight.reshape(rd, 3, 4, 192), ((0, 0), (0, 0), (0, 0), (0, 64))).transpose(2, 0, 1, 3).reshape(4, rd, D)
    chooser = [(jnp.arange(pass_table.shape[1], dtype=jnp.int32) == pass_index[n]).astype(F32) for n in range(2)]
    emb = jnp.stack([jnp.sum(pass_table.astype(F32) * ch[None, :], axis=1) for ch in chooser], axis=1).astype(BF)
    e = jnp.concatenate([norm_gains, emb, up_bias.reshape(rd, 4), jnp.zeros((rd, 120), BF)], axis=1)
    ou = jnp.concatenate([out_weight, up_weight, e], axis=1)
    if rd == 24:
        wq, wou, we, wd = gather(q4, ou, down_weight, lax.axis_size("dp") // 2)
    else:
        wq, wou, we, wd = gather_any(q4, ou, down_weight)
    vecs = we[:, 0:4].T.astype(F32)
    vec = [jnp.concatenate([vecs[0:2], vecs[2 + n:3 + n], jnp.zeros((5, D), F32)], axis=0) for n in range(2)]
    bias = we[:, 4:8].reshape(1, FF).astype(F32)
    row_pos = lax.axis_index("fsdp") * T + jnp.arange(T, dtype=jnp.int32)
    valid = (row_pos < lengths[0]).astype(F32)[:, None]
    xs = [tokens.astype(F32)]; kept = []
    for n in range(2):
        res = fwd(lengths, xs[n], vec[n], bias, wq, wou, wd, 1)
        xs.append(res[0]); kept.append(res[1:])
    block_out = (xs[2] * valid).astype(BF)
    g = cotangent.astype(F32) * valid
    grads = [None, None]; sums = [None, None]; bs = [None, None]
    for n in (1, 0):
        n1, qkv, o, lse, og, r, n2, gp, a = kept[n]
        g, dm, du, da, dqkv, sums[n], bs[n] = bwd(lengths, g, xs[n], vec[n], wq, wou, wd, qkv, o, lse, r, gp, 2)
        grads[n] = (a, dm, n2, du, og, da, n1, dqkv)
    tn = lambda a, b: lax.dot_general(a, b, (((0,), (0,)), ((), ())), preferred_element_type=F32)
    cat = lambda i, sh: jnp.concatenate([grads[0][i].reshape(sh), grads[1][i].reshape(sh)], axis=0)
    a, dm, n2, du = cat(0, (T, FF)), cat(1, (T, D)), cat(2, (T, D)), cat(3, (T, FF))
    og = jnp.concatenate([grads[n][4][:, :, :192].transpose(1, 0, 2).reshape(T, D) for n in range(2)], axis=0)
    da, n1, dqkv = cat(5, (T, D)), cat(6, (S, D)), cat(7, (S, D))
    down_grad = tn(a, dm); up_grad = tn(n2, du); out_grad = tn(og, da); qg = tn(n1, dqkv)
    ps = lambda v: lax.psum_scatter(v, ("dp", "fsdp"), scatter_dimension=0, tiled=True)
    f = lax.axis_index("fsdp")
    qg = qg.reshape(D, 3, 256)[:, :, :192]
    full = lax.dynamic_update_slice(jnp.zeros((D, 3, D), F32), qg, (0, 0, f * 192)).reshape(D, 3 * D)
    tot = lax.psum((sums[0], sums[1], bs[0] + bs[1]), ("dp", "fsdp"))
    idx = lax.axis_index("dp") * 4 + f
    own = lambda v: lax.dynamic_slice_in_dim(v, idx * rd, rd, 0)
    gains = own(jnp.stack([tot[0][0] + tot[1][0], tot[0][1] + tot[1][1]], axis=1))
    table = own(tot[0][2])[:, None] * chooser[0][None] + own(tot[1][2])[:, None] * chooser[1][None]
    bias_grad = lax.dynamic_slice_in_dim(tot[2][0], idx * rd * 4, rd * 4, 0)
    return (block_out, g, ps(full), ps(out_grad), ps(up_grad), ps(down_grad), gains, bias_grad, table)

def solution(mesh):
    a = P(("dp", "fsdp"), None); b = P(("dp", "fsdp"))
    return jax.shard_map(body, mesh=mesh, in_specs=(a, a, a, a, a, a, b, a, P(), P("dp"), a), out_specs=(a, a, a, a, a, a, a, b, a), check_vma=False)
```

```python
from functools import partial
import jax
import jax.numpy as jnp
from jax import lax
from jax.experimental import pallas as pl
from jax.experimental.pallas import tpu as pltpu
from jax.sharding import PartitionSpec as P
BF=jnp.bfloat16; F32=jnp.float32
MESH = pl.DeviceIdType.MESH
NEG = -1e30
QB = 512
VMEM_LIMIT = 58 * 2**20

def remote(src, dst, ssem, rsem, dev):
    return pltpu.make_async_remote_copy(src_ref=src, dst_ref=dst, send_sem=ssem, recv_sem=rsem, device_id=dev, device_id_type=MESH)

def rows_at(start, count, step=16):
    return pl.ds(pl.multiple_of(start, step), count)

def normed(values):
    center = values - jnp.mean(values, axis=-1, keepdims=True)
    spread = jnp.mean(center * center, axis=-1, keepdims=True)
    scale = lax.rsqrt(spread + 1e-05)
    return center * scale, scale

def norm_back(xhat, scale, grad_out, gain):
    eg = grad_out * gain
    first = jnp.mean(eg, axis=-1, keepdims=True)
    second = jnp.mean(eg * xhat, axis=-1, keepdims=True)
    return scale * (eg - first - xhat * second)

def nt(left, right):
    return lax.dot_general(left, right, (((1,), (1,)), ((), ())), preferred_element_type=F32)

def dot(left, right):
    return jnp.dot(left, right, preferred_element_type=F32)

def mask_scores(sT, i, limit):
    lo = i * QB
    free = min(lo, 1024)
    parts = []
    if free: parts.append(sT[:free])
    if lo > free:
        kpos = free + lax.broadcasted_iota(jnp.int32, (lo - free, QB), 0)
        parts.append(jnp.where(kpos < limit, sT[free:lo], NEG))
    kpos = lo + lax.broadcasted_iota(jnp.int32, (QB, QB), 0)
    ok = kpos <= lo + lax.broadcasted_iota(jnp.int32, (QB, QB), 1)
    if lo + QB > 1024: ok = ok & (kpos < limit)
    parts.append(jnp.where(ok, sT[lo:], NEG))
    return parts[0] if len(parts) == 1 else jnp.concatenate(parts, 0)

def pick(xT, h):
    r = lax.broadcasted_iota(jnp.int32, xT.shape, 0)
    return jnp.where((r // 64) == (h % 2), xT, jnp.zeros_like(xT))

def slot_of(h, base=0):
    return pl.ds(pl.multiple_of(base + (h // 2) * 128, 128), 128)

def fwd_block(i, qkv, limit, qT, vT, oT, lse):
    keys = (i + 1) * QB
    cols = pl.ds(i * QB, QB)
    def head(h, _):
        hr = pl.ds(pl.multiple_of(h * 64, 64), 64)
        sT = dot(qkv[0:keys, slot_of(h, 256)], pick(qT[slot_of(h), cols], h))
        sT = mask_scores(sT, i, limit)
        m = jnp.max(sT, axis=0, keepdims=True)
        p = jnp.exp(sT - m)
        l = jnp.sum(p, axis=0, keepdims=True)
        oT[hr, cols] = dot(vT[hr, 0:keys], p.astype(BF)) * (1.0 / l)
        lse[pl.ds(h, 1), cols] = m + jnp.log(l)
        return 0
    lax.fori_loop(0, 3, head, 0)

def bwd_block(i, qkv, do, lse, limit, qT, kT, doT, dqT, delta, dkv):
    keys = (i + 1) * QB
    cols = pl.ds(i * QB, QB)
    def head(h, _):
        hr = pl.ds(pl.multiple_of(h * 64, 64), 64)
        lm = (lax.broadcasted_iota(jnp.int32, (QB, 128), 1) // 64) == (h % 2)
        sT = dot(qkv[0:keys, slot_of(h, 256)], pick(qT[slot_of(h), cols], h))
        sT = mask_scores(sT, i, limit)
        p = jnp.exp(sT - lse[pl.ds(h, 1), cols])
        dp = dot(qkv[0:keys, slot_of(h, 512)], pick(doT[slot_of(h), cols], h))
        dsT = (p * (dp - delta[pl.ds(h, 1), cols])).astype(BF)
        dqT[hr, cols] = dot(kT[hr, 0:keys], dsT)
        qn = qkv[cols, slot_of(h)]
        dn = do[cols, slot_of(h)]
        dkv[0:keys, slot_of(h)] += dot(dsT, jnp.where(lm, qn, jnp.zeros_like(qn)))
        dkv[0:keys, slot_of(h, 256)] += dot(p.astype(BF), jnp.where(lm, dn, jnp.zeros_like(dn)))
        return 0
    lax.fori_loop(0, 3, head, 0)

def group_barrier(d, f):
    bar = pltpu.get_barrier_semaphore()
    for k in (1, 2, 3):
        pl.semaphore_signal(bar, inc=1, device_id=(d, f ^ k), device_id_type=MESH)
    pl.semaphore_wait(bar, 3)

T, D, FF, S = 384, 768, 3072, 1536
CH = 128

def fwd_kernel(lim, x, vec, bias, wq_h, wou_h, wd_h,
               xo_h, n1_h, qkv_h, o_h, lse_h, og_h, r_h, n2_h, gp_h, a_h,
               wq, wou, wd, n1, qkv, qT, vT, oT, o, lse, og, r, n2, gp, a, xo,
               lsem, osem, ssem, rsem):
    d = lax.axis_index("dp"); f = lax.axis_index("fsdp")
    loads = [pltpu.make_async_copy(s, t, lsem.at[i]) for i, (s, t) in enumerate([(wq_h, wq), (wou_h, wou), (wd_h, wd)])]
    for c in loads: c.start()
    group_barrier(d, f)
    stores = []
    def store(src, dst):
        c = pltpu.make_async_copy(src, dst, osem.at[len(stores)])
        c.start(); stores.append(c)
    limit = lim[0]
    g0, g1, emb = vec[0:1, :], vec[1:2, :], vec[2:3, :]
    sends = []
    def send(src, dst, k, dev):
        c = remote(src, dst, ssem.at[k], rsem.at[k], dev)
        c.start(); sends.append(c)
    def got(region, k):
        remote(region, region, ssem.at[k], rsem.at[k], (d, f ^ 1)).wait_recv()
    for j in range(T // CH):
        rows = pl.ds(j * CH, CH)
        xhat, _ = normed(x[rows, :].astype(F32) + emb)
        n1[f, rows, :] = (xhat * g0).astype(BF)
        reg = n1.at[f, rows, :]
        send(reg, reg, j, (d, f ^ 2))
        send(reg, reg, 3 + j, (d, f ^ 1))
    loads[0].wait()
    def project(k):
        def tile(j, _):
            rows = rows_at(j * 192, 192)
            qkv[rows_at(k * T + j * 192, 192), :] = dot(n1[k, rows, :], wq[...]).astype(BF)
            return 0
        lax.fori_loop(0, 2, tile, 0)
    project(f)
    for j in range(3): got(n1.at[f ^ 1, pl.ds(j * CH, CH), :], 3 + j)
    project(f ^ 1)
    for j in range(3):
        reg = n1.at[f ^ 2, pl.ds(j * CH, CH), :]
        got(reg, j)
        send(reg, reg, 6 + j, (d, f ^ 1))
    project(f ^ 2)
    for j in range(3): got(n1.at[f ^ 3, pl.ds(j * CH, CH), :], 6 + j)
    project(f ^ 3)
    store(n1, n1_h); store(qkv, qkv_h)
    qT[...] = (qkv[:, 0:256] * 0.125).astype(BF).T
    vT[...] = qkv[:, 512:768].T
    oT[192:256, :] = jnp.zeros((64, S), F32)
    lse[...] = jnp.zeros_like(lse)
    def finish(b):
        rows = pl.ds(b * T, T)
        o[rows, :] = oT[:, rows].astype(BF).T
        @pl.when(f == b)
        def _(): og[b] = o[rows, :]
        for k in (1, 2, 3):
            @pl.when((f ^ k) == b)
            def _(): remote(o.at[rows, :], og.at[f], ssem.at[8 + k], rsem.at[8 + k], (d, f ^ k)).start()
    for i in reversed(range(S // QB)):
        fwd_block(i, qkv, limit, qT, vT, oT, lse)
        for b in reversed(range(4)):
            if i * QB <= b * T and not (b * T >= (i + 1) * QB): finish(b)
    store(o, o_h); store(lse, lse_h)
    for k in (1, 2, 3): got(og.at[f ^ k], 8 + k)
    store(og, og_h)
    loads[1].wait()
    def out_rows(j, _):
        rows = rows_at(j * 192, 192)
        acc = x[rows, :].astype(F32) + emb
        for k in range(4):
            acc = acc + dot(og[k, rows, 0:192], wou[k * 192:(k + 1) * 192, 0:D])
        r[rows, :] = acc
        xhat, _ = normed(acc)
        n2[rows, :] = (xhat * g1).astype(BF)
        return 0
    lax.fori_loop(0, 2, out_rows, 0)
    store(r, r_h); store(n2, n2_h)
    W = 768
    def up_tile(j, _):
        cols = pl.ds(pl.multiple_of(j * W, 128), W)
        u = dot(n2[...], wou[:, pl.ds(pl.multiple_of(D + j * W, 128), W)]) + bias[:, cols]
        sq = u * u
        t = jnp.tanh(0.7978845608028654 * u * (1.0 + 0.044715 * sq))
        half = 0.5 * (1.0 + t)
        a[:, cols] = (u * half).astype(BF)
        gp[:, cols] = (half + 0.5 * u * (1.0 - t * t) * (0.7978845608028654 * (1.0 + 0.134145 * sq))).astype(BF)
        return 0
    lax.fori_loop(0, FF // W, up_tile, 0)
    store(gp, gp_h); store(a, a_h)
    loads[2].wait()
    def down_tile(j, _):
        cols = pl.ds(pl.multiple_of(j * 256, 128), 256)
        xo[:, cols] = r[:, cols] + dot(a[...], wd[:, cols])
        return 0
    lax.fori_loop(0, D // 256, down_tile, 0)
    store(xo, xo_h)
    for c in sends: c.wait_send()
    for k in (1, 2, 3): remote(o.at[pl.ds(0, T), :], og.at[f], ssem.at[8 + k], rsem.at[8 + k], (d, f ^ k)).wait_send()
    for c in stores: c.wait()

def fwd(lim, x, vec, bias, wq, wou, wd, cid):
    Z = jax.ShapeDtypeStruct
    hbm = pl.BlockSpec(memory_space=pltpu.HBM); vm = pl.BlockSpec(memory_space=pltpu.VMEM); sm = pl.BlockSpec(memory_space=pltpu.SMEM)
    V = pltpu.VMEM
    outs = [((T, D), F32), ((4, T, D), BF), ((S, D), BF), ((S, 256), BF), ((8, S), F32), ((4, T, 256), BF), ((T, D), F32), ((T, D), BF), ((T, FF), BF), ((T, FF), BF)]
    return pl.pallas_call(fwd_kernel, out_shape=[Z(*s) for s in outs],
        in_specs=[sm, vm, vm, vm, hbm, hbm, hbm], out_specs=[hbm] * len(outs),
        scratch_shapes=[V((D, D), BF), V((D, 3840), BF), V((FF, D), BF), V((4, T, D), BF), V((S, D), BF), V((256, S), BF), V((256, S), BF), V((256, S), F32),
            V((S, 256), BF), V((8, S), F32), V((4, T, 256), BF), V((T, D), F32), V((T, D), BF), V((T, FF), BF), V((T, FF), BF), V((T, D), F32),
            pltpu.SemaphoreType.DMA((3,)), pltpu.SemaphoreType.DMA((16,)), pltpu.SemaphoreType.DMA((12,)), pltpu.SemaphoreType.DMA((12,))],
        compiler_params=pltpu.CompilerParams(collective_id=cid, has_side_effects=True, vmem_limit_bytes=VMEM_LIMIT))(lim, x, vec, bias, wq, wou, wd)

def bwd_kernel(lim, g, x, vec, wq_h, wou_h, wd_h, qkv_h, o_h, lse_h, r_h, gp_h,
               go_h, dm_h, du_h, da_h, dqkv_h, sums, bsum,
               wq, wou, wd, qkv, o, lse, r, gp, dm, du, da, dr, dos, do, qT, kT, doT, dqT, delta, dkv, dqkv, mine, part, inc, go,
               lsem, osem, ssem, rsem):
    d = lax.axis_index("dp"); f = lax.axis_index("fsdp")
    loads = [pltpu.make_async_copy(s, t, lsem.at[i]) for i, (s, t) in enumerate(
        [(wd_h, wd), (gp_h, gp), (wou_h, wou), (r_h, r), (qkv_h, qkv), (o_h, o), (lse_h, lse), (wq_h, wq)])]
    for c in loads: c.start()
    group_barrier(d, f)
    stores = []
    def store(src, dst):
        c = pltpu.make_async_copy(src, dst, osem.at[len(stores)])
        c.start(); stores.append(c)
    limit = lim[0]
    g0, g1, emb = vec[0:1, :], vec[1:2, :], vec[2:3, :]
    sends = []
    def send(src, dst, k, dev):
        c = remote(src, dst, ssem.at[k], rsem.at[k], dev)
        c.start(); sends.append(c)
    def got(region, k):
        remote(region, region, ssem.at[k], rsem.at[k], (d, f ^ 1)).wait_recv()
    dm[...] = g[...].astype(BF)
    store(dm, dm_h)
    loads[0].wait(); loads[1].wait()
    W = 768
    def up_tile(j, _):
        cols = pl.ds(pl.multiple_of(j * W, 128), W)
        t = (nt(dm[...], wd[cols, :]) * gp[:, cols].astype(F32)).astype(BF)
        du[:, cols] = t
        bsum[:, cols] = jnp.sum(t.astype(F32), axis=0, keepdims=True)
        return 0
    lax.fori_loop(0, FF // W, up_tile, 0)
    store(du, du_h)
    loads[2].wait(); loads[3].wait()
    sums[...] = jnp.zeros_like(sums)
    def norm2(j, _):
        rows = rows_at(j * 128, 128)
        e = nt(du[rows, :], wou[:, D:])
        xhat, scale = normed(r[rows, :])
        sums[1:2, :] += jnp.sum(e * xhat, axis=0, keepdims=True)
        t = g[rows, :] + norm_back(xhat, scale, e, g1)
        dr[rows, :] = t
        da[rows, :] = t.astype(BF)
        return 0
    lax.fori_loop(0, T // 128, norm2, 0)
    store(da, da_h)
    for k in (3, 2, 1, 0):
        b = f ^ k
        dos[b, :, 0:192] = nt(da[...], wou[rows_at(b * 192, 192), 0:D]).astype(BF)
        dos[b, :, 192:256] = jnp.zeros((T, 64), BF)
        if k:
            send(dos.at[b], do.at[rows_at(f * T, T), :], k, (d, b))
        else:
            do[rows_at(f * T, T), :] = dos[b]
    for c in loads[4:]: c.wait()
    qT[...] = (qkv[:, 0:256] * 0.125).astype(BF).T
    kT[...] = qkv[:, 256:512].T
    dqT[192:256, :] = jnp.zeros((64, S), F32)
    dkv[...] = jnp.zeros_like(dkv)
    for k in (1, 2, 3): got(do.at[rows_at((f ^ k) * T, T), :], k)
    doT[...] = do[...].T
    prod = (do[...].astype(F32) * o[...].astype(F32)).T
    for h in range(3):
        delta[h:h + 1, :] = jnp.sum(prod[h * 64:h * 64 + 64], axis=0, keepdims=True)
    for i in range(S // QB):
        bwd_block(i, qkv, do, lse, limit, qT, kT, doT, dqT, delta, dkv)
    dqkv[:, 0:256] = (dqT[...] * 0.125).astype(BF).T
    dqkv[:, 256:512] = (dkv[:, 0:256] * 0.125).astype(BF)
    dqkv[:, 512:768] = dkv[:, 256:512].astype(BF)
    store(dqkv, dqkv_h)
    def partial_rows(b, j):
        return nt(dqkv[rows_at(b * T + j * CH, CH), :], wq[...])
    for j in range(3):
        rows = pl.ds(j * CH, CH)
        mine[0, rows, :] = partial_rows(f ^ 3, j).astype(BF)
        send(mine.at[0, rows, :], part.at[0, rows, :], 4 + j, (d, f ^ 1))
    for j in range(3):
        rows = pl.ds(j * CH, CH)
        t = partial_rows(f ^ 2, j)
        got(part.at[0, rows, :], 4 + j)
        inc[rows, :] = (t + part[0, rows, :].astype(F32)).astype(BF)
        send(inc.at[rows, :], part.at[2, rows, :], 7 + j, (d, f ^ 2))
    for j in range(3):
        rows = pl.ds(j * CH, CH)
        mine[1, rows, :] = partial_rows(f ^ 1, j).astype(BF)
        send(mine.at[1, rows, :], part.at[1, rows, :], 10 + j, (d, f ^ 1))
    for j in range(3):
        rows = pl.ds(j * CH, CH)
        go[rows, :] = partial_rows(f, j)
    for j in range(3):
        rows = pl.ds(j * CH, CH)
        got(part.at[1, rows, :], 10 + j)
        got(part.at[2, rows, :], 7 + j)
        e = go[rows, :] + part[1, rows, :].astype(F32) + part[2, rows, :].astype(F32)
        xhat, scale = normed(x[rows, :].astype(F32) + emb)
        sums[0:1, :] += jnp.sum(e * xhat, axis=0, keepdims=True)
        t = dr[rows, :] + norm_back(xhat, scale, e, g0)
        sums[2:3, :] += jnp.sum(t, axis=0, keepdims=True)
        go[rows, :] = t
    store(go, go_h)
    for c in sends: c.wait_send()
    for c in stores: c.wait()

def bwd(lim, g, x, vec, wq, wou, wd, qkv, o, lse, r, gp, cid):
    Z = jax.ShapeDtypeStruct
    hbm = pl.BlockSpec(memory_space=pltpu.HBM); vm = pl.BlockSpec(memory_space=pltpu.VMEM); sm = pl.BlockSpec(memory_space=pltpu.SMEM)
    V = pltpu.VMEM
    outs = [((T, D), F32), ((T, D), BF), ((T, FF), BF), ((T, D), BF), ((S, D), BF), ((8, D), F32), ((1, FF), F32)]
    return pl.pallas_call(bwd_kernel, out_shape=[Z(*s) for s in outs],
        in_specs=[sm, vm, vm, vm] + [hbm] * 8, out_specs=[hbm] * 5 + [vm] * 2,
        scratch_shapes=[V((D, D), BF), V((D, 3840), BF), V((FF, D), BF), V((S, D), BF), V((S, 256), BF), V((8, S), F32), V((T, D), F32), V((T, FF), BF),
            V((T, D), BF), V((T, FF), BF), V((T, D), BF), V((T, D), F32), V((4, T, 256), BF), V((S, 256), BF),
            V((256, S), BF), V((256, S), BF), V((256, S), BF), V((256, S), F32), V((8, S), F32), V((S, 512), F32), V((S, D), BF),
            V((2, T, D), BF), V((3, T, D), BF), V((T, D), BF), V((T, D), F32),
            pltpu.SemaphoreType.DMA((8,)), pltpu.SemaphoreType.DMA((8,)), pltpu.SemaphoreType.DMA((13,)), pltpu.SemaphoreType.DMA((13,))],
        compiler_params=pltpu.CompilerParams(collective_id=cid, has_side_effects=True, vmem_limit_bytes=VMEM_LIMIT))(lim, g, x, vec, wq, wou, wd, qkv, o, lse, r, gp)

def place():
    d = lax.axis_index("dp"); f = lax.axis_index("fsdp")
    return d, f, d // 2, d % 2, f // 2, f % 2

def gather_kernel(nz, q4, ou, dn, wq, wou, we, wd, rq, rou, blk, blkq, local, ssem, rsem):
    d, f, z, y, x, c = place()
    q = z * 4 + y * 2 + x
    up, down = (d + 2, f), (d - 2, f)
    yp, xp, sp = (d ^ 1, f), (d, f ^ 2), (d, f ^ 1)
    bar = pltpu.get_barrier_semaphore()
    for dev in (sp, xp, (d, f ^ 3), yp):
        pl.semaphore_signal(bar, inc=1, device_id=dev, device_id_type=MESH)
    @pl.when(z > 0)
    def _(): pl.semaphore_signal(bar, inc=1, device_id=down, device_id_type=MESH)
    @pl.when(z < nz - 1)
    def _(): pl.semaphore_signal(bar, inc=1, device_id=up, device_id_type=MESH)
    pl.semaphore_wait(bar, 4 + (z > 0).astype(jnp.int32) + (z < nz - 1).astype(jnp.int32))

    sends = []
    def go(copy, pred=None):
        if pred is None:
            copy.start()
        else:
            pl.when(pred)(copy.start)
        sends.append((pred, copy))
    def got(region, sem, pred=None):
        w = remote(region, region, ssem.at[0], sem, sp)
        if pred is None: w.wait_recv()
        else: pl.when(pred)(w.wait_recv)

    n = [0]
    def sem():
        n[0] += 1
        return ssem.at[n[0] - 1], rsem.at[n[0] - 1]
    s_ou = sem(); go(remote(ou, rou, *s_ou, sp))
    s_q = [sem() for _ in range(4)]
    for k in range(1, 4):
        dst = f ^ k
        go(remote(q4.at[dst], rq.at[f], s_q[k][0], rsem.at[n[0] - 4 + k], (d, dst)))
    own_dn = wd.at[pl.ds(pl.multiple_of((q * 2 + c) * 96, 16), 96), :]
    s_dn = sem(); go(remote(dn, own_dn, *s_dn, sp))
    loc = [pltpu.make_async_copy(dn, own_dn, local.at[0])]
    loc[0].start()
    rq[f] = q4[f]
    got(rou, s_ou[1])
    mine, other = ou[...].astype(F32), rou[...].astype(F32)
    blk[...] = jnp.concatenate([jnp.where(c == 0, mine, other), jnp.where(c == 0, other, mine)], axis=0).astype(BF)
    row = pl.ds(pl.multiple_of(q * 48, 16), 48)
    l1 = pltpu.make_async_copy(blk.at[:, pl.ds(0, 3840)], wou.at[row, :], local.at[1]); l1.start()
    l2 = pltpu.make_async_copy(blk.at[:, pl.ds(3840, 128)], we.at[row, :], local.at[2]); l2.start()
    for k in range(1, 4):
        got(rq.at[f ^ k], s_q[k][1])
    blkq[...] = jnp.concatenate([rq[k].astype(F32) for k in range(4)], axis=0).astype(BF)
    l3 = pltpu.make_async_copy(blkq, wq.at[pl.ds(pl.multiple_of(d * 96, 16), 96), :], local.at[3]); l3.start()
    l2.wait(); l3.wait(); l1.wait(); loc[0].wait()
    other_dn = wd.at[pl.ds(pl.multiple_of((q * 2 + 1 - c) * 96, 16), 96), :]
    got(other_dn, s_dn[1])

    c1 = pl.multiple_of(c * 1920, 128)
    NA = 1280
    parts = {
        "Q": dict(ref=wq, rows=96, col0=0, cols=768, order="zy", sib=False),
        "E": dict(ref=we, rows=48, col0=0, cols=128, order="xyz", sib=False),
        "O": dict(ref=wou, rows=48, col0=c1, cols=NA, order="zxy", sib=True),
        "D": dict(ref=wd, rows=192, col0=pl.multiple_of(c * 384, 128), cols=384, order="zyx", sib=True),
        "P": dict(ref=wou, rows=48, col0=pl.multiple_of(c1 + NA, 128), cols=1920 - NA, order="xyz", sib=True),
    }
    def reg(p, r0, cnt):
        p = parts[p]
        return p["ref"].at[pl.ds(pl.multiple_of(r0 * p["rows"], 16), cnt * p["rows"]), pl.ds(p["col0"], p["cols"])]
    def push(p, r0, cnt, dev, pred=None):
        s, r = sem()
        region = reg(p, r0, cnt)
        go(remote(region, region, s, r, dev), pred)
        return r
    def recv(p, r0, cnt, r, pred=None, sib=True):
        got(reg(p, r0, cnt), r, pred)
        if sib and parts[p]["sib"]:
            rs = push(p, r0, cnt, sp, pred)
            late.append((p, r0, cnt, rs, pred))
    late = []
    slots = [(0, 0)] + [(s, k) for s in range(1, nz) for k in (0, 1)]
    def slot_z(s, k):
        return z - s if k == 0 else z + s
    def slot_ok(s, k):
        if s == 0: return None
        return (z - s >= 0) if k == 0 else (z + s < nz)
    def both(a, b):
        if a is None: return b
        return a & b
    zr = {}
    def zblock(p, zz):
        o = parts[p]["order"]
        if o == "zy": return zz * 2 + y, 1
        if o[0] == "z": return zz * 4 + y * 2 + x, 1
        return zz * 4, 4
    def zsend(p, s):
        for k in (0, 1):
            okc = slot_ok(s - 1, k) if s > 1 else None
            edge = (z < nz - 1) if k == 0 else (z > 0)
            r0, cnt = zblock(p, slot_z(s - 1, k))
            zr[p, s, k] = push(p, r0, cnt, up if k == 0 else down, both(okc, edge))
    def zrecv(p, s, then):
        for k in (0, 1):
            r0, cnt = zblock(p, slot_z(s, k))
            recv(p, r0, cnt, zr[p, s, k], slot_ok(s, k))
            if then: then(p, s, k)
    second = {}; third = {}
    def step2(p, s, k):
        o = parts[p]["order"]; zz = slot_z(s, k)
        if o == "zy": second[p, s, k] = push(p, zz * 2 + y, 1, yp, slot_ok(s, k))
        elif o[1] == "x": second[p, s, k] = push(p, zz * 4 + y * 2 + x, 1, xp, slot_ok(s, k))
        else: second[p, s, k] = push(p, zz * 4 + y * 2 + x, 1, yp, slot_ok(s, k))
    def recv2(p, s, k):
        o = parts[p]["order"]; zz = slot_z(s, k); ok = slot_ok(s, k)
        if o == "zy":
            recv(p, zz * 2 + 1 - y, 1, second[p, s, k], ok)
        elif o[1] == "x":
            recv(p, zz * 4 + y * 2 + 1 - x, 1, second[p, s, k], ok)
            third[p, s, k] = [(zz * 4 + (1 - y) * 2, 2, push(p, zz * 4 + y * 2, 2, yp, ok))]
        else:
            recv(p, zz * 4 + (1 - y) * 2 + x, 1, second[p, s, k], ok)
            third[p, s, k] = [(zz * 4 + yy * 2 + 1 - x, 1, push(p, zz * 4 + yy * 2 + x, 1, xp, ok)) for yy in range(2)]
    def recv3(p, s, k):
        for r0, cnt, r in third[p, s, k]:
            recv(p, r0, cnt, r, slot_ok(s, k))
    zp = ("Q", "O", "D")
    for p in zp: zsend(p, 1)
    e1 = push("E", q, 1, xp); p1 = push("P", q, 1, xp)
    for p in zp: step2(p, 0, 0)
    recv("E", z * 4 + y * 2 + 1 - x, 1, e1); e2 = push("E", z * 4 + y * 2, 2, yp)
    recv("P", z * 4 + y * 2 + 1 - x, 1, p1); p2 = push("P", z * 4 + y * 2, 2, yp)
    recv("E", z * 4 + (1 - y) * 2, 2, e2); zsend("E", 1)
    for p in zp:
        zrecv(p, 1, step2)
        if nz > 2: zsend(p, 2)
    recv("P", z * 4 + (1 - y) * 2, 2, p2); zsend("P", 1)
    for p in zp: recv2(p, 0, 0)
    zrecv("E", 1, None)
    if nz > 2: zsend("E", 2)
    for s in range(2, nz):
        for p in zp:
            zrecv(p, s, step2)
            if s + 1 < nz: zsend(p, s + 1)
        zrecv("E", s, None)
        if s + 1 < nz: zsend("E", s + 1)
        for p in zp:
            for k in (0, 1): recv2(p, s - 1, k)
        zrecv("P", s - 1, None)
        zsend("P", s)
        for p in zp[1:]:
            for k in ((0,) if s == 2 else (0, 1)): recv3(p, s - 2, k)
    for p in zp:
        for k in (0, 1): recv2(p, nz - 1, k)
    for s in ([nz - 2, nz - 1]):
        for p in zp[1:]:
            for k in (0, 1): recv3(p, s, k)
    zrecv("P", nz - 1, None)
    for p, r0, cnt, rs, pred in late:
        pp = parts[p]
        other = dict(pp); base = {"O": 0, "P": NA, "D": 0}[p]
        half = 384 if p == "D" else 1920
        col = pl.multiple_of((1 - c) * half + base, 128)
        region = pp["ref"].at[pl.ds(pl.multiple_of(r0 * pp["rows"], 16), cnt * pp["rows"]), pl.ds(col, pp["cols"])]
        got(region, rs, pred)
    for pred, copy in sends:
        if pred is None: copy.wait_send()
        else: pl.when(pred)(copy.wait_send)

NSEM = 400
def gather(q4, ou, dn, nz):
    hbm = pl.BlockSpec(memory_space=pltpu.HBM); vm = pl.BlockSpec(memory_space=pltpu.VMEM)
    S = jax.ShapeDtypeStruct
    return pl.pallas_call(partial(gather_kernel, nz),
        out_shape=(S((768, 768), BF), S((768, 3840), BF), S((768, 128), BF), S((3072, 768), BF)),
        in_specs=[vm] * 3, out_specs=[hbm] * 4,
        scratch_shapes=[pltpu.VMEM((4, 24, 768), BF), pltpu.VMEM((24, 3968), BF), pltpu.VMEM((48, 3968), BF), pltpu.VMEM((96, 768), BF),
            pltpu.SemaphoreType.DMA((4,)), pltpu.SemaphoreType.DMA((NSEM,)), pltpu.SemaphoreType.DMA((NSEM,))],
        compiler_params=pltpu.CompilerParams(collective_id=0, has_side_effects=True, vmem_limit_bytes=32 * 2**20))(q4, ou, dn)

def tn(left, right):
    return lax.dot_general(left, right, (((0,), (0,)), ((), ())), preferred_element_type=F32)

class Links:
    def __init__(self, ssem, rsem, dev):
        self.ssem, self.rsem, self.dev, self.n, self.sent = ssem, rsem, dev, 0, []
    def sem(self):
        self.n += 1
        return self.n - 1
    def send(self, src, dst, k, dev, pred=None):
        copy = remote(src, dst, self.ssem.at[k], self.rsem.at[k], dev)
        if pred is None: copy.start()
        else: pl.when(pred)(copy.start)
        self.sent.append((pred, copy))
    def got(self, region, k, pred=None):
        wait = remote(region, region, self.ssem.at[k], self.rsem.at[k], self.dev).wait_recv
        if pred is None: wait()
        else: pl.when(pred)(wait)
    def close(self):
        for pred, copy in self.sent:
            if pred is None: copy.wait_send()
            else: pl.when(pred)(copy.wait_send)

def add_to(acc, inc):
    acc[...] = (acc[...].astype(F32) + inc[...].astype(F32)).astype(BF)

def line_sum(net, nz, z, up, down, block, recv):
    sems = [[net.sem() for _ in range(nz)] for _ in range(2)]
    for k in range(nz - 1):
        for way, t, edge, behind, dev in ((0, nz - 1 - k, z < nz - 1 - k, z > 0, up), (1, k, z > k, z < nz - 1, down)):
            inc = recv.at[way, t]
            net.got(inc, sems[way][t], edge & behind)
            pl.when(edge & behind)(lambda t=t, inc=inc: add_to(block(t), inc))
            net.send(block(t), inc, sems[way][t], dev, edge)
        yield
    for t in range(nz):
        if t > 0: net.got(recv.at[0, t], sems[0][t], z == t)
        if t < nz - 1: net.got(recv.at[1, t], sems[1][t], z == t)

def grads_kernel(nz, a_0, a_1, dm_0, dm_1, n2_0, n2_1, du_0, du_1, og_0, og_1, da_0, da_1, n1_0, n1_1, dq_0, dq_1, vin,
                 down_o, outw_o, up_o, qkv_o, v_o,
                 a, dm, n2, du, og, da, n1, dq, acc_d, stg_d, sib_d, acc_o, stg_o, sib_o, acc_p, stg_p, sib_p, acc_q,
                 dx, dy, dz, oy, ox, oz, pz, py, px, qy, qz, qf, hop, half, vb, vr, lsem, ssem, rsem):
    d, f, z, y, x, c = place()
    up, down = (d + 2, f), (d - 2, f)
    yp, xp, sp = (d ^ 1, f), (d, f ^ 2), (d, f ^ 1)
    loads = []
    def load(src, dst):
        copy = pltpu.make_async_copy(src, dst, lsem.at[len(loads)])
        copy.start(); loads.append(copy)
    for src, dst, rows in ((a_0, a, T), (dm_0, dm, T), (n2_0, n2, T), (du_0, du, T), (da_0, da, T), (n1_0, n1, S), (dq_0, dq, S)):
        other = {id(a_0): a_1, id(dm_0): dm_1, id(n2_0): n2_1, id(du_0): du_1, id(da_0): da_1, id(n1_0): n1_1, id(dq_0): dq_1}[id(src)]
        load(src, dst.at[pl.ds(0, rows), :]); load(other, dst.at[pl.ds(rows, rows), :])
    load(og_0, og.at[0]); load(og_1, og.at[1])
    bar = pltpu.get_barrier_semaphore()
    for dev in (sp, xp, (d, f ^ 3), yp):
        pl.semaphore_signal(bar, inc=1, device_id=dev, device_id_type=MESH)
    @pl.when(z > 0)
    def _(): pl.semaphore_signal(bar, inc=1, device_id=down, device_id_type=MESH)
    @pl.when(z < nz - 1)
    def _(): pl.semaphore_signal(bar, inc=1, device_id=up, device_id_type=MESH)
    pl.semaphore_wait(bar, 4 + (z > 0).astype(jnp.int32) + (z < nz - 1).astype(jnp.int32))
    net = Links(ssem, rsem, sp)
    turn = []
    lo, hi = 0, nz - 1
    while lo <= hi:
        turn += [hi, lo] if lo < hi else [lo]
        lo, hi = lo + 1, hi - 1
    first = lambda v: jnp.where(c == 0, v[0], v[1])
    second = lambda v: jnp.where(c == 0, v[1], v[0])

    def vectors():
        vb[...] = vin[...]
        for i, dev in enumerate((sp, xp, yp)):
            k = net.sem()
            hop[i] = vb[...]
            net.send(hop.at[i], vr.at[i], k, dev)
            yield
            net.got(vr.at[i], k)
            vb[...] += vr[i]
        for i in (3, 4): hop[i] = vb[...]
        ks = [net.sem(), net.sem()]
        for step in range(nz - 1):
            yield
            for way, pos, dev in ((0, z, up), (1, nz - 1 - z, down)):
                @pl.when((pos == step) & (pos > 0))
                def _(way=way):
                    net.got(vr.at[3 + way], ks[way])
                    hop[3 + way] += vr[3 + way]
                net.send(hop.at[3 + way], vr.at[3 + way], ks[way], dev, pos == step)
        for way, pos in ((0, z), (1, nz - 1 - z)):
            net.got(vr.at[3 + way], ks[way], pos == nz - 1)
        @pl.when(z > 0)
        def _(): vb[...] += vr[3]
        @pl.when(z < nz - 1)
        def _(): vb[...] += vr[4]
        v_o[...] = vb[...]

    def down_part():
        ks = {t: net.sem() for t in turn}
        for t in turn:
            g = tn(a[:, t * 768:(t + 1) * 768], dm[...]).reshape(4, 2, 96, D)
            for q in range(4):
                acc_d[t * 4 + q] = first(g[q]).astype(BF)
                stg_d[t * 4 + q] = second(g[q]).astype(BF)
            net.send(stg_d.at[pl.ds(t * 4, 4)], sib_d.at[pl.ds(t * 4, 4)], ks[t], sp)
            yield
        kx = {(t, j): net.sem() for t in turn for j in range(2)}
        for t in turn:
            net.got(sib_d.at[pl.ds(t * 4, 4)], ks[t])
            add_to(acc_d.at[pl.ds(t * 4, 4)], sib_d.at[pl.ds(t * 4, 4)])
            for j in range(2):
                net.send(acc_d.at[t * 4 + j * 2 + 1 - x], dx.at[t * 2 + j], kx[t, j], xp)
            yield
        ky = {t: net.sem() for t in turn}
        for t in turn:
            for j in range(2):
                net.got(dx.at[t * 2 + j], kx[t, j])
                add_to(acc_d.at[t * 4 + j * 2 + x], dx.at[t * 2 + j])
            net.send(acc_d.at[t * 4 + (1 - y) * 2 + x], dy.at[t], ky[t], yp)
            yield
        for t in turn:
            net.got(dy.at[t], ky[t])
            add_to(acc_d.at[t * 4 + y * 2 + x], dy.at[t])
            if t != turn[-1]: yield
        yield from line_sum(net, nz, z, up, down, lambda t: acc_d.at[t * 4 + y * 2 + x], dz)
        down_o[...] = acc_d[z * 4 + y * 2 + x].astype(F32)
        @pl.when(z > 0)
        def _(): down_o[...] += dz[0, z].astype(F32)
        @pl.when(z < nz - 1)
        def _(): down_o[...] += dz[1, z].astype(F32)

    def own_cols(ref, base, width, off, cols, mine):
        cc = c if mine else 1 - c
        return ref[:, pl.ds(pl.multiple_of(base + cc * width + off, 128), cols)]
    def fill(dst, base, g):
        n = g.shape[1]
        dst[:, :, base:base + n] = g.astype(BF).reshape(16, 48, n)
    def finish_cols(acc_block, incs, base, n):
        total = acc_block.astype(F32)
        for pred, inc in incs:
            total = total + jnp.where(pred, inc.astype(F32), 0.0)
        keep = jnp.where(c == 0, total[0:24], total[24:48])
        give = jnp.where(c == 0, total[24:48], total[0:24])
        half[0, :, base:base + n] = keep
        half[1, :, base:base + n] = give

    def wide_part():
        for dst, mine in ((acc_p, True), (stg_p, False)):
            fill(dst, 0, tn(n2[...], own_cols(du, 0, 1536, 896, 640, mine)))
        kp = net.sem()
        net.send(stg_p, sib_p, kp, sp)
        yield
        for dst, mine in ((acc_o, True), (stg_o, False)):
            for j in range(4):
                g = tn(og[0, j, :, 0:192], own_cols(da, 0, 384, 0, 384, mine)[0:T]) + tn(og[1, j, :, 0:192], own_cols(da, 0, 384, 0, 384, mine)[T:2 * T])
                dst[j * 4:(j + 1) * 4, :, 0:384] = g.astype(BF).reshape(4, 48, 384)
            fill(dst, 384, tn(n2[...], own_cols(du, 0, 1536, 0, 896, mine)))
        ko = net.sem()
        net.send(stg_o, sib_o, ko, sp)
        net.got(sib_p, kp)
        add_to(acc_p, sib_p)
        lines = line_sum(net, nz, z, up, down, lambda t: acc_p.at[pl.ds(t * 4, 4)], pz)
        next(lines)
        yield
        net.got(sib_o, ko)
        ky = {t: net.sem() for t in turn}
        for t in turn:
            add_to(acc_o.at[pl.ds(t * 4, 4)], sib_o.at[pl.ds(t * 4, 4)])
            net.send(acc_o.at[pl.ds(t * 4 + (1 - y) * 2, 2)], oy.at[pl.ds(t * 2, 2)], ky[t], yp)
        yield
        next(lines)
        kx = {t: net.sem() for t in turn}
        for t in turn:
            net.got(oy.at[pl.ds(t * 2, 2)], ky[t])
            add_to(acc_o.at[pl.ds(t * 4 + y * 2, 2)], oy.at[pl.ds(t * 2, 2)])
            net.send(acc_o.at[t * 4 + y * 2 + 1 - x], ox.at[t], kx[t], xp)
            yield
        for _ in lines: yield
        own = acc_p.at[pl.ds(z * 4, 4)]
        @pl.when(z > 0)
        def _(): add_to(own, pz.at[0, z])
        @pl.when(z < nz - 1)
        def _(): add_to(own, pz.at[1, z])
        k1 = net.sem()
        net.send(acc_p.at[pl.ds(z * 4 + (1 - y) * 2, 2)], py, k1, yp)
        yield
        for t in turn:
            net.got(ox.at[t], kx[t])
            add_to(acc_o.at[t * 4 + y * 2 + x], ox.at[t])
        lines = line_sum(net, nz, z, up, down, lambda t: acc_o.at[t * 4 + y * 2 + x], oz)
        next(lines)
        yield
        net.got(py, k1)
        add_to(acc_p.at[pl.ds(z * 4 + y * 2, 2)], py)
        k2 = net.sem()
        net.send(acc_p.at[z * 4 + y * 2 + 1 - x], px, k2, xp)
        yield
        for _ in lines: yield
        net.got(px, k2)
        q = z * 4 + y * 2 + x
        finish_cols(acc_p[q], [(True, px[...])], 1280, 640)
        finish_cols(acc_o[q], [(z > 0, oz[0, z]), (z < nz - 1, oz[1, z])], 0, 1280)
        k3 = net.sem()
        net.send(half.at[1], half.at[2], k3, sp)
        yield
        net.got(half.at[2], k3)
        for cc, s in ((c, 0), (1 - c, 2)):
            outw_o[:, pl.ds(pl.multiple_of(cc * 384, 128), 384)] = half[s, :, 0:384]
            up_o[:, pl.ds(pl.multiple_of(cc * 1536, 128), 1536)] = half[s, :, 384:1920]

    def qkv_part():
        ky = {t: net.sem() for t in turn}
        for j in range(2):
            g = tn(n1[:, j * 384:(j + 1) * 384], dq[...])
            acc_q[j * 4:(j + 1) * 4] = g.astype(BF).reshape(4, 96, D)
        for t in turn:
            net.send(acc_q.at[t * 2 + 1 - y], qy.at[t], ky[t], yp)
        yield
        for t in turn:
            net.got(qy.at[t], ky[t])
            add_to(acc_q.at[t * 2 + y], qy.at[t])
        yield from line_sum(net, nz, z, up, down, lambda t: acc_q.at[t * 2 + y], qz)
        total = acc_q[z * 2 + y].astype(F32)
        total = total + jnp.where(z > 0, qz[0, z].astype(F32), 0.0) + jnp.where(z < nz - 1, qz[1, z].astype(F32), 0.0)
        for j in range(4): qf[0, j] = total[j * 24:(j + 1) * 24]
        ks = [net.sem() for _ in range(4)]
        for k in (1, 2, 3):
            net.send(qf.at[0, f ^ k], qf.at[1, f], ks[k], (d, f ^ k))
        qkv_o[f] = qf[0, f]
        yield
        for k in (1, 2, 3):
            net.got(qf.at[1, f ^ k], ks[k])
            qkv_o[f ^ k] = qf[1, f ^ k]

    def need(*which):
        for i in which: loads[i].wait()
    need(0, 1, 2, 3)
    dp_, wp, qp, vp = down_part(), wide_part(), qkv_part(), vectors()
    alive = []
    def turn_of(g):
        try:
            next(g)
        except StopIteration:
            alive.remove(g)
    alive += [dp_, vp]
    for _ in turn: turn_of(dp_)
    turn_of(vp)
    need(4, 5, 6, 7, 8, 9, 14, 15)
    alive.append(wp)
    turn_of(wp)
    turn_of(dp_); turn_of(vp); turn_of(dp_)
    turn_of(wp)
    turn_of(dp_); turn_of(dp_)
    need(10, 11, 12, 13)
    alive.append(qp)
    turn_of(wp)
    turn_of(qp)
    while alive:
        for g in list(alive): turn_of(g)
    net.close()

def grads_sum(kept0, kept1, vin, nz):
    Z = jax.ShapeDtypeStruct
    hbm = pl.BlockSpec(memory_space=pltpu.HBM); vm = pl.BlockSpec(memory_space=pltpu.VMEM)
    V = pltpu.VMEM
    q = nz * 4
    ins = []
    for u, v in zip(kept0, kept1): ins += [u, v]
    outs = [((96, D), F32), ((24, D), F32), ((24, FF), F32), ((4, 24, D), F32), ((8, D), F32)]
    three = lambda *s: [V(s, BF)] * 3
    return pl.pallas_call(partial(grads_kernel, nz), out_shape=[Z(*s) for s in outs],
        in_specs=[hbm] * 16 + [vm], out_specs=[vm] * 5,
        scratch_shapes=[V((2 * T, FF), BF), V((2 * T, D), BF), V((2 * T, D), BF), V((2 * T, FF), BF), V((2, 4, T, 256), BF), V((2 * T, D), BF), V((2 * S, D), BF), V((2 * S, D), BF)]
            + three(q, 96, D) + three(q, 48, 1280) + three(q, 48, 640) + [V((2 * nz, 96, D), BF)]
            + [V((2 * nz, 96, D), BF), V((nz, 96, D), BF), V((2, nz, 96, D), BF), V((2 * nz, 48, 1280), BF), V((nz, 48, 1280), BF), V((2, nz, 48, 1280), BF),
               V((2, nz, 4, 48, 640), BF), V((2, 48, 640), BF), V((48, 640), BF), V((nz, 96, D), BF), V((2, nz, 96, D), BF), V((2, 4, 24, D), F32),
               V((5, 8, D), F32), V((3, 24, 1920), F32), V((8, D), F32), V((5, 8, D), F32),
               pltpu.SemaphoreType.DMA((16,)), pltpu.SemaphoreType.DMA((96,)), pltpu.SemaphoreType.DMA((96,))],
        compiler_params=pltpu.CompilerParams(collective_id=3, has_side_effects=True, vmem_limit_bytes=VMEM_LIMIT))(*ins, vin)

def gather_any(q4, ou, dn):
    both = ("dp", "fsdp")
    mine = lax.dynamic_index_in_dim(lax.all_gather(q4, both, axis=0), lax.axis_index("fsdp"), 1, keepdims=False)
    full = lax.all_gather(ou, both, axis=0, tiled=True)
    return mine.reshape(D, D), full[:, :3840], full[:, 3840:], lax.all_gather(dn, both, axis=0, tiled=True)

def body(tokens, qkv_weight, out_weight, up_weight, down_weight, norm_gains, up_bias, pass_table, pass_index, lengths, cotangent):
    rd = qkv_weight.shape[0]
    q4 = jnp.pad(qkv_weight.reshape(rd, 3, 4, 192), ((0, 0), (0, 0), (0, 0), (0, 64))).transpose(2, 0, 1, 3).reshape(4, rd, D)
    chooser = [(jnp.arange(pass_table.shape[1], dtype=jnp.int32) == pass_index[n]).astype(F32) for n in range(2)]
    emb = jnp.stack([jnp.sum(pass_table.astype(F32) * ch[None, :], axis=1) for ch in chooser], axis=1).astype(BF)
    e = jnp.concatenate([norm_gains, emb, up_bias.reshape(rd, 4), jnp.zeros((rd, 120), BF)], axis=1)
    ou = jnp.concatenate([out_weight, up_weight, e], axis=1)
    if rd == 24:
        wq, wou, we, wd = gather(q4, ou, down_weight, lax.axis_size("dp") // 2)
    else:
        wq, wou, we, wd = gather_any(q4, ou, down_weight)
    vecs = we[:, 0:4].T.astype(F32)
    vec = [jnp.concatenate([vecs[0:2], vecs[2 + n:3 + n], jnp.zeros((5, D), F32)], axis=0) for n in range(2)]
    bias = we[:, 4:8].reshape(1, FF).astype(F32)
    row_pos = lax.axis_index("fsdp") * T + jnp.arange(T, dtype=jnp.int32)
    valid = (row_pos < lengths[0]).astype(F32)[:, None]
    xs = [tokens.astype(F32)]; kept = []
    for n in range(2):
        res = fwd(lengths, xs[n], vec[n], bias, wq, wou, wd, 1)
        xs.append(res[0]); kept.append(res[1:])
    block_out = (xs[2] * valid).astype(BF)
    g = cotangent.astype(F32) * valid
    grads = [None, None]; sums = [None, None]; bs = [None, None]
    for n in (1, 0):
        n1, qkv, o, lse, og, r, n2, gp, a = kept[n]
        g, dm, du, da, dqkv, sums[n], bs[n] = bwd(lengths, g, xs[n], vec[n], wq, wou, wd, qkv, o, lse, r, gp, 2)
        grads[n] = (a, dm, n2, du, og, da, n1, dqkv)
    flat = lambda n: [grads_of.reshape(S, D) if k == 6 else grads_of for k, grads_of in enumerate(grads[n])]
    vin = jnp.concatenate([sums[0][0:2] + sums[1][0:2], sums[0][2:3], sums[1][2:3], (bs[0] + bs[1]).reshape(4, D)], axis=0)
    f = lax.axis_index("fsdp")
    if rd == 24:
        down_grad, out_grad, up_grad, q_grad, tot = grads_sum(flat(0), flat(1), vin, lax.axis_size("dp") // 2)
    else:
        down_grad, out_grad, up_grad, q_grad, tot = grads_any(flat(0), flat(1), vin, rd)
    qkv_grad = q_grad.reshape(4, rd, 3, 256)[..., :192].transpose(1, 2, 0, 3).reshape(rd, 3 * D)
    idx = lax.axis_index("dp") * 4 + f
    own = lambda v: lax.dynamic_slice_in_dim(v, idx * rd, rd, 0)
    gains = own(tot[0:2].T)
    table = own(tot[2])[:, None] * chooser[0][None] + own(tot[3])[:, None] * chooser[1][None]
    bias_grad = lax.dynamic_slice_in_dim(tot[4:8].reshape(FF), idx * rd * 4, rd * 4, 0)
    return (block_out, g, qkv_grad, out_grad, up_grad, down_grad, gains, bias_grad, table)

def grads_any(kept0, kept1, vin, rd):
    both = ("dp", "fsdp")
    a, dm, n2, du, og, da, n1, dq = [jnp.concatenate([u, v], axis=0) for u, v in zip(kept0, kept1)]
    heads = og.reshape(2, 4, T, 256)[..., :192].transpose(0, 2, 1, 3).reshape(2 * T, D)
    scatter = lambda v: lax.psum_scatter(v, both, scatter_dimension=0, tiled=True)
    q = tn(n1, dq).reshape(-1, 4, rd, D)
    place_q = lax.dynamic_update_slice(jnp.zeros((4,) + (D // rd, rd, D), F32), q.reshape(1, D // rd, rd, D), (lax.axis_index("fsdp"), 0, 0, 0))
    q_grad = lax.psum_scatter(place_q, both, scatter_dimension=1, tiled=True).reshape(4, rd, D)
    return scatter(tn(a, dm)), scatter(tn(heads, da)), scatter(tn(n2, du)), q_grad, lax.psum(vin, both)

def solution(mesh):
    a = P(("dp", "fsdp"), None); b = P(("dp", "fsdp"))
    return jax.shard_map(body, mesh=mesh, in_specs=(a, a, a, a, a, a, b, a, P(), P("dp"), a), out_specs=(a, a, a, a, a, a, a, b, a), check_vma=False)
```

```python
from functools import partial
import jax
import jax.numpy as jnp
from jax import lax
from jax.experimental import pallas as pl
from jax.experimental.pallas import tpu as pltpu
from jax.sharding import PartitionSpec as P
BF=jnp.bfloat16; F32=jnp.float32
MESH = pl.DeviceIdType.MESH
NEG = -1e30
QB = 512
VMEM_LIMIT = 62 * 2**20

def remote(src, dst, ssem, rsem, dev):
    return pltpu.make_async_remote_copy(src_ref=src, dst_ref=dst, send_sem=ssem, recv_sem=rsem, device_id=dev, device_id_type=MESH)

def rows_at(start, count, step=16):
    return pl.ds(pl.multiple_of(start, step), count)

def normed(values):
    center = values - jnp.mean(values, axis=-1, keepdims=True)
    spread = jnp.mean(center * center, axis=-1, keepdims=True)
    scale = lax.rsqrt(spread + 1e-05)
    return center * scale, scale

def norm_back(xhat, scale, grad_out, gain):
    eg = grad_out * gain
    first = jnp.mean(eg, axis=-1, keepdims=True)
    second = jnp.mean(eg * xhat, axis=-1, keepdims=True)
    return scale * (eg - first - xhat * second)

def nt(left, right):
    return lax.dot_general(left, right, (((1,), (1,)), ((), ())), preferred_element_type=F32)

def dot(left, right):
    return jnp.dot(left, right, preferred_element_type=F32)

def mask_scores(sT, i, limit):
    lo = i * QB
    free = min(lo, 1024)
    parts = []
    if free: parts.append(sT[:free])
    if lo > free:
        kpos = free + lax.broadcasted_iota(jnp.int32, (lo - free, QB), 0)
        parts.append(jnp.where(kpos < limit, sT[free:lo], NEG))
    kpos = lo + lax.broadcasted_iota(jnp.int32, (QB, QB), 0)
    ok = kpos <= lo + lax.broadcasted_iota(jnp.int32, (QB, QB), 1)
    if lo + QB > 1024: ok = ok & (kpos < limit)
    parts.append(jnp.where(ok, sT[lo:], NEG))
    return parts[0] if len(parts) == 1 else jnp.concatenate(parts, 0)

def half_mask(index, h):
    edge = lax.full_like(index, 64)
    return lax.lt(index, edge) if h % 2 == 0 else lax.ge(index, edge)

def pick(xT, h):
    r = lax.broadcasted_iota(jnp.int32, xT.shape, 0)
    mine = half_mask(r, h) if isinstance(h, int) else (r // 64) == (h % 2)
    return jnp.where(mine, xT, jnp.zeros_like(xT))

def slot_of(h, base=0):
    return pl.ds(pl.multiple_of(base + (h // 2) * 128, 128), 128)

def fwd_block(i, qkv, limit, qT, vT, oT, lse):
    keys = (i + 1) * QB
    cols = pl.ds(i * QB, QB)
    def head(h, _):
        hr = pl.ds(pl.multiple_of(h * 64, 64), 64)
        sT = dot(qkv[0:keys, slot_of(h, 256)], pick(qT[slot_of(h), cols], h))
        sT = mask_scores(sT, i, limit)
        m = jnp.max(sT, axis=0, keepdims=True)
        p = jnp.exp(sT - m)
        l = jnp.sum(p, axis=0, keepdims=True)
        oT[hr, cols] = dot(vT[hr, 0:keys], p.astype(BF)) * (1.0 / l)
        lse[pl.ds(h, 1), cols] = m + jnp.log(l)
        return 0
    lax.fori_loop(0, 3, head, 0)

def bwd_block(i, kc, h, qkv, do, lse, limit, qT, kT, doT, dqT, delta, dkv):
    keys, cols = pl.ds(kc * QB, QB), pl.ds(i * QB, QB)
    slot, hr = pl.ds((h // 2) * 128, 128), pl.ds(h * 64, 64)
    after = lambda base: pl.ds(base + (h // 2) * 128, 128)
    lane = lax.broadcasted_iota(jnp.int32, (QB, 128), 1)
    lm = half_mask(lane, h)
    sT = dot(qkv[keys, after(256)], pick(qT[slot, cols], h))
    p = jnp.exp(sT - lse[h:h + 1, cols])
    if kc == i or (kc + 1) * QB > 1024:
        kpos = kc * QB + lax.broadcasted_iota(jnp.int32, (QB, QB), 0)
        ok = kpos < limit
        if kc == i: ok = ok & (kpos <= i * QB + lax.broadcasted_iota(jnp.int32, (QB, QB), 1))
        p = jnp.where(ok, p, 0.0)
    dp = dot(qkv[keys, after(512)], pick(doT[slot, cols], h))
    dsT = (p * (dp - delta[h:h + 1, cols])).astype(BF)
    step = dot(kT[hr, keys], dsT)
    dqT[hr, cols] = step if kc == 0 else dqT[hr, cols] + step
    qn, dn = qkv[cols, slot], do[cols, slot]
    dkv[keys, slot] += dot(dsT, jnp.where(lm, qn, jnp.zeros_like(qn)))
    dkv[keys, after(256)] += dot(p.astype(BF), jnp.where(lm, dn, jnp.zeros_like(dn)))

def group_barrier(d, f):
    bar = pltpu.get_barrier_semaphore()
    for k in (1, 2, 3):
        pl.semaphore_signal(bar, inc=1, device_id=(d, f ^ k), device_id_type=MESH)
    pl.semaphore_wait(bar, 3)

T, D, FF, S = 384, 768, 3072, 1536
CH = 128

def fwd_kernel(lim, x, vec, bias, wq_h, wou_h, wd_h,
               xo_h, n1_h, qkv_h, o_h, lse_h, og_h, r_h, n2_h, gp_h, a_h,
               wq, wou, wd, n1, qkv, qT, vT, oT, o, lse, og, r, n2, gp, a, xo,
               lsem, osem, ssem, rsem):
    d = lax.axis_index("dp"); f = lax.axis_index("fsdp")
    loads = [pltpu.make_async_copy(s, t, lsem.at[i]) for i, (s, t) in enumerate([(wq_h, wq), (wou_h, wou), (wd_h, wd)])]
    for c in loads: c.start()
    group_barrier(d, f)
    stores = []
    def store(src, dst):
        c = pltpu.make_async_copy(src, dst, osem.at[len(stores)])
        c.start(); stores.append(c)
    limit = lim[0]
    g0, g1, emb = vec[0:1, :], vec[1:2, :], vec[2:3, :]
    sends = []
    def send(src, dst, k, dev):
        c = remote(src, dst, ssem.at[k], rsem.at[k], dev)
        c.start(); sends.append(c)
    def got(region, k):
        remote(region, region, ssem.at[k], rsem.at[k], (d, f ^ 1)).wait_recv()
    for j in range(T // CH):
        rows = pl.ds(j * CH, CH)
        xhat, _ = normed(x[rows, :].astype(F32) + emb)
        n1[f, rows, :] = (xhat * g0).astype(BF)
        reg = n1.at[f, rows, :]
        send(reg, reg, j, (d, f ^ 2))
        send(reg, reg, 3 + j, (d, f ^ 1))
    loads[0].wait()
    def project(k):
        def tile(j, _):
            rows = rows_at(j * 192, 192)
            qkv[rows_at(k * T + j * 192, 192), :] = dot(n1[k, rows, :], wq[...]).astype(BF)
            return 0
        lax.fori_loop(0, 2, tile, 0)
    project(f)
    for j in range(3): got(n1.at[f ^ 1, pl.ds(j * CH, CH), :], 3 + j)
    project(f ^ 1)
    for j in range(3):
        reg = n1.at[f ^ 2, pl.ds(j * CH, CH), :]
        got(reg, j)
        send(reg, reg, 6 + j, (d, f ^ 1))
    project(f ^ 2)
    for j in range(3): got(n1.at[f ^ 3, pl.ds(j * CH, CH), :], 6 + j)
    project(f ^ 3)
    store(n1, n1_h); store(qkv, qkv_h)
    qT[...] = (qkv[:, 0:256] * 0.125).astype(BF).T
    vT[...] = qkv[:, 512:768].T
    oT[192:256, :] = jnp.zeros((64, S), F32)
    lse[...] = jnp.zeros_like(lse)
    def finish(b):
        rows = pl.ds(b * T, T)
        o[rows, :] = oT[:, rows].astype(BF).T
        @pl.when(f == b)
        def _(): og[b] = o[rows, :]
        for k in (1, 2, 3):
            @pl.when((f ^ k) == b)
            def _(): remote(o.at[rows, :], og.at[f], ssem.at[8 + k], rsem.at[8 + k], (d, f ^ k)).start()
    for i in reversed(range(S // QB)):
        fwd_block(i, qkv, limit, qT, vT, oT, lse)
        for b in reversed(range(4)):
            if i * QB <= b * T and not (b * T >= (i + 1) * QB): finish(b)
    store(o, o_h); store(lse, lse_h)
    for k in (1, 2, 3): got(og.at[f ^ k], 8 + k)
    store(og, og_h)
    loads[1].wait()
    def out_rows(j, _):
        rows = rows_at(j * 192, 192)
        acc = x[rows, :].astype(F32) + emb
        for k in range(4):
            acc = acc + dot(og[k, rows, 0:192], wou[k * 192:(k + 1) * 192, 0:D])
        r[rows, :] = acc
        xhat, _ = normed(acc)
        n2[rows, :] = (xhat * g1).astype(BF)
        return 0
    lax.fori_loop(0, 2, out_rows, 0)
    store(r, r_h); store(n2, n2_h)
    W = 768
    def up_tile(j, _):
        cols = pl.ds(pl.multiple_of(j * W, 128), W)
        u = dot(n2[...], wou[:, pl.ds(pl.multiple_of(D + j * W, 128), W)]) + bias[:, cols]
        sq = u * u
        t = jnp.tanh(0.7978845608028654 * u * (1.0 + 0.044715 * sq))
        half = 0.5 * (1.0 + t)
        a[:, cols] = (u * half).astype(BF)
        gp[:, cols] = (half + 0.5 * u * (1.0 - t * t) * (0.7978845608028654 * (1.0 + 0.134145 * sq))).astype(BF)
        return 0
    lax.fori_loop(0, FF // W, up_tile, 0)
    store(gp, gp_h); store(a, a_h)
    loads[2].wait()
    def down_tile(j, _):
        cols = pl.ds(pl.multiple_of(j * 256, 128), 256)
        xo[:, cols] = r[:, cols] + dot(a[...], wd[:, cols])
        return 0
    lax.fori_loop(0, D // 256, down_tile, 0)
    store(xo, xo_h)
    for c in sends: c.wait_send()
    for k in (1, 2, 3): remote(o.at[pl.ds(0, T), :], og.at[f], ssem.at[8 + k], rsem.at[8 + k], (d, f ^ k)).wait_send()
    for c in stores: c.wait()

def fwd(lim, x, vec, bias, wq, wou, wd, cid):
    Z = jax.ShapeDtypeStruct
    hbm = pl.BlockSpec(memory_space=pltpu.HBM); vm = pl.BlockSpec(memory_space=pltpu.VMEM); sm = pl.BlockSpec(memory_space=pltpu.SMEM)
    V = pltpu.VMEM
    outs = [((T, D), F32), ((4, T, D), BF), ((S, D), BF), ((S, 256), BF), ((8, S), F32), ((4, T, 256), BF), ((T, D), F32), ((T, D), BF), ((T, FF), BF), ((T, FF), BF)]
    return pl.pallas_call(fwd_kernel, out_shape=[Z(*s) for s in outs],
        in_specs=[sm, vm, vm, vm, hbm, hbm, hbm], out_specs=[hbm] * len(outs),
        scratch_shapes=[V((D, D), BF), V((D, 3840), BF), V((FF, D), BF), V((4, T, D), BF), V((S, D), BF), V((256, S), BF), V((256, S), BF), V((256, S), F32),
            V((S, 256), BF), V((8, S), F32), V((4, T, 256), BF), V((T, D), F32), V((T, D), BF), V((T, FF), BF), V((T, FF), BF), V((T, D), F32),
            pltpu.SemaphoreType.DMA((3,)), pltpu.SemaphoreType.DMA((16,)), pltpu.SemaphoreType.DMA((12,)), pltpu.SemaphoreType.DMA((12,))],
        compiler_params=pltpu.CompilerParams(collective_id=cid, has_side_effects=True, vmem_limit_bytes=VMEM_LIMIT))(lim, x, vec, bias, wq, wou, wd)


ZERO = [None]

def at(ref, *index):
    return ref.at[tuple(ZERO[0] + i if isinstance(i, int) else i for i in index)]

def tn(left, right):
    return lax.dot_general(left, right, (((0,), (0,)), ((), ())), preferred_element_type=F32)

def when(pred, act):
    if pred is None: act()
    else: pl.when(pred)(act)

class Links:
    def __init__(self, ssem, rsem, dev):
        self.ssem, self.rsem, self.dev, self.n, self.sent = ssem, rsem, dev, 0, []
    def sem(self):
        self.n += 1
        return self.n - 1
    def send(self, src, dst, k, dev, pred=None):
        when(pred, remote(src, dst, at(self.ssem, k), at(self.rsem, k), dev).start)
        self.sent.append((pred, src, k))
    def got(self, region, k, pred=None):
        when(pred, remote(region, region, at(self.ssem, k), at(self.rsem, k), self.dev).wait_recv)
    def close(self):
        for pred, src, k in self.sent:
            base = getattr(src, "ref", src)
            like = at(base, *([0] * (len(base.shape) - len(src.shape)) + [pl.ds(0, n) for n in src.shape]))
            when(pred, remote(like, like, at(self.ssem, k), at(self.rsem, k), self.dev).wait_send)
        self.sent = []

PLAN = (
    (), ("a3", "b3"), ("a0", "b0"), ("a2", "b2"), ("a3", "b3", "a1", "b1"), (), ("a0", "b0"), (), ("a3", "b3", "a2", "b2", "a1", "b1"),
    ("a3", "a0", "b0", "b2"), ("a3", "b3", "a0", "b0", "a2", "b2", "b1", "p3", "p0", "p2", "p1", "o3", "o0", "o2", "o1", "a3", "b3", "a0", "a2", "a1"),
    (), (), ("b0", "b2"), ("b1",), ("b3",), ("a0", "a2"), (), ("b0", "o3", "b1"), ("p3", "p0"), (), (), (), ("o3", "o0"), ("p2",), (), (),
    ("p3", "p0"), ("o0", "o2"), ("p1",), ("a1",), ("p2",), (), ("o3", "o0", "o2", "o1", "p3"), ("p0",),
    ("a1", "p1", "o3", "o2", "o1", "G", "q3", "q0", "q2", "q1", "o0", "pe"),
    ("o3", "o2", "o1", "G", "q3", "q0", "r3", "r0", "r2", "r1", "o0", "G", "V", "q2"),
    ("V", "q1", "q3", "q0", "o1", "V", "pe", "r3", "r0", "q3", "q0", "V", "pe", "r2", "q3", "q0", "r3", "r0", "r1", "q2", "r2", "q1", "V", "r3", "r0", "q2", "r1", "re", "q1", "V", "re", "V"),
)

class Agenda:
    def __init__(self, plan): self.plan, self.jobs, self.point = plan, {}, 0
    def add(self, name, job): self.jobs[name] = job
    def step(self, name):
        if next(self.jobs[name], self) is self: del self.jobs[name]
    def run(self, hold=False):
        names = self.plan[self.point] if self.point < len(self.plan) else ()
        self.point += 1
        for name in names: self.step(name)
    def finish(self):
        for name in self.plan[self.point] if self.point < len(self.plan) else (): self.step(name)
        while self.jobs:
            for name in list(self.jobs): self.step(name)

def add_to(acc, inc):
    acc[...] = (acc[...].astype(F32) + inc[...].astype(F32)).astype(BF)

class Copies:
    def __init__(self, sems): self.sems, self.n = sems, 0
    def go(self, src, dst):
        copy = pltpu.make_async_copy(src, dst, at(self.sems, self.n))
        self.n += 1
        copy.start()
        return copy

def turns(nz):
    out, lo, hi = [], 0, nz - 1
    while lo <= hi:
        out += [hi, lo] if lo < hi else [lo]
        lo, hi = lo + 1, hi - 1
    return out

def place():
    d = lax.axis_index("dp"); f = lax.axis_index("fsdp")
    return d, f, d // 2, d % 2, f // 2, f % 2

def wide_barrier(nz):
    d, f, z, y, x, c = place()
    bar = pltpu.get_barrier_semaphore()
    for dev in ((d, f ^ 1), (d, f ^ 2), (d, f ^ 3), (d ^ 1, f)):
        pl.semaphore_signal(bar, inc=1, device_id=dev, device_id_type=MESH)
    @pl.when(z > 0)
    def _(): pl.semaphore_signal(bar, inc=1, device_id=(d - 2, f), device_id_type=MESH)
    @pl.when(z < nz - 1)
    def _(): pl.semaphore_signal(bar, inc=1, device_id=(d + 2, f), device_id_type=MESH)
    pl.semaphore_wait(bar, 4 + (z > 0).astype(jnp.int32) + (z < nz - 1).astype(jnp.int32))

D_PIECES = (("a", "yxz", 0, 384), ("b", "xyz", 384, 768))
W_PIECES = (("p", "zyx", 1280, 1920), ("o", "xyz", 0, 1280))
Q_PIECES = (("q", "yz", 0, 384), ("r", "zy", 384, 768))

class Piece:
    def __init__(self, name, order, rows, cols, nz, pair=True):
        self.name, self.order, self.rows, self.cols, self.nz, self.pair = name, order, rows, cols, nz, pair
        self.nx = 2 if pair else 1
    def live(self, done):
        return ((2,) if "y" not in done else ()) + ((self.nx,) if "x" not in done else ()) + (self.rows, self.cols)
    def buffers(self):
        out = {"acc": (self.nz, 2, self.nx, self.rows, self.cols)}
        if self.pair: out["stg"] = out["sib"] = out["acc"]
        done = ""
        for axis in self.order:
            if axis == "z": out["z"] = (2, self.nz) + self.live(done)
            else: out[axis] = (() if "z" in done else (self.nz,)) + self.live(done + axis)
            done += axis
        return {self.name + k: (s, BF) for k, s in out.items()}
    def bind(self, bufs, s):
        self.s, self.net, self.agenda = s, s.net, s.agenda
        self.b = {k[len(self.name):]: v for k, v in bufs.items() if k.startswith(self.name) and k[len(self.name):] in ("acc", "stg", "sib", "x", "y", "z")}
        self.sems, self.flows, self.done = {}, 0, False
        return self
    def view(self, t, done, other=""):
        s = self.s
        ys = pl.ds(0, 2) if "y" not in done else 1 - s.y if other == "y" else s.y
        xs = pl.ds(0, self.nx) if "x" not in done else 1 - s.x if other == "x" else s.x
        return at(self.b["acc"], t, ys, xs)
    def start(self, t):
        if self.pair:
            self.sems[t] = self.net.sem()
            self.net.send(at(self.b["stg"], t), at(self.b["sib"], t), self.sems[t], self.s.sp)
        self.agenda.add(self.name + str(t), self.plane(t))
    def exchange(self, axis, t, done):
        k = self.net.sem()
        self.net.send(self.view(t, done + axis, axis), self.inbox(axis, t, done), k, self.s.xp if axis == "x" else self.s.yp)
        return k
    def inbox(self, axis, t, done):
        return self.b[axis] if "z" in done else at(self.b[axis], t)
    def plane(self, t):
        if self.pair:
            self.net.got(at(self.b["sib"], t), self.sems[t])
            add_to(at(self.b["acc"], t), at(self.b["sib"], t))
        done = ""
        for axis in self.order:
            if axis == "z": break
            k = self.exchange(axis, t, done)
            done += axis
            yield
            buf = self.inbox(axis, t, done)
            self.net.got(buf, k)
            add_to(self.view(t, done), buf)
        yield from self.flow(t, done)
        self.flows += 1
        if self.flows == self.nz:
            if self.order[-1] == "z": self.done = True
            else: self.agenda.add(self.name + "e", self.rest())
    def flow(self, t, done):
        nz, s, ks, recv = self.nz, self.s, (self.net.sem(), self.net.sem()), self.b["z"]
        far = max(t, nz - 1 - t)
        for h in range(far):
            if h: yield
            for way, total, here, dev in ((0, t, s.is_z[h], s.up), (1, nz - 1 - t, s.is_z[nz - 1 - h], s.down)):
                if h < total:
                    inc = at(recv, way, t)
                    if h:
                        self.net.got(inc, ks[way], here)
                        pl.when(here)(lambda inc=inc: add_to(self.view(t, done), inc))
                    self.net.send(self.view(t, done), inc, ks[way], dev, here)
        yield
        if t > 0: self.net.got(at(recv, 0, t), ks[0], s.is_z[t])
        if t < nz - 1: self.net.got(at(recv, 1, t), ks[1], s.is_z[t])
    def rest(self):
        s, i = self.s, self.order.index("z")
        done = self.order[:i + 1]
        own = self.view(s.z, done)
        for pred, way in ((s.has_below, 0), (s.has_above, 1)):
            pl.when(pred)(lambda way=way: add_to(own, at(self.b["z"], way, s.z)))
        for axis in self.order[i + 1:]:
            k = self.exchange(axis, s.z, done)
            done += axis
            yield
            buf = self.inbox(axis, s.z, done)
            self.net.got(buf, k)
            if axis != self.order[-1]: add_to(self.view(s.z, done), buf)
        self.done = True
    def total(self):
        assert self.done
        s, last = self.s, self.order[-1]
        sum_ = self.b["acc"][s.z, s.y, s.x if self.pair else 0].astype(F32)
        if last != "z": return sum_ + self.b[last][...].astype(F32).reshape(sum_.shape)
        for pred, way in ((s.has_below, 0), (s.has_above, 1)):
            sum_ = sum_ + jnp.where(pred, self.b["z"][way, s.z].astype(F32).reshape(sum_.shape), 0.0)
        return sum_

class Sums:
    def __init__(self, nz, net, agenda, bufs, outs, vin):
        self.nz, self.net, self.agenda, self.b, self.o, self.vin = nz, net, agenda, bufs, outs, vin
        self.d, self.f, self.z, self.y, self.x, self.c = place()
        d, f = self.d, self.f
        self.up, self.down = (d + 2, f), (d - 2, f)
        self.yp, self.xp, self.sp = (d ^ 1, f), (d, f ^ 2), (d, f ^ 1)
        self.turn = turns(nz)
        z = self.z
        self.is_z = [z == h for h in range(nz)]
        self.has_below, self.has_above, self.core0 = z > 0, z < nz - 1, self.c == 0
        self.D, self.W, self.Q = [[p.bind(bufs, self) for p in ps] for ps in pieces(nz)]
    def first(self, v): return jnp.where(self.core0, v[0], v[1])
    def second(self, v): return jnp.where(self.core0, v[1], v[0])
    def cols(self, ref, width, off, n, mine, rows=None):
        cc = self.c if mine else 1 - self.c
        return ref[slice(None) if rows is None else rows, pl.ds(pl.multiple_of(cc * width + off, 128), n)]

    def vectors(self):
        net, b, z, nz = self.net, self.b, self.z, self.nz
        vb, vr, hop = b["vb"], b["vr"], b["hop"]
        vb[...] = self.vin()
        for i, dev in enumerate((self.sp, self.xp, self.yp)):
            k = net.sem()
            hop[i] = vb[...]
            net.send(at(hop, i), at(vr, i), k, dev)
            yield
            net.got(at(vr, i), k)
            vb[...] += vr[i]
        for i in (3, 4): hop[i] = vb[...]
        ks = [net.sem(), net.sem()]
        for step in range(nz - 1):
            if step: yield
            for way, here, dev in ((0, self.is_z[step], self.up), (1, self.is_z[nz - 1 - step], self.down)):
                if step:
                    net.got(at(vr, 3 + way), ks[way], here)
                    @pl.when(here)
                    def _(way=way): hop[3 + way] += vr[3 + way]
                net.send(at(hop, 3 + way), at(vr, 3 + way), ks[way], dev, here)
        yield
        for way, last, some in ((0, self.is_z[nz - 1], self.has_below), (1, self.is_z[0], self.has_above)):
            net.got(at(vr, 3 + way), ks[way], last)
            @pl.when(some)
            def _(way=way): vb[...] += vr[3 + way]
        self.o["v"][...] = vb[...]

    def down_tile(self, t, g):
        g = g.reshape(2, 2, 2, 96, D)
        for p, (_, _, c0, c1) in zip(self.D, D_PIECES):
            for y in range(2):
                for x in range(2):
                    p.b["acc"][t, y, x] = self.first(g[y, x, :, :, c0:c1]).astype(BF)
                    p.b["stg"][t, y, x] = self.second(g[y, x, :, :, c0:c1]).astype(BF)
            p.start(t)
    def wide_piece(self, p, c0, c1, n2, du, og, da):
        for dst, mine in (("acc", True), ("stg", False)):
            if c0 < 384:
                n = min(c1, 384) - c0
                for j in range(4):
                    g = sum(tn(og[k, j, :, 0:192], self.cols(da, 384, c0, n, mine, pl.ds(k * T, T))) for k in range(2))
                    p.b[dst][j * self.nz // 4:(j + 1) * self.nz // 4, :, :, :, 0:n] = g.astype(BF).reshape(self.nz // 4, 2, 2, 48, n)
            if c1 > 384:
                lo = max(c0, 384)
                g = tn(n2[...], self.cols(du, 1536, lo - 384, c1 - lo, mine))
                p.b[dst][:, :, :, :, lo - c0:c1 - c0] = g.astype(BF).reshape(self.nz, 2, 2, 48, c1 - lo)
        for t in self.turn: p.start(t)
    def q_piece(self, p, c0, c1, n1s, dqs):
        for j in range(2):
            g = sum(tn(n1[:, j * 384:(j + 1) * 384], dq[:, c0:c1]) for n1, dq in zip(n1s, dqs))
            p.b["acc"][j * self.nz // 2:(j + 1) * self.nz // 2] = g.astype(BF).reshape(self.nz // 2, 2, 1, 96, c1 - c0)
        for t in self.turn: p.start(t)
    def ends(self):
        net, half, c, f, qf = self.net, self.b["half"], self.c, self.f, self.b["qf"]
        for p, (_, _, c0, c1) in zip(self.W, W_PIECES):
            total = p.total()
            half[0, :, c0:c1] = self.first((total[0:24], total[24:48]))
            half[1, :, c0:c1] = self.second((total[0:24], total[24:48]))
        kw = net.sem()
        net.send(at(half, 1), at(half, 2), kw, self.sp)
        for p, (_, _, c0, c1) in zip(self.Q, Q_PIECES):
            total = p.total()
            for j in range(4): qf[0, j, :, c0:c1] = total[j * 24:(j + 1) * 24]
        ks = [net.sem() for _ in range(4)]
        for k in (1, 2, 3):
            net.send(at(qf, 0, f ^ k), at(qf, 1, f), ks[k], (self.d, f ^ k))
        self.o["qkv"][f] = qf[0, f]
        for p, (_, _, c0, c1) in zip(self.D, D_PIECES):
            self.o["down"][:, c0:c1] = p.total()
        net.got(at(half, 2), kw)
        for cc, s in ((c, 0), (1 - c, 2)):
            self.o["outw"][:, pl.ds(pl.multiple_of(cc * 384, 128), 384)] = half[s, :, 0:384]
            self.o["up"][:, pl.ds(pl.multiple_of(cc * 1536, 128), 1536)] = half[s, :, 384:1920]
        for k in (1, 2, 3):
            net.got(at(qf, 1, f ^ k), ks[k])
            self.o["qkv"][f ^ k] = qf[1, f ^ k]

def pieces(nz):
    return ([Piece(n, o, 96, c1 - c0, nz) for n, o, c0, c1 in D_PIECES], [Piece(n, o, 48, c1 - c0, nz) for n, o, c0, c1 in W_PIECES],
            [Piece(n, o, 96, c1 - c0, nz, False) for n, o, c0, c1 in Q_PIECES])

def sum_buffers(nz):
    out = dict(qf=((2, 4, 24, D), F32), hop=((5, 8, D), F32), half=((3, 24, 1920), F32), vb=((8, D), F32), vr=((5, 8, D), F32))
    for group in pieces(nz):
        for p in group: out.update(p.buffers())
    return out

def bwd_kernel(last, nz, names, *refs):
    r_ = dict(zip(names, refs))
    R = lambda *ns: [r_[n] for n in ns]
    lim, vec, g_h, x_h, wq_h, wou_h, wd_h, qkv_h, o_h, lse_h, r_h, gp_h = R("lim", "vec", "g", "x", "wq", "wou", "wd", "qkv", "o", "lse", "r", "gp")
    dos, do, mine, part, inc, go, dr, dqkv, sums, bsum = R("dos", "do", "mine", "part", "inc", "go_v", "dr", "dqkv_v", "sums", "bsum")
    d = lax.axis_index("dp"); f = lax.axis_index("fsdp")
    ZERO[0] = f * 0
    mem = Copies(r_["lsem"])
    net = Links(r_["ssem"], r_["rsem"], (d, f ^ 1))
    agenda = Agenda(PLAN if last and nz == 4 else ())
    limit = lim[0]
    g0, g1, emb = vec[0:1, :], vec[1:2, :], vec[2:3, :]
    W = 768
    V = pltpu.VMEM
    N = 2 * T if last else T
    if last:
        gs = Sums(nz, net, agenda, r_, dict(v=r_["v_o"], down=r_["down_o"], outw=r_["outw_o"], up=r_["up_o"], qkv=r_["qkv_o"]), None)
        sums1, bsum1 = r_["sums_1"], r_["bsum_1"]
        def all_sums():
            bias = [bsum[:, j * D:(j + 1) * D] + bsum1[:, j * D:(j + 1) * D] for j in range(4)]
            return jnp.concatenate([sums[0:2, :] + sums1[0:2, :], sums[2:3, :], sums1[2:3, :]] + bias, axis=0)
        gs.vin = all_sums
    g_in = mem.go(g_h, dr)
    sums[...] = jnp.zeros_like(sums)

    def phase1(du, dm, da):
        def phase1a(a, wd, gp):
            lw, lg = mem.go(wd_h, wd), mem.go(gp_h, gp)
            if last:
                la = [mem.go(r_["a_0"], at(a, pl.ds(0, T))), mem.go(r_["a_1"], at(a, pl.ds(T, T))), mem.go(r_["dm_1"], at(dm, pl.ds(T, T)))]
                late = [mem.go(r_["du_1"], at(du, pl.ds(T, T))), mem.go(r_["da_1"], at(da, pl.ds(T, T)))]
            if last: wide_barrier(nz)
            else: group_barrier(d, f)
            g_in.wait()
            dm[0:T, :] = dr[...].astype(BF)
            if last:
                for c in la: c.wait()
                for t in gs.turn:
                    gs.down_tile(t, tn(a[:, t * W:(t + 1) * W], dm[...]))
                    agenda.run()
            out = [] if last else [mem.go(dm, r_["dm_o"])]
            lw.wait(); lg.wait()
            for j in range(FF // W):
                cols = pl.ds(j * W, W)
                t = (nt(dm[0:T, :], wd[cols, :]) * gp[:, cols].astype(F32)).astype(BF)
                du[0:T, cols] = t
                bsum[:, cols] = jnp.sum(t.astype(F32), axis=0, keepdims=True)
                agenda.run()
            if not last: out.append(mem.go(du, r_["du_o"]))
            for c in out: c.wait()
            if last:
                for c in late: c.wait()
        if last: pl.run_scoped(phase1a, V((N, FF), BF), V((FF, D), BF), V((T, FF), BF))
        else: pl.run_scoped(partial(phase1a, None), V((FF, D), BF), V((T, FF), BF))

        def phase1b(wou, r, n2, og):
            lr, lw = mem.go(r_h, r), mem.go(wou_h, wou)
            if last:
                late = [mem.go(r_["n2_0"], at(n2, pl.ds(0, T))), mem.go(r_["n2_1"], at(n2, pl.ds(T, T))), mem.go(r_["og_0"], at(og, 0)), mem.go(r_["og_1"], at(og, 1))]
            lr.wait(); lw.wait()
            def norm2(j, _):
                rows = rows_at(j * 128, 128)
                e = nt(du[rows, :], wou[:, D:])
                xhat, scale = normed(r[rows, :])
                sums[1:2, :] += jnp.sum(e * xhat, axis=0, keepdims=True)
                t = dr[rows, :] + norm_back(xhat, scale, e, g1)
                dr[rows, :] = t
                da[rows, :] = t.astype(BF)
                return 0
            lax.fori_loop(0, T // 128, norm2, 0)
            out = [] if last else [mem.go(da, r_["da_o"])]
            for k in (3, 2, 1, 0):
                b = f ^ k
                dos[b, :, 0:192] = nt(da[0:T, :], wou[rows_at(b * 192, 192), 0:D]).astype(BF)
                dos[b, :, 192:256] = jnp.zeros((T, 64), BF)
                if k: net.send(at(dos, b), at(do, rows_at(f * T, T)), do_sems[k], (d, b))
                else: do[rows_at(f * T, T), :] = dos[b]
            if last:
                agenda.run()
                for c in late: c.wait()
                for p, (_, _, c0, c1) in zip(gs.W, W_PIECES):
                    gs.wide_piece(p, c0, c1, n2, du, og, da)
                    agenda.run()
            for c in out: c.wait()
        if last: pl.run_scoped(phase1b, V((D, 3840), BF), V((T, D), F32), V((N, D), BF), V((2, 4, T, 256), BF))
        else: pl.run_scoped(lambda w, r: phase1b(w, r, None, None), V((D, 3840), BF), V((T, D), F32))
    do_sems = [net.sem() for _ in range(4)]
    pl.run_scoped(phase1, V((N, FF), BF), V((N, D), BF), V((N, D), BF))

    def phase2(qkv, o, lse, qT, kT, doT, dqT, delta, dkv):
        loads = [mem.go(*p) for p in ((qkv_h, qkv), (o_h, o), (lse_h, lse))]
        dkv[...] = jnp.zeros_like(dkv)
        dqT[192:256, :] = jnp.zeros((64, S), F32)
        agenda.run()
        for c in loads: c.wait()
        qT[...] = (qkv[:, 0:256] * 0.125).astype(BF).T
        kT[...] = qkv[:, 256:512].T
        agenda.run(hold=True)
        for k in (1, 2, 3): net.got(at(do, rows_at((f ^ k) * T, T)), do_sems[k])
        doT[...] = do[...].T
        prod = (do[...].astype(F32) * o[...].astype(F32)).T
        for h in range(3):
            delta[h:h + 1, :] = jnp.sum(prod[h * 64:h * 64 + 64], axis=0, keepdims=True)
        for i in range(S // QB):
            for kc in range(i + 1):
                for h in range(3):
                    bwd_block(i, kc, h, qkv, do, lse, limit, qT, kT, doT, dqT, delta, dkv)
                    agenda.run()
        dqkv[:, 0:256] = (dqT[...] * 0.125).astype(BF).T
        dqkv[:, 256:512] = (dkv[:, 0:256] * 0.125).astype(BF)
        dqkv[:, 512:768] = dkv[:, 256:512].astype(BF)
    pl.run_scoped(phase2, V((S, D), BF), V((S, 256), BF), V((8, S), F32), V((256, S), BF), V((256, S), BF), V((256, S), BF), V((256, S), F32), V((8, S), F32), V((S, 512), F32))

    def phase3(wq, x, n1a, n1b, dq1):
        lw, lx = mem.go(wq_h, wq), mem.go(x_h, x)
        if last:
            late = [mem.go(r_["n1_0"], n1a), mem.go(r_["n1_1"], n1b), mem.go(r_["dq_1"], dq1)]
        out = [] if last else [mem.go(dqkv, r_["dqkv_o"])]
        lw.wait()
        def partial_rows(b, j):
            return nt(dqkv[rows_at(b * T + j * CH, CH), :], wq[...])
        k0, k1, k2 = [[net.sem() for _ in range(3)] for _ in range(3)]
        for j in range(3):
            rows = pl.ds(j * CH, CH)
            mine[0, rows, :] = partial_rows(f ^ 3, j).astype(BF)
            net.send(at(mine, 0, rows), at(part, 0, rows), k0[j], (d, f ^ 1))
        for j in range(3):
            rows = pl.ds(j * CH, CH)
            t = partial_rows(f ^ 2, j)
            agenda.run(hold=True)
            net.got(at(part, 0, rows), k0[j])
            inc[rows, :] = (t + part[0, rows, :].astype(F32)).astype(BF)
            net.send(at(inc, rows), at(part, 2, rows), k2[j], (d, f ^ 2))
        for j in range(3):
            rows = pl.ds(j * CH, CH)
            mine[1, rows, :] = partial_rows(f ^ 1, j).astype(BF)
            net.send(at(mine, 1, rows), at(part, 1, rows), k1[j], (d, f ^ 1))
        for j in range(3):
            rows = pl.ds(j * CH, CH)
            go[rows, :] = partial_rows(f, j)
        lx.wait()
        def finish_rows():
            for j in range(3):
                rows = pl.ds(j * CH, CH)
                net.got(at(part, 1, rows), k1[j])
                net.got(at(part, 2, rows), k2[j])
                e = go[rows, :] + part[1, rows, :].astype(F32) + part[2, rows, :].astype(F32)
                xhat, scale = normed(x[rows, :].astype(F32) + emb)
                sums[0:1, :] += jnp.sum(e * xhat, axis=0, keepdims=True)
                t = dr[rows, :] + norm_back(xhat, scale, e, g0)
                sums[2:3, :] += jnp.sum(t, axis=0, keepdims=True)
                go[rows, :] = t
                if j < 2: yield
            out.append(mem.go(go, r_["go_o"]))
            if last: agenda.add("V", gs.vectors())
        agenda.add("G", finish_rows())
        if last:
            agenda.run()
            for c in late: c.wait()
            for p, (_, _, c0, c1) in zip(gs.Q, Q_PIECES):
                gs.q_piece(p, c0, c1, (n1a, n1b), (dqkv, dq1))
                agenda.run()
        agenda.finish()
        if last:
            gs.ends()
        for c in out: c.wait()
    if last: pl.run_scoped(phase3, V((D, D), BF), V((T, D), F32), V((S, D), BF), V((S, D), BF), V((S, D), BF))
    else: pl.run_scoped(lambda w, x: phase3(w, x, None, None, None), V((D, D), BF), V((T, D), F32))
    net.close()

def bwd(lim, g, x, vec, wq, wou, wd, kept, cid, last=None, nz=None):
    n1, qkv, o, lse, og, r, n2, gp, a = kept
    hbm = pl.BlockSpec(memory_space=pltpu.HBM); vm = pl.BlockSpec(memory_space=pltpu.VMEM); sm = pl.BlockSpec(memory_space=pltpu.SMEM)
    ins = dict(lim=lim, vec=vec, g=g, x=x, wq=wq, wou=wou, wd=wd, qkv=qkv, o=o, lse=lse, r=r, gp=gp)
    outs = dict(go_o=((T, D), F32), sums=((8, D), F32), bsum=((1, FF), F32))
    if last is None:
        outs.update(dm_o=((T, D), BF), du_o=((T, FF), BF), da_o=((T, D), BF), dqkv_o=((S, D), BF))
    else:
        ins.update(last)
        ins.update(a_0=a, n2_0=n2, og_0=og, n1_0=n1)
        outs.update(down_o=((96, D), F32), outw_o=((24, D), F32), up_o=((24, FF), F32), qkv_o=((4, 24, D), F32), v_o=((8, D), F32))
    scratch = dict(dos=((4, T, 256), BF), do=((S, 256), BF), mine=((2, T, D), BF), part=((3, T, D), BF), inc=((T, D), BF), go_v=((T, D), F32), dr=((T, D), F32), dqkv_v=((S, D), BF))
    if last is not None: scratch.update(sum_buffers(nz))
    sems = 320 if last is not None else 16
    names = list(ins) + list(outs) + list(scratch) + ["lsem", "ssem", "rsem"]
    place_of = lambda n: sm if n == "lim" else vm if n in ("vec", "sums", "bsum", "sums_1", "bsum_1", "down_o", "outw_o", "up_o", "qkv_o", "v_o") else hbm
    res = pl.pallas_call(partial(bwd_kernel, last is not None, nz, names),
        out_shape=[jax.ShapeDtypeStruct(*s) for s in outs.values()],
        in_specs=[place_of(n) for n in ins], out_specs=[place_of(n) for n in outs],
        scratch_shapes=[pltpu.VMEM(*s) for s in scratch.values()] + [pltpu.SemaphoreType.DMA((32,)), pltpu.SemaphoreType.DMA((sems,)), pltpu.SemaphoreType.DMA((sems,))],
        compiler_params=pltpu.CompilerParams(collective_id=cid, has_side_effects=True, vmem_limit_bytes=VMEM_LIMIT))(*ins.values())
    return dict(zip(outs, res))

def gather_kernel(nz, q4, ou, dn, wq, wou, we, wd, rq, rou, blk, blkq, local, ssem, rsem):
    d, f, z, y, x, c = place()
    q = z * 4 + y * 2 + x
    up, down = (d + 2, f), (d - 2, f)
    yp, xp, sp = (d ^ 1, f), (d, f ^ 2), (d, f ^ 1)
    bar = pltpu.get_barrier_semaphore()
    for dev in (sp, xp, (d, f ^ 3), yp):
        pl.semaphore_signal(bar, inc=1, device_id=dev, device_id_type=MESH)
    @pl.when(z > 0)
    def _(): pl.semaphore_signal(bar, inc=1, device_id=down, device_id_type=MESH)
    @pl.when(z < nz - 1)
    def _(): pl.semaphore_signal(bar, inc=1, device_id=up, device_id_type=MESH)
    pl.semaphore_wait(bar, 4 + (z > 0).astype(jnp.int32) + (z < nz - 1).astype(jnp.int32))

    sends = []
    def go(copy, pred=None):
        if pred is None:
            copy.start()
        else:
            pl.when(pred)(copy.start)
        sends.append((pred, copy))
    def got(region, sem, pred=None):
        w = remote(region, region, ssem.at[0], sem, sp)
        if pred is None: w.wait_recv()
        else: pl.when(pred)(w.wait_recv)

    n = [0]
    def sem():
        n[0] += 1
        return ssem.at[n[0] - 1], rsem.at[n[0] - 1]
    s_ou = sem(); go(remote(ou, rou, *s_ou, sp))
    s_q = [sem() for _ in range(4)]
    for k in range(1, 4):
        dst = f ^ k
        go(remote(q4.at[dst], rq.at[f], s_q[k][0], rsem.at[n[0] - 4 + k], (d, dst)))
    own_dn = wd.at[pl.ds(pl.multiple_of((q * 2 + c) * 96, 16), 96), :]
    s_dn = sem(); go(remote(dn, own_dn, *s_dn, sp))
    loc = [pltpu.make_async_copy(dn, own_dn, local.at[0])]
    loc[0].start()
    rq[f] = q4[f]
    got(rou, s_ou[1])
    mine, other = ou[...].astype(F32), rou[...].astype(F32)
    blk[...] = jnp.concatenate([jnp.where(c == 0, mine, other), jnp.where(c == 0, other, mine)], axis=0).astype(BF)
    row = pl.ds(pl.multiple_of(q * 48, 16), 48)
    l1 = pltpu.make_async_copy(blk.at[:, pl.ds(0, 3840)], wou.at[row, :], local.at[1]); l1.start()
    l2 = pltpu.make_async_copy(blk.at[:, pl.ds(3840, 128)], we.at[row, :], local.at[2]); l2.start()
    for k in range(1, 4):
        got(rq.at[f ^ k], s_q[k][1])
    blkq[...] = jnp.concatenate([rq[k].astype(F32) for k in range(4)], axis=0).astype(BF)
    l3 = pltpu.make_async_copy(blkq, wq.at[pl.ds(pl.multiple_of(d * 96, 16), 96), :], local.at[3]); l3.start()
    l2.wait(); l3.wait(); l1.wait(); loc[0].wait()
    other_dn = wd.at[pl.ds(pl.multiple_of((q * 2 + 1 - c) * 96, 16), 96), :]
    got(other_dn, s_dn[1])

    c1 = pl.multiple_of(c * 1920, 128)
    NA = 1280
    parts = {
        "Q": dict(ref=wq, rows=96, col0=0, cols=768, order="zy", sib=False),
        "E": dict(ref=we, rows=48, col0=0, cols=128, order="xyz", sib=False),
        "O": dict(ref=wou, rows=48, col0=c1, cols=NA, order="zxy", sib=True),
        "D": dict(ref=wd, rows=192, col0=pl.multiple_of(c * 384, 128), cols=384, order="zyx", sib=True),
        "P": dict(ref=wou, rows=48, col0=pl.multiple_of(c1 + NA, 128), cols=1920 - NA, order="xyz", sib=True),
    }
    def reg(p, r0, cnt):
        p = parts[p]
        return p["ref"].at[pl.ds(pl.multiple_of(r0 * p["rows"], 16), cnt * p["rows"]), pl.ds(p["col0"], p["cols"])]
    def push(p, r0, cnt, dev, pred=None):
        s, r = sem()
        region = reg(p, r0, cnt)
        go(remote(region, region, s, r, dev), pred)
        return r
    def recv(p, r0, cnt, r, pred=None, sib=True):
        got(reg(p, r0, cnt), r, pred)
        if sib and parts[p]["sib"]:
            rs = push(p, r0, cnt, sp, pred)
            late.append((p, r0, cnt, rs, pred))
    late = []
    slots = [(0, 0)] + [(s, k) for s in range(1, nz) for k in (0, 1)]
    def slot_z(s, k):
        return z - s if k == 0 else z + s
    def slot_ok(s, k):
        if s == 0: return None
        return (z - s >= 0) if k == 0 else (z + s < nz)
    def both(a, b):
        if a is None: return b
        return a & b
    zr = {}
    def zblock(p, zz):
        o = parts[p]["order"]
        if o == "zy": return zz * 2 + y, 1
        if o[0] == "z": return zz * 4 + y * 2 + x, 1
        return zz * 4, 4
    def zsend(p, s):
        for k in (0, 1):
            okc = slot_ok(s - 1, k) if s > 1 else None
            edge = (z < nz - 1) if k == 0 else (z > 0)
            r0, cnt = zblock(p, slot_z(s - 1, k))
            zr[p, s, k] = push(p, r0, cnt, up if k == 0 else down, both(okc, edge))
    def zrecv(p, s, then):
        for k in (0, 1):
            r0, cnt = zblock(p, slot_z(s, k))
            recv(p, r0, cnt, zr[p, s, k], slot_ok(s, k))
            if then: then(p, s, k)
    second = {}; third = {}
    def step2(p, s, k):
        o = parts[p]["order"]; zz = slot_z(s, k)
        if o == "zy": second[p, s, k] = push(p, zz * 2 + y, 1, yp, slot_ok(s, k))
        elif o[1] == "x": second[p, s, k] = push(p, zz * 4 + y * 2 + x, 1, xp, slot_ok(s, k))
        else: second[p, s, k] = push(p, zz * 4 + y * 2 + x, 1, yp, slot_ok(s, k))
    def recv2(p, s, k):
        o = parts[p]["order"]; zz = slot_z(s, k); ok = slot_ok(s, k)
        if o == "zy":
            recv(p, zz * 2 + 1 - y, 1, second[p, s, k], ok)
        elif o[1] == "x":
            recv(p, zz * 4 + y * 2 + 1 - x, 1, second[p, s, k], ok)
            third[p, s, k] = [(zz * 4 + (1 - y) * 2, 2, push(p, zz * 4 + y * 2, 2, yp, ok))]
        else:
            recv(p, zz * 4 + (1 - y) * 2 + x, 1, second[p, s, k], ok)
            third[p, s, k] = [(zz * 4 + yy * 2 + 1 - x, 1, push(p, zz * 4 + yy * 2 + x, 1, xp, ok)) for yy in range(2)]
    def recv3(p, s, k):
        for r0, cnt, r in third[p, s, k]:
            recv(p, r0, cnt, r, slot_ok(s, k))
    zp = ("Q", "O", "D")
    for p in zp: zsend(p, 1)
    e1 = push("E", q, 1, xp); p1 = push("P", q, 1, xp)
    for p in zp: step2(p, 0, 0)
    recv("E", z * 4 + y * 2 + 1 - x, 1, e1); e2 = push("E", z * 4 + y * 2, 2, yp)
    recv("P", z * 4 + y * 2 + 1 - x, 1, p1); p2 = push("P", z * 4 + y * 2, 2, yp)
    recv("E", z * 4 + (1 - y) * 2, 2, e2); zsend("E", 1)
    for p in zp:
        zrecv(p, 1, step2)
        if nz > 2: zsend(p, 2)
    recv("P", z * 4 + (1 - y) * 2, 2, p2); zsend("P", 1)
    for p in zp: recv2(p, 0, 0)
    zrecv("E", 1, None)
    if nz > 2: zsend("E", 2)
    for s in range(2, nz):
        for p in zp:
            zrecv(p, s, step2)
            if s + 1 < nz: zsend(p, s + 1)
        zrecv("E", s, None)
        if s + 1 < nz: zsend("E", s + 1)
        for p in zp:
            for k in (0, 1): recv2(p, s - 1, k)
        zrecv("P", s - 1, None)
        zsend("P", s)
        for p in zp[1:]:
            for k in ((0,) if s == 2 else (0, 1)): recv3(p, s - 2, k)
    for p in zp:
        for k in (0, 1): recv2(p, nz - 1, k)
    for s in ([nz - 2, nz - 1]):
        for p in zp[1:]:
            for k in (0, 1): recv3(p, s, k)
    zrecv("P", nz - 1, None)
    for p, r0, cnt, rs, pred in late:
        pp = parts[p]
        other = dict(pp); base = {"O": 0, "P": NA, "D": 0}[p]
        half = 384 if p == "D" else 1920
        col = pl.multiple_of((1 - c) * half + base, 128)
        region = pp["ref"].at[pl.ds(pl.multiple_of(r0 * pp["rows"], 16), cnt * pp["rows"]), pl.ds(col, pp["cols"])]
        got(region, rs, pred)
    for pred, copy in sends:
        if pred is None: copy.wait_send()
        else: pl.when(pred)(copy.wait_send)

NSEM = 400
def gather(q4, ou, dn, nz):
    hbm = pl.BlockSpec(memory_space=pltpu.HBM); vm = pl.BlockSpec(memory_space=pltpu.VMEM)
    S = jax.ShapeDtypeStruct
    return pl.pallas_call(partial(gather_kernel, nz),
        out_shape=(S((768, 768), BF), S((768, 3840), BF), S((768, 128), BF), S((3072, 768), BF)),
        in_specs=[vm] * 3, out_specs=[hbm] * 4,
        scratch_shapes=[pltpu.VMEM((4, 24, 768), BF), pltpu.VMEM((24, 3968), BF), pltpu.VMEM((48, 3968), BF), pltpu.VMEM((96, 768), BF),
            pltpu.SemaphoreType.DMA((4,)), pltpu.SemaphoreType.DMA((NSEM,)), pltpu.SemaphoreType.DMA((NSEM,))],
        compiler_params=pltpu.CompilerParams(collective_id=0, has_side_effects=True, vmem_limit_bytes=32 * 2**20))(q4, ou, dn)

def gather_any(q4, ou, dn):
    both = ("dp", "fsdp")
    mine = lax.dynamic_index_in_dim(lax.all_gather(q4, both, axis=0), lax.axis_index("fsdp"), 1, keepdims=False)
    full = lax.all_gather(ou, both, axis=0, tiled=True)
    return mine.reshape(D, D), full[:, :3840], full[:, 3840:], lax.all_gather(dn, both, axis=0, tiled=True)

def grads_any(kept0, kept1, vin, rd):
    both = ("dp", "fsdp")
    a, dm, n2, du, og, da, n1, dq = [jnp.concatenate([u, v], axis=0) for u, v in zip(kept0, kept1)]
    heads = og.reshape(2, 4, T, 256)[..., :192].transpose(0, 2, 1, 3).reshape(2 * T, D)
    scatter = lambda v: lax.psum_scatter(v, both, scatter_dimension=0, tiled=True)
    q = tn(n1, dq).reshape(1, D // rd, rd, D)
    q = lax.dynamic_update_slice(jnp.zeros((4, D // rd, rd, D), F32), q, (lax.axis_index("fsdp"), 0, 0, 0))
    q_grad = lax.psum_scatter(q, both, scatter_dimension=1, tiled=True).reshape(4, rd, D)
    return scatter(tn(a, dm)), scatter(tn(heads, da)), scatter(tn(n2, du)), q_grad, lax.psum(vin, both)

def body(tokens, qkv_weight, out_weight, up_weight, down_weight, norm_gains, up_bias, pass_table, pass_index, lengths, cotangent):
    rd = qkv_weight.shape[0]
    nz = lax.axis_size("dp") // 2
    f = lax.axis_index("fsdp")
    q4 = jnp.pad(qkv_weight.reshape(rd, 3, 4, 192), ((0, 0), (0, 0), (0, 0), (0, 64))).transpose(2, 0, 1, 3).reshape(4, rd, D)
    chooser = [(jnp.arange(pass_table.shape[1], dtype=jnp.int32) == pass_index[n]).astype(F32) for n in range(2)]
    emb = jnp.stack([jnp.sum(pass_table.astype(F32) * ch[None, :], axis=1) for ch in chooser], axis=1).astype(BF)
    e = jnp.concatenate([norm_gains, emb, up_bias.reshape(rd, 4), jnp.zeros((rd, 120), BF)], axis=1)
    ou = jnp.concatenate([out_weight, up_weight, e], axis=1)
    if rd == 24:
        wq, wou, we, wd = gather(q4, ou, down_weight, nz)
    else:
        wq, wou, we, wd = gather_any(q4, ou, down_weight)
    vecs = we[:, 0:4].T.astype(F32)
    vec = [jnp.concatenate([vecs[0:2], vecs[2 + n:3 + n], jnp.zeros((5, D), F32)], axis=0) for n in range(2)]
    bias = we[:, 4:8].reshape(1, FF).astype(F32)
    row_pos = f * T + jnp.arange(T, dtype=jnp.int32)
    valid = (row_pos < lengths[0]).astype(F32)[:, None]
    xs = [tokens.astype(F32)]; kept = []
    for n in range(2):
        res = fwd(lengths, xs[n], vec[n], bias, wq, wou, wd, 1)
        xs.append(res[0]); kept.append(res[1:])
    block_out = (xs[2] * valid).astype(BF)
    g = cotangent.astype(F32) * valid
    b1 = bwd(lengths, g, xs[1], vec[1], wq, wou, wd, kept[1], 2)
    n1, qkv, o, lse, og, r, n2, gp, a = kept[1]
    if rd == 24:
        left = dict(a_1=a, dm_1=b1["dm_o"], n2_1=n2, du_1=b1["du_o"], og_1=og, da_1=b1["da_o"], n1_1=n1.reshape(S, D), dq_1=b1["dqkv_o"], sums_1=b1["sums"], bsum_1=b1["bsum"])
        mine = (kept[0][0].reshape(S, D),) + tuple(kept[0][1:])
        b0 = bwd(lengths, b1["go_o"], xs[0], vec[0], wq, wou, wd, mine, 3, left, nz)
        down_grad, out_grad, up_grad, q_grad, tot = b0["down_o"], b0["outw_o"], b0["up_o"], b0["qkv_o"], b0["v_o"]
    else:
        b0 = bwd(lengths, b1["go_o"], xs[0], vec[0], wq, wou, wd, kept[0], 2)
        groups = [(k[8], b["dm_o"], k[6], b["du_o"], k[4], b["da_o"], k[0].reshape(S, D), b["dqkv_o"]) for k, b in zip(kept, (b0, b1))]
        s0, s1 = b0["sums"], b1["sums"]
        vin = jnp.concatenate([s0[0:2] + s1[0:2], s0[2:3], s1[2:3], (b0["bsum"] + b1["bsum"]).reshape(4, D)], axis=0)
        down_grad, out_grad, up_grad, q_grad, tot = grads_any(*groups, vin, rd)
    qkv_grad = q_grad.reshape(4, rd, 3, 256)[..., :192].transpose(1, 2, 0, 3).reshape(rd, 3 * D)
    idx = lax.axis_index("dp") * 4 + f
    own = lambda v: lax.dynamic_slice_in_dim(v, idx * rd, rd, 0)
    gains = own(tot[0:2].T)
    table = own(tot[2])[:, None] * chooser[0][None] + own(tot[3])[:, None] * chooser[1][None]
    bias_grad = lax.dynamic_slice_in_dim(tot[4:8].reshape(FF), idx * rd * 4, rd * 4, 0)
    return (block_out, b0["go_o"], qkv_grad, out_grad, up_grad, down_grad, gains, bias_grad, table)

def solution(mesh):
    a = P(("dp", "fsdp"), None); b = P(("dp", "fsdp"))
    return jax.shard_map(body, mesh=mesh, in_specs=(a, a, a, a, a, a, b, a, P(), P("dp"), a), out_specs=(a, a, a, a, a, a, a, b, a), check_vma=False)
```

```python
from functools import partial
import jax
import jax.numpy as jnp
from jax import lax
from jax.experimental import pallas as pl
from jax.experimental.pallas import tpu as pltpu
from jax.sharding import PartitionSpec as P
BF=jnp.bfloat16; F32=jnp.float32
MESH = pl.DeviceIdType.MESH
NEG = -1e30
QB = 512
VMEM_LIMIT = 62 * 2**20

def remote(src, dst, ssem, rsem, dev):
    return pltpu.make_async_remote_copy(src_ref=src, dst_ref=dst, send_sem=ssem, recv_sem=rsem, device_id=dev, device_id_type=MESH)

def rows_at(start, count, step=16):
    return pl.ds(pl.multiple_of(start, step), count)

def normed(values):
    center = values - jnp.mean(values, axis=-1, keepdims=True)
    spread = jnp.mean(center * center, axis=-1, keepdims=True)
    scale = lax.rsqrt(spread + 1e-05)
    return center * scale, scale

def norm_back(xhat, scale, grad_out, gain):
    eg = grad_out * gain
    first = jnp.mean(eg, axis=-1, keepdims=True)
    second = jnp.mean(eg * xhat, axis=-1, keepdims=True)
    return scale * (eg - first - xhat * second)

def nt(left, right):
    return lax.dot_general(left, right, (((1,), (1,)), ((), ())), preferred_element_type=F32)

def dot(left, right):
    return jnp.dot(left, right, preferred_element_type=F32)

def mask_scores(sT, i, limit):
    lo = i * QB
    free = min(lo, 1024)
    parts = []
    if free: parts.append(sT[:free])
    if lo > free:
        kpos = free + lax.broadcasted_iota(jnp.int32, (lo - free, QB), 0)
        parts.append(jnp.where(kpos < limit, sT[free:lo], NEG))
    kpos = lo + lax.broadcasted_iota(jnp.int32, (QB, QB), 0)
    ok = kpos <= lo + lax.broadcasted_iota(jnp.int32, (QB, QB), 1)
    if lo + QB > 1024: ok = ok & (kpos < limit)
    parts.append(jnp.where(ok, sT[lo:], NEG))
    return parts[0] if len(parts) == 1 else jnp.concatenate(parts, 0)

def half_mask(index, h):
    edge = lax.full_like(index, 64)
    return lax.lt(index, edge) if h % 2 == 0 else lax.ge(index, edge)

def pick(xT, h):
    r = lax.broadcasted_iota(jnp.int32, xT.shape, 0)
    mine = half_mask(r, h) if isinstance(h, int) else (r // 64) == (h % 2)
    return jnp.where(mine, xT, jnp.zeros_like(xT))

def slot_of(h, base=0):
    return pl.ds(pl.multiple_of(base + (h // 2) * 128, 128), 128)

BWD_STEPS = ((0, 0, 1), (1, 0, 2), (2, 0, 2), (2, 2, 3))

def bwd_block(i, k0, k1, h, qkv, do, lse, limit, qT, kT, doT, dqT, delta, dkv):
    keys, cols, n = pl.ds(k0 * QB, (k1 - k0) * QB), pl.ds(i * QB, QB), (k1 - k0) * QB
    slot, hr = pl.ds((h // 2) * 128, 128), pl.ds(h * 64, 64)
    after = lambda base: pl.ds(base + (h // 2) * 128, 128)
    lane = lax.broadcasted_iota(jnp.int32, (QB, 128), 1)
    lm = half_mask(lane, h)
    sT = dot(qkv[keys, after(256)], pick(qT[slot, cols], h))
    p = jnp.exp(sT - lse[h:h + 1, cols])
    if k1 == i + 1:
        kpos = i * QB + lax.broadcasted_iota(jnp.int32, (QB, QB), 0)
        ok = kpos <= i * QB + lax.broadcasted_iota(jnp.int32, (QB, QB), 1)
        if k1 * QB > 1024: ok = ok & (kpos < limit)
        diagonal = jnp.where(ok, p[n - QB:], 0.0)
        p = diagonal if n == QB else jnp.concatenate([p[:n - QB], diagonal], axis=0)
    assert k1 == i + 1 or k1 * QB <= 1024
    dp = dot(qkv[keys, after(512)], pick(doT[slot, cols], h))
    dsT = (p * (dp - delta[h:h + 1, cols])).astype(BF)
    step = dot(kT[hr, keys], dsT)
    dqT[hr, cols] = step if k0 == 0 else dqT[hr, cols] + step
    qn, dn = qkv[cols, slot], do[cols, slot]
    dkv[keys, slot] += dot(dsT, jnp.where(lm, qn, jnp.zeros_like(qn)))
    dkv[keys, after(256)] += dot(p.astype(BF), jnp.where(lm, dn, jnp.zeros_like(dn)))

def group_barrier(d, f):
    bar = pltpu.get_barrier_semaphore()
    for k in (1, 2, 3):
        pl.semaphore_signal(bar, inc=1, device_id=(d, f ^ k), device_id_type=MESH)
    pl.semaphore_wait(bar, 3)

T, D, FF, S = 384, 768, 3072, 1536
CH = 128


ZERO = [None]

def at(ref, *index):
    return ref.at[tuple(ZERO[0] + i if isinstance(i, int) else i for i in index)]

def tn(left, right):
    return lax.dot_general(left, right, (((0,), (0,)), ((), ())), preferred_element_type=F32)

def when(pred, act):
    if pred is None: act()
    else: pl.when(pred)(act)

class Links:
    def __init__(self, ssem, rsem, dev):
        self.ssem, self.rsem, self.dev, self.n, self.sent, self.all = ssem, rsem, dev, 0, [], []
    def sem(self):
        self.n += 1
        return self.n - 1
    def send(self, src, dst, k, dev, pred=None):
        when(pred, remote(src, dst, at(self.ssem, k), at(self.rsem, k), dev).start)
        self.sent.append((pred, src, k))
    def got(self, region, k, pred=None):
        when(pred, remote(region, region, at(self.ssem, k), at(self.rsem, k), self.dev).wait_recv)
    def send_all(self, src, dst, nz):
        k, me = self.sem(), lax.axis_index("dp") * 4 + lax.axis_index("fsdp")
        for b, dev in enumerate(everyone(nz)):
            one = src if len(src.shape) == 2 else at(src, b)
            pl.when(me != b)(remote(one, at(dst, me), at(self.ssem, k), at(self.rsem, k), dev).start)
        self.all.append((dst, k))
        return k
    def got_all(self, dst, k):
        every = at(dst, pl.ds(0, dst.shape[0] - 1))
        remote(every, every, at(self.ssem, k), at(self.rsem, k), self.dev).wait_recv()
    def close(self):
        for pred, src, k in self.sent:
            base = getattr(src, "ref", src)
            like = at(base, *([0] * (len(base.shape) - len(src.shape)) + [pl.ds(0, n) for n in src.shape]))
            when(pred, remote(like, like, at(self.ssem, k), at(self.rsem, k), self.dev).wait_send)
        for dst, k in self.all:
            every = at(dst, pl.ds(0, dst.shape[0] - 1))
            remote(every, every, at(self.ssem, k), at(self.rsem, k), self.dev).wait_send()
        self.sent, self.all = [], []

PLAN = (
    (), (), (), (), (), (), (), (), (), (973, 983), (970, 980), (972, 982), (983, 971, 981, 1113, 1110, 973, 1112, 1111, 970),
    (983, 970, 980, 972, 982, 971, 1123, 973, 1120, 1113), (), (), (1122, 1121, 970, 981, 1110, 972), (983,), (980, 1112),
    (973, 970, 982, 1111, 1123, 972), (), (983, 980, 1113, 1120, 973), (982, 971, 1123), (), (980, 981, 1113, 1112, 1120, 1122, 971, 1110, 979), (),
    (), (1121,), (1113, 1112, 1123, 1122, 979, 981, 1111, 989), (), (), (), (1110, 1120, 1121, 1143, 1140, 1142, 1141),
    (1111, 1123, 1122, 989, 1133, 1130, 1132, 1131),
    (1110, 1120, 1121, 710, 1119, 1143, 1140, 1133, 1123, 1122, 1142, 1130, 710, 1120, 1121, 1141, 1143, 1132, 1140, 1133, 1142, 1131, 1130, 710, 860, 1143, 1140, 1141, 1132, 1119, 1133, 1149, 1131, 1130, 860, 1149, 1132, 1133, 1131, 1130),
)
GATHER_PLAN = (
    (1140,), (1180,),
    (1110, 1010, 1180, 1141, 1170, 1140, 1110, 1181, 1010, 1011, 1000, 1142, 1180, 1182, 1012, 1001, 1141, 1110, 1170, 1143, 1011, 1183, 1013, 1181, 1142, 1143),
    (1010, 1012, 1002, 1013), (), (), (), (1000, 1111), (1182,), (1003,), (), (1001, 1112, 1181), (), (1170, 1183), (), (), (1000,), (),
    (1113, 1011, 1012, 1013, 1182, 1171, 1002, 1003, 1183, 1172, 1001), (), (), (), (1002, 1003, 1173), (), (), (), (), (), (), (), (),
)

def job(letter, i=0):
    return ord(letter) * 10 + i

class Agenda:
    def __init__(self, plan): self.plan, self.jobs, self.point = plan, {}, 0
    def add(self, name, job): self.jobs[name] = job
    def step(self, name):
        if next(self.jobs[name], self) is self: del self.jobs[name]
    def run(self, hold=False):
        names = self.plan[self.point] if self.point < len(self.plan) else ()
        self.point += 1
        for name in names: self.step(name)
    def need(self, names):
        for name in names:
            while name in self.jobs: self.step(name)
    def finish(self):
        for name in self.plan[self.point] if self.point < len(self.plan) else (): self.step(name)
        while self.jobs:
            for name in list(self.jobs): self.step(name)

def add_to(acc, inc):
    acc[...] = (acc[...].astype(F32) + inc[...].astype(F32)).astype(BF)

class Copies:
    def __init__(self, sems): self.sems, self.n = sems, 0
    def go(self, src, dst):
        copy = pltpu.make_async_copy(src, dst, at(self.sems, self.n))
        self.n += 1
        copy.start()
        return copy
    def wait(self, n, src, dst):
        pltpu.make_async_copy(src, dst, at(self.sems, n)).wait()

def turns(nz):
    out, lo, hi = [], 0, nz - 1
    while lo <= hi:
        out += [hi, lo] if lo < hi else [lo]
        lo, hi = lo + 1, hi - 1
    return out

def place():
    d = lax.axis_index("dp"); f = lax.axis_index("fsdp")
    return d, f, d // 2, d % 2, f // 2, f % 2

D_PIECES = (("a", "xzy", 0, 256), ("b", "yzx", 256, 768))
W_PIECES = (("o", "xzy", 0, 640), ("p", "yxz", 640, 1920))
Q_PIECES = (("r", "zy", 0, 256), ("q", "yz", 256, 768))

class Piece:
    def __init__(self, name, order, rows, cols, nz, pair=True):
        self.name, self.order, self.rows, self.cols, self.nz, self.pair = name, order, rows, cols, nz, pair
        self.nx = 2 if pair else 1
    def live(self, done):
        return ((2,) if "y" not in done else ()) + ((self.nx,) if "x" not in done else ()) + (self.rows, self.cols)
    def buffers(self):
        out = {"acc": (self.nz, 2, self.nx, self.rows, self.cols)}
        if self.pair: out["stg"] = out["sib"] = out["acc"]
        done = ""
        for axis in self.order:
            if axis == "z": out["z"] = (2, self.nz) + self.live(done)
            else: out[axis] = (() if "z" in done else (self.nz,)) + self.live(done + axis)
            done += axis
        return {self.name + k: (s, BF) for k, s in out.items()}
    def bind(self, bufs, s):
        self.s, self.net, self.agenda = s, s.net, s.agenda
        self.b = {k[len(self.name):]: v for k, v in bufs.items() if k.startswith(self.name) and k[len(self.name):] in ("acc", "stg", "sib", "x", "y", "z")}
        self.sems, self.flows, self.done = {}, 0, False
        return self
    def view(self, t, done, other=""):
        s = self.s
        ys = pl.ds(0, 2) if "y" not in done else 1 - s.y if other == "y" else s.y
        xs = pl.ds(0, self.nx) if "x" not in done else 1 - s.x if other == "x" else s.x
        return at(self.b["acc"], t, ys, xs)
    def start(self, t):
        if self.pair:
            self.sems[t] = self.net.sem()
            self.net.send(at(self.b["stg"], t), at(self.b["sib"], t), self.sems[t], self.s.sp)
        self.agenda.add(job(self.name, t), self.plane(t))
    def exchange(self, axis, t, done):
        k = self.net.sem()
        self.net.send(self.view(t, done + axis, axis), self.inbox(axis, t, done), k, self.s.xp if axis == "x" else self.s.yp)
        return k
    def inbox(self, axis, t, done):
        return self.b[axis] if "z" in done else at(self.b[axis], t)
    def plane(self, t):
        if self.pair:
            self.net.got(at(self.b["sib"], t), self.sems[t])
            add_to(at(self.b["acc"], t), at(self.b["sib"], t))
        done = ""
        for axis in self.order:
            if axis == "z": break
            k = self.exchange(axis, t, done)
            done += axis
            yield
            buf = self.inbox(axis, t, done)
            self.net.got(buf, k)
            add_to(self.view(t, done), buf)
        yield from self.flow(t, done)
        self.flows += 1
        if self.flows == self.nz:
            if self.order[-1] == "z": self.done = True
            else: self.agenda.add(job(self.name, 9), self.rest())
    def flow(self, t, done):
        nz, s, ks, recv = self.nz, self.s, (self.net.sem(), self.net.sem()), self.b["z"]
        far = max(t, nz - 1 - t)
        for h in range(far):
            if h: yield
            for way, total, here, dev in ((0, t, s.is_z[h], s.up), (1, nz - 1 - t, s.is_z[nz - 1 - h], s.down)):
                if h < total:
                    inc = at(recv, way, t)
                    if h:
                        self.net.got(inc, ks[way], here)
                        pl.when(here)(lambda inc=inc: add_to(self.view(t, done), inc))
                    self.net.send(self.view(t, done), inc, ks[way], dev, here)
        yield
        if t > 0: self.net.got(at(recv, 0, t), ks[0], s.is_z[t])
        if t < nz - 1: self.net.got(at(recv, 1, t), ks[1], s.is_z[t])
    def rest(self):
        s, i = self.s, self.order.index("z")
        done = self.order[:i + 1]
        own = self.view(s.z, done)
        for pred, way in ((s.has_below, 0), (s.has_above, 1)):
            pl.when(pred)(lambda way=way: add_to(own, at(self.b["z"], way, s.z)))
        for axis in self.order[i + 1:]:
            k = self.exchange(axis, s.z, done)
            done += axis
            yield
            buf = self.inbox(axis, s.z, done)
            self.net.got(buf, k)
            if axis != self.order[-1]: add_to(self.view(s.z, done), buf)
        self.done = True
    def total(self):
        assert self.done
        s, last = self.s, self.order[-1]
        sum_ = self.b["acc"][s.z, s.y, s.x if self.pair else 0].astype(F32)
        if last != "z": return sum_ + self.b[last][...].astype(F32).reshape(sum_.shape)
        for pred, way in ((s.has_below, 0), (s.has_above, 1)):
            sum_ = sum_ + jnp.where(pred, self.b["z"][way, s.z].astype(F32).reshape(sum_.shape), 0.0)
        return sum_

class Sums:
    def __init__(self, nz, net, agenda, bufs, outs, vin):
        self.nz, self.net, self.agenda, self.b, self.o, self.vin = nz, net, agenda, bufs, outs, vin
        self.d, self.f, self.z, self.y, self.x, self.c = place()
        d, f = self.d, self.f
        self.up, self.down = (d + 2, f), (d - 2, f)
        self.yp, self.xp, self.sp = (d ^ 1, f), (d, f ^ 2), (d, f ^ 1)
        self.turn = turns(nz)
        z = self.z
        self.is_z = [z == h for h in range(nz)]
        self.has_below, self.has_above, self.core0 = z > 0, z < nz - 1, self.c == 0
        self.D, self.W, self.Q = [[p.bind(bufs, self) for p in ps] for ps in pieces(nz)]
    def first(self, v): return jnp.where(self.core0, v[0], v[1])
    def second(self, v): return jnp.where(self.core0, v[1], v[0])
    def cols(self, ref, width, off, n, mine, rows=None):
        cc = self.c if mine else 1 - self.c
        return ref[slice(None) if rows is None else rows, pl.ds(pl.multiple_of(cc * width + off, 128), n)]

    def vectors(self):
        vb, vr = self.b["vb"], self.b["vr"]
        self.vin(vb)
        k = self.net.send_all(vb, vr, self.nz)
        vr[self.d * 4 + self.f] = vb[self.d * 4 + self.f]
        yield
        self.net.got_all(vr, k)
        total = vr[0]
        for n in range(1, self.nz * 8): total = total + vr[n]
        self.o["v"][...] = total

    def down_tile(self, t, g):
        g = g.reshape(2, 2, 2, 96, D)
        for p, (_, _, c0, c1) in zip(self.D, D_PIECES):
            for y in range(2):
                for x in range(2):
                    p.b["acc"][t, y, x] = self.first(g[y, x, :, :, c0:c1]).astype(BF)
                    p.b["stg"][t, y, x] = self.second(g[y, x, :, :, c0:c1]).astype(BF)
            p.start(t)
    def wide_piece(self, p, c0, c1, n2, du, og, da, gu, gw):
        for dst, mine in (("acc", True), ("stg", False)):
            if c0 < 384:
                n = min(c1, 384) - c0
                for j in range(4):
                    g = tn(og[j, :, 0:192], self.cols(da, 384, c0, n, mine)) + self.cols(gw, 384, c0, n, mine, pl.ds(j * 192, 192)).astype(F32)
                    p.b[dst][j * self.nz // 4:(j + 1) * self.nz // 4, :, :, :, 0:n] = g.astype(BF).reshape(self.nz // 4, 2, 2, 48, n)
            if c1 > 384:
                lo = max(c0, 384)
                g = tn(n2[...], self.cols(du, 1536, lo - 384, c1 - lo, mine)) + self.cols(gu, 1536, lo - 384, c1 - lo, mine).astype(F32)
                p.b[dst][:, :, :, :, lo - c0:c1 - c0] = g.astype(BF).reshape(self.nz, 2, 2, 48, c1 - lo)
        for t in self.turn: p.start(t)
    def q_piece(self, p, c0, c1, n1, dq, gq):
        for j in range(2):
            g = tn(n1[:, j * 384:(j + 1) * 384], dq[:, c0:c1]) + gq[j * 384:(j + 1) * 384, c0:c1].astype(F32)
            p.b["acc"][j * self.nz // 2:(j + 1) * self.nz // 2] = g.astype(BF).reshape(self.nz // 2, 2, 1, 96, c1 - c0)
        for t in self.turn: p.start(t)
    def ends(self):
        net, half, c, f, qf = self.net, self.b["half"], self.c, self.f, self.b["qf"]
        for p, (_, _, c0, c1) in zip(self.W, W_PIECES):
            total = p.total()
            half[0, :, c0:c1] = self.first((total[0:24], total[24:48]))
            half[1, :, c0:c1] = self.second((total[0:24], total[24:48]))
        kw = net.sem()
        net.send(at(half, 1), at(half, 2), kw, self.sp)
        for p, (_, _, c0, c1) in zip(self.Q, Q_PIECES):
            total = p.total()
            for j in range(4): qf[0, j, :, c0:c1] = total[j * 24:(j + 1) * 24]
        ks = [net.sem() for _ in range(4)]
        for k in (1, 2, 3):
            net.send(at(qf, 0, f ^ k), at(qf, 1, f), ks[k], (self.d, f ^ k))
        self.o["qkv"][f] = qf[0, f]
        for p, (_, _, c0, c1) in zip(self.D, D_PIECES):
            self.o["down"][:, c0:c1] = p.total()
        net.got(at(half, 2), kw)
        for cc, s in ((c, 0), (1 - c, 2)):
            self.o["outw"][:, pl.ds(pl.multiple_of(cc * 384, 128), 384)] = half[s, :, 0:384]
            self.o["up"][:, pl.ds(pl.multiple_of(cc * 1536, 128), 1536)] = half[s, :, 384:1920]
        for k in (1, 2, 3):
            net.got(at(qf, 1, f ^ k), ks[k])
            self.o["qkv"][f ^ k] = qf[1, f ^ k]

def pieces(nz):
    return ([Piece(n, o, 96, c1 - c0, nz) for n, o, c0, c1 in D_PIECES], [Piece(n, o, 48, c1 - c0, nz) for n, o, c0, c1 in W_PIECES],
            [Piece(n, o, 96, c1 - c0, nz, False) for n, o, c0, c1 in Q_PIECES])

def sum_buffers(nz):
    out = dict(rows24=((8, D), F32), rows96=((8, FF), F32), qf=((2, 4, 24, D), F32), half=((3, 24, 1920), F32), vb=((nz * 8, 8, 128), F32), vr=((nz * 8, 8, 128), F32))
    for group in pieces(nz):
        for p in group: out.update(p.buffers())
    return out

def bwd_kernel(last, nz, names, *refs):
    r_ = dict(zip(names, refs))
    R = lambda *ns: [r_[n] for n in ns]
    lim, vec, g_h, x_h, wq_h, wou_h, wd_h, qkv_h, o_h, lse_h, r_h, gp_h = R("lim", "vec", "g", "x", "wq", "wou", "wd", "qkv", "o", "lse", "r", "gp")
    dos, do, mine, part, inc, go, dr, dqkv, sums, bsum = R("dos", "do", "mine", "part", "inc", "go_v", "dr", "dqkv_v", "sums", "bsum")
    d = lax.axis_index("dp"); f = lax.axis_index("fsdp")
    ZERO[0] = f * 0
    mem = Copies(r_["lsem"])
    net = Links(r_["ssem"], r_["rsem"], (d, f ^ 1))
    agenda = Agenda(PLAN if last and nz == 4 else ())
    limit = lim[0]
    g0, g1, emb = vec[0:1, :], vec[1:2, :], vec[2:3, :] if last else vec[3:4, :]
    W = 768
    V, ws = pltpu.VMEM, wide_shapes(nz)
    if last:
        gs = Sums(nz, net, agenda, r_, dict(v=r_["v_o"], down=r_["down_o"], outw=r_["outw_o"], up=r_["up_o"], qkv=r_["qkv_o"]), None)
        sums1, bsum1 = r_["sums_1"], r_["bsum_1"]
        def all_sums(out):
            rows24, rows96 = r_["rows24"], r_["rows96"]
            rows24[...] = jnp.concatenate([jnp.zeros((1, D), F32), sums[0:2, :] + sums1[0:2, :], sums[2:3, :], sums1[2:3, :], jnp.zeros((3, D), F32)], axis=0)
            rows96[...] = jnp.concatenate([bsum[...] + bsum1[...], jnp.zeros((7, FF), F32)], axis=0)
            rows_to_slabs(rows24, rows96, nz * 8, out)
        gs.vin = all_sums
    g_in = mem.go(g_h, dr) if last else None
    sums[...] = jnp.zeros_like(sums)

    def phase1(du, dm, da):
        held = []
        def phase1a(wou, r, wd, gp):
            lw, lg = mem.go(wd_h, wd), mem.go(gp_h, gp)
            if last:
                full_barrier(nz, d * 4 + f)
                g_in.wait()
            else:
                group_barrier(d, f)
                ok = lax.lt(lax.broadcasted_iota(jnp.int32, (T, 1), 0) + f * T, lax.broadcast(limit, (T, 1)))
                dr[...] = jnp.where(ok, g_h[...].astype(F32), 0.0)
            dm[...] = dr[...].astype(BF)
            lw.wait(); lg.wait()
            held.append((mem.n, mem.go(wou_h, wou), mem.go(r_h, r)))
            for j in range(FF // W):
                cols = pl.ds(j * W, W)
                t = (nt(dm[...], wd[j * nz // 4:(j + 1) * nz // 4].reshape(W, D)) * gp[:, cols].astype(F32)).astype(BF)
                du[:, cols] = t
                bsum[:, cols] = jnp.sum(t.astype(F32), axis=0, keepdims=True)
                agenda.run()
        def phase1b(wou, r, a, gt, n2, og, gu, gw):
            la = mem.go(r_["a"], a)
            late = [mem.go(r_["n2"], n2), mem.go(r_["og"], og)]
            if last:
                tile = lambda n: mem.go(at(r_["gd_1"], pl.ds(gs.turn[n] * W, W)), at(gt, n % 2))
                tiles = [tile(0), tile(1)]
                late += [mem.go(r_["gu_1"], gu), mem.go(r_["gw_1"], gw)]
            mem.wait(held[0][0], wou_h, wou)
            mem.wait(held[0][0] + 1, r_h, r)
            for j in range(T // 128):
                rows = pl.ds(j * 128, 128)
                e = nt(du[rows, :], wou[:, :, :, :, D:].reshape(D, FF))
                xhat, scale = normed(r[rows, :])
                sums[1:2, :] += jnp.sum(e * xhat, axis=0, keepdims=True)
                t = dr[rows, :] + norm_back(xhat, scale, e, g1)
                dr[rows, :] = t
                da[rows, :] = t.astype(BF)
                agenda.run()
            for k in (3, 2, 1, 0):
                b = f ^ k
                dos[b, :, 0:192] = nt(da[...], wou[pl.ds(b * (nz // 4), nz // 4), :, :, :, 0:D].reshape(192, D)).astype(BF)
                dos[b, :, 192:256] = jnp.zeros((T, 64), BF)
                if k: net.send(at(dos, b), at(do, rows_at(f * T, T)), do_sems[k], (d, b))
                else: do[rows_at(f * T, T), :] = dos[b]
            agenda.run()
            la.wait()
            if last:
                for n, t in enumerate(gs.turn):
                    tiles[n].wait()
                    gs.down_tile(t, tn(a[:, t * W:(t + 1) * W], dm[...]) + gt[n % 2].astype(F32))
                    if n + 2 < nz: tiles.append(tile(n + 2))
                    agenda.run()
            for c in late: c.wait()
            if last:
                for p, (_, _, c0, c1) in zip(gs.W, W_PIECES):
                    gs.wide_piece(p, c0, c1, n2, du, og, da, gu, gw)
                    agenda.run()
            else:
                for j in range(FF // W):
                    rows = pl.ds(j * W, W)
                    r_["gd_v"][rows, :] = tn(a[:, rows], dm[...]).astype(BF)
                for j in range(FF // W):
                    cols = pl.ds(j * W, W)
                    r_["gu_v"][:, cols] = tn(n2[...], du[:, cols]).astype(BF)
                for j in range(4):
                    r_["gw_v"][j * 192:(j + 1) * 192, :] = tn(og[j, :, 0:192], da[...]).astype(BF)
        big, wide = [V((T, FF), BF)], [V((T, D), BF), V((4, T, 256), BF)]
        def with_wide(wou, r):
            pl.run_scoped(partial(phase1a, wou, r), V(*ws["wd"]), V((T, FF), BF))
            if last: pl.run_scoped(partial(phase1b, wou, r), *big, V((2, W, D), BF), *wide, V((D, FF), BF), V((D, D), BF))
            else: pl.run_scoped(lambda a, *v: phase1b(wou, r, a, None, *v, None, None), *big, *wide)
        pl.run_scoped(with_wide, V(*ws["wou"]), V((T, D), F32))
    do_sems = [net.sem() for _ in range(4)]
    pl.run_scoped(phase1, V((T, FF), BF), V((T, D), BF), V((T, D), BF))
    made = [] if last else [mem.go(r_[n + "_v"], r_[n + "_o"]) for n in ("gd", "gu", "gw")]

    def phase2(qkv, o, lse, qT, kT, doT, dqT, delta, dkv):
        loads = [mem.go(*p) for p in ((qkv_h, qkv), (o_h, o), (lse_h, lse))]
        dkv[...] = jnp.zeros_like(dkv)
        dqT[192:256, :] = jnp.zeros((64, S), F32)
        agenda.run()
        for c in loads: c.wait()
        qT[...] = (qkv[:, 0:256] * 0.125).astype(BF).T
        kT[...] = qkv[:, 256:512].T
        agenda.run(hold=True)
        for k in (1, 2, 3): net.got(at(do, rows_at((f ^ k) * T, T)), do_sems[k])
        doT[...] = do[...].T
        prod = (do[...].astype(F32) * o[...].astype(F32)).T
        for h in range(3):
            delta[h:h + 1, :] = jnp.sum(prod[h * 64:h * 64 + 64], axis=0, keepdims=True)
        for step in BWD_STEPS:
            for h in range(3):
                bwd_block(*step, h, qkv, do, lse, limit, qT, kT, doT, dqT, delta, dkv)
                agenda.run()
        dqkv[:, 0:256] = (dqT[...] * 0.125).astype(BF).T
        dqkv[:, 256:512] = (dkv[:, 0:256] * 0.125).astype(BF)
        dqkv[:, 512:768] = dkv[:, 256:512].astype(BF)
    two = (V((S, D), BF), V((S, 256), BF), V((8, S), F32), V((256, S), BF), V((256, S), BF), V((256, S), BF), V((256, S), F32), V((8, S), F32), V((S, 512), F32))

    def phase3(wq, x, n1, gq):
        lw, lx, late = mem.go(wq_h, wq), mem.go(x_h, x), [mem.go(r_["n1"], n1)]
        if last: late.append(mem.go(r_["gq_1"], gq))
        pl.run_scoped(phase2, *two)
        out = []
        lw.wait()
        def partial_rows(b, j):
            return nt(dqkv[rows_at(b * T + j * CH, CH), :], wq[...].reshape(D, D))
        k0, k1, k2 = [[net.sem() for _ in range(3)] for _ in range(3)]
        for j in range(3):
            rows = pl.ds(j * CH, CH)
            mine[0, rows, :] = partial_rows(f ^ 3, j).astype(BF)
            net.send(at(mine, 0, rows), at(part, 0, rows), k0[j], (d, f ^ 1))
        for j in range(3):
            rows = pl.ds(j * CH, CH)
            t = partial_rows(f ^ 2, j)
            agenda.run(hold=True)
            net.got(at(part, 0, rows), k0[j])
            inc[rows, :] = (t + part[0, rows, :].astype(F32)).astype(BF)
            net.send(at(inc, rows), at(part, 2, rows), k2[j], (d, f ^ 2))
        for c in late: c.wait()
        if last:
            agenda.run()
            for p, (_, _, c0, c1) in zip(gs.Q, Q_PIECES):
                gs.q_piece(p, c0, c1, n1, dqkv, gq)
                agenda.run()
        else:
            r_["gq_v"][...] = tn(n1[...], dqkv[...]).astype(BF)
        for j in range(3):
            rows = pl.ds(j * CH, CH)
            mine[1, rows, :] = partial_rows(f ^ 1, j).astype(BF)
            net.send(at(mine, 1, rows), at(part, 1, rows), k1[j], (d, f ^ 1))
        for j in range(3):
            rows = pl.ds(j * CH, CH)
            go[rows, :] = partial_rows(f, j)
        lx.wait()
        def finish_rows():
            for j in range(3):
                rows = pl.ds(j * CH, CH)
                net.got(at(part, 1, rows), k1[j])
                net.got(at(part, 2, rows), k2[j])
                e = go[rows, :] + part[1, rows, :].astype(F32) + part[2, rows, :].astype(F32)
                xhat, scale = normed(x[rows, :].astype(F32) + emb)
                sums[0:1, :] += jnp.sum(e * xhat, axis=0, keepdims=True)
                t = dr[rows, :] + norm_back(xhat, scale, e, g0)
                sums[2:3, :] += jnp.sum(t, axis=0, keepdims=True)
                go[rows, :] = t
                if j < 2: yield
            out.append(mem.go(go, r_["go_o"]))
            if last: agenda.add(job("V"), gs.vectors())
        agenda.add(job("G"), finish_rows())
        agenda.finish()
        if last:
            gs.ends()
        for c in out: c.wait()
    pl.run_scoped(phase3, V(*ws["wq"]), V((T, D), x_h.dtype), V((S, D), BF), V((D, D), BF) if last else V((16, 128), BF))
    if not last: made.append(mem.go(r_["gq_v"], r_["gq_o"]))
    for c in made: c.wait()
    net.close()

def bwd(lim, g, x, vec, wq, wou, wd, kept, cid, nz, last=None):
    n1, qkv, o, lse, og, r, n2, gp, a = [kept[n] for n in ("n1", "qkv", "o", "lse", "og", "r", "n2", "gp", "a")]
    n1 = n1.reshape(S, D)
    hbm = pl.BlockSpec(memory_space=pltpu.HBM); vm = pl.BlockSpec(memory_space=pltpu.VMEM); sm = pl.BlockSpec(memory_space=pltpu.SMEM)
    ins = dict(lim=lim, vec=vec, g=g, x=x, wq=wq, wou=wou, wd=wd, qkv=qkv, o=o, lse=lse, r=r, gp=gp, a=a, n2=n2, og=og, n1=n1)
    scratch = dict(dos=((4, T, 256), BF), do=((S, 256), BF), mine=((2, T, D), BF), part=((3, T, D), BF), inc=((T, D), BF), go_v=((T, D), F32), dr=((T, D), F32), dqkv_v=((S, D), BF))
    outs = dict(go_o=((T, D), F32), sums=((8, D), F32), bsum=((1, FF), F32))
    if last is None:
        for n, s in (("gd", (FF, D)), ("gu", (D, FF)), ("gw", (D, D)), ("gq", (D, D))):
            outs[n + "_o"] = scratch[n + "_v"] = (s, BF)
    else:
        ins.update(last)
        outs.update(down_o=((96, D), F32), outw_o=((24, D), F32), up_o=((24, FF), F32), qkv_o=((4, 24, D), F32), v_o=((8, 128), F32))
    if last is not None: scratch.update(sum_buffers(nz))
    sems = 320 if last is not None else 16
    names = list(ins) + list(outs) + list(scratch) + ["lsem", "ssem", "rsem"]
    place_of = lambda n: sm if n == "lim" else vm if (n == "g" and last is None) or n in ("vec", "sums", "bsum", "sums_1", "bsum_1", "down_o", "outw_o", "up_o", "qkv_o", "v_o") else hbm
    res = pl.pallas_call(partial(bwd_kernel, last is not None, nz, names),
        out_shape=[jax.ShapeDtypeStruct(*s) for s in outs.values()],
        in_specs=[place_of(n) for n in ins], out_specs=[place_of(n) for n in outs],
        scratch_shapes=[pltpu.VMEM(*s) for s in scratch.values()] + [pltpu.SemaphoreType.DMA((32,)), pltpu.SemaphoreType.DMA((sems,)), pltpu.SemaphoreType.DMA((sems,))],
        compiler_params=pltpu.CompilerParams(collective_id=cid, has_side_effects=True, vmem_limit_bytes=VMEM_LIMIT))(*ins.values())
    return dict(zip(outs, res))

class Spread:
    def __init__(self, name, ref, order, rows, cols, width, off, s, pair=True):
        self.name, self.ref, self.order, self.rows, self.cols, self.s = name, ref, order, rows, cols, s
        self.nx, self.sib = (2, True) if pair else (1, False)
        self.mine = pl.multiple_of(off + s.c * width, 128) if pair else off
        self.other = pl.multiple_of(off + (1 - s.c) * width, 128) if pair else off
        self.net, self.agenda, self.late, self.names = s.net, s.agenda, [], []
        self.zsem = {(i, k): s.net.sem() for i in range(1, s.nz) for k in (0, 1)}
    def view(self, t, done, other="", col=None):
        s = self.s
        ys = pl.ds(0, 2) if "y" in done else 1 - s.y if other == "y" else s.y
        xs = pl.ds(0, self.nx) if "x" in done or self.nx == 1 else 1 - s.x if other == "x" else s.x
        return at(self.ref, t, ys, xs, pl.ds(0, self.rows), pl.ds(self.mine if col is None else col, self.cols))
    def add(self, i, steps):
        self.names.append(job(self.name, i))
        self.agenda.add(self.names[-1], steps)
    def start(self): self.add(0, self.first())
    def planes(self, i):
        s = self.s
        return [(s.z, None, 0)] if i == 0 else [(s.z - i, s.ok[i, 0], 0), (s.z + i, s.ok[i, 1], 1)]
    def first(self):
        s, done = self.s, ""
        for axis in self.order:
            if axis == "z": break
            k = self.net.sem()
            self.net.send(self.view(s.z, done), self.view(s.z, done), k, s.xp if axis == "x" else s.yp)
            yield
            self.net.got(self.view(s.z, done, axis), k)
            done += axis
        for k, dev in ((0, s.up), (1, s.down)):
            self.net.send(self.view(s.z, done), self.view(s.z, done), self.zsem[1, k], dev, s.go_on[0, k])
        for i in range(1, s.nz): self.add(i, self.distance(i, done))
        yield from self.after(0, done + "z")
    def distance(self, i, done):
        s = self.s
        for t, ok, k in self.planes(i):
            self.net.got(self.view(t, done), self.zsem[i, k], ok)
            if i + 1 < s.nz:
                self.net.send(self.view(t, done), self.view(t, done), self.zsem[i + 1, k], (s.up, s.down)[k], s.go_on[i, k])
        yield from self.after(i, done + "z")
    def after(self, i, done):
        s = self.s
        for axis in self.order[self.order.index("z") + 1:]:
            ks = []
            for t, ok, _ in self.planes(i):
                ks.append(self.net.sem())
                self.net.send(self.view(t, done), self.view(t, done), ks[-1], s.xp if axis == "x" else s.yp, ok)
            yield
            for k, (t, ok, _) in zip(ks, self.planes(i)): self.net.got(self.view(t, done, axis), k, ok)
            done += axis
        if self.sib:
            for t, ok, _ in self.planes(i):
                k = self.net.sem()
                self.net.send(self.view(t, "xy"), self.view(t, "xy"), k, s.sp, ok)
                self.late.append((i, len(self.late), k))
    def wait(self):
        self.agenda.need(self.names)
        n = {}
        for i, _, k in self.late:
            t, ok, _ = self.planes(i)[n.setdefault(i, 0)]
            n[i] += 1
            self.net.got(self.view(t, "xy", col=self.other), k, ok)

class Spreads:
    def __init__(self, nz, net, agenda, wq, wou, wd):
        self.nz, self.net, self.agenda = nz, net, agenda
        self.d, self.f, self.z, self.y, self.x, self.c = place()
        d, f, z = self.d, self.f, self.z
        self.up, self.down = (d + 2, f), (d - 2, f)
        self.yp, self.xp, self.sp = (d ^ 1, f), (d, f ^ 2), (d, f ^ 1)
        self.ok = {(i, k): (z >= i if k == 0 else z + i < nz) for i in range(1, nz) for k in (0, 1)}
        self.go_on = {(0, 0): z < nz - 1, (0, 1): z > 0}
        for i in range(1, nz - 1):
            self.go_on[i, 0] = self.ok[i, 0] & (z < nz - 1)
            self.go_on[i, 1] = self.ok[i, 1] & (z > 0)
        self.Q = [Spread(n, wq, o, 96, c1 - c0, 0, c0, self, False) for n, o, c0, c1 in GQ]
        self.O = [Spread(n, wou, o, 48, c1 - c0, 384, c0, self) for n, o, c0, c1 in GO]
        self.U = [Spread(n, wou, o, 48, c1 - c0, 1536, D + c0, self) for n, o, c0, c1 in GU]
        self.D = [Spread(n, wd, o, 192, c1 - c0, 384, c0, self) for n, o, c0, c1 in GD]
    def pred_sets(self):
        nz = self.nz
        out = [(self.ok[i, k], [z for z in range(nz) if (z >= i if k == 0 else z + i < nz)]) for i, k in self.ok]
        return out + [(p, [z for z in range(nz) if (i == 0 or (z >= i if k == 0 else z + i < nz)) and (z < nz - 1 if k == 0 else z > 0)]) for (i, k), p in self.go_on.items()]

GQ = (("r", "zy", 0, 768),)
GO = (("o", "yxz", 0, 384),)
GU = (("u", "yxz", 0, 512), ("v", "zxy", 512, 1536))
GD = (("d", "zxy", 0, 256), ("e", "zyx", 256, 384))

def everyone(nz):
    return [(b // 4, b % 4) for b in range(nz * 8)]

def full_barrier(nz, me):
    bar = pltpu.get_barrier_semaphore()
    for b, dev in enumerate(everyone(nz)):
        @pl.when(me != b)
        def _(): pl.semaphore_signal(bar, inc=1, device_id=dev, device_id_type=MESH)
    pl.semaphore_wait(bar, nz * 8 - 1)

def slabs_to_rows(slabs, count, width, out):
    lane = lax.broadcasted_iota(jnp.int32, (8, 128), 1)
    tiles = [None] * (count * width // 128)
    for b in range(count):
        tile, shift = b * width // 128, b * width % 128
        turned = pltpu.roll(slabs[b], shift, 1) if shift else slabs[b]
        parts = [(tile, turned)]
        if shift + width > 128:
            low = lax.lt(lane, lax.full_like(lane, shift))
            parts = [(tile, jnp.where(low, 0.0, turned)), (tile + 1, jnp.where(low, turned, 0.0))]
        for i, p in parts: tiles[i] = p if tiles[i] is None else tiles[i] + p
    for i, t in enumerate(tiles): out[:, i * 128:(i + 1) * 128] = t

def rows_to_slabs(rows24, rows96, count, out):
    lane = lax.broadcasted_iota(jnp.int32, (8, 128), 1)
    for b in range(count):
        total = None
        for rows, width in ((rows24, 24), (rows96, 96)):
            tile, shift = b * width // 128, b * width % 128
            part = rows[:, tile * 128:(tile + 1) * 128]
            if shift: part = pltpu.roll(part, 128 - shift, 1)
            if shift + width > 128:
                low = lax.lt(lane, lax.full_like(lane, 128 - shift))
                part = jnp.where(low, part, pltpu.roll(rows[:, (tile + 1) * 128:(tile + 2) * 128], 128 - shift, 1))
            part = jnp.where(lax.lt(lane, lax.full_like(lane, width)), part, 0.0)
            total = part if total is None else total + part
        out[b] = total

def fwd_head(i, h, qkv, limit, qT, vT, oT, lse):
    keys, cols = (i + 1) * QB, pl.ds(i * QB, QB)
    slot, hr = pl.ds((h // 2) * 128, 128), pl.ds(h * 64, 64)
    sT = dot(qkv[0:keys, 256 + (h // 2) * 128:384 + (h // 2) * 128], pick(qT[slot, cols], h))
    sT = mask_scores(sT, i, limit)
    m = jnp.max(sT, axis=0, keepdims=True)
    p = jnp.exp(sT - m)
    l = jnp.sum(p, axis=0, keepdims=True)
    oT[hr, cols] = dot(vT[hr, 0:keys], p.astype(BF)) * (1.0 / l)
    lse[h:h + 1, cols] = m + jnp.log(l)

def fwd_kernel(first, final, nz, names, *refs):
    r_ = dict(zip(names, refs))
    R = lambda *ns: [r_[n] for n in ns]
    lim, x, wq, wou, wd, n1, qkv, qT, vT, oT, o, lse, og, r, n2, gp, a, xo = R("lim", "x", "wq_v", "wou_v", "wd_v", "n1_v", "qkv_v", "qT", "vT", "oT", "o_v", "lse_v", "og_v", "r_v", "n2_v", "gp_v", "a_v", "xo_v")
    d = lax.axis_index("dp"); f = lax.axis_index("fsdp")
    ZERO[0] = f * 0
    mem = Copies(r_["lsem"])
    net = Links(r_["ssem"], r_["rsem"], (d, f ^ 1))
    agenda = Agenda(GATHER_PLAN if first and nz == 4 else ())
    limit = lim[0]
    stores = []
    def store(name): stores.append(mem.go(r_[name + "_v"], r_[name]))
    if first:
        me = d * 4 + f
        c = f % 2
        vecs, bias, slabs, slab = r_["vecs"], r_["biasr"], r_["slabs"], r_["slab"]
        q4, ow, uw, dn, rq, ro, ru = R("q4", "ow", "uw", "dn", "rq", "ro", "ru")
        full_barrier(nz, me)
        sp = (d, f ^ 1)
        k_all = net.send_all(slab, slabs, nz)
        slabs[me] = slab[...]
        z, y, xx = d // 2, d % 2, f // 2
        k_o, k_u, k_d = net.sem(), net.sem(), net.sem()
        net.send(ow, ro, k_o, sp)
        net.send(uw, ru, k_u, sp)
        k_q = [net.sem() for _ in range(4)]
        for k in (1, 2, 3): net.send(q4.at[f ^ k], rq.at[f], k_q[k], (d, f ^ k))
        half = lambda cc: pl.ds(pl.multiple_of(cc * 384, 128), 384)
        net.send(dn.at[:, half(1 - c)], wd.at[z, y, xx, pl.ds(pl.multiple_of(c * 96, 16), 96), half(1 - c)], k_d, sp)
        own_d = pltpu.make_async_copy(dn.at[:, half(c)], wd.at[z, y, xx, pl.ds(pl.multiple_of(c * 96, 16), 96), half(c)], at(r_["lsem"], 31))
        own_d.start()
        rq[f] = q4[f]
        S_ = Spreads(nz, net, agenda, wq, wou, wd)
        first_core = c == 0
        def merge(own, other):
            m_, o_ = own[...].astype(F32), other[...].astype(F32)
            return jnp.concatenate([jnp.where(first_core, m_, o_), jnp.where(first_core, o_, m_)], axis=0).astype(BF)
        for k in (1, 2, 3): net.got(rq.at[f ^ k], k_q[k])
        wq[z, y, 0] = jnp.concatenate([rq[k].astype(F32) for k in range(4)], axis=0).astype(BF)
        for p in S_.Q: p.start()
        agenda.run()
        net.got(ro, k_o)
        r_["bo"][...] = merge(ow, ro)
        net.got(ru, k_u)
        r_["bu"][...] = merge(uw, ru)
        wide = lambda cc: pl.ds(pl.multiple_of(cc * 1536, 128), 1536)
        lo = [pltpu.make_async_copy(r_["bo"].at[:, half(c)], wou.at[z, y, xx, pl.ds(0, 48), half(c)], at(r_["lsem"], 30)),
              pltpu.make_async_copy(r_["bu"].at[:, wide(c)], wou.at[z, y, xx, pl.ds(0, 48), pl.ds(pl.multiple_of(D + c * 1536, 128), 1536)], at(r_["lsem"], 29))]
        for w in lo: w.start()
        for w in lo: w.wait()
        for p in S_.O + S_.U: p.start()
        agenda.run()
        own_d.wait()
        net.got(wd.at[z, y, xx, pl.ds(pl.multiple_of((1 - c) * 96, 16), 96), half(c)], k_d)
        for p in S_.D: p.start()
        net.got_all(slabs, k_all)
        slabs_to_rows(slabs, nz * 8, 24, r_["rows24"])
        slabs_to_rows(slabs, nz * 8, 96, r_["rows96"])
        vecs[0:4, :] = r_["rows24"][1:5, :]
        vecs[4:8, :] = jnp.zeros((4, D), F32)
        bias[...] = r_["rows96"][0:1, :]
        g0, g1, emb = vecs[0:1, :], vecs[1:2, :], vecs[2:3, :]
    else:
        loads = [mem.go(r_[n], r_[n + "_v"]) for n in ("wq", "wou", "wd")]
        vecs, bias = r_["vecs"], r_["biasr"]
        g0, g1, emb = vecs[0:1, :], vecs[1:2, :], vecs[3:4, :]
        group_barrier(d, f)
    k_n = [[net.sem() for _ in range(3)] for _ in range(3)]
    for j in range(T // CH):
        rows = pl.ds(j * CH, CH)
        xhat, _ = normed(x[rows, :].astype(F32) + emb)
        n1[f, rows, :] = (xhat * g0).astype(BF)
        reg = n1.at[f, rows, :]
        net.send(reg, reg, k_n[0][j], (d, f ^ 2))
        net.send(reg, reg, k_n[1][j], (d, f ^ 1))
    if first:
        for p in S_.Q:
            agenda.run(hold=True)
            p.wait()
        store("wq")
    else: loads[0].wait()
    def project(k):
        for j in range(2):
            rows = rows_at(j * 192, 192)
            qkv[rows_at(k * T + j * 192, 192), :] = dot(n1[k, rows, :], wq[...].reshape(D, D)).astype(BF)
    project(f)
    agenda.run()
    for j in range(3): net.got(n1.at[f ^ 1, pl.ds(j * CH, CH), :], k_n[1][j])
    project(f ^ 1)
    for j in range(3):
        agenda.run(hold=True)
        reg = n1.at[f ^ 2, pl.ds(j * CH, CH), :]
        net.got(reg, k_n[0][j])
        net.send(reg, reg, k_n[2][j], (d, f ^ 1))
    project(f ^ 2)
    agenda.run()
    for j in range(3): net.got(n1.at[f ^ 3, pl.ds(j * CH, CH), :], k_n[2][j])
    project(f ^ 3)
    store("n1"); store("qkv")
    qT[...] = (qkv[:, 0:256] * 0.125).astype(BF).T
    vT[...] = qkv[:, 512:768].T
    oT[192:256, :] = jnp.zeros((64, S), F32)
    lse[...] = jnp.zeros_like(lse)
    agenda.run()
    k_og = [net.sem() for _ in range(4)]
    def finish(b):
        rows = pl.ds(b * T, T)
        o[rows, :] = oT[:, rows].astype(BF).T
        @pl.when(f == b)
        def _(): og[b] = o[rows, :]
        for k in (1, 2, 3):
            net.send(o.at[rows, :], og.at[f], k_og[k], (d, f ^ k), (f ^ k) == b)
    for i in reversed(range(S // QB)):
        for h in range(3):
            fwd_head(i, h, qkv, limit, qT, vT, oT, lse)
            agenda.run()
        for b in reversed(range(4)):
            if i * QB <= b * T and not (b * T >= (i + 1) * QB): finish(b)
    store("o"); store("lse")
    agenda.run(hold=True)
    for k in (1, 2, 3): net.got(og.at[f ^ k], k_og[k])
    store("og")
    if first:
        for p in S_.O:
            agenda.run(hold=True)
            p.wait()
    else: loads[1].wait()
    for j in range(2):
        rows = rows_at(j * 192, 192)
        acc = x[rows, :].astype(F32) + emb
        for k in range(4):
            acc = acc + dot(og[k, rows, 0:192], wou[k * nz // 4:(k + 1) * nz // 4, :, :, :, 0:D].reshape(192, D))
        r[rows, :] = acc
        xhat, _ = normed(acc)
        n2[rows, :] = (xhat * g1).astype(BF)
        agenda.run()
    store("r"); store("n2")
    if first:
        for p in S_.U:
            agenda.run(hold=True)
            p.wait()
        store("wou")
    W = 768
    for j in range(FF // W):
        cols = pl.ds(j * W, W)
        u = dot(n2[...], wou[:, :, :, :, D + j * W:D + (j + 1) * W].reshape(D, W)) + bias[:, cols]
        sq = u * u
        t = jnp.tanh(0.7978845608028654 * u * (1.0 + 0.044715 * sq))
        half_ = 0.5 * (1.0 + t)
        a[:, cols] = (u * half_).astype(BF)
        gp[:, cols] = (half_ + 0.5 * u * (1.0 - t * t) * (0.7978845608028654 * (1.0 + 0.134145 * sq))).astype(BF)
        agenda.run()
    store("gp"); store("a")
    if first:
        for p in S_.D:
            agenda.run(hold=True)
            p.wait()
        store("wd")
    else: loads[2].wait()
    for j in range(D // 256):
        cols = pl.ds(j * 256, 256)
        xo[:, cols] = r[:, cols] + dot(a[...], wd[:, :, :, :, j * 256:(j + 1) * 256].reshape(FF, 256))
    if final:
        ok = lax.broadcasted_iota(jnp.int32, (T, 1), 0) + f * T < limit
        r_["out_v"][...] = jnp.where(ok, xo[...], 0.0).astype(BF)
        store("out")
    else: store("xo")
    agenda.finish()
    net.close()
    for w in stores: w.wait()

def wide_shapes(nz):
    rows = D // (nz * 4)
    return dict(wq=((nz, 2, 1, D // (nz * 2), D), BF), wou=((nz, 2, 2, rows, 3840), BF), wd=((nz, 2, 2, rows * 4, D), BF))

def fwd(lim, x, weights, cid, nz, first=False, final=False):
    hbm = pl.BlockSpec(memory_space=pltpu.HBM); vm = pl.BlockSpec(memory_space=pltpu.VMEM); sm = pl.BlockSpec(memory_space=pltpu.SMEM)
    ins = dict(lim=lim, x=x, **weights)
    ws = wide_shapes(nz)
    kept = dict(n1=((4, T, D), BF), qkv=((S, D), BF), o=((S, 256), BF), lse=((8, S), F32), og=((4, T, 256), BF), r=((T, D), F32), n2=((T, D), BF), gp=((T, FF), BF), a=((T, FF), BF))
    outs = dict(kept)
    if final: outs.update(out=((T, D), BF))
    else: outs.update(xo=((T, D), F32))
    if first: outs.update(ws, vecs=((8, D), F32), biasr=((1, FF), F32))
    scratch = {n + "_v": s for n, s in dict(kept, xo=((T, D), F32), **ws).items()}
    if final: scratch.update(out_v=((T, D), BF))
    scratch.update(qT=((256, S), BF), vT=((256, S), BF), oT=((256, S), F32))
    if first:
        scratch.update(slabs=((nz * 8, 8, 128), F32), rows24=((8, D), F32), rows96=((8, FF), F32), rq=((4, 24, D), BF), ro=((24, D), BF), ru=((24, FF), BF), bo=((48, D), BF), bu=((48, FF), BF))
    sems = 320 if first else 24
    names = list(ins) + list(outs) + list(scratch) + ["lsem", "ssem", "rsem"]
    inner = ("wq", "wou", "wd")
    place_of = lambda n: sm if n == "lim" else vm if n in ("x", "vecs", "biasr", "q4", "ow", "uw", "dn", "slab") else hbm
    res = pl.pallas_call(partial(fwd_kernel, first, final, nz, names),
        out_shape=[jax.ShapeDtypeStruct(*s) for s in outs.values()],
        in_specs=[place_of(n) for n in ins], out_specs=[place_of(n) for n in outs],
        scratch_shapes=[pltpu.VMEM(*s) for s in scratch.values()] + [pltpu.SemaphoreType.DMA((32,)), pltpu.SemaphoreType.DMA((sems,)), pltpu.SemaphoreType.DMA((sems,))],
        compiler_params=pltpu.CompilerParams(collective_id=cid, has_side_effects=True, vmem_limit_bytes=VMEM_LIMIT))(*ins.values())
    return dict(zip(outs, res))

def gather_any(q4, ow, uw, dn, slab, nz):
    both = ("dp", "fsdp")
    wq = lax.dynamic_index_in_dim(lax.all_gather(q4, both, axis=0), lax.axis_index("fsdp"), 1, keepdims=False)
    slabs = lax.all_gather(slab, both, axis=0)
    rd = q4.shape[1]
    vecs = jnp.concatenate([slabs[:, 1:5, :rd].transpose(1, 0, 2).reshape(4, D), jnp.zeros((4, D), F32)], axis=0)
    wou = lax.all_gather(jnp.concatenate([ow, uw], axis=1), both, axis=0, tiled=True)
    shapes = wide_shapes(nz)
    return dict(wq=wq.reshape(shapes["wq"][0]), wou=wou.reshape(shapes["wou"][0]), wd=lax.all_gather(dn, both, axis=0, tiled=True).reshape(shapes["wd"][0]),
                vecs=vecs, biasr=slabs[:, 0, :4 * rd].reshape(1, FF))

def grads_any(own, vin, rd):
    both = ("dp", "fsdp")
    scatter = lambda v: lax.psum_scatter(v, both, scatter_dimension=0, tiled=True)
    down, out, up, q = own
    q = lax.dynamic_update_slice(jnp.zeros((4, D // rd, rd, D), F32), q.reshape(1, D // rd, rd, D), (lax.axis_index("fsdp"), 0, 0, 0))
    q_grad = lax.psum_scatter(q, both, scatter_dimension=1, tiled=True).reshape(4, rd, D)
    idx = lax.axis_index("dp") * 4 + lax.axis_index("fsdp")
    tot = lax.psum(vin, both)
    rows = lax.dynamic_slice_in_dim(tot[0:4], idx * rd, rd, 1)
    bias = lax.dynamic_slice_in_dim(tot[4:8].reshape(1, FF), idx * rd * 4, rd * 4, 1)
    slab = jnp.concatenate([jnp.pad(bias, ((0, 0), (0, 128 - rd * 4))), jnp.pad(rows, ((0, 3), (0, 128 - rd)))], axis=0)
    return scatter(down), scatter(out), scatter(up), q_grad, slab

def w_emb(w, n):
    return dict(w, vecs=jnp.concatenate([w["vecs"][0:3], w["vecs"][2 + n:3 + n], w["vecs"][4:8]], axis=0))

def body(tokens, qkv_weight, out_weight, up_weight, down_weight, norm_gains, up_bias, pass_table, pass_index, lengths, cotangent):
    rd = qkv_weight.shape[0]
    fast = rd == 24
    nz = lax.axis_size("dp") // 2 if fast else 4
    f = lax.axis_index("fsdp")
    q4 = jnp.pad(qkv_weight.reshape(rd, 3, 4, 192), ((0, 0), (0, 0), (0, 0), (0, 64))).transpose(2, 0, 1, 3).reshape(4, rd, D)
    chooser = [(jnp.arange(pass_table.shape[1], dtype=jnp.int32) == pass_index[n]).astype(F32) for n in range(2)]
    emb = [jnp.sum(pass_table.astype(F32) * ch[None, :], axis=1) for ch in chooser]
    rows = jnp.stack([norm_gains[:, 0].astype(F32), norm_gains[:, 1].astype(F32)] + emb)
    slab = jnp.concatenate([jnp.pad(up_bias.astype(F32)[None, :], ((0, 0), (0, 128 - 4 * rd))), jnp.pad(rows, ((0, 3), (0, 128 - rd)))], axis=0)
    own = dict(q4=q4, ow=out_weight, uw=up_weight, dn=down_weight, slab=slab)
    if fast:
        k0 = fwd(lengths, tokens, own, 0, nz, first=True)
        w = {n: k0[n] for n in ("wq", "wou", "wd", "vecs", "biasr")}
    else:
        w = gather_any(*own.values(), nz)
        k0 = fwd(lengths, tokens, w_emb(w, 0), 1, nz)
    k1 = fwd(lengths, k0["xo"], w, 1, nz, final=True)
    big = (w["wq"], w["wou"], w["wd"])
    b1 = bwd(lengths, cotangent, k0["xo"], w["vecs"], *big, k1, 2, nz)
    if fast:
        left = dict(gd_1=b1["gd_o"], gu_1=b1["gu_o"], gw_1=b1["gw_o"], gq_1=b1["gq_o"], sums_1=b1["sums"], bsum_1=b1["bsum"])
        b0 = bwd(lengths, b1["go_o"], tokens, w["vecs"], *big, k0, 3, nz, left)
        down_grad, out_grad, up_grad, q_grad, tot = b0["down_o"], b0["outw_o"], b0["up_o"], b0["qkv_o"], b0["v_o"]
    else:
        b0 = bwd(lengths, b1["go_o"], tokens, w_emb(w, 0)["vecs"], *big, k0, 2, nz)
        s0, s1 = b0["sums"], b1["sums"]
        vin = jnp.concatenate([s0[0:2] + s1[0:2], s0[2:3], s1[2:3], (b0["bsum"] + b1["bsum"]).reshape(4, D)], axis=0)
        down_grad, out_grad, up_grad, q_grad, tot = grads_any([b0[n].astype(F32) + b1[n].astype(F32) for n in ("gd_o", "gw_o", "gu_o", "gq_o")], vin, rd)
    qkv_grad = q_grad.reshape(4, rd, 3, 256)[..., :192].transpose(1, 2, 0, 3).reshape(rd, 3 * D)
    gains = tot[1:3, :rd].T
    table = tot[3, :rd][:, None] * chooser[0][None] + tot[4, :rd][:, None] * chooser[1][None]
    bias_grad = tot[0, :rd * 4]
    return (k1["out"], b0["go_o"], qkv_grad, out_grad, up_grad, down_grad, gains, bias_grad, table)

def solution(mesh):
    a = P(("dp", "fsdp"), None); b = P(("dp", "fsdp"))
    return jax.shard_map(body, mesh=mesh, in_specs=(a, a, a, a, a, a, b, a, P(), P("dp"), a), out_specs=(a, a, a, a, a, a, a, b, a), check_vma=False)
```

```python
from functools import partial
import jax
import jax.numpy as jnp
from jax import lax
from jax.experimental import pallas as pl
from jax.experimental.pallas import tpu as pltpu
from jax.sharding import PartitionSpec as P
BF=jnp.bfloat16; F32=jnp.float32
MESH = pl.DeviceIdType.MESH
NEG = -1e30
QB = 512
VMEM_LIMIT = 62 * 2**20

def remote(src, dst, ssem, rsem, dev):
    return pltpu.make_async_remote_copy(src_ref=src, dst_ref=dst, send_sem=ssem, recv_sem=rsem, device_id=dev, device_id_type=MESH)

def rows_at(start, count, step=16):
    return pl.ds(pl.multiple_of(start, step), count)

def normed(values):
    center = values - jnp.mean(values, axis=-1, keepdims=True)
    spread = jnp.mean(center * center, axis=-1, keepdims=True)
    scale = lax.rsqrt(spread + 1e-05)
    return center * scale, scale

def norm_back(xhat, scale, grad_out, gain):
    eg = grad_out * gain
    first = jnp.mean(eg, axis=-1, keepdims=True)
    second = jnp.mean(eg * xhat, axis=-1, keepdims=True)
    return scale * (eg - first - xhat * second)

def nt(left, right):
    return lax.dot_general(left, right, (((1,), (1,)), ((), ())), preferred_element_type=F32)

def dot(left, right):
    return jnp.dot(left, right, preferred_element_type=F32)

def mask_scores(sT, i, limit):
    lo = i * QB
    free = min(lo, 1024)
    parts = []
    if free: parts.append(sT[:free])
    if lo > free:
        kpos = free + lax.broadcasted_iota(jnp.int32, (lo - free, QB), 0)
        parts.append(jnp.where(kpos < limit, sT[free:lo], NEG))
    kpos = lo + lax.broadcasted_iota(jnp.int32, (QB, QB), 0)
    ok = kpos <= lo + lax.broadcasted_iota(jnp.int32, (QB, QB), 1)
    if lo + QB > 1024: ok = ok & (kpos < limit)
    parts.append(jnp.where(ok, sT[lo:], NEG))
    return parts[0] if len(parts) == 1 else jnp.concatenate(parts, 0)

def half_mask(index, h):
    edge = lax.full_like(index, 64)
    return lax.lt(index, edge) if h % 2 == 0 else lax.ge(index, edge)

def pick(xT, h):
    r = lax.broadcasted_iota(jnp.int32, xT.shape, 0)
    mine = half_mask(r, h) if isinstance(h, int) else (r // 64) == (h % 2)
    return jnp.where(mine, xT, jnp.zeros_like(xT))

def slot_of(h, base=0):
    return pl.ds(pl.multiple_of(base + (h // 2) * 128, 128), 128)

BWD_STEPS = ((0, 0, 1), (1, 0, 2), (2, 0, 2), (2, 2, 3))

def bwd_block(i, k0, k1, h, qkv, do, lse, limit, qT, kT, doT, dqT, delta, dkv):
    keys, cols, n = pl.ds(k0 * QB, (k1 - k0) * QB), pl.ds(i * QB, QB), (k1 - k0) * QB
    slot, hr = pl.ds((h // 2) * 128, 128), pl.ds(h * 64, 64)
    after = lambda base: pl.ds(base + (h // 2) * 128, 128)
    lane = lax.broadcasted_iota(jnp.int32, (QB, 128), 1)
    lm = half_mask(lane, h)
    sT = dot(qkv[keys, after(256)], pick(qT[slot, cols], h))
    p = jnp.exp(sT - lse[h:h + 1, cols])
    if k1 == i + 1:
        kpos = i * QB + lax.broadcasted_iota(jnp.int32, (QB, QB), 0)
        ok = kpos <= i * QB + lax.broadcasted_iota(jnp.int32, (QB, QB), 1)
        if k1 * QB > 1024: ok = ok & (kpos < limit)
        diagonal = jnp.where(ok, p[n - QB:], 0.0)
        p = diagonal if n == QB else jnp.concatenate([p[:n - QB], diagonal], axis=0)
    assert k1 == i + 1 or k1 * QB <= 1024
    dp = dot(qkv[keys, after(512)], pick(doT[slot, cols], h))
    dsT = (p * (dp - delta[h:h + 1, cols])).astype(BF)
    step = dot(kT[hr, keys], dsT)
    dqT[hr, cols] = step if k0 == 0 else dqT[hr, cols] + step
    qn, dn = qkv[cols, slot], do[cols, slot]
    dkv[keys, slot] += dot(dsT, jnp.where(lm, qn, jnp.zeros_like(qn)))
    dkv[keys, after(256)] += dot(p.astype(BF), jnp.where(lm, dn, jnp.zeros_like(dn)))

def group_barrier(d, f):
    bar = pltpu.get_barrier_semaphore()
    for k in (1, 2, 3):
        pl.semaphore_signal(bar, inc=1, device_id=(d, f ^ k), device_id_type=MESH)
    pl.semaphore_wait(bar, 3)

T, D, FF, S = 384, 768, 3072, 1536
CH = 128


ZERO = [None]

def at(ref, *index):
    return ref.at[tuple(ZERO[0] + i if isinstance(i, int) else i for i in index)]

def tn(left, right):
    return lax.dot_general(left, right, (((0,), (0,)), ((), ())), preferred_element_type=F32)

def when(pred, act):
    if pred is None: act()
    else: pl.when(pred)(act)

class Links:
    def __init__(self, ssem, rsem, dev):
        self.ssem, self.rsem, self.dev, self.n, self.sent, self.all = ssem, rsem, dev, 0, [], []
    def sem(self):
        self.n += 1
        return self.n - 1
    def send(self, src, dst, k, dev, pred=None):
        when(pred, remote(src, dst, at(self.ssem, k), at(self.rsem, k), dev).start)
        self.sent.append((pred, src, k))
    def got(self, region, k, pred=None):
        when(pred, remote(region, region, at(self.ssem, k), at(self.rsem, k), self.dev).wait_recv)
    def send_all(self, src, dst, nz):
        k, me = self.sem(), lax.axis_index("dp") * 4 + lax.axis_index("fsdp")
        for b, dev in enumerate(everyone(nz)):
            one = src if len(src.shape) == 2 else at(src, b)
            pl.when(me != b)(remote(one, at(dst, me), at(self.ssem, k), at(self.rsem, k), dev).start)
        self.all.append((dst, k))
        return k
    def got_all(self, dst, k):
        every = at(dst, pl.ds(0, dst.shape[0] - 1))
        remote(every, every, at(self.ssem, k), at(self.rsem, k), self.dev).wait_recv()
    def close(self):
        for pred, src, k in self.sent:
            base = getattr(src, "ref", src)
            like = at(base, *([0] * (len(base.shape) - len(src.shape)) + [pl.ds(0, n) for n in src.shape]))
            when(pred, remote(like, like, at(self.ssem, k), at(self.rsem, k), self.dev).wait_send)
        for dst, k in self.all:
            every = at(dst, pl.ds(0, dst.shape[0] - 1))
            remote(every, every, at(self.ssem, k), at(self.rsem, k), self.dev).wait_send()
        self.sent, self.all = [], []

PLAN = (
    (), (), (), (), (), (), (), (), (), (973, 983), (970, 980), (972, 982), (983, 971, 981, 1113, 1110, 973, 1112, 1111, 970),
    (983, 970, 980, 972, 982, 971, 1123, 973, 1120, 1113), (), (), (1122, 1121, 970, 981, 1110, 972), (983,), (980, 1112),
    (973, 970, 982, 1111, 1123, 972), (), (983, 980, 1113, 1120, 973), (982, 971, 1123), (), (980, 981, 1113, 1112, 1120, 1122, 971, 1110, 979), (),
    (), (1121,), (1113, 1112, 1123, 1122, 979, 981, 1111, 989), (), (), (), (1110, 1120, 1121, 1143, 1140, 1142, 1141),
    (1111, 1123, 1122, 989, 1133, 1130, 1132, 1131),
    (1110, 1120, 1121, 710, 1119, 1143, 1140, 1133, 1123, 1122, 1142, 1130, 710, 1120, 1121, 1141, 1143, 1132, 1140, 1133, 1142, 1131, 1130, 710, 860, 1143, 1140, 1141, 1132, 1119, 1133, 1149, 1131, 1130, 860, 1149, 1132, 1133, 1131, 1130),
)
GATHER_PLAN = (
    (1140,), (1180, 1110),
    (1010, 1170, 1180, 1141, 1140, 1110, 1181, 1010, 1011, 1170, 1000, 1142, 1180, 1182, 1012, 1001, 1141, 1110, 1143, 1011, 1183, 1013, 1181, 1142, 1143),
    (1010, 1012, 1002, 1013), (), (), (), (1170, 1111), (1000,), (1003,), (), (), (1182,), (1181,), (1171, 1183, 1001), (), (1000, 1112), (),
    (1011, 1172, 1182, 1012, 1013, 1183, 1002, 1003, 1113, 1173, 1001), (), (), (), (), (), (1002,), (), (1003,), (), (), (), (),
)

def job(letter, i=0):
    return ord(letter) * 10 + i

class Agenda:
    def __init__(self, plan): self.plan, self.jobs, self.point = plan, {}, 0
    def add(self, name, job): self.jobs[name] = job
    def step(self, name):
        if next(self.jobs[name], self) is self: del self.jobs[name]
    def run(self, hold=False):
        names = self.plan[self.point] if self.point < len(self.plan) else ()
        self.point += 1
        for name in names: self.step(name)
    def need(self, names):
        for name in names:
            while name in self.jobs: self.step(name)
    def finish(self):
        for name in self.plan[self.point] if self.point < len(self.plan) else (): self.step(name)
        while self.jobs:
            for name in list(self.jobs): self.step(name)

def add_to(acc, inc):
    acc[...] = (acc[...].astype(F32) + inc[...].astype(F32)).astype(BF)

class Copies:
    def __init__(self, sems): self.sems, self.n = sems, 0
    def go(self, src, dst):
        copy = pltpu.make_async_copy(src, dst, at(self.sems, self.n))
        self.n += 1
        copy.start()
        return copy
    def wait(self, n, src, dst):
        pltpu.make_async_copy(src, dst, at(self.sems, n)).wait()

def turns(nz):
    out, lo, hi = [], 0, nz - 1
    while lo <= hi:
        out += [hi, lo] if lo < hi else [lo]
        lo, hi = lo + 1, hi - 1
    return out

def place():
    d = lax.axis_index("dp"); f = lax.axis_index("fsdp")
    return d, f, d // 2, d % 2, f // 2, f % 2

D_PIECES = (("a", "xzy", 0, 256), ("b", "yzx", 256, 768))
W_PIECES = (("o", "xzy", 0, 640), ("p", "yxz", 640, 1920))
Q_PIECES = (("r", "zy", 0, 256), ("q", "yz", 256, 768))

class Piece:
    def __init__(self, name, order, rows, cols, nz, pair=True):
        self.name, self.order, self.rows, self.cols, self.nz, self.pair = name, order, rows, cols, nz, pair
        self.nx = 2 if pair else 1
    def live(self, done):
        return ((2,) if "y" not in done else ()) + ((self.nx,) if "x" not in done else ()) + (self.rows, self.cols)
    def buffers(self):
        out = {"acc": (self.nz, 2, self.nx, self.rows, self.cols)}
        if self.pair: out["stg"] = out["sib"] = out["acc"]
        done = ""
        for axis in self.order:
            if axis == "z": out["z"] = (2, self.nz) + self.live(done)
            else: out[axis] = (() if "z" in done else (self.nz,)) + self.live(done + axis)
            done += axis
        return {self.name + k: (s, BF) for k, s in out.items()}
    def bind(self, bufs, s):
        self.s, self.net, self.agenda = s, s.net, s.agenda
        self.b = {k[len(self.name):]: v for k, v in bufs.items() if k.startswith(self.name) and k[len(self.name):] in ("acc", "stg", "sib", "x", "y", "z")}
        self.sems, self.flows, self.done = {}, 0, False
        return self
    def view(self, t, done, other=""):
        s = self.s
        ys = pl.ds(0, 2) if "y" not in done else 1 - s.y if other == "y" else s.y
        xs = pl.ds(0, self.nx) if "x" not in done else 1 - s.x if other == "x" else s.x
        return at(self.b["acc"], t, ys, xs)
    def start(self, t):
        if self.pair:
            self.sems[t] = self.net.sem()
            self.net.send(at(self.b["stg"], t), at(self.b["sib"], t), self.sems[t], self.s.sp)
        self.agenda.add(job(self.name, t), self.plane(t))
    def exchange(self, axis, t, done):
        k = self.net.sem()
        self.net.send(self.view(t, done + axis, axis), self.inbox(axis, t, done), k, self.s.xp if axis == "x" else self.s.yp)
        return k
    def inbox(self, axis, t, done):
        return self.b[axis] if "z" in done else at(self.b[axis], t)
    def plane(self, t):
        if self.pair:
            self.net.got(at(self.b["sib"], t), self.sems[t])
            add_to(at(self.b["acc"], t), at(self.b["sib"], t))
        done = ""
        for axis in self.order:
            if axis == "z": break
            k = self.exchange(axis, t, done)
            done += axis
            yield
            buf = self.inbox(axis, t, done)
            self.net.got(buf, k)
            add_to(self.view(t, done), buf)
        yield from self.flow(t, done)
        self.flows += 1
        if self.flows == self.nz:
            if self.order[-1] == "z": self.done = True
            else: self.agenda.add(job(self.name, 9), self.rest())
    def flow(self, t, done):
        nz, s, ks, recv = self.nz, self.s, (self.net.sem(), self.net.sem()), self.b["z"]
        far = max(t, nz - 1 - t)
        for h in range(far):
            if h: yield
            for way, total, here, dev in ((0, t, s.is_z[h], s.up), (1, nz - 1 - t, s.is_z[nz - 1 - h], s.down)):
                if h < total:
                    inc = at(recv, way, t)
                    if h:
                        self.net.got(inc, ks[way], here)
                        pl.when(here)(lambda inc=inc: add_to(self.view(t, done), inc))
                    self.net.send(self.view(t, done), inc, ks[way], dev, here)
        yield
        if t > 0: self.net.got(at(recv, 0, t), ks[0], s.is_z[t])
        if t < nz - 1: self.net.got(at(recv, 1, t), ks[1], s.is_z[t])
    def rest(self):
        s, i = self.s, self.order.index("z")
        done = self.order[:i + 1]
        own = self.view(s.z, done)
        for pred, way in ((s.has_below, 0), (s.has_above, 1)):
            pl.when(pred)(lambda way=way: add_to(own, at(self.b["z"], way, s.z)))
        for axis in self.order[i + 1:]:
            k = self.exchange(axis, s.z, done)
            done += axis
            yield
            buf = self.inbox(axis, s.z, done)
            self.net.got(buf, k)
            if axis != self.order[-1]: add_to(self.view(s.z, done), buf)
        self.done = True
    def total(self):
        assert self.done
        s, last = self.s, self.order[-1]
        sum_ = self.b["acc"][s.z, s.y, s.x if self.pair else 0].astype(F32)
        if last != "z": return sum_ + self.b[last][...].astype(F32).reshape(sum_.shape)
        for pred, way in ((s.has_below, 0), (s.has_above, 1)):
            sum_ = sum_ + jnp.where(pred, self.b["z"][way, s.z].astype(F32).reshape(sum_.shape), 0.0)
        return sum_

class Sums:
    def __init__(self, nz, net, agenda, bufs, outs, vin):
        self.nz, self.net, self.agenda, self.b, self.o, self.vin = nz, net, agenda, bufs, outs, vin
        self.d, self.f, self.z, self.y, self.x, self.c = place()
        d, f = self.d, self.f
        self.up, self.down = (d + 2, f), (d - 2, f)
        self.yp, self.xp, self.sp = (d ^ 1, f), (d, f ^ 2), (d, f ^ 1)
        self.turn = turns(nz)
        z = self.z
        self.is_z = [z == h for h in range(nz)]
        self.has_below, self.has_above, self.core0 = z > 0, z < nz - 1, self.c == 0
        self.D, self.W, self.Q = [[p.bind(bufs, self) for p in ps] for ps in pieces(nz)]
    def first(self, v): return jnp.where(self.core0, v[0], v[1])
    def second(self, v): return jnp.where(self.core0, v[1], v[0])
    def cols(self, ref, width, off, n, mine, rows=None):
        cc = self.c if mine else 1 - self.c
        return ref[slice(None) if rows is None else rows, pl.ds(pl.multiple_of(cc * width + off, 128), n)]

    def vectors(self):
        vb, vr = self.b["vb"], self.b["vr"]
        self.vin(vb)
        k = self.net.send_all(vb, vr, self.nz)
        vr[self.d * 4 + self.f] = vb[self.d * 4 + self.f]
        yield
        self.net.got_all(vr, k)
        total = vr[0]
        for n in range(1, self.nz * 8): total = total + vr[n]
        self.o["v"][...] = total

    def down_tile(self, t, g):
        g = g.reshape(2, 2, 2, 96, D)
        for p, (_, _, c0, c1) in zip(self.D, D_PIECES):
            for y in range(2):
                for x in range(2):
                    p.b["acc"][t, y, x] = self.first(g[y, x, :, :, c0:c1]).astype(BF)
                    p.b["stg"][t, y, x] = self.second(g[y, x, :, :, c0:c1]).astype(BF)
            p.start(t)
    def wide_piece(self, p, c0, c1, n2, du, og, da, gu, gw):
        for dst, mine in (("acc", True), ("stg", False)):
            if c0 < 384:
                n = min(c1, 384) - c0
                for j in range(4):
                    g = tn(og[j, :, 0:192], self.cols(da, 384, c0, n, mine)) + self.cols(gw, 384, c0, n, mine, pl.ds(j * 192, 192)).astype(F32)
                    p.b[dst][j * self.nz // 4:(j + 1) * self.nz // 4, :, :, :, 0:n] = g.astype(BF).reshape(self.nz // 4, 2, 2, 48, n)
            if c1 > 384:
                lo = max(c0, 384)
                g = tn(n2[...], self.cols(du, 1536, lo - 384, c1 - lo, mine)) + self.cols(gu, 1536, lo - 384, c1 - lo, mine).astype(F32)
                p.b[dst][:, :, :, :, lo - c0:c1 - c0] = g.astype(BF).reshape(self.nz, 2, 2, 48, c1 - lo)
        for t in self.turn: p.start(t)
    def q_piece(self, p, c0, c1, n1, dq, gq):
        for j in range(2):
            g = tn(n1[:, j * 384:(j + 1) * 384], dq[:, c0:c1]) + gq[j * 384:(j + 1) * 384, c0:c1].astype(F32)
            p.b["acc"][j * self.nz // 2:(j + 1) * self.nz // 2] = g.astype(BF).reshape(self.nz // 2, 2, 1, 96, c1 - c0)
        for t in self.turn: p.start(t)
    def ends(self):
        net, half, c, f, qf = self.net, self.b["half"], self.c, self.f, self.b["qf"]
        for p, (_, _, c0, c1) in zip(self.W, W_PIECES):
            total = p.total()
            half[0, :, c0:c1] = self.first((total[0:24], total[24:48]))
            half[1, :, c0:c1] = self.second((total[0:24], total[24:48]))
        kw = net.sem()
        net.send(at(half, 1), at(half, 2), kw, self.sp)
        for p, (_, _, c0, c1) in zip(self.Q, Q_PIECES):
            total = p.total()
            for j in range(4): qf[0, j, :, c0:c1] = total[j * 24:(j + 1) * 24]
        ks = [net.sem() for _ in range(4)]
        for k in (1, 2, 3):
            net.send(at(qf, 0, f ^ k), at(qf, 1, f), ks[k], (self.d, f ^ k))
        self.o["qkv"][f] = qf[0, f]
        for p, (_, _, c0, c1) in zip(self.D, D_PIECES):
            self.o["down"][:, c0:c1] = p.total()
        net.got(at(half, 2), kw)
        for cc, s in ((c, 0), (1 - c, 2)):
            self.o["outw"][:, pl.ds(pl.multiple_of(cc * 384, 128), 384)] = half[s, :, 0:384]
            self.o["up"][:, pl.ds(pl.multiple_of(cc * 1536, 128), 1536)] = half[s, :, 384:1920]
        for k in (1, 2, 3):
            net.got(at(qf, 1, f ^ k), ks[k])
            self.o["qkv"][f ^ k] = qf[1, f ^ k]

def pieces(nz):
    return ([Piece(n, o, 96, c1 - c0, nz) for n, o, c0, c1 in D_PIECES], [Piece(n, o, 48, c1 - c0, nz) for n, o, c0, c1 in W_PIECES],
            [Piece(n, o, 96, c1 - c0, nz, False) for n, o, c0, c1 in Q_PIECES])

def sum_buffers(nz):
    out = dict(rows24=((8, D), F32), rows96=((8, FF), F32), qf=((2, 4, 24, D), F32), half=((3, 24, 1920), F32), vb=((nz * 8, 8, 128), F32), vr=((nz * 8, 8, 128), F32))
    for group in pieces(nz):
        for p in group: out.update(p.buffers())
    return out

def bwd_kernel(last, nz, names, *refs):
    r_ = dict(zip(names, refs))
    R = lambda *ns: [r_[n] for n in ns]
    lim, vec, g_h, x_h, wq_h, wou_h, wd_h, qkv_h, o_h, lse_h, r_h, gp_h = R("lim", "vec", "g", "x", "wq", "wou", "wd", "qkv", "o", "lse", "r", "gp")
    dos, do, mine, part, inc, go, dr, dqkv, sums, bsum = R("dos", "do", "mine", "part", "inc", "go_v", "dr", "dqkv_v", "sums", "bsum")
    d = lax.axis_index("dp"); f = lax.axis_index("fsdp")
    ZERO[0] = f * 0
    mem = Copies(r_["lsem"])
    net = Links(r_["ssem"], r_["rsem"], (d, f ^ 1))
    agenda = Agenda(PLAN if last and nz == 4 else ())
    limit = lim[0]
    g0, g1, emb = vec[0:1, :], vec[1:2, :], vec[2:3, :] if last else vec[3:4, :]
    W = 768
    V, ws = pltpu.VMEM, wide_shapes(nz)
    if last:
        gs = Sums(nz, net, agenda, r_, dict(v=r_["v_o"], down=r_["down_o"], outw=r_["outw_o"], up=r_["up_o"], qkv=r_["qkv_o"]), None)
        sums1, bsum1 = r_["sums_1"], r_["bsum_1"]
        def all_sums(out):
            rows24, rows96 = r_["rows24"], r_["rows96"]
            rows24[...] = jnp.concatenate([jnp.zeros((1, D), F32), sums[0:2, :] + sums1[0:2, :], sums[2:3, :], sums1[2:3, :], jnp.zeros((3, D), F32)], axis=0)
            rows96[...] = jnp.concatenate([bsum[...] + bsum1[...], jnp.zeros((7, FF), F32)], axis=0)
            rows_to_slabs(rows24, rows96, nz * 8, out)
        gs.vin = all_sums
    g_in = mem.go(g_h, dr) if last else None
    sums[...] = jnp.zeros_like(sums)

    def phase1(du, dm, da):
        held = []
        def phase1a(wou, r, wd, gp):
            lw, lg = mem.go(wd_h, wd), mem.go(gp_h, gp)
            if last:
                full_barrier(nz, d * 4 + f)
                g_in.wait()
            else:
                group_barrier(d, f)
                ok = lax.lt(lax.broadcasted_iota(jnp.int32, (T, 1), 0) + f * T, lax.broadcast(limit, (T, 1)))
                dr[...] = jnp.where(ok, g_h[...].astype(F32), 0.0)
            dm[...] = dr[...].astype(BF)
            lw.wait(); lg.wait()
            held.append((mem.n, mem.go(wou_h, wou), mem.go(r_h, r)))
            for j in range(FF // W):
                cols = pl.ds(j * W, W)
                t = (nt(dm[...], wd[j * nz // 4:(j + 1) * nz // 4].reshape(W, D)) * gp[:, cols].astype(F32)).astype(BF)
                du[:, cols] = t
                bsum[:, cols] = jnp.sum(t.astype(F32), axis=0, keepdims=True)
                agenda.run()
        def phase1b(wou, r, a, gt, n2, og, gu, gw):
            la = mem.go(r_["a"], a)
            late = [mem.go(r_["n2"], n2), mem.go(r_["og"], og)]
            if last:
                tile = lambda n: mem.go(at(r_["gd_1"], pl.ds(gs.turn[n] * W, W)), at(gt, n % 2))
                tiles = [tile(0), tile(1)]
                late += [mem.go(r_["gu_1"], gu), mem.go(r_["gw_1"], gw)]
            mem.wait(held[0][0], wou_h, wou)
            mem.wait(held[0][0] + 1, r_h, r)
            for j in range(T // 128):
                rows = pl.ds(j * 128, 128)
                e = nt(du[rows, :], wou[:, :, :, :, D:].reshape(D, FF))
                xhat, scale = normed(r[rows, :])
                sums[1:2, :] += jnp.sum(e * xhat, axis=0, keepdims=True)
                t = dr[rows, :] + norm_back(xhat, scale, e, g1)
                dr[rows, :] = t
                da[rows, :] = t.astype(BF)
                agenda.run()
            for k in (3, 2, 1, 0):
                b = f ^ k
                dos[b, :, 0:192] = nt(da[...], wou[pl.ds(b * (nz // 4), nz // 4), :, :, :, 0:D].reshape(192, D)).astype(BF)
                dos[b, :, 192:256] = jnp.zeros((T, 64), BF)
                if k: net.send(at(dos, b), at(do, rows_at(f * T, T)), do_sems[k], (d, b))
                else: do[rows_at(f * T, T), :] = dos[b]
            agenda.run()
            la.wait()
            if last:
                for n, t in enumerate(gs.turn):
                    tiles[n].wait()
                    gs.down_tile(t, tn(a[:, t * W:(t + 1) * W], dm[...]) + gt[n % 2].astype(F32))
                    if n + 2 < nz: tiles.append(tile(n + 2))
                    agenda.run()
            for c in late: c.wait()
            if last:
                for p, (_, _, c0, c1) in zip(gs.W, W_PIECES):
                    gs.wide_piece(p, c0, c1, n2, du, og, da, gu, gw)
                    agenda.run()
            else:
                for j in range(FF // W):
                    rows = pl.ds(j * W, W)
                    r_["gd_v"][rows, :] = tn(a[:, rows], dm[...]).astype(BF)
                for j in range(FF // W):
                    cols = pl.ds(j * W, W)
                    r_["gu_v"][:, cols] = tn(n2[...], du[:, cols]).astype(BF)
                for j in range(4):
                    r_["gw_v"][j * 192:(j + 1) * 192, :] = tn(og[j, :, 0:192], da[...]).astype(BF)
        big, wide = [V((T, FF), BF)], [V((T, D), BF), V((4, T, 256), BF)]
        def with_wide(wou, r):
            pl.run_scoped(partial(phase1a, wou, r), V(*ws["wd"]), V((T, FF), BF))
            if last: pl.run_scoped(partial(phase1b, wou, r), *big, V((2, W, D), BF), *wide, V((D, FF), BF), V((D, D), BF))
            else: pl.run_scoped(lambda a, *v: phase1b(wou, r, a, None, *v, None, None), *big, *wide)
        pl.run_scoped(with_wide, V(*ws["wou"]), V((T, D), F32))
    do_sems = [net.sem() for _ in range(4)]
    pl.run_scoped(phase1, V((T, FF), BF), V((T, D), BF), V((T, D), BF))
    made = [] if last else [mem.go(r_[n + "_v"], r_[n + "_o"]) for n in ("gd", "gu", "gw")]

    def phase2(qkv, o, lse, qT, kT, doT, dqT, delta, dkv):
        loads = [mem.go(*p) for p in ((qkv_h, qkv), (o_h, o), (lse_h, lse))]
        dkv[...] = jnp.zeros_like(dkv)
        dqT[192:256, :] = jnp.zeros((64, S), F32)
        agenda.run()
        for c in loads: c.wait()
        qT[...] = (qkv[:, 0:256] * 0.125).astype(BF).T
        kT[...] = qkv[:, 256:512].T
        agenda.run(hold=True)
        for k in (1, 2, 3): net.got(at(do, rows_at((f ^ k) * T, T)), do_sems[k])
        doT[...] = do[...].T
        prod = (do[...].astype(F32) * o[...].astype(F32)).T
        for h in range(3):
            delta[h:h + 1, :] = jnp.sum(prod[h * 64:h * 64 + 64], axis=0, keepdims=True)
        for step in BWD_STEPS:
            for h in range(3):
                bwd_block(*step, h, qkv, do, lse, limit, qT, kT, doT, dqT, delta, dkv)
                agenda.run()
        dqkv[:, 0:256] = (dqT[...] * 0.125).astype(BF).T
        dqkv[:, 256:512] = (dkv[:, 0:256] * 0.125).astype(BF)
        dqkv[:, 512:768] = dkv[:, 256:512].astype(BF)
    two = (V((S, D), BF), V((S, 256), BF), V((8, S), F32), V((256, S), BF), V((256, S), BF), V((256, S), BF), V((256, S), F32), V((8, S), F32), V((S, 512), F32))

    def phase3(wq, x, n1, gq):
        lw, lx, late = mem.go(wq_h, wq), mem.go(x_h, x), [mem.go(r_["n1"], n1)]
        if last: late.append(mem.go(r_["gq_1"], gq))
        pl.run_scoped(phase2, *two)
        out = []
        lw.wait()
        def partial_rows(b, j):
            return nt(dqkv[rows_at(b * T + j * CH, CH), :], wq[...].reshape(D, D))
        k0, k1, k2 = [[net.sem() for _ in range(3)] for _ in range(3)]
        for j in range(3):
            rows = pl.ds(j * CH, CH)
            mine[0, rows, :] = partial_rows(f ^ 3, j).astype(BF)
            net.send(at(mine, 0, rows), at(part, 0, rows), k0[j], (d, f ^ 1))
        for j in range(3):
            rows = pl.ds(j * CH, CH)
            t = partial_rows(f ^ 2, j)
            agenda.run(hold=True)
            net.got(at(part, 0, rows), k0[j])
            inc[rows, :] = (t + part[0, rows, :].astype(F32)).astype(BF)
            net.send(at(inc, rows), at(part, 2, rows), k2[j], (d, f ^ 2))
        for c in late: c.wait()
        if last:
            agenda.run()
            for p, (_, _, c0, c1) in zip(gs.Q, Q_PIECES):
                gs.q_piece(p, c0, c1, n1, dqkv, gq)
                agenda.run()
        else:
            r_["gq_v"][...] = tn(n1[...], dqkv[...]).astype(BF)
        for j in range(3):
            rows = pl.ds(j * CH, CH)
            mine[1, rows, :] = partial_rows(f ^ 1, j).astype(BF)
            net.send(at(mine, 1, rows), at(part, 1, rows), k1[j], (d, f ^ 1))
        for j in range(3):
            rows = pl.ds(j * CH, CH)
            go[rows, :] = partial_rows(f, j)
        lx.wait()
        def finish_rows():
            for j in range(3):
                rows = pl.ds(j * CH, CH)
                net.got(at(part, 1, rows), k1[j])
                net.got(at(part, 2, rows), k2[j])
                e = go[rows, :] + part[1, rows, :].astype(F32) + part[2, rows, :].astype(F32)
                xhat, scale = normed(x[rows, :].astype(F32) + emb)
                sums[0:1, :] += jnp.sum(e * xhat, axis=0, keepdims=True)
                t = dr[rows, :] + norm_back(xhat, scale, e, g0)
                sums[2:3, :] += jnp.sum(t, axis=0, keepdims=True)
                go[rows, :] = t
                if j < 2: yield
            out.append(mem.go(go, r_["go_o"]))
            if last: agenda.add(job("V"), gs.vectors())
        agenda.add(job("G"), finish_rows())
        agenda.finish()
        if last:
            gs.ends()
        for c in out: c.wait()
    pl.run_scoped(phase3, V(*ws["wq"]), V((T, D), x_h.dtype), V((S, D), BF), V((D, D), BF) if last else V((16, 128), BF))
    if not last: made.append(mem.go(r_["gq_v"], r_["gq_o"]))
    for c in made: c.wait()
    net.close()

def bwd(lim, g, x, vec, wq, wou, wd, kept, cid, nz, last=None):
    n1, qkv, o, lse, og, r, n2, gp, a = [kept[n] for n in ("n1", "qkv", "o", "lse", "og", "r", "n2", "gp", "a")]
    n1 = n1.reshape(S, D)
    hbm = pl.BlockSpec(memory_space=pltpu.HBM); vm = pl.BlockSpec(memory_space=pltpu.VMEM); sm = pl.BlockSpec(memory_space=pltpu.SMEM)
    ins = dict(lim=lim, vec=vec, g=g, x=x, wq=wq, wou=wou, wd=wd, qkv=qkv, o=o, lse=lse, r=r, gp=gp, a=a, n2=n2, og=og, n1=n1)
    scratch = dict(dos=((4, T, 256), BF), do=((S, 256), BF), mine=((2, T, D), BF), part=((3, T, D), BF), inc=((T, D), BF), go_v=((T, D), F32), dr=((T, D), F32), dqkv_v=((S, D), BF))
    outs = dict(go_o=((T, D), F32), sums=((8, D), F32), bsum=((1, FF), F32))
    if last is None:
        for n, s in (("gd", (FF, D)), ("gu", (D, FF)), ("gw", (D, D)), ("gq", (D, D))):
            outs[n + "_o"] = scratch[n + "_v"] = (s, BF)
    else:
        ins.update(last)
        outs.update(down_o=((96, D), F32), outw_o=((24, D), F32), up_o=((24, FF), F32), qkv_o=((4, 24, D), F32), v_o=((8, 128), F32))
    if last is not None: scratch.update(sum_buffers(nz))
    sems = 320 if last is not None else 16
    names = list(ins) + list(outs) + list(scratch) + ["lsem", "ssem", "rsem"]
    place_of = lambda n: sm if n == "lim" else vm if (n == "g" and last is None) or n in ("vec", "sums", "bsum", "sums_1", "bsum_1", "down_o", "outw_o", "up_o", "qkv_o", "v_o") else hbm
    res = pl.pallas_call(partial(bwd_kernel, last is not None, nz, names),
        out_shape=[jax.ShapeDtypeStruct(*s) for s in outs.values()],
        in_specs=[place_of(n) for n in ins], out_specs=[place_of(n) for n in outs],
        scratch_shapes=[pltpu.VMEM(*s) for s in scratch.values()] + [pltpu.SemaphoreType.DMA((32,)), pltpu.SemaphoreType.DMA((sems,)), pltpu.SemaphoreType.DMA((sems,))],
        compiler_params=pltpu.CompilerParams(collective_id=cid, has_side_effects=True, vmem_limit_bytes=VMEM_LIMIT))(*ins.values())
    return dict(zip(outs, res))

class Spread:
    def __init__(self, name, ref, order, rows, cols, width, off, s, pair=True):
        self.name, self.ref, self.order, self.rows, self.cols, self.s = name, ref, order, rows, cols, s
        self.nx, self.sib = (2, True) if pair else (1, False)
        self.mine = pl.multiple_of(off + s.c * width, 128) if pair else off
        self.other = pl.multiple_of(off + (1 - s.c) * width, 128) if pair else off
        self.net, self.agenda, self.late, self.names = s.net, s.agenda, [], []
        self.zsem = {(i, k): s.net.sem() for i in range(1, s.nz) for k in (0, 1)}
    def view(self, t, done, other="", col=None):
        s = self.s
        ys = pl.ds(0, 2) if "y" in done else 1 - s.y if other == "y" else s.y
        xs = pl.ds(0, self.nx) if "x" in done or self.nx == 1 else 1 - s.x if other == "x" else s.x
        return at(self.ref, t, ys, xs, pl.ds(0, self.rows), pl.ds(self.mine if col is None else col, self.cols))
    def add(self, i, steps):
        self.names.append(job(self.name, i))
        self.agenda.add(self.names[-1], steps)
    def start(self): self.add(0, self.first())
    def planes(self, i):
        s = self.s
        return [(s.z, None, 0)] if i == 0 else [(s.z - i, s.ok[i, 0], 0), (s.z + i, s.ok[i, 1], 1)]
    def first(self):
        s, done = self.s, ""
        for axis in self.order:
            if axis == "z": break
            k = self.net.sem()
            self.net.send(self.view(s.z, done), self.view(s.z, done), k, s.xp if axis == "x" else s.yp)
            yield
            self.net.got(self.view(s.z, done, axis), k)
            done += axis
        for k, dev in ((0, s.up), (1, s.down)):
            self.net.send(self.view(s.z, done), self.view(s.z, done), self.zsem[1, k], dev, s.go_on[0, k])
        for i in range(1, s.nz): self.add(i, self.distance(i, done))
        yield from self.after(0, done + "z")
    def distance(self, i, done):
        s = self.s
        for t, ok, k in self.planes(i):
            self.net.got(self.view(t, done), self.zsem[i, k], ok)
            if i + 1 < s.nz:
                self.net.send(self.view(t, done), self.view(t, done), self.zsem[i + 1, k], (s.up, s.down)[k], s.go_on[i, k])
        yield from self.after(i, done + "z")
    def after(self, i, done):
        s = self.s
        for axis in self.order[self.order.index("z") + 1:]:
            ks = []
            for t, ok, _ in self.planes(i):
                ks.append(self.net.sem())
                self.net.send(self.view(t, done), self.view(t, done), ks[-1], s.xp if axis == "x" else s.yp, ok)
            yield
            for k, (t, ok, _) in zip(ks, self.planes(i)): self.net.got(self.view(t, done, axis), k, ok)
            done += axis
        if self.sib:
            for t, ok, _ in self.planes(i):
                k = self.net.sem()
                self.net.send(self.view(t, "xy"), self.view(t, "xy"), k, s.sp, ok)
                self.late.append((i, len(self.late), k))
    def wait(self):
        self.agenda.need(self.names)
        n = {}
        for i, _, k in self.late:
            t, ok, _ = self.planes(i)[n.setdefault(i, 0)]
            n[i] += 1
            self.net.got(self.view(t, "xy", col=self.other), k, ok)

class Spreads:
    def __init__(self, nz, net, agenda, wq, wou, wd):
        self.nz, self.net, self.agenda = nz, net, agenda
        self.d, self.f, self.z, self.y, self.x, self.c = place()
        d, f, z = self.d, self.f, self.z
        self.up, self.down = (d + 2, f), (d - 2, f)
        self.yp, self.xp, self.sp = (d ^ 1, f), (d, f ^ 2), (d, f ^ 1)
        self.ok = {(i, k): (z >= i if k == 0 else z + i < nz) for i in range(1, nz) for k in (0, 1)}
        self.go_on = {(0, 0): z < nz - 1, (0, 1): z > 0}
        for i in range(1, nz - 1):
            self.go_on[i, 0] = self.ok[i, 0] & (z < nz - 1)
            self.go_on[i, 1] = self.ok[i, 1] & (z > 0)
        self.Q = [Spread(n, wq, o, 96, c1 - c0, 0, c0, self, False) for n, o, c0, c1 in GQ]
        self.O = [Spread(n, wou, o, 48, c1 - c0, 384, c0, self) for n, o, c0, c1 in GO]
        self.U = [Spread(n, wou, o, 48, c1 - c0, 1536, D + c0, self) for n, o, c0, c1 in GU]
        self.D = [Spread(n, wd, o, 192, c1 - c0, 384, c0, self) for n, o, c0, c1 in GD]
    def pred_sets(self):
        nz = self.nz
        out = [(self.ok[i, k], [z for z in range(nz) if (z >= i if k == 0 else z + i < nz)]) for i, k in self.ok]
        return out + [(p, [z for z in range(nz) if (i == 0 or (z >= i if k == 0 else z + i < nz)) and (z < nz - 1 if k == 0 else z > 0)]) for (i, k), p in self.go_on.items()]

GQ = (("r", "zy", 0, 768),)
GO = (("o", "yxz", 0, 384),)
GU = (("u", "yxz", 0, 512), ("v", "zxy", 512, 1536))
GD = (("d", "zxy", 0, 256), ("e", "zyx", 256, 384))

def prepare(pidx, gains, table, ub, qw, slab, q4):
    rd = gains.shape[1]
    row = lax.broadcasted_iota(jnp.int32, table.shape, 0)
    slab[...] = jnp.zeros((8, 128), F32)
    slab[0:1, 0:4 * rd] = ub[...].astype(F32)
    slab[1:3, 0:rd] = gains[...].astype(F32)
    for n in range(2):
        slab[3 + n:4 + n, 0:rd] = jnp.sum(jnp.where(row == pidx[n], table[...].astype(F32), 0.0), axis=0, keepdims=True)
    w = qw[...].astype(F32)
    lane = lax.broadcasted_iota(jnp.int32, (rd, 256), 1)
    for k in range(4):
        for part in range(3):
            base = part * D + k * 192
            seg = w[:, base:base + 256] if base % 128 == 0 else pltpu.roll(w[:, base - 64:base + 192], 192, 1)
            q4[k, :, part * 256:(part + 1) * 256] = jnp.where(lane < 192, seg, 0.0).astype(BF)

def last_kernel(pidx, v, q, *refs):
    n = (len(refs) - 4) // 2
    qkv_o, gain_o, bias_o, table_o = refs[n:n + 4]
    rd = gain_o.shape[1]
    for src, dst in zip(refs[:n], refs[n + 4:]): dst[...] = src[...]
    lane = lax.broadcasted_iota(jnp.int32, (rd, 256), 1)
    for part in range(3):
        for pair in range(2):
            one, two = [jnp.where(lane < 192, q[2 * pair + i, :, part * 256:(part + 1) * 256], 0.0) for i in range(2)]
            col = part * D + pair * 384
            two = pltpu.roll(two, 64, 1)
            qkv_o[:, col:col + 128] = one[:, 0:128]
            qkv_o[:, col + 128:col + 256] = one[:, 128:256] + two[:, 0:128]
            qkv_o[:, col + 256:col + 384] = two[:, 128:256]
    bias_o[...] = v[0:1, 0:4 * rd]
    gain_o[...] = v[1:3, 0:rd]
    row = lax.broadcasted_iota(jnp.int32, table_o.shape, 0)
    table_o[...] = jnp.where(row == pidx[0], v[3:4, 0:rd], 0.0) + jnp.where(row == pidx[1], v[4:5, 0:rd], 0.0)

def finish(pidx, v, q, repeats, copied):
    rd = q.shape[1]
    vm = pl.BlockSpec(memory_space=pltpu.VMEM); sm = pl.BlockSpec(memory_space=pltpu.SMEM)
    outs = [jax.ShapeDtypeStruct(s, F32) for s in ((rd, 3 * D), (2, rd), (1, 4 * rd), (repeats, rd))] + [jax.ShapeDtypeStruct(a.shape, a.dtype) for a in copied]
    return pl.pallas_call(last_kernel, out_shape=outs, in_specs=[sm, vm, vm] + [vm] * len(copied), out_specs=[vm] * (4 + len(copied)),
        compiler_params=pltpu.CompilerParams(vmem_limit_bytes=VMEM_LIMIT))(pidx, v, q, *copied)

def everyone(nz):
    return [(b // 4, b % 4) for b in range(nz * 8)]

def full_barrier(nz, me):
    bar = pltpu.get_barrier_semaphore()
    for b, dev in enumerate(everyone(nz)):
        @pl.when(me != b)
        def _(): pl.semaphore_signal(bar, inc=1, device_id=dev, device_id_type=MESH)
    pl.semaphore_wait(bar, nz * 8 - 1)

def slabs_to_rows(slabs, count, width, out):
    lane = lax.broadcasted_iota(jnp.int32, (8, 128), 1)
    tiles = [None] * (count * width // 128)
    for b in range(count):
        tile, shift = b * width // 128, b * width % 128
        turned = pltpu.roll(slabs[b], shift, 1) if shift else slabs[b]
        parts = [(tile, turned)]
        if shift + width > 128:
            low = lax.lt(lane, lax.full_like(lane, shift))
            parts = [(tile, jnp.where(low, 0.0, turned)), (tile + 1, jnp.where(low, turned, 0.0))]
        for i, p in parts: tiles[i] = p if tiles[i] is None else tiles[i] + p
    for i, t in enumerate(tiles): out[:, i * 128:(i + 1) * 128] = t

def rows_to_slabs(rows24, rows96, count, out):
    lane = lax.broadcasted_iota(jnp.int32, (8, 128), 1)
    for b in range(count):
        total = None
        for rows, width in ((rows24, 24), (rows96, 96)):
            tile, shift = b * width // 128, b * width % 128
            part = rows[:, tile * 128:(tile + 1) * 128]
            if shift: part = pltpu.roll(part, 128 - shift, 1)
            if shift + width > 128:
                low = lax.lt(lane, lax.full_like(lane, 128 - shift))
                part = jnp.where(low, part, pltpu.roll(rows[:, (tile + 1) * 128:(tile + 2) * 128], 128 - shift, 1))
            part = jnp.where(lax.lt(lane, lax.full_like(lane, width)), part, 0.0)
            total = part if total is None else total + part
        out[b] = total

def fwd_head(i, h, qkv, limit, qT, vT, oT, lse):
    keys, cols = (i + 1) * QB, pl.ds(i * QB, QB)
    slot, hr = pl.ds((h // 2) * 128, 128), pl.ds(h * 64, 64)
    sT = dot(qkv[0:keys, 256 + (h // 2) * 128:384 + (h // 2) * 128], pick(qT[slot, cols], h))
    sT = mask_scores(sT, i, limit)
    m = jnp.max(sT, axis=0, keepdims=True)
    p = jnp.exp(sT - m)
    l = jnp.sum(p, axis=0, keepdims=True)
    oT[hr, cols] = dot(vT[hr, 0:keys], p.astype(BF)) * (1.0 / l)
    lse[h:h + 1, cols] = m + jnp.log(l)

def fwd_kernel(first, final, nz, names, *refs):
    r_ = dict(zip(names, refs))
    R = lambda *ns: [r_[n] for n in ns]
    lim, x, wq, wou, wd, n1, qkv, qT, vT, oT, o, lse, og, r, n2, gp, a, xo = R("lim", "x", "wq_v", "wou_v", "wd_v", "n1_v", "qkv_v", "qT", "vT", "oT", "o_v", "lse_v", "og_v", "r_v", "n2_v", "gp_v", "a_v", "xo_v")
    d = lax.axis_index("dp"); f = lax.axis_index("fsdp")
    ZERO[0] = f * 0
    mem = Copies(r_["lsem"])
    net = Links(r_["ssem"], r_["rsem"], (d, f ^ 1))
    agenda = Agenda(GATHER_PLAN if first and nz == 4 else ())
    limit = lim[0]
    stores = []
    def store(name): stores.append(mem.go(r_[name + "_v"], r_[name]))
    if first:
        me = d * 4 + f
        c = f % 2
        prepare(*R("pidx", "gains", "table", "ub", "qw", "slab", "q4"))
        vecs, bias, slabs, slab = r_["vecs"], r_["biasr"], r_["slabs"], r_["slab"]
        q4, ow, uw, dn, rq, ro, ru = R("q4", "ow", "uw", "dn", "rq", "ro", "ru")
        full_barrier(nz, me)
        sp = (d, f ^ 1)
        k_all = net.send_all(slab, slabs, nz)
        slabs[me] = slab[...]
        z, y, xx = d // 2, d % 2, f // 2
        k_o, k_u, k_d = net.sem(), net.sem(), net.sem()
        net.send(ow, ro, k_o, sp)
        net.send(uw, ru, k_u, sp)
        k_q = [net.sem() for _ in range(4)]
        for k in (1, 2, 3): net.send(q4.at[f ^ k], rq.at[f], k_q[k], (d, f ^ k))
        half = lambda cc: pl.ds(pl.multiple_of(cc * 384, 128), 384)
        net.send(dn.at[:, half(1 - c)], wd.at[z, y, xx, pl.ds(pl.multiple_of(c * 96, 16), 96), half(1 - c)], k_d, sp)
        own_d = pltpu.make_async_copy(dn.at[:, half(c)], wd.at[z, y, xx, pl.ds(pl.multiple_of(c * 96, 16), 96), half(c)], at(r_["lsem"], 31))
        own_d.start()
        rq[f] = q4[f]
        S_ = Spreads(nz, net, agenda, wq, wou, wd)
        first_core = c == 0
        def merge(own, other):
            m_, o_ = own[...].astype(F32), other[...].astype(F32)
            return jnp.concatenate([jnp.where(first_core, m_, o_), jnp.where(first_core, o_, m_)], axis=0).astype(BF)
        for k in (1, 2, 3): net.got(rq.at[f ^ k], k_q[k])
        wq[z, y, 0] = jnp.concatenate([rq[k].astype(F32) for k in range(4)], axis=0).astype(BF)
        for p in S_.Q: p.start()
        agenda.run()
        net.got(ro, k_o)
        r_["bo"][...] = merge(ow, ro)
        net.got(ru, k_u)
        r_["bu"][...] = merge(uw, ru)
        wide = lambda cc: pl.ds(pl.multiple_of(cc * 1536, 128), 1536)
        lo = [pltpu.make_async_copy(r_["bo"].at[:, half(c)], wou.at[z, y, xx, pl.ds(0, 48), half(c)], at(r_["lsem"], 30)),
              pltpu.make_async_copy(r_["bu"].at[:, wide(c)], wou.at[z, y, xx, pl.ds(0, 48), pl.ds(pl.multiple_of(D + c * 1536, 128), 1536)], at(r_["lsem"], 29))]
        for w in lo: w.start()
        for w in lo: w.wait()
        for p in S_.O + S_.U: p.start()
        agenda.run()
        own_d.wait()
        net.got(wd.at[z, y, xx, pl.ds(pl.multiple_of((1 - c) * 96, 16), 96), half(c)], k_d)
        for p in S_.D: p.start()
        net.got_all(slabs, k_all)
        slabs_to_rows(slabs, nz * 8, 24, r_["rows24"])
        slabs_to_rows(slabs, nz * 8, 96, r_["rows96"])
        vecs[0:4, :] = r_["rows24"][1:5, :]
        vecs[4:8, :] = jnp.zeros((4, D), F32)
        bias[...] = r_["rows96"][0:1, :]
        g0, g1, emb = vecs[0:1, :], vecs[1:2, :], vecs[2:3, :]
    else:
        loads = [mem.go(r_[n], r_[n + "_v"]) for n in ("wq", "wou", "wd")]
        vecs, bias = r_["vecs"], r_["biasr"]
        g0, g1, emb = vecs[0:1, :], vecs[1:2, :], vecs[3:4, :]
        group_barrier(d, f)
    k_n = [[net.sem() for _ in range(3)] for _ in range(3)]
    for j in range(T // CH):
        rows = pl.ds(j * CH, CH)
        xhat, _ = normed(x[rows, :].astype(F32) + emb)
        n1[f, rows, :] = (xhat * g0).astype(BF)
        reg = n1.at[f, rows, :]
        net.send(reg, reg, k_n[0][j], (d, f ^ 2))
        net.send(reg, reg, k_n[1][j], (d, f ^ 1))
    if first:
        for p in S_.Q:
            agenda.run(hold=True)
            p.wait()
        store("wq")
    else: loads[0].wait()
    def project(k):
        for j in range(2):
            rows = rows_at(j * 192, 192)
            qkv[rows_at(k * T + j * 192, 192), :] = dot(n1[k, rows, :], wq[...].reshape(D, D)).astype(BF)
    project(f)
    agenda.run()
    for j in range(3): net.got(n1.at[f ^ 1, pl.ds(j * CH, CH), :], k_n[1][j])
    project(f ^ 1)
    for j in range(3):
        agenda.run(hold=True)
        reg = n1.at[f ^ 2, pl.ds(j * CH, CH), :]
        net.got(reg, k_n[0][j])
        net.send(reg, reg, k_n[2][j], (d, f ^ 1))
    project(f ^ 2)
    agenda.run()
    for j in range(3): net.got(n1.at[f ^ 3, pl.ds(j * CH, CH), :], k_n[2][j])
    project(f ^ 3)
    store("n1"); store("qkv")
    qT[...] = (qkv[:, 0:256] * 0.125).astype(BF).T
    vT[...] = qkv[:, 512:768].T
    oT[192:256, :] = jnp.zeros((64, S), F32)
    lse[...] = jnp.zeros_like(lse)
    agenda.run()
    k_og = [net.sem() for _ in range(4)]
    def finish(b):
        rows = pl.ds(b * T, T)
        o[rows, :] = oT[:, rows].astype(BF).T
        @pl.when(f == b)
        def _(): og[b] = o[rows, :]
        for k in (1, 2, 3):
            net.send(o.at[rows, :], og.at[f], k_og[k], (d, f ^ k), (f ^ k) == b)
    for i, ready in ((0, (0,)), (2, (3,)), (1, (1, 2))):
        for h in range(3):
            fwd_head(i, h, qkv, limit, qT, vT, oT, lse)
            agenda.run()
        for b in ready: finish(b)
    store("o"); store("lse")
    agenda.run(hold=True)
    for k in (1, 2, 3): net.got(og.at[f ^ k], k_og[k])
    store("og")
    if first:
        for p in S_.O:
            agenda.run(hold=True)
            p.wait()
    else: loads[1].wait()
    for j in range(2):
        rows = rows_at(j * 192, 192)
        acc = x[rows, :].astype(F32) + emb
        for k in range(4):
            acc = acc + dot(og[k, rows, 0:192], wou[k * nz // 4:(k + 1) * nz // 4, :, :, :, 0:D].reshape(192, D))
        r[rows, :] = acc
        xhat, _ = normed(acc)
        n2[rows, :] = (xhat * g1).astype(BF)
        agenda.run()
    store("r"); store("n2")
    if first:
        for p in S_.U:
            agenda.run(hold=True)
            p.wait()
        store("wou")
    W = 768
    for j in range(FF // W):
        cols = pl.ds(j * W, W)
        u = dot(n2[...], wou[:, :, :, :, D + j * W:D + (j + 1) * W].reshape(D, W)) + bias[:, cols]
        sq = u * u
        t = jnp.tanh(0.7978845608028654 * u * (1.0 + 0.044715 * sq))
        half_ = 0.5 * (1.0 + t)
        a[:, cols] = (u * half_).astype(BF)
        gp[:, cols] = (half_ + 0.5 * u * (1.0 - t * t) * (0.7978845608028654 * (1.0 + 0.134145 * sq))).astype(BF)
        agenda.run()
    store("gp"); store("a")
    if first:
        for p in S_.D:
            agenda.run(hold=True)
            p.wait()
        store("wd")
    else: loads[2].wait()
    for j in range(D // 256):
        cols = pl.ds(j * 256, 256)
        xo[:, cols] = r[:, cols] + dot(a[...], wd[:, :, :, :, j * 256:(j + 1) * 256].reshape(FF, 256))
    if final:
        ok = lax.broadcasted_iota(jnp.int32, (T, 1), 0) + f * T < limit
        r_["out_v"][...] = jnp.where(ok, xo[...], 0.0).astype(BF)
        store("out")
    else: store("xo")
    agenda.finish()
    net.close()
    for w in stores: w.wait()

def wide_shapes(nz):
    rows = D // (nz * 4)
    return dict(wq=((nz, 2, 1, D // (nz * 2), D), BF), wou=((nz, 2, 2, rows, 3840), BF), wd=((nz, 2, 2, rows * 4, D), BF))

def fwd(lim, x, weights, cid, nz, first=False, final=False):
    hbm = pl.BlockSpec(memory_space=pltpu.HBM); vm = pl.BlockSpec(memory_space=pltpu.VMEM); sm = pl.BlockSpec(memory_space=pltpu.SMEM)
    ins = dict(lim=lim, x=x, **weights)
    ws = wide_shapes(nz)
    kept = dict(n1=((4, T, D), BF), qkv=((S, D), BF), o=((S, 256), BF), lse=((8, S), F32), og=((4, T, 256), BF), r=((T, D), F32), n2=((T, D), BF), gp=((T, FF), BF), a=((T, FF), BF))
    outs = dict(kept)
    if final: outs.update(out=((T, D), BF))
    else: outs.update(xo=((T, D), F32))
    if first: outs.update(ws, vecs=((8, D), F32), biasr=((1, FF), F32))
    scratch = {n + "_v": s for n, s in dict(kept, xo=((T, D), F32), **ws).items()}
    if final: scratch.update(out_v=((T, D), BF))
    scratch.update(qT=((256, S), BF), vT=((256, S), BF), oT=((256, S), F32))
    if first:
        scratch.update(slab=((8, 128), F32), q4=((4, 24, D), BF), slabs=((nz * 8, 8, 128), F32), rows24=((8, D), F32), rows96=((8, FF), F32), rq=((4, 24, D), BF), ro=((24, D), BF), ru=((24, FF), BF), bo=((48, D), BF), bu=((48, FF), BF))
    sems = 320 if first else 24
    names = list(ins) + list(outs) + list(scratch) + ["lsem", "ssem", "rsem"]
    inner = ("wq", "wou", "wd")
    place_of = lambda n: sm if n in ("lim", "pidx") else vm if n in ("x", "vecs", "biasr", "qw", "ow", "uw", "dn", "gains", "table", "ub") else hbm
    res = pl.pallas_call(partial(fwd_kernel, first, final, nz, names),
        out_shape=[jax.ShapeDtypeStruct(*s) for s in outs.values()],
        in_specs=[place_of(n) for n in ins], out_specs=[place_of(n) for n in outs],
        scratch_shapes=[pltpu.VMEM(*s) for s in scratch.values()] + [pltpu.SemaphoreType.DMA((32,)), pltpu.SemaphoreType.DMA((sems,)), pltpu.SemaphoreType.DMA((sems,))],
        compiler_params=pltpu.CompilerParams(collective_id=cid, has_side_effects=True, vmem_limit_bytes=VMEM_LIMIT))(*ins.values())
    return dict(zip(outs, res))

def gather_any(q4, ow, uw, dn, slab, nz):
    both = ("dp", "fsdp")
    wq = lax.dynamic_index_in_dim(lax.all_gather(q4, both, axis=0), lax.axis_index("fsdp"), 1, keepdims=False)
    slabs = lax.all_gather(slab, both, axis=0)
    rd = q4.shape[1]
    vecs = jnp.concatenate([slabs[:, 1:5, :rd].transpose(1, 0, 2).reshape(4, D), jnp.zeros((4, D), F32)], axis=0)
    wou = lax.all_gather(jnp.concatenate([ow, uw], axis=1), both, axis=0, tiled=True)
    shapes = wide_shapes(nz)
    return dict(wq=wq.reshape(shapes["wq"][0]), wou=wou.reshape(shapes["wou"][0]), wd=lax.all_gather(dn, both, axis=0, tiled=True).reshape(shapes["wd"][0]),
                vecs=vecs, biasr=slabs[:, 0, :4 * rd].reshape(1, FF))

def grads_any(own, vin, rd):
    both = ("dp", "fsdp")
    scatter = lambda v: lax.psum_scatter(v, both, scatter_dimension=0, tiled=True)
    down, out, up, q = own
    q = lax.dynamic_update_slice(jnp.zeros((4, D // rd, rd, D), F32), q.reshape(1, D // rd, rd, D), (lax.axis_index("fsdp"), 0, 0, 0))
    q_grad = lax.psum_scatter(q, both, scatter_dimension=1, tiled=True).reshape(4, rd, D)
    idx = lax.axis_index("dp") * 4 + lax.axis_index("fsdp")
    tot = lax.psum(vin, both)
    rows = lax.dynamic_slice_in_dim(tot[0:4], idx * rd, rd, 1)
    bias = lax.dynamic_slice_in_dim(tot[4:8].reshape(1, FF), idx * rd * 4, rd * 4, 1)
    slab = jnp.concatenate([jnp.pad(bias, ((0, 0), (0, 128 - rd * 4))), jnp.pad(rows, ((0, 3), (0, 128 - rd)))], axis=0)
    return scatter(down), scatter(out), scatter(up), q_grad, slab

def w_emb(w, n):
    return dict(w, vecs=jnp.concatenate([w["vecs"][0:3], w["vecs"][2 + n:3 + n], w["vecs"][4:8]], axis=0))

def body(tokens, qkv_weight, out_weight, up_weight, down_weight, norm_gains, up_bias, pass_table, pass_index, lengths, cotangent):
    rd = qkv_weight.shape[0]
    fast = rd == 24
    nz = lax.axis_size("dp") // 2 if fast else 4
    if fast:
        own = dict(pidx=pass_index, qw=qkv_weight, ow=out_weight, uw=up_weight, dn=down_weight, gains=norm_gains.T, table=pass_table.T, ub=up_bias.reshape(1, 4 * rd))
        k0 = fwd(lengths, tokens, own, 0, nz, first=True)
        w = {n: k0[n] for n in ("wq", "wou", "wd", "vecs", "biasr")}
    else:
        q4 = jnp.pad(qkv_weight.reshape(rd, 3, 4, 192), ((0, 0), (0, 0), (0, 0), (0, 64))).transpose(2, 0, 1, 3).reshape(4, rd, D)
        chooser = [(jnp.arange(pass_table.shape[1], dtype=jnp.int32) == pass_index[n]).astype(F32) for n in range(2)]
        emb = [jnp.sum(pass_table.astype(F32) * ch[None, :], axis=1) for ch in chooser]
        rows = jnp.stack([norm_gains[:, 0].astype(F32), norm_gains[:, 1].astype(F32)] + emb)
        slab = jnp.concatenate([jnp.pad(up_bias.astype(F32)[None, :], ((0, 0), (0, 128 - 4 * rd))), jnp.pad(rows, ((0, 3), (0, 128 - rd)))], axis=0)
        w = gather_any(q4, out_weight, up_weight, down_weight, slab, nz)
        k0 = fwd(lengths, tokens, w_emb(w, 0), 1, nz)
    k1 = fwd(lengths, k0["xo"], w, 1, nz, final=True)
    big = (w["wq"], w["wou"], w["wd"])
    b1 = bwd(lengths, cotangent, k0["xo"], w["vecs"], *big, k1, 2, nz)
    if fast:
        left = dict(gd_1=b1["gd_o"], gu_1=b1["gu_o"], gw_1=b1["gw_o"], gq_1=b1["gq_o"], sums_1=b1["sums"], bsum_1=b1["bsum"])
        b0 = bwd(lengths, b1["go_o"], tokens, w["vecs"], *big, k0, 3, nz, left)
        down_grad, out_grad, up_grad, q_grad, tot = b0["down_o"], b0["outw_o"], b0["up_o"], b0["qkv_o"], b0["v_o"]
    else:
        b0 = bwd(lengths, b1["go_o"], tokens, w_emb(w, 0)["vecs"], *big, k0, 2, nz)
        s0, s1 = b0["sums"], b1["sums"]
        vin = jnp.concatenate([s0[0:2] + s1[0:2], s0[2:3], s1[2:3], (b0["bsum"] + b1["bsum"]).reshape(4, D)], axis=0)
        down_grad, out_grad, up_grad, q_grad, tot = grads_any([b0[n].astype(F32) + b1[n].astype(F32) for n in ("gd_o", "gw_o", "gu_o", "gq_o")], vin, rd)
    qkv_grad, gains, bias_grad, table, block_out, input_grad, down_grad, out_grad, up_grad = finish(
        pass_index, tot, q_grad, pass_table.shape[1], (k1["out"], b0["go_o"], down_grad, out_grad, up_grad))
    return (block_out, input_grad, qkv_grad, out_grad, up_grad, down_grad, gains.T, bias_grad.reshape(4 * rd), table.T)

def solution(mesh):
    a = P(("dp", "fsdp"), None); b = P(("dp", "fsdp"))
    return jax.shard_map(body, mesh=mesh, in_specs=(a, a, a, a, a, a, b, a, P(), P("dp"), a), out_specs=(a, a, a, a, a, a, a, b, a), check_vma=False)
```

```python
from functools import partial
import jax
import jax.numpy as jnp
from jax import lax
from jax.experimental import pallas as pl
from jax.experimental.pallas import tpu as pltpu
from jax.sharding import PartitionSpec as P
BF=jnp.bfloat16; F32=jnp.float32
MESH = pl.DeviceIdType.MESH
NEG = -1e30
QB = 512
VMEM_LIMIT = 62 * 2**20

def remote(src, dst, ssem, rsem, dev):
    return pltpu.make_async_remote_copy(src_ref=src, dst_ref=dst, send_sem=ssem, recv_sem=rsem, device_id=dev, device_id_type=MESH)

def rows_at(start, count, step=16):
    return pl.ds(pl.multiple_of(start, step), count)

def normed(values):
    center = values - jnp.mean(values, axis=-1, keepdims=True)
    spread = jnp.mean(center * center, axis=-1, keepdims=True)
    scale = lax.rsqrt(spread + 1e-05)
    return center * scale, scale

def norm_back(xhat, scale, grad_out, gain):
    eg = grad_out * gain
    first = jnp.mean(eg, axis=-1, keepdims=True)
    second = jnp.mean(eg * xhat, axis=-1, keepdims=True)
    return scale * (eg - first - xhat * second)

def nt(left, right):
    return lax.dot_general(left, right, (((1,), (1,)), ((), ())), preferred_element_type=F32)

def dot(left, right):
    return jnp.dot(left, right, preferred_element_type=F32)

def mask_scores(sT, i, limit):
    lo = i * QB
    free = min(lo, 1024)
    parts = []
    if free: parts.append(sT[:free])
    if lo > free:
        kpos = free + lax.broadcasted_iota(jnp.int32, (lo - free, QB), 0)
        parts.append(jnp.where(kpos < limit, sT[free:lo], NEG))
    kpos = lo + lax.broadcasted_iota(jnp.int32, (QB, QB), 0)
    ok = kpos <= lo + lax.broadcasted_iota(jnp.int32, (QB, QB), 1)
    if lo + QB > 1024: ok = ok & (kpos < limit)
    parts.append(jnp.where(ok, sT[lo:], NEG))
    return parts[0] if len(parts) == 1 else jnp.concatenate(parts, 0)

def half_mask(index, h):
    edge = lax.full_like(index, 64)
    return lax.lt(index, edge) if h % 2 == 0 else lax.ge(index, edge)

def pick(xT, h):
    r = lax.broadcasted_iota(jnp.int32, xT.shape, 0)
    mine = half_mask(r, h) if isinstance(h, int) else (r // 64) == (h % 2)
    return jnp.where(mine, xT, jnp.zeros_like(xT))

def slot_of(h, base=0):
    return pl.ds(pl.multiple_of(base + (h // 2) * 128, 128), 128)

BWD_STEPS = ((0, 0, 1), (1, 0, 2), (2, 0, 2), (2, 2, 3))

def bwd_block(i, k0, k1, h, qkv, do, lse, limit, qT, kT, doT, dqT, delta, dkv):
    keys, cols, n = pl.ds(k0 * QB, (k1 - k0) * QB), pl.ds(i * QB, QB), (k1 - k0) * QB
    slot, hr = pl.ds((h // 2) * 128, 128), pl.ds(h * 64, 64)
    after = lambda base: pl.ds(base + (h // 2) * 128, 128)
    lane = lax.broadcasted_iota(jnp.int32, (QB, 128), 1)
    lm = half_mask(lane, h)
    sT = dot(qkv[keys, after(256)], pick(qT[slot, cols], h))
    p = jnp.exp(sT - lse[h:h + 1, cols])
    if k1 == i + 1:
        kpos = i * QB + lax.broadcasted_iota(jnp.int32, (QB, QB), 0)
        ok = kpos <= i * QB + lax.broadcasted_iota(jnp.int32, (QB, QB), 1)
        if k1 * QB > 1024: ok = ok & (kpos < limit)
        diagonal = jnp.where(ok, p[n - QB:], 0.0)
        p = diagonal if n == QB else jnp.concatenate([p[:n - QB], diagonal], axis=0)
    assert k1 == i + 1 or k1 * QB <= 1024
    dp = dot(qkv[keys, after(512)], pick(doT[slot, cols], h))
    dsT = (p * (dp - delta[h:h + 1, cols])).astype(BF)
    step = dot(kT[hr, keys], dsT)
    dqT[hr, cols] = step if k0 == 0 else dqT[hr, cols] + step
    qn, dn = qkv[cols, slot], do[cols, slot]
    dkv[keys, slot] += dot(dsT, jnp.where(lm, qn, jnp.zeros_like(qn)))
    dkv[keys, after(256)] += dot(p.astype(BF), jnp.where(lm, dn, jnp.zeros_like(dn)))

def group_barrier(d, f):
    bar = pltpu.get_barrier_semaphore()
    for k in (1, 2, 3):
        pl.semaphore_signal(bar, inc=1, device_id=(d, f ^ k), device_id_type=MESH)
    pl.semaphore_wait(bar, 3)

T, D, FF, S = 384, 768, 3072, 1536
CH = 128


ZERO = [None]

def at(ref, *index):
    return ref.at[tuple(ZERO[0] + i if isinstance(i, int) else i for i in index)]

def tn(left, right):
    return lax.dot_general(left, right, (((0,), (0,)), ((), ())), preferred_element_type=F32)

def when(pred, act):
    if pred is None: act()
    else: pl.when(pred)(act)

def pack(rows, out):
    h = T // 2
    out[0:T, :] = rows[:, 0:128]
    low, high = rows[0:h, 128:256].astype(F32), rows[h:T, 128:256].astype(F32)
    out[T:T + h, :] = (low + pltpu.roll(high, 64, 1)).astype(BF)

def unpack(packed):
    h = T // 2
    both = packed[T:T + h, :].astype(F32)
    low = lax.lt(lax.broadcasted_iota(jnp.int32, (h, 128), 1), lax.full((h, 128), 64, jnp.int32))
    rest = jnp.concatenate([jnp.where(low, both, 0.0), jnp.where(low, pltpu.roll(both, 64, 1), 0.0)], axis=0)
    return jnp.concatenate([packed[0:T, :], rest.astype(BF)], axis=1)

class Links:
    def __init__(self, ssem, rsem, dev):
        self.ssem, self.rsem, self.dev, self.n, self.sent, self.all = ssem, rsem, dev, 0, [], []
    def sem(self):
        self.n += 1
        return self.n - 1
    def send(self, src, dst, k, dev, pred=None):
        when(pred, remote(src, dst, at(self.ssem, k), at(self.rsem, k), dev).start)
        self.sent.append((pred, src, k))
    def got(self, region, k, pred=None):
        when(pred, remote(region, region, at(self.ssem, k), at(self.rsem, k), self.dev).wait_recv)
    def send_all(self, src, dst, nz):
        k, me = self.sem(), lax.axis_index("dp") * 4 + lax.axis_index("fsdp")
        for b, dev in enumerate(everyone(nz)):
            one = src if len(src.shape) == 2 else at(src, b)
            pl.when(me != b)(remote(one, at(dst, me), at(self.ssem, k), at(self.rsem, k), dev).start)
        self.all.append((dst, k))
        return k
    def got_all(self, dst, k):
        every = at(dst, pl.ds(0, dst.shape[0] - 1))
        remote(every, every, at(self.ssem, k), at(self.rsem, k), self.dev).wait_recv()
    def close(self):
        for pred, src, k in self.sent:
            base = getattr(src, "ref", src)
            like = at(base, *([0] * (len(base.shape) - len(src.shape)) + [pl.ds(0, n) for n in src.shape]))
            when(pred, remote(like, like, at(self.ssem, k), at(self.rsem, k), self.dev).wait_send)
        for dst, k in self.all:
            every = at(dst, pl.ds(0, dst.shape[0] - 1))
            remote(every, every, at(self.ssem, k), at(self.rsem, k), self.dev).wait_send()
        self.sent, self.all = [], []

PLAN = (
    (), (), (), (), (), (), (), (), (), (973, 983), (980,), (972,), (982, 971, 981, 1113, 972), (980, 971, 1112, 1111), (), (), (982, 1120),
    (1122, 983, 970, 1123), (981, 1112), (), (971, 970), (1120,), (973, 983, 982, 971, 1121), (981, 1120, 1122), (1113, 1110, 1112, 1111), (970, 1123),
    (1122,), (980, 972, 981, 1120), (982, 1110), (1111, 1121, 1112), (1123,), (1113,), (972, 1122, 1143, 1140, 1142, 1141),
    (980, 1133, 1130, 1132, 1131, 1123, 1120, 973, 983, 970, 1113, 1110, 1140, 1143, 1121),
    (1111, 1122, 1142, 1133, 710, 1123, 1141, 1130, 980, 710, 1110, 983, 989, 973, 1121, 1132, 1120, 1140, 1143, 1113, 1131, 1130, 710, 970, 1141, 1133, 860, 1110, 1123, 1121, 1142, 1132, 989, 1119, 973, 1131, 979, 1140, 1130, 1133, 1143, 1149, 860, 1119, 1132, 1131, 979, 1130, 1133, 1149),
)
GATHER_PLAN = (
    (1140,), (1110, 1180),
    (1170, 1000, 1010, 1180, 1141, 1140, 1110, 1181, 1011, 1170, 1142, 1012, 1182, 1001, 1141, 1000, 1143, 1013, 1110, 1183, 1142, 1012, 1002, 1181, 1170, 1111, 1143),
    (1182, 1000), (1003,), (), (), (), (1180, 1011), (1001, 1171), (), (), (1012,), (1183, 1003, 1112), (), (), (1182, 1172), (1181, 1002),
    (1113, 1183, 1010, 1011, 1013), (), (1173,), (1001, 1003), (), (), (1010,), (), (), (1013,), (1002,), (), (),
)

def job(letter, i=0):
    return ord(letter) * 10 + i

class Agenda:
    def __init__(self, plan): self.plan, self.jobs, self.point = plan, {}, 0
    def add(self, name, job): self.jobs[name] = job
    def step(self, name):
        if next(self.jobs[name], self) is self: del self.jobs[name]
    def run(self, hold=False):
        names = self.plan[self.point] if self.point < len(self.plan) else ()
        self.point += 1
        for name in names: self.step(name)
    def need(self, names):
        for name in names:
            while name in self.jobs: self.step(name)
    def finish(self):
        for name in self.plan[self.point] if self.point < len(self.plan) else (): self.step(name)
        while self.jobs:
            for name in list(self.jobs): self.step(name)

def add_to(acc, inc):
    acc[...] = (acc[...].astype(F32) + inc[...].astype(F32)).astype(BF)

class Copies:
    def __init__(self, sems): self.sems, self.n = sems, 0
    def go(self, src, dst):
        copy = pltpu.make_async_copy(src, dst, at(self.sems, self.n))
        self.n += 1
        copy.start()
        return copy
    def wait(self, n, src, dst):
        pltpu.make_async_copy(src, dst, at(self.sems, n)).wait()

def turns(nz):
    out, lo, hi = [], 0, nz - 1
    while lo <= hi:
        out += [hi, lo] if lo < hi else [lo]
        lo, hi = lo + 1, hi - 1
    return out

def place():
    d = lax.axis_index("dp"); f = lax.axis_index("fsdp")
    return d, f, d // 2, d % 2, f // 2, f % 2

D_PIECES = (("a", "xzy", 0, 256), ("b", "yzx", 256, 768))
W_PIECES = (("o", "xzy", 0, 640), ("p", "yxz", 640, 1920))
WIDE_FIRST = False
Q_PIECES = (("r", "zy", 0, 256), ("q", "yz", 256, 768))

class Piece:
    def __init__(self, name, order, rows, cols, nz, pair=True):
        self.name, self.order, self.rows, self.cols, self.nz, self.pair = name, order, rows, cols, nz, pair
        self.nx = 2 if pair else 1
    def live(self, done):
        return ((2,) if "y" not in done else ()) + ((self.nx,) if "x" not in done else ()) + (self.rows, self.cols)
    def buffers(self):
        out = {"acc": (self.nz, 2, self.nx, self.rows, self.cols)}
        if self.pair: out["stg"] = out["sib"] = out["acc"]
        done = ""
        for axis in self.order:
            if axis == "z": out["z"] = (2, self.nz) + self.live(done)
            else: out[axis] = (() if "z" in done else (self.nz,)) + self.live(done + axis)
            done += axis
        return {self.name + k: (s, BF) for k, s in out.items()}
    def bind(self, bufs, s):
        self.s, self.net, self.agenda = s, s.net, s.agenda
        self.b = {k[len(self.name):]: v for k, v in bufs.items() if k.startswith(self.name) and k[len(self.name):] in ("acc", "stg", "sib", "x", "y", "z")}
        self.sems, self.flows, self.done = {}, 0, False
        return self
    def view(self, t, done, other=""):
        s = self.s
        ys = pl.ds(0, 2) if "y" not in done else 1 - s.y if other == "y" else s.y
        xs = pl.ds(0, self.nx) if "x" not in done else 1 - s.x if other == "x" else s.x
        return at(self.b["acc"], t, ys, xs)
    def start(self, t):
        if self.pair:
            self.sems[t] = self.net.sem()
            self.net.send(at(self.b["stg"], t), at(self.b["sib"], t), self.sems[t], self.s.sp)
        self.agenda.add(job(self.name, t), self.plane(t))
    def exchange(self, axis, t, done):
        k = self.net.sem()
        self.net.send(self.view(t, done + axis, axis), self.inbox(axis, t, done), k, self.s.xp if axis == "x" else self.s.yp)
        return k
    def inbox(self, axis, t, done):
        return self.b[axis] if "z" in done else at(self.b[axis], t)
    def plane(self, t):
        if self.pair:
            self.net.got(at(self.b["sib"], t), self.sems[t])
            add_to(at(self.b["acc"], t), at(self.b["sib"], t))
        done = ""
        for axis in self.order:
            if axis == "z": break
            k = self.exchange(axis, t, done)
            done += axis
            yield
            buf = self.inbox(axis, t, done)
            self.net.got(buf, k)
            add_to(self.view(t, done), buf)
        yield from self.flow(t, done)
        self.flows += 1
        if self.flows == self.nz:
            if self.order[-1] == "z": self.done = True
            else: self.agenda.add(job(self.name, 9), self.rest())
    def flow(self, t, done):
        nz, s, ks, recv = self.nz, self.s, (self.net.sem(), self.net.sem()), self.b["z"]
        far = max(t, nz - 1 - t)
        for h in range(far):
            if h: yield
            for way, total, here, dev in ((0, t, s.is_z[h], s.up), (1, nz - 1 - t, s.is_z[nz - 1 - h], s.down)):
                if h < total:
                    inc = at(recv, way, t)
                    if h:
                        self.net.got(inc, ks[way], here)
                        pl.when(here)(lambda inc=inc: add_to(self.view(t, done), inc))
                    self.net.send(self.view(t, done), inc, ks[way], dev, here)
        yield
        if t > 0: self.net.got(at(recv, 0, t), ks[0], s.is_z[t])
        if t < nz - 1: self.net.got(at(recv, 1, t), ks[1], s.is_z[t])
    def rest(self):
        s, i = self.s, self.order.index("z")
        done = self.order[:i + 1]
        own = self.view(s.z, done)
        for pred, way in ((s.has_below, 0), (s.has_above, 1)):
            pl.when(pred)(lambda way=way: add_to(own, at(self.b["z"], way, s.z)))
        for axis in self.order[i + 1:]:
            k = self.exchange(axis, s.z, done)
            done += axis
            yield
            buf = self.inbox(axis, s.z, done)
            self.net.got(buf, k)
            if axis != self.order[-1]: add_to(self.view(s.z, done), buf)
        self.done = True
    def total(self):
        assert self.done
        s, last = self.s, self.order[-1]
        sum_ = self.b["acc"][s.z, s.y, s.x if self.pair else 0].astype(F32)
        if last != "z": return sum_ + self.b[last][...].astype(F32).reshape(sum_.shape)
        for pred, way in ((s.has_below, 0), (s.has_above, 1)):
            sum_ = sum_ + jnp.where(pred, self.b["z"][way, s.z].astype(F32).reshape(sum_.shape), 0.0)
        return sum_

class Sums:
    def __init__(self, nz, net, agenda, bufs, outs, vin):
        self.nz, self.net, self.agenda, self.b, self.o, self.vin = nz, net, agenda, bufs, outs, vin
        self.d, self.f, self.z, self.y, self.x, self.c = place()
        d, f = self.d, self.f
        self.up, self.down = (d + 2, f), (d - 2, f)
        self.yp, self.xp, self.sp = (d ^ 1, f), (d, f ^ 2), (d, f ^ 1)
        self.turn = turns(nz)
        z = self.z
        self.is_z = [z == h for h in range(nz)]
        self.has_below, self.has_above, self.core0 = z > 0, z < nz - 1, self.c == 0
        self.D, self.W, self.Q = [[p.bind(bufs, self) for p in ps] for ps in pieces(nz)]
    def first(self, v): return jnp.where(self.core0, v[0], v[1])
    def second(self, v): return jnp.where(self.core0, v[1], v[0])
    def cols(self, ref, width, off, n, mine, rows=None):
        cc = self.c if mine else 1 - self.c
        return ref[slice(None) if rows is None else rows, pl.ds(pl.multiple_of(cc * width + off, 128), n)]

    def vectors(self):
        vb, vr = self.b["vb"], self.b["vr"]
        self.vin(vb)
        k = self.net.send_all(vb, vr, self.nz)
        vr[self.d * 4 + self.f] = vb[self.d * 4 + self.f]
        yield
        self.net.got_all(vr, k)
        total = vr[0]
        for n in range(1, self.nz * 8): total = total + vr[n]
        self.o["v"][...] = total

    def down_tile(self, t, g):
        g = g.reshape(2, 2, 2, 96, D)
        for p, (_, _, c0, c1) in zip(self.D, D_PIECES):
            for y in range(2):
                for x in range(2):
                    p.b["acc"][t, y, x] = self.first(g[y, x, :, :, c0:c1]).astype(BF)
                    p.b["stg"][t, y, x] = self.second(g[y, x, :, :, c0:c1]).astype(BF)
            p.start(t)
    def wide_piece(self, p, c0, c1, n2, du, og, da, gu, gw):
        for dst, mine in (("acc", True), ("stg", False)):
            if c0 < 384:
                n = min(c1, 384) - c0
                for j in range(4):
                    g = tn(og[j, :, 0:192], self.cols(da, 384, c0, n, mine)) + self.cols(gw, 384, c0, n, mine, pl.ds(j * 192, 192)).astype(F32)
                    p.b[dst][j * self.nz // 4:(j + 1) * self.nz // 4, :, :, :, 0:n] = g.astype(BF).reshape(self.nz // 4, 2, 2, 48, n)
            if c1 > 384:
                lo = max(c0, 384)
                g = tn(n2[...], self.cols(du, 1536, lo - 384, c1 - lo, mine)) + self.cols(gu, 1536, lo - 384, c1 - lo, mine).astype(F32)
                p.b[dst][:, :, :, :, lo - c0:c1 - c0] = g.astype(BF).reshape(self.nz, 2, 2, 48, c1 - lo)
        for t in self.turn: p.start(t)
    def q_piece(self, p, c0, c1, n1, dq, gq):
        for j in range(2):
            g = tn(n1[:, j * 384:(j + 1) * 384], dq[:, c0:c1]) + gq[j * 384:(j + 1) * 384, c0:c1].astype(F32)
            p.b["acc"][j * self.nz // 2:(j + 1) * self.nz // 2] = g.astype(BF).reshape(self.nz // 2, 2, 1, 96, c1 - c0)
        for t in self.turn: p.start(t)
    def ends(self):
        net, half, c, f, qf = self.net, self.b["half"], self.c, self.f, self.b["qf"]
        own = self.b["q_own"]
        for p, (_, _, c0, c1) in zip(self.Q, Q_PIECES):
            total = p.total()
            for j in range(4):
                own[j, :, c0:c1] = total[j * 24:(j + 1) * 24]
                qf[0, j, :, c0:c1] = total[j * 24:(j + 1) * 24].astype(BF)
        ks = [net.sem() for _ in range(4)]
        for k in (2, 3, 1):
            net.send(at(qf, 0, f ^ k), at(qf, 1, f), ks[k], (self.d, f ^ k))
        for p, (_, _, c0, c1) in zip(self.W, W_PIECES):
            total = p.total()
            half[0, :, c0:c1] = self.first((total[0:24], total[24:48]))
            half[1, :, c0:c1] = self.second((total[0:24], total[24:48]))
        kw = net.sem()
        net.send(at(half, 1), at(half, 2), kw, self.sp)
        self.o["qkv"][f] = own[f]
        for p, (_, _, c0, c1) in zip(self.D, D_PIECES):
            self.o["down"][:, c0:c1] = p.total()
        net.got(at(half, 2), kw)
        for cc, s in ((c, 0), (1 - c, 2)):
            self.o["outw"][:, pl.ds(pl.multiple_of(cc * 384, 128), 384)] = half[s, :, 0:384]
            self.o["up"][:, pl.ds(pl.multiple_of(cc * 1536, 128), 1536)] = half[s, :, 384:1920]
        for k in (1, 2, 3):
            net.got(at(qf, 1, f ^ k), ks[k])
            self.o["qkv"][f ^ k] = qf[1, f ^ k].astype(F32)

def pieces(nz):
    return ([Piece(n, o, 96, c1 - c0, nz) for n, o, c0, c1 in D_PIECES], [Piece(n, o, 48, c1 - c0, nz) for n, o, c0, c1 in W_PIECES],
            [Piece(n, o, 96, c1 - c0, nz, False) for n, o, c0, c1 in Q_PIECES])

def sum_buffers(nz):
    out = dict(rows24=((8, D), F32), rows96=((8, FF), F32), qf=((2, 4, 24, D), BF), q_own=((4, 24, D), F32), half=((3, 24, 1920), F32), vb=((nz * 8, 8, 128), F32), vr=((nz * 8, 8, 128), F32))
    for group in pieces(nz):
        for p in group: out.update(p.buffers())
    return out

def bwd_kernel(last, nz, names, *refs):
    r_ = dict(zip(names, refs))
    R = lambda *ns: [r_[n] for n in ns]
    lim, vec, g_h, x_h, wq_h, wou_h, wd_h, qkv_h, o_h, lse_h, r_h, gp_h = R("lim", "vec", "g", "x", "wq", "wou", "wd", "qkv", "o", "lse", "r", "gp")
    dos, dop, do, mine, part, inc, go, dr, dqkv, sums, bsum = R("dos", "dop", "do", "mine", "part", "inc", "go_v", "dr", "dqkv_v", "sums", "bsum")
    d = lax.axis_index("dp"); f = lax.axis_index("fsdp")
    ZERO[0] = f * 0
    mem = Copies(r_["lsem"])
    net = Links(r_["ssem"], r_["rsem"], (d, f ^ 1))
    agenda = Agenda(PLAN if last and nz == 4 else ())
    limit = lim[0]
    g0, g1, emb = vec[0:1, :], vec[1:2, :], vec[2:3, :] if last else vec[3:4, :]
    W = 768
    V, ws = pltpu.VMEM, wide_shapes(nz)
    if last:
        gs = Sums(nz, net, agenda, r_, dict(v=r_["v_o"], down=r_["down_o"], outw=r_["outw_o"], up=r_["up_o"], qkv=r_["qkv_o"]), None)
        sums1, bsum1 = r_["sums_1"], r_["bsum_1"]
        def all_sums(out):
            rows24, rows96 = r_["rows24"], r_["rows96"]
            rows24[...] = jnp.concatenate([jnp.zeros((1, D), F32), sums[0:2, :] + sums1[0:2, :], sums[2:3, :], sums1[2:3, :], jnp.zeros((3, D), F32)], axis=0)
            rows96[...] = jnp.concatenate([bsum[...] + bsum1[...], jnp.zeros((7, FF), F32)], axis=0)
            rows_to_slabs(rows24, rows96, nz * 8, out)
        gs.vin = all_sums
    g_in = mem.go(g_h, dr) if last else None
    sums[...] = jnp.zeros_like(sums)

    def phase1(du, dm, da):
        held = []
        def phase1a(wou, r, wd, gp):
            lw, lg = mem.go(wd_h, wd), mem.go(gp_h, gp)
            if last:
                full_barrier(nz, d * 4 + f)
                g_in.wait()
            else:
                group_barrier(d, f)
                ok = lax.lt(lax.broadcasted_iota(jnp.int32, (T, 1), 0) + f * T, lax.broadcast(limit, (T, 1)))
                dr[...] = jnp.where(ok, g_h[...].astype(F32), 0.0)
            dm[...] = dr[...].astype(BF)
            lw.wait(); lg.wait()
            held.append((mem.n, mem.go(wou_h, wou), mem.go(r_h, r)))
            for j in range(FF // W):
                cols = pl.ds(j * W, W)
                t = (nt(dm[...], wd[j * nz // 4:(j + 1) * nz // 4].reshape(W, D)) * gp[:, cols].astype(F32)).astype(BF)
                du[:, cols] = t
                bsum[:, cols] = jnp.sum(t.astype(F32), axis=0, keepdims=True)
                agenda.run()
        def phase1b(wou, r, a, gt, n2, og, gu, gw):
            la = mem.go(r_["a"], a)
            late = [mem.go(r_["n2"], n2), mem.go(r_["og"], og)]
            if last:
                tile = lambda n: mem.go(at(r_["gd_1"], pl.ds(gs.turn[n] * W, W)), at(gt, n % 2))
                tiles = [tile(0), tile(1)]
                late += [mem.go(r_["gu_1"], gu), mem.go(r_["gw_1"], gw)]
            mem.wait(held[0][0], wou_h, wou)
            mem.wait(held[0][0] + 1, r_h, r)
            for j in range(T // 128):
                rows = pl.ds(j * 128, 128)
                e = nt(du[rows, :], wou[:, :, :, :, D:].reshape(D, FF))
                xhat, scale = normed(r[rows, :])
                sums[1:2, :] += jnp.sum(e * xhat, axis=0, keepdims=True)
                t = dr[rows, :] + norm_back(xhat, scale, e, g1)
                dr[rows, :] = t
                da[rows, :] = t.astype(BF)
                agenda.run()
            for k in (3, 2, 1, 0):
                b = f ^ k
                piece = nt(da[...], wou[pl.ds(b * (nz // 4), nz // 4), :, :, :, 0:D].reshape(192, D)).astype(BF)
                piece = jnp.concatenate([piece, jnp.zeros((T, 64), BF)], axis=1)
                if k:
                    pack(piece, at(dos, k))
                    net.send(at(dos, k), at(dop, f), do_sems[k], (d, b))
                else: do[rows_at(f * T, T), :] = piece
            agenda.run()
            la.wait()
            def down_tiles():
                for n, t in enumerate(gs.turn):
                    tiles[n].wait()
                    gs.down_tile(t, tn(a[:, t * W:(t + 1) * W], dm[...]) + gt[n % 2].astype(F32))
                    if n + 2 < nz: tiles.append(tile(n + 2))
                    agenda.run()
            if last and not WIDE_FIRST: down_tiles()
            for c in late: c.wait()
            if last:
                for p, (_, _, c0, c1) in zip(gs.W, W_PIECES):
                    gs.wide_piece(p, c0, c1, n2, du, og, da, gu, gw)
                    agenda.run()
                if WIDE_FIRST: down_tiles()
            else:
                for j in range(FF // W):
                    rows = pl.ds(j * W, W)
                    r_["gd_v"][rows, :] = tn(a[:, rows], dm[...]).astype(BF)
                for j in range(FF // W):
                    cols = pl.ds(j * W, W)
                    r_["gu_v"][:, cols] = tn(n2[...], du[:, cols]).astype(BF)
                for j in range(4):
                    r_["gw_v"][j * 192:(j + 1) * 192, :] = tn(og[j, :, 0:192], da[...]).astype(BF)
        big, wide = [V((T, FF), BF)], [V((T, D), BF), V((4, T, 256), BF)]
        def with_wide(wou, r):
            pl.run_scoped(partial(phase1a, wou, r), V(*ws["wd"]), V((T, FF), BF))
            if last: pl.run_scoped(partial(phase1b, wou, r), *big, V((2, W, D), BF), *wide, V((D, FF), BF), V((D, D), BF))
            else: pl.run_scoped(lambda a, *v: phase1b(wou, r, a, None, *v, None, None), *big, *wide)
        pl.run_scoped(with_wide, V(*ws["wou"]), V((T, D), F32))
    do_sems = [net.sem() for _ in range(4)]
    pl.run_scoped(phase1, V((T, FF), BF), V((T, D), BF), V((T, D), BF))
    made = [] if last else [mem.go(r_[n + "_v"], r_[n + "_o"]) for n in ("gd", "gu", "gw")]

    def phase2(qkv, o, lse, qT, kT, doT, dqT, delta, dkv):
        loads = [mem.go(*p) for p in ((qkv_h, qkv), (o_h, o), (lse_h, lse))]
        dkv[...] = jnp.zeros_like(dkv)
        dqT[192:256, :] = jnp.zeros((64, S), F32)
        agenda.run()
        for c in loads: c.wait()
        qT[...] = (qkv[:, 0:256] * 0.125).astype(BF).T
        kT[...] = qkv[:, 256:512].T
        agenda.run(hold=True)
        for k in (1, 2, 3):
            net.got(at(dop, f ^ k), do_sems[k])
            do[rows_at((f ^ k) * T, T), :] = unpack(at(dop, f ^ k))
        doT[...] = do[...].T
        prod = (do[...].astype(F32) * o[...].astype(F32)).T
        for h in range(3):
            delta[h:h + 1, :] = jnp.sum(prod[h * 64:h * 64 + 64], axis=0, keepdims=True)
        for step in BWD_STEPS:
            for h in range(3):
                bwd_block(*step, h, qkv, do, lse, limit, qT, kT, doT, dqT, delta, dkv)
                agenda.run()
        dqkv[:, 0:256] = (dqT[...] * 0.125).astype(BF).T
        dqkv[:, 256:512] = (dkv[:, 0:256] * 0.125).astype(BF)
        dqkv[:, 512:768] = dkv[:, 256:512].astype(BF)
    two = (V((S, D), BF), V((S, 256), BF), V((8, S), F32), V((256, S), BF), V((256, S), BF), V((256, S), BF), V((256, S), F32), V((8, S), F32), V((S, 512), F32))

    def phase3(wq, x, n1, gq):
        lw, lx, late = mem.go(wq_h, wq), mem.go(x_h, x), [mem.go(r_["n1"], n1)]
        if last: late.append(mem.go(r_["gq_1"], gq))
        pl.run_scoped(phase2, *two)
        out = []
        lw.wait()
        def partial_rows(b, j):
            return nt(dqkv[rows_at(b * T + j * CH, CH), :], wq[...].reshape(D, D))
        k0, k1, k2 = [[net.sem() for _ in range(3)] for _ in range(3)]
        def for_sibling(j):
            rows = pl.ds(j * CH, CH)
            mine[0, rows, :] = partial_rows(f ^ 3, j).astype(BF)
            net.send(at(mine, 0, rows), at(part, 0, rows), k0[j], (d, f ^ 1))
        def for_chip(j):
            rows = pl.ds(j * CH, CH)
            t = partial_rows(f ^ 2, j)
            agenda.run(hold=True)
            net.got(at(part, 0, rows), k0[j])
            inc[rows, :] = (t + part[0, rows, :].astype(F32)).astype(BF)
            net.send(at(inc, rows), at(part, 2, rows), k2[j], (d, f ^ 2))
        for_sibling(0)
        for_sibling(1)
        for_chip(0)
        for_sibling(2)
        for_chip(1)
        for_chip(2)
        for c in late: c.wait()
        if last:
            agenda.run()
            for p, (_, _, c0, c1) in zip(gs.Q, Q_PIECES):
                gs.q_piece(p, c0, c1, n1, dqkv, gq)
                agenda.run()
        else:
            r_["gq_v"][...] = tn(n1[...], dqkv[...]).astype(BF)
        for j in range(3):
            rows = pl.ds(j * CH, CH)
            mine[1, rows, :] = partial_rows(f ^ 1, j).astype(BF)
            net.send(at(mine, 1, rows), at(part, 1, rows), k1[j], (d, f ^ 1))
        for j in range(3):
            rows = pl.ds(j * CH, CH)
            go[rows, :] = partial_rows(f, j)
        lx.wait()
        def finish_rows():
            for j in range(3):
                rows = pl.ds(j * CH, CH)
                net.got(at(part, 1, rows), k1[j])
                net.got(at(part, 2, rows), k2[j])
                e = go[rows, :] + part[1, rows, :].astype(F32) + part[2, rows, :].astype(F32)
                xhat, scale = normed(x[rows, :].astype(F32) + emb)
                sums[0:1, :] += jnp.sum(e * xhat, axis=0, keepdims=True)
                t = dr[rows, :] + norm_back(xhat, scale, e, g0)
                sums[2:3, :] += jnp.sum(t, axis=0, keepdims=True)
                go[rows, :] = t
                if j < 2: yield
            out.append(mem.go(go, r_["go_o"]))
            if last: agenda.add(job("V"), gs.vectors())
        agenda.add(job("G"), finish_rows())
        agenda.finish()
        if last:
            gs.ends()
        for c in out: c.wait()
    pl.run_scoped(phase3, V(*ws["wq"]), V((T, D), x_h.dtype), V((S, D), BF), V((D, D), BF) if last else V((16, 128), BF))
    if not last: made.append(mem.go(r_["gq_v"], r_["gq_o"]))
    for c in made: c.wait()
    net.close()

def bwd(lim, g, x, vec, wq, wou, wd, kept, cid, nz, last=None):
    n1, qkv, o, lse, og, r, n2, gp, a = [kept[n] for n in ("n1", "qkv", "o", "lse", "og", "r", "n2", "gp", "a")]
    n1 = n1.reshape(S, D)
    hbm = pl.BlockSpec(memory_space=pltpu.HBM); vm = pl.BlockSpec(memory_space=pltpu.VMEM); sm = pl.BlockSpec(memory_space=pltpu.SMEM)
    ins = dict(lim=lim, vec=vec, g=g, x=x, wq=wq, wou=wou, wd=wd, qkv=qkv, o=o, lse=lse, r=r, gp=gp, a=a, n2=n2, og=og, n1=n1)
    scratch = dict(dos=((4, T * 3 // 2, 128), BF), dop=((4, T * 3 // 2, 128), BF), do=((S, 256), BF), mine=((2, T, D), BF), part=((3, T, D), BF), inc=((T, D), BF), go_v=((T, D), F32), dr=((T, D), F32), dqkv_v=((S, D), BF))
    outs = dict(go_o=((T, D), F32), sums=((8, D), F32), bsum=((1, FF), F32))
    if last is None:
        for n, s in (("gd", (FF, D)), ("gu", (D, FF)), ("gw", (D, D)), ("gq", (D, D))):
            outs[n + "_o"] = scratch[n + "_v"] = (s, BF)
    else:
        ins.update(last)
        outs.update(down_o=((96, D), F32), outw_o=((24, D), F32), up_o=((24, FF), F32), qkv_o=((4, 24, D), F32), v_o=((8, 128), F32))
    if last is not None: scratch.update(sum_buffers(nz))
    sems = 320 if last is not None else 16
    names = list(ins) + list(outs) + list(scratch) + ["lsem", "ssem", "rsem"]
    place_of = lambda n: sm if n == "lim" else vm if (n == "g" and last is None) or n in ("vec", "sums", "bsum", "sums_1", "bsum_1", "down_o", "outw_o", "up_o", "qkv_o", "v_o") else hbm
    res = pl.pallas_call(partial(bwd_kernel, last is not None, nz, names),
        out_shape=[jax.ShapeDtypeStruct(*s) for s in outs.values()],
        in_specs=[place_of(n) for n in ins], out_specs=[place_of(n) for n in outs],
        scratch_shapes=[pltpu.VMEM(*s) for s in scratch.values()] + [pltpu.SemaphoreType.DMA((32,)), pltpu.SemaphoreType.DMA((sems,)), pltpu.SemaphoreType.DMA((sems,))],
        compiler_params=pltpu.CompilerParams(collective_id=cid, has_side_effects=True, vmem_limit_bytes=VMEM_LIMIT))(*ins.values())
    return dict(zip(outs, res))

class Spread:
    def __init__(self, name, ref, order, rows, cols, width, off, s, pair=True):
        self.name, self.ref, self.order, self.rows, self.cols, self.s = name, ref, order, rows, cols, s
        self.nx, self.sib = (2, True) if pair else (1, False)
        self.mine = pl.multiple_of(off + s.c * width, 128) if pair else off
        self.other = pl.multiple_of(off + (1 - s.c) * width, 128) if pair else off
        self.net, self.agenda, self.late, self.names = s.net, s.agenda, [], []
        self.zsem = {(i, k): s.net.sem() for i in range(1, s.nz) for k in (0, 1)}
    def view(self, t, done, other="", col=None):
        s = self.s
        ys = pl.ds(0, 2) if "y" in done else 1 - s.y if other == "y" else s.y
        xs = pl.ds(0, self.nx) if "x" in done or self.nx == 1 else 1 - s.x if other == "x" else s.x
        return at(self.ref, t, ys, xs, pl.ds(0, self.rows), pl.ds(self.mine if col is None else col, self.cols))
    def add(self, i, steps):
        self.names.append(job(self.name, i))
        self.agenda.add(self.names[-1], steps)
    def start(self): self.add(0, self.first())
    def planes(self, i):
        s = self.s
        return [(s.z, None, 0)] if i == 0 else [(s.z - i, s.ok[i, 0], 0), (s.z + i, s.ok[i, 1], 1)]
    def first(self):
        s, done = self.s, ""
        for axis in self.order:
            if axis == "z": break
            k = self.net.sem()
            self.net.send(self.view(s.z, done), self.view(s.z, done), k, s.xp if axis == "x" else s.yp)
            yield
            self.net.got(self.view(s.z, done, axis), k)
            done += axis
        for k, dev in ((0, s.up), (1, s.down)):
            self.net.send(self.view(s.z, done), self.view(s.z, done), self.zsem[1, k], dev, s.go_on[0, k])
        for i in range(1, s.nz): self.add(i, self.distance(i, done))
        yield from self.after(0, done + "z")
    def distance(self, i, done):
        s = self.s
        for t, ok, k in self.planes(i):
            self.net.got(self.view(t, done), self.zsem[i, k], ok)
            if i + 1 < s.nz:
                self.net.send(self.view(t, done), self.view(t, done), self.zsem[i + 1, k], (s.up, s.down)[k], s.go_on[i, k])
        yield from self.after(i, done + "z")
    def after(self, i, done):
        s = self.s
        for axis in self.order[self.order.index("z") + 1:]:
            ks = []
            for t, ok, _ in self.planes(i):
                ks.append(self.net.sem())
                self.net.send(self.view(t, done), self.view(t, done), ks[-1], s.xp if axis == "x" else s.yp, ok)
            yield
            for k, (t, ok, _) in zip(ks, self.planes(i)): self.net.got(self.view(t, done, axis), k, ok)
            done += axis
        if self.sib:
            for t, ok, _ in self.planes(i):
                k = self.net.sem()
                self.net.send(self.view(t, "xy"), self.view(t, "xy"), k, s.sp, ok)
                self.late.append((i, len(self.late), k))
    def wait(self):
        self.agenda.need(self.names)
        n = {}
        for i, _, k in self.late:
            t, ok, _ = self.planes(i)[n.setdefault(i, 0)]
            n[i] += 1
            self.net.got(self.view(t, "xy", col=self.other), k, ok)

class Spreads:
    def __init__(self, nz, net, agenda, wq, wou, wd):
        self.nz, self.net, self.agenda = nz, net, agenda
        self.d, self.f, self.z, self.y, self.x, self.c = place()
        d, f, z = self.d, self.f, self.z
        self.up, self.down = (d + 2, f), (d - 2, f)
        self.yp, self.xp, self.sp = (d ^ 1, f), (d, f ^ 2), (d, f ^ 1)
        self.ok = {(i, k): (z >= i if k == 0 else z + i < nz) for i in range(1, nz) for k in (0, 1)}
        self.go_on = {(0, 0): z < nz - 1, (0, 1): z > 0}
        for i in range(1, nz - 1):
            self.go_on[i, 0] = self.ok[i, 0] & (z < nz - 1)
            self.go_on[i, 1] = self.ok[i, 1] & (z > 0)
        self.Q = [Spread(n, wq, o, 96, c1 - c0, 0, c0, self, False) for n, o, c0, c1 in GQ]
        self.O = [Spread(n, wou, o, 48, c1 - c0, 384, c0, self) for n, o, c0, c1 in GO]
        self.U = [Spread(n, wou, o, 48, c1 - c0, 1536, D + c0, self) for n, o, c0, c1 in GU]
        self.D = [Spread(n, wd, o, 192, c1 - c0, 384, c0, self) for n, o, c0, c1 in GD]
    def pred_sets(self):
        nz = self.nz
        out = [(self.ok[i, k], [z for z in range(nz) if (z >= i if k == 0 else z + i < nz)]) for i, k in self.ok]
        return out + [(p, [z for z in range(nz) if (i == 0 or (z >= i if k == 0 else z + i < nz)) and (z < nz - 1 if k == 0 else z > 0)]) for (i, k), p in self.go_on.items()]

GQ = (("r", "zy", 0, 768),)
GO = (("o", "yxz", 0, 384),)
GU = (("u", "yxz", 0, 512), ("v", "zxy", 512, 1536))
GD = (("d", "zxy", 0, 256), ("e", "zyx", 256, 384))

def prepare(pidx, gains, table, ub, qw, slab, q4):
    rd = gains.shape[1]
    row = lax.broadcasted_iota(jnp.int32, table.shape, 0)
    slab[...] = jnp.zeros((8, 128), F32)
    slab[0:1, 0:4 * rd] = ub[...].astype(F32)
    slab[1:3, 0:rd] = gains[...].astype(F32)
    for n in range(2):
        slab[3 + n:4 + n, 0:rd] = jnp.sum(jnp.where(row == pidx[n], table[...].astype(F32), 0.0), axis=0, keepdims=True)
    w = qw[...].astype(F32)
    lane = lax.broadcasted_iota(jnp.int32, (rd, 256), 1)
    for k in range(4):
        for part in range(3):
            base = part * D + k * 192
            seg = w[:, base:base + 256] if base % 128 == 0 else pltpu.roll(w[:, base - 64:base + 192], 192, 1)
            q4[k, :, part * 256:(part + 1) * 256] = jnp.where(lane < 192, seg, 0.0).astype(BF)

def last_kernel(pidx, v, q, *refs):
    n = (len(refs) - 4) // 2
    qkv_o, gain_o, bias_o, table_o = refs[n:n + 4]
    rd = gain_o.shape[1]
    for src, dst in zip(refs[:n], refs[n + 4:]): dst[...] = src[...]
    lane = lax.broadcasted_iota(jnp.int32, (rd, 256), 1)
    for part in range(3):
        for pair in range(2):
            one, two = [jnp.where(lane < 192, q[2 * pair + i, :, part * 256:(part + 1) * 256], 0.0) for i in range(2)]
            col = part * D + pair * 384
            two = pltpu.roll(two, 64, 1)
            qkv_o[:, col:col + 128] = one[:, 0:128]
            qkv_o[:, col + 128:col + 256] = one[:, 128:256] + two[:, 0:128]
            qkv_o[:, col + 256:col + 384] = two[:, 128:256]
    bias_o[...] = v[0:1, 0:4 * rd]
    gain_o[...] = v[1:3, 0:rd]
    row = lax.broadcasted_iota(jnp.int32, table_o.shape, 0)
    table_o[...] = jnp.where(row == pidx[0], v[3:4, 0:rd], 0.0) + jnp.where(row == pidx[1], v[4:5, 0:rd], 0.0)

def finish(pidx, v, q, repeats, copied):
    rd = q.shape[1]
    vm = pl.BlockSpec(memory_space=pltpu.VMEM); sm = pl.BlockSpec(memory_space=pltpu.SMEM)
    outs = [jax.ShapeDtypeStruct(s, F32) for s in ((rd, 3 * D), (2, rd), (1, 4 * rd), (repeats, rd))] + [jax.ShapeDtypeStruct(a.shape, a.dtype) for a in copied]
    return pl.pallas_call(last_kernel, out_shape=outs, in_specs=[sm, vm, vm] + [vm] * len(copied), out_specs=[vm] * (4 + len(copied)),
        compiler_params=pltpu.CompilerParams(vmem_limit_bytes=VMEM_LIMIT))(pidx, v, q, *copied)

def everyone(nz):
    return [(b // 4, b % 4) for b in range(nz * 8)]

def full_barrier(nz, me):
    bar = pltpu.get_barrier_semaphore()
    for b, dev in enumerate(everyone(nz)):
        @pl.when(me != b)
        def _(): pl.semaphore_signal(bar, inc=1, device_id=dev, device_id_type=MESH)
    pl.semaphore_wait(bar, nz * 8 - 1)

def slabs_to_rows(slabs, count, width, out):
    lane = lax.broadcasted_iota(jnp.int32, (8, 128), 1)
    tiles = [None] * (count * width // 128)
    for b in range(count):
        tile, shift = b * width // 128, b * width % 128
        turned = pltpu.roll(slabs[b], shift, 1) if shift else slabs[b]
        parts = [(tile, turned)]
        if shift + width > 128:
            low = lax.lt(lane, lax.full_like(lane, shift))
            parts = [(tile, jnp.where(low, 0.0, turned)), (tile + 1, jnp.where(low, turned, 0.0))]
        for i, p in parts: tiles[i] = p if tiles[i] is None else tiles[i] + p
    for i, t in enumerate(tiles): out[:, i * 128:(i + 1) * 128] = t

def rows_to_slabs(rows24, rows96, count, out):
    lane = lax.broadcasted_iota(jnp.int32, (8, 128), 1)
    for b in range(count):
        total = None
        for rows, width in ((rows24, 24), (rows96, 96)):
            tile, shift = b * width // 128, b * width % 128
            part = rows[:, tile * 128:(tile + 1) * 128]
            if shift: part = pltpu.roll(part, 128 - shift, 1)
            if shift + width > 128:
                low = lax.lt(lane, lax.full_like(lane, 128 - shift))
                part = jnp.where(low, part, pltpu.roll(rows[:, (tile + 1) * 128:(tile + 2) * 128], 128 - shift, 1))
            part = jnp.where(lax.lt(lane, lax.full_like(lane, width)), part, 0.0)
            total = part if total is None else total + part
        out[b] = total

def fwd_head(i, h, qkv, limit, qT, vT, oT, lse):
    keys, cols = (i + 1) * QB, pl.ds(i * QB, QB)
    slot, hr = pl.ds((h // 2) * 128, 128), pl.ds(h * 64, 64)
    sT = dot(qkv[0:keys, 256 + (h // 2) * 128:384 + (h // 2) * 128], pick(qT[slot, cols], h))
    sT = mask_scores(sT, i, limit)
    m = jnp.max(sT, axis=0, keepdims=True)
    p = jnp.exp(sT - m)
    l = jnp.sum(p, axis=0, keepdims=True)
    oT[hr, cols] = dot(vT[hr, 0:keys], p.astype(BF)) * (1.0 / l)
    lse[h:h + 1, cols] = m + jnp.log(l)

def fwd_kernel(first, final, nz, names, *refs):
    r_ = dict(zip(names, refs))
    R = lambda *ns: [r_[n] for n in ns]
    lim, x, wq, wou, wd, n1, qkv, qT, vT, oT, o, lse, og, r, n2, gp, a, xo = R("lim", "x", "wq_v", "wou_v", "wd_v", "n1_v", "qkv_v", "qT", "vT", "oT", "o_v", "lse_v", "og_v", "r_v", "n2_v", "gp_v", "a_v", "xo_v")
    d = lax.axis_index("dp"); f = lax.axis_index("fsdp")
    ZERO[0] = f * 0
    mem = Copies(r_["lsem"])
    net = Links(r_["ssem"], r_["rsem"], (d, f ^ 1))
    agenda = Agenda(GATHER_PLAN if first and nz == 4 else ())
    limit = lim[0]
    stores = []
    def store(name): stores.append(mem.go(r_[name + "_v"], r_[name]))
    if first:
        me = d * 4 + f
        c = f % 2
        prepare(*R("pidx", "gains", "table", "ub", "qw", "slab", "q4"))
        vecs, bias, slabs, slab = r_["vecs"], r_["biasr"], r_["slabs"], r_["slab"]
        q4, ow, uw, dn, rq, ro, ru = R("q4", "ow", "uw", "dn", "rq", "ro", "ru")
        full_barrier(nz, me)
        sp = (d, f ^ 1)
        k_all = net.send_all(slab, slabs, nz)
        slabs[me] = slab[...]
        z, y, xx = d // 2, d % 2, f // 2
        k_o, k_u, k_d = net.sem(), net.sem(), net.sem()
        net.send(ow, ro, k_o, sp)
        net.send(uw, ru, k_u, sp)
        k_q = [net.sem() for _ in range(4)]
        for k in (1, 2, 3): net.send(q4.at[f ^ k], rq.at[f], k_q[k], (d, f ^ k))
        half = lambda cc: pl.ds(pl.multiple_of(cc * 384, 128), 384)
        net.send(dn.at[:, half(1 - c)], wd.at[z, y, xx, pl.ds(pl.multiple_of(c * 96, 16), 96), half(1 - c)], k_d, sp)
        own_d = pltpu.make_async_copy(dn.at[:, half(c)], wd.at[z, y, xx, pl.ds(pl.multiple_of(c * 96, 16), 96), half(c)], at(r_["lsem"], 31))
        own_d.start()
        rq[f] = q4[f]
        S_ = Spreads(nz, net, agenda, wq, wou, wd)
        first_core = c == 0
        def merge(own, other):
            m_, o_ = own[...].astype(F32), other[...].astype(F32)
            return jnp.concatenate([jnp.where(first_core, m_, o_), jnp.where(first_core, o_, m_)], axis=0).astype(BF)
        for k in (1, 2, 3): net.got(rq.at[f ^ k], k_q[k])
        wq[z, y, 0] = jnp.concatenate([rq[k].astype(F32) for k in range(4)], axis=0).astype(BF)
        for p in S_.Q: p.start()
        agenda.run()
        net.got(ro, k_o)
        r_["bo"][...] = merge(ow, ro)
        net.got(ru, k_u)
        r_["bu"][...] = merge(uw, ru)
        wide = lambda cc: pl.ds(pl.multiple_of(cc * 1536, 128), 1536)
        lo = [pltpu.make_async_copy(r_["bo"].at[:, half(c)], wou.at[z, y, xx, pl.ds(0, 48), half(c)], at(r_["lsem"], 30)),
              pltpu.make_async_copy(r_["bu"].at[:, wide(c)], wou.at[z, y, xx, pl.ds(0, 48), pl.ds(pl.multiple_of(D + c * 1536, 128), 1536)], at(r_["lsem"], 29))]
        for w in lo: w.start()
        for w in lo: w.wait()
        for p in S_.O + S_.U: p.start()
        agenda.run()
        own_d.wait()
        net.got(wd.at[z, y, xx, pl.ds(pl.multiple_of((1 - c) * 96, 16), 96), half(c)], k_d)
        for p in S_.D: p.start()
        net.got_all(slabs, k_all)
        slabs_to_rows(slabs, nz * 8, 24, r_["rows24"])
        slabs_to_rows(slabs, nz * 8, 96, r_["rows96"])
        vecs[0:4, :] = r_["rows24"][1:5, :]
        vecs[4:8, :] = jnp.zeros((4, D), F32)
        bias[...] = r_["rows96"][0:1, :]
        g0, g1, emb = vecs[0:1, :], vecs[1:2, :], vecs[2:3, :]
    else:
        loads = [mem.go(r_[n], r_[n + "_v"]) for n in ("wq", "wou", "wd")]
        vecs, bias = r_["vecs"], r_["biasr"]
        g0, g1, emb = vecs[0:1, :], vecs[1:2, :], vecs[3:4, :]
        group_barrier(d, f)
    k_n = [[net.sem() for _ in range(3)] for _ in range(3)]
    for j in range(T // CH):
        rows = pl.ds(j * CH, CH)
        xhat, _ = normed(x[rows, :].astype(F32) + emb)
        n1[f, rows, :] = (xhat * g0).astype(BF)
        reg = n1.at[f, rows, :]
        net.send(reg, reg, k_n[0][j], (d, f ^ 2))
        net.send(reg, reg, k_n[1][j], (d, f ^ 1))
    if first:
        for p in S_.Q:
            agenda.run(hold=True)
            p.wait()
        store("wq")
    else: loads[0].wait()
    def project(k):
        for j in range(2):
            rows = rows_at(j * 192, 192)
            qkv[rows_at(k * T + j * 192, 192), :] = dot(n1[k, rows, :], wq[...].reshape(D, D)).astype(BF)
    project(f)
    agenda.run()
    for j in range(3): net.got(n1.at[f ^ 1, pl.ds(j * CH, CH), :], k_n[1][j])
    project(f ^ 1)
    for j in range(3):
        agenda.run(hold=True)
        reg = n1.at[f ^ 2, pl.ds(j * CH, CH), :]
        net.got(reg, k_n[0][j])
        net.send(reg, reg, k_n[2][j], (d, f ^ 1))
    project(f ^ 2)
    agenda.run()
    for j in range(3): net.got(n1.at[f ^ 3, pl.ds(j * CH, CH), :], k_n[2][j])
    project(f ^ 3)
    store("n1"); store("qkv")
    qT[...] = (qkv[:, 0:256] * 0.125).astype(BF).T
    vT[...] = qkv[:, 512:768].T
    oT[192:256, :] = jnp.zeros((64, S), F32)
    lse[...] = jnp.zeros_like(lse)
    agenda.run()
    k_og = [net.sem() for _ in range(4)]
    def finish(b):
        rows = pl.ds(b * T, T)
        o[rows, :] = oT[:, rows].astype(BF).T
        @pl.when(f == b)
        def _(): og[b] = o[rows, :]
        pack(o[rows, :], r_["op"].at[b])
        for k in (1, 2, 3):
            net.send(r_["op"].at[b], r_["ogp"].at[f], k_og[k], (d, f ^ k), (f ^ k) == b)
    for i, ready in ((0, (0,)), (2, (3,)), (1, (1, 2))):
        for h in range(3):
            fwd_head(i, h, qkv, limit, qT, vT, oT, lse)
            agenda.run()
        for b in ready: finish(b)
    store("o"); store("lse")
    agenda.run(hold=True)
    for k in (1, 2, 3):
        net.got(r_["ogp"].at[f ^ k], k_og[k])
        og[f ^ k] = unpack(r_["ogp"].at[f ^ k])
    store("og")
    if first:
        for p in S_.O:
            agenda.run(hold=True)
            p.wait()
    else: loads[1].wait()
    for j in range(2):
        rows = rows_at(j * 192, 192)
        acc = x[rows, :].astype(F32) + emb
        for k in range(4):
            acc = acc + dot(og[k, rows, 0:192], wou[k * nz // 4:(k + 1) * nz // 4, :, :, :, 0:D].reshape(192, D))
        r[rows, :] = acc
        xhat, _ = normed(acc)
        n2[rows, :] = (xhat * g1).astype(BF)
        agenda.run()
    store("r"); store("n2")
    if first:
        for p in S_.U:
            agenda.run(hold=True)
            p.wait()
        store("wou")
    W = 768
    for j in range(FF // W):
        cols = pl.ds(j * W, W)
        u = dot(n2[...], wou[:, :, :, :, D + j * W:D + (j + 1) * W].reshape(D, W)) + bias[:, cols]
        sq = u * u
        t = jnp.tanh(0.7978845608028654 * u * (1.0 + 0.044715 * sq))
        half_ = 0.5 * (1.0 + t)
        a[:, cols] = (u * half_).astype(BF)
        gp[:, cols] = (half_ + 0.5 * u * (1.0 - t * t) * (0.7978845608028654 * (1.0 + 0.134145 * sq))).astype(BF)
        agenda.run()
    store("gp"); store("a")
    if first:
        for p in S_.D:
            agenda.run(hold=True)
            p.wait()
        store("wd")
    else: loads[2].wait()
    for j in range(D // 256):
        cols = pl.ds(j * 256, 256)
        xo[:, cols] = r[:, cols] + dot(a[...], wd[:, :, :, :, j * 256:(j + 1) * 256].reshape(FF, 256))
    if final:
        ok = lax.broadcasted_iota(jnp.int32, (T, 1), 0) + f * T < limit
        r_["out_v"][...] = jnp.where(ok, xo[...], 0.0).astype(BF)
        store("out")
    else: store("xo")
    agenda.finish()
    net.close()
    for w in stores: w.wait()

def wide_shapes(nz):
    rows = D // (nz * 4)
    return dict(wq=((nz, 2, 1, D // (nz * 2), D), BF), wou=((nz, 2, 2, rows, 3840), BF), wd=((nz, 2, 2, rows * 4, D), BF))

def fwd(lim, x, weights, cid, nz, first=False, final=False):
    hbm = pl.BlockSpec(memory_space=pltpu.HBM); vm = pl.BlockSpec(memory_space=pltpu.VMEM); sm = pl.BlockSpec(memory_space=pltpu.SMEM)
    ins = dict(lim=lim, x=x, **weights)
    ws = wide_shapes(nz)
    kept = dict(n1=((4, T, D), BF), qkv=((S, D), BF), o=((S, 256), BF), lse=((8, S), F32), og=((4, T, 256), BF), r=((T, D), F32), n2=((T, D), BF), gp=((T, FF), BF), a=((T, FF), BF))
    outs = dict(kept)
    if final: outs.update(out=((T, D), BF))
    else: outs.update(xo=((T, D), F32))
    if first: outs.update(ws, vecs=((8, D), F32), biasr=((1, FF), F32))
    scratch = {n + "_v": s for n, s in dict(kept, xo=((T, D), F32), **ws).items()}
    if final: scratch.update(out_v=((T, D), BF))
    scratch.update(op=((4, T * 3 // 2, 128), BF), ogp=((4, T * 3 // 2, 128), BF), qT=((256, S), BF), vT=((256, S), BF), oT=((256, S), F32))
    if first:
        scratch.update(slab=((8, 128), F32), q4=((4, 24, D), BF), slabs=((nz * 8, 8, 128), F32), rows24=((8, D), F32), rows96=((8, FF), F32), rq=((4, 24, D), BF), ro=((24, D), BF), ru=((24, FF), BF), bo=((48, D), BF), bu=((48, FF), BF))
    sems = 320 if first else 24
    names = list(ins) + list(outs) + list(scratch) + ["lsem", "ssem", "rsem"]
    inner = ("wq", "wou", "wd")
    place_of = lambda n: sm if n in ("lim", "pidx") else vm if n in ("x", "vecs", "biasr", "qw", "ow", "uw", "dn", "gains", "table", "ub") else hbm
    res = pl.pallas_call(partial(fwd_kernel, first, final, nz, names),
        out_shape=[jax.ShapeDtypeStruct(*s) for s in outs.values()],
        in_specs=[place_of(n) for n in ins], out_specs=[place_of(n) for n in outs],
        scratch_shapes=[pltpu.VMEM(*s) for s in scratch.values()] + [pltpu.SemaphoreType.DMA((32,)), pltpu.SemaphoreType.DMA((sems,)), pltpu.SemaphoreType.DMA((sems,))],
        compiler_params=pltpu.CompilerParams(collective_id=cid, has_side_effects=True, vmem_limit_bytes=VMEM_LIMIT))(*ins.values())
    return dict(zip(outs, res))

def gather_any(q4, ow, uw, dn, slab, nz):
    both = ("dp", "fsdp")
    wq = lax.dynamic_index_in_dim(lax.all_gather(q4, both, axis=0), lax.axis_index("fsdp"), 1, keepdims=False)
    slabs = lax.all_gather(slab, both, axis=0)
    rd = q4.shape[1]
    vecs = jnp.concatenate([slabs[:, 1:5, :rd].transpose(1, 0, 2).reshape(4, D), jnp.zeros((4, D), F32)], axis=0)
    wou = lax.all_gather(jnp.concatenate([ow, uw], axis=1), both, axis=0, tiled=True)
    shapes = wide_shapes(nz)
    return dict(wq=wq.reshape(shapes["wq"][0]), wou=wou.reshape(shapes["wou"][0]), wd=lax.all_gather(dn, both, axis=0, tiled=True).reshape(shapes["wd"][0]),
                vecs=vecs, biasr=slabs[:, 0, :4 * rd].reshape(1, FF))

def grads_any(own, vin, rd):
    both = ("dp", "fsdp")
    scatter = lambda v: lax.psum_scatter(v, both, scatter_dimension=0, tiled=True)
    down, out, up, q = own
    q = lax.dynamic_update_slice(jnp.zeros((4, D // rd, rd, D), F32), q.reshape(1, D // rd, rd, D), (lax.axis_index("fsdp"), 0, 0, 0))
    q_grad = lax.psum_scatter(q, both, scatter_dimension=1, tiled=True).reshape(4, rd, D)
    idx = lax.axis_index("dp") * 4 + lax.axis_index("fsdp")
    tot = lax.psum(vin, both)
    rows = lax.dynamic_slice_in_dim(tot[0:4], idx * rd, rd, 1)
    bias = lax.dynamic_slice_in_dim(tot[4:8].reshape(1, FF), idx * rd * 4, rd * 4, 1)
    slab = jnp.concatenate([jnp.pad(bias, ((0, 0), (0, 128 - rd * 4))), jnp.pad(rows, ((0, 3), (0, 128 - rd)))], axis=0)
    return scatter(down), scatter(out), scatter(up), q_grad, slab

def w_emb(w, n):
    return dict(w, vecs=jnp.concatenate([w["vecs"][0:3], w["vecs"][2 + n:3 + n], w["vecs"][4:8]], axis=0))

def body(tokens, qkv_weight, out_weight, up_weight, down_weight, norm_gains, up_bias, pass_table, pass_index, lengths, cotangent):
    rd = qkv_weight.shape[0]
    fast = rd == 24
    nz = lax.axis_size("dp") // 2 if fast else 4
    if fast:
        own = dict(pidx=pass_index, qw=qkv_weight, ow=out_weight, uw=up_weight, dn=down_weight, gains=norm_gains.T, table=pass_table.T, ub=up_bias.reshape(1, 4 * rd))
        k0 = fwd(lengths, tokens, own, 0, nz, first=True)
        w = {n: k0[n] for n in ("wq", "wou", "wd", "vecs", "biasr")}
    else:
        q4 = jnp.pad(qkv_weight.reshape(rd, 3, 4, 192), ((0, 0), (0, 0), (0, 0), (0, 64))).transpose(2, 0, 1, 3).reshape(4, rd, D)
        chooser = [(jnp.arange(pass_table.shape[1], dtype=jnp.int32) == pass_index[n]).astype(F32) for n in range(2)]
        emb = [jnp.sum(pass_table.astype(F32) * ch[None, :], axis=1) for ch in chooser]
        rows = jnp.stack([norm_gains[:, 0].astype(F32), norm_gains[:, 1].astype(F32)] + emb)
        slab = jnp.concatenate([jnp.pad(up_bias.astype(F32)[None, :], ((0, 0), (0, 128 - 4 * rd))), jnp.pad(rows, ((0, 3), (0, 128 - rd)))], axis=0)
        w = gather_any(q4, out_weight, up_weight, down_weight, slab, nz)
        k0 = fwd(lengths, tokens, w_emb(w, 0), 1, nz)
    k1 = fwd(lengths, k0["xo"], w, 1, nz, final=True)
    big = (w["wq"], w["wou"], w["wd"])
    b1 = bwd(lengths, cotangent, k0["xo"], w["vecs"], *big, k1, 2, nz)
    if fast:
        left = dict(gd_1=b1["gd_o"], gu_1=b1["gu_o"], gw_1=b1["gw_o"], gq_1=b1["gq_o"], sums_1=b1["sums"], bsum_1=b1["bsum"])
        b0 = bwd(lengths, b1["go_o"], tokens, w["vecs"], *big, k0, 3, nz, left)
        down_grad, out_grad, up_grad, q_grad, tot = b0["down_o"], b0["outw_o"], b0["up_o"], b0["qkv_o"], b0["v_o"]
    else:
        b0 = bwd(lengths, b1["go_o"], tokens, w_emb(w, 0)["vecs"], *big, k0, 2, nz)
        s0, s1 = b0["sums"], b1["sums"]
        vin = jnp.concatenate([s0[0:2] + s1[0:2], s0[2:3], s1[2:3], (b0["bsum"] + b1["bsum"]).reshape(4, D)], axis=0)
        down_grad, out_grad, up_grad, q_grad, tot = grads_any([b0[n].astype(F32) + b1[n].astype(F32) for n in ("gd_o", "gw_o", "gu_o", "gq_o")], vin, rd)
    qkv_grad, gains, bias_grad, table, block_out, input_grad, down_grad, out_grad, up_grad = finish(
        pass_index, tot, q_grad, pass_table.shape[1], (k1["out"], b0["go_o"], down_grad, out_grad, up_grad))
    return (block_out, input_grad, qkv_grad, out_grad, up_grad, down_grad, gains.T, bias_grad.reshape(4 * rd), table.T)

def solution(mesh):
    a = P(("dp", "fsdp"), None); b = P(("dp", "fsdp"))
    return jax.shard_map(body, mesh=mesh, in_specs=(a, a, a, a, a, a, b, a, P(), P("dp"), a), out_specs=(a, a, a, a, a, a, a, b, a), check_vma=False)
```

```python
from functools import partial
import jax
import jax.numpy as jnp
from jax import lax
from jax.experimental import pallas as pl
from jax.experimental.pallas import tpu as pltpu
from jax.sharding import PartitionSpec as P
BF=jnp.bfloat16; F32=jnp.float32
MESH = pl.DeviceIdType.MESH
NEG = -1e30
QB = 512
VMEM_LIMIT = 62 * 2**20

def remote(src, dst, ssem, rsem, dev):
    return pltpu.make_async_remote_copy(src_ref=src, dst_ref=dst, send_sem=ssem, recv_sem=rsem, device_id=dev, device_id_type=MESH)

def rows_at(start, count, step=16):
    return pl.ds(pl.multiple_of(start, step), count)

def normed(values):
    center = values - jnp.mean(values, axis=-1, keepdims=True)
    spread = jnp.mean(center * center, axis=-1, keepdims=True)
    scale = lax.rsqrt(spread + 1e-05)
    return center * scale, scale

def norm_back(xhat, scale, grad_out, gain):
    eg = grad_out * gain
    first = jnp.mean(eg, axis=-1, keepdims=True)
    second = jnp.mean(eg * xhat, axis=-1, keepdims=True)
    return scale * (eg - first - xhat * second)

def nt(left, right):
    return lax.dot_general(left, right, (((1,), (1,)), ((), ())), preferred_element_type=F32)

def dot(left, right):
    return jnp.dot(left, right, preferred_element_type=F32)

def mask_scores(sT, i, limit):
    lo = i * QB
    free = min(lo, 1024)
    parts = []
    if free: parts.append(sT[:free])
    if lo > free:
        kpos = free + lax.broadcasted_iota(jnp.int32, (lo - free, QB), 0)
        parts.append(jnp.where(kpos < limit, sT[free:lo], NEG))
    kpos = lo + lax.broadcasted_iota(jnp.int32, (QB, QB), 0)
    ok = kpos <= lo + lax.broadcasted_iota(jnp.int32, (QB, QB), 1)
    if lo + QB > 1024: ok = ok & (kpos < limit)
    parts.append(jnp.where(ok, sT[lo:], NEG))
    return parts[0] if len(parts) == 1 else jnp.concatenate(parts, 0)

def half_mask(index, h):
    edge = lax.full_like(index, 64)
    return lax.lt(index, edge) if h % 2 == 0 else lax.ge(index, edge)

def pick(xT, h):
    r = lax.broadcasted_iota(jnp.int32, xT.shape, 0)
    mine = half_mask(r, h) if isinstance(h, int) else (r // 64) == (h % 2)
    return jnp.where(mine, xT, jnp.zeros_like(xT))

def slot_of(h, base=0):
    return pl.ds(pl.multiple_of(base + (h // 2) * 128, 128), 128)

BWD_STEPS = ((0, 0, 1), (1, 0, 2), (2, 0, 2), (2, 2, 3))

def bwd_block(i, k0, k1, h, qkv, do, lse, limit, qT, kT, doT, dqT, delta, dkv):
    keys, cols, n = pl.ds(k0 * QB, (k1 - k0) * QB), pl.ds(i * QB, QB), (k1 - k0) * QB
    slot, hr = pl.ds((h // 2) * 128, 128), pl.ds(h * 64, 64)
    after = lambda base: pl.ds(base + (h // 2) * 128, 128)
    lane = lax.broadcasted_iota(jnp.int32, (QB, 128), 1)
    lm = half_mask(lane, h)
    sT = dot(qkv[keys, after(256)], pick(qT[slot, cols], h))
    p = jnp.exp(sT - lse[h:h + 1, cols])
    if k1 == i + 1:
        kpos = i * QB + lax.broadcasted_iota(jnp.int32, (QB, QB), 0)
        ok = kpos <= i * QB + lax.broadcasted_iota(jnp.int32, (QB, QB), 1)
        if k1 * QB > 1024: ok = ok & (kpos < limit)
        diagonal = jnp.where(ok, p[n - QB:], 0.0)
        p = diagonal if n == QB else jnp.concatenate([p[:n - QB], diagonal], axis=0)
    assert k1 == i + 1 or k1 * QB <= 1024
    dp = dot(qkv[keys, after(512)], pick(doT[slot, cols], h))
    dsT = (p * (dp - delta[h:h + 1, cols])).astype(BF)
    step = dot(kT[hr, keys], dsT)
    dqT[hr, cols] = step if k0 == 0 else dqT[hr, cols] + step
    qn, dn = qkv[cols, slot], do[cols, slot]
    dkv[keys, slot] += dot(dsT, jnp.where(lm, qn, jnp.zeros_like(qn)))
    dkv[keys, after(256)] += dot(p.astype(BF), jnp.where(lm, dn, jnp.zeros_like(dn)))

def group_barrier(d, f):
    bar = pltpu.get_barrier_semaphore()
    for k in (1, 2, 3):
        pl.semaphore_signal(bar, inc=1, device_id=(d, f ^ k), device_id_type=MESH)
    pl.semaphore_wait(bar, 3)

T, D, FF, S = 384, 768, 3072, 1536
CH = 128


ZERO = [None]

def at(ref, *index):
    return ref.at[tuple(ZERO[0] + i if isinstance(i, int) else i for i in index)]

def tn(left, right):
    return lax.dot_general(left, right, (((0,), (0,)), ((), ())), preferred_element_type=F32)

def when(pred, act):
    if pred is None: act()
    else: pl.when(pred)(act)

def pack(rows, out):
    h = T // 2
    out[0:T, :] = rows[:, 0:128]
    low, high = rows[0:h, 128:256].astype(F32), rows[h:T, 128:256].astype(F32)
    out[T:T + h, :] = (low + pltpu.roll(high, 64, 1)).astype(BF)

def unpack(packed):
    h = T // 2
    both = packed[T:T + h, :].astype(F32)
    low = lax.lt(lax.broadcasted_iota(jnp.int32, (h, 128), 1), lax.full((h, 128), 64, jnp.int32))
    rest = jnp.concatenate([jnp.where(low, both, 0.0), jnp.where(low, pltpu.roll(both, 64, 1), 0.0)], axis=0)
    return jnp.concatenate([packed[0:T, :], rest.astype(BF)], axis=1)

class Links:
    def __init__(self, ssem, rsem, dev):
        self.ssem, self.rsem, self.dev, self.n, self.sent, self.all = ssem, rsem, dev, 0, [], []
    def sem(self):
        self.n += 1
        return self.n - 1
    def send(self, src, dst, k, dev, pred=None):
        when(pred, remote(src, dst, at(self.ssem, k), at(self.rsem, k), dev).start)
        self.sent.append((pred, src, k))
    def got(self, region, k, pred=None):
        when(pred, remote(region, region, at(self.ssem, k), at(self.rsem, k), self.dev).wait_recv)
    def send_all(self, src, dst, nz):
        k, me = self.sem(), lax.axis_index("dp") * 4 + lax.axis_index("fsdp")
        for b, dev in enumerate(everyone(nz)):
            one = src if len(src.shape) == 2 else at(src, b)
            pl.when(me != b)(remote(one, at(dst, me), at(self.ssem, k), at(self.rsem, k), dev).start)
        self.all.append((dst, k))
        return k
    def got_all(self, dst, k):
        every = at(dst, pl.ds(0, dst.shape[0] - 1))
        remote(every, every, at(self.ssem, k), at(self.rsem, k), self.dev).wait_recv()
    def close(self):
        for pred, src, k in self.sent:
            base = getattr(src, "ref", src)
            like = at(base, *([0] * (len(base.shape) - len(src.shape)) + [pl.ds(0, n) for n in src.shape]))
            when(pred, remote(like, like, at(self.ssem, k), at(self.rsem, k), self.dev).wait_send)
        for dst, k in self.all:
            every = at(dst, pl.ds(0, dst.shape[0] - 1))
            remote(every, every, at(self.ssem, k), at(self.rsem, k), self.dev).wait_send()
        self.sent, self.all = [], []

PLAN = (
    (), (), (), (), (), (), (), (), (), (973, 983), (980,), (972,), (982, 971, 981, 1113, 972), (980, 971, 1112, 1111), (), (), (982, 1120),
    (1122, 983, 970, 1123), (981, 1112), (), (971, 970), (1120,), (973, 983, 982, 971, 1121), (981, 1120, 1122), (1113, 1110, 1112, 1111), (970, 1123),
    (1122,), (980, 972, 981, 1120), (982, 1110), (1111, 1121, 1112), (1123,), (1113,), (972, 1122, 1143, 1140, 1142, 1141),
    (980, 1133, 1130, 1132, 1131, 1123, 1120, 973, 983, 970, 1113, 1110, 1140, 1143, 1121),
    (1111, 1122, 1142, 1133, 710, 1123, 1141, 1130, 980, 710, 1110, 983, 989, 973, 1121, 1132, 1120, 1140, 1143, 1113, 1131, 1130, 710, 970, 1141, 1133, 860, 1110, 1123, 1121, 1142, 1132, 989, 1119, 973, 1131, 979, 1140, 1130, 1133, 1143, 1149, 860, 1119, 1132, 1131, 979, 1130, 1133, 1149),
)
GATHER_PLAN = (
    (1110, 1180), (1000, 1010, 1140),
    (1170, 1180, 1140, 1141, 1110, 1181, 1011, 1170, 1142, 1012, 1141, 1182, 1000, 1001, 1110, 1143, 1013, 1183, 1142, 1181, 1012, 1002, 1170, 1182, 1143),
    (1000, 1111), (), (), (), (1003,), (1001,), (1180, 1011), (1012,), (1171,), (), (1112,), (1183, 1003), (), (1182,), (1172,),
    (1181, 1002, 1113, 1183), (), (1010, 1011, 1013), (1001, 1003, 1173), (), (), (1010,), (1002,), (1013,), (), (), (), (),
)

def job(letter, i=0):
    return ord(letter) * 10 + i

class Agenda:
    def __init__(self, plan): self.plan, self.jobs, self.point = plan, {}, 0
    def add(self, name, job): self.jobs[name] = job
    def step(self, name):
        if next(self.jobs[name], self) is self: del self.jobs[name]
    def run(self, hold=False):
        names = self.plan[self.point] if self.point < len(self.plan) else ()
        self.point += 1
        for name in names: self.step(name)
    def need(self, names):
        for name in names:
            while name in self.jobs: self.step(name)
    def finish(self):
        for name in self.plan[self.point] if self.point < len(self.plan) else (): self.step(name)
        while self.jobs:
            for name in list(self.jobs): self.step(name)

def add_to(acc, inc):
    acc[...] = (acc[...].astype(F32) + inc[...].astype(F32)).astype(BF)

class Copies:
    def __init__(self, sems): self.sems, self.n = sems, 0
    def go(self, src, dst):
        copy = pltpu.make_async_copy(src, dst, at(self.sems, self.n))
        self.n += 1
        copy.start()
        return copy
    def wait(self, n, src, dst):
        pltpu.make_async_copy(src, dst, at(self.sems, n)).wait()

def turns(nz):
    out, lo, hi = [], 0, nz - 1
    while lo <= hi:
        out += [hi, lo] if lo < hi else [lo]
        lo, hi = lo + 1, hi - 1
    return out

def place():
    d = lax.axis_index("dp"); f = lax.axis_index("fsdp")
    return d, f, d // 2, d % 2, f // 2, f % 2

D_PIECES = (("a", "xzy", 0, 256), ("b", "yzx", 256, 768))
W_PIECES = (("o", "xzy", 0, 640), ("p", "yxz", 640, 1920))
WIDE_FIRST = False
Q_PIECES = (("r", "zy", 0, 256), ("q", "yz", 256, 768))

class Piece:
    def __init__(self, name, order, rows, cols, nz, pair=True):
        self.name, self.order, self.rows, self.cols, self.nz, self.pair = name, order, rows, cols, nz, pair
        self.nx = 2 if pair else 1
    def live(self, done):
        return ((2,) if "y" not in done else ()) + ((self.nx,) if "x" not in done else ()) + (self.rows, self.cols)
    def buffers(self):
        out = {"acc": (self.nz, 2, self.nx, self.rows, self.cols)}
        if self.pair: out["stg"] = out["sib"] = out["acc"]
        done = ""
        for axis in self.order:
            if axis == "z": out["z"] = (2, self.nz) + self.live(done)
            else: out[axis] = (() if "z" in done else (self.nz,)) + self.live(done + axis)
            done += axis
        return {self.name + k: (s, BF) for k, s in out.items()}
    def bind(self, bufs, s):
        self.s, self.net, self.agenda = s, s.net, s.agenda
        self.b = {k[len(self.name):]: v for k, v in bufs.items() if k.startswith(self.name) and k[len(self.name):] in ("acc", "stg", "sib", "x", "y", "z")}
        self.sems, self.flows, self.done = {}, 0, False
        return self
    def view(self, t, done, other=""):
        s = self.s
        ys = pl.ds(0, 2) if "y" not in done else 1 - s.y if other == "y" else s.y
        xs = pl.ds(0, self.nx) if "x" not in done else 1 - s.x if other == "x" else s.x
        return at(self.b["acc"], t, ys, xs)
    def start(self, t):
        if self.pair:
            self.sems[t] = self.net.sem()
            self.net.send(at(self.b["stg"], t), at(self.b["sib"], t), self.sems[t], self.s.sp)
        self.agenda.add(job(self.name, t), self.plane(t))
    def exchange(self, axis, t, done):
        k = self.net.sem()
        self.net.send(self.view(t, done + axis, axis), self.inbox(axis, t, done), k, self.s.xp if axis == "x" else self.s.yp)
        return k
    def inbox(self, axis, t, done):
        return self.b[axis] if "z" in done else at(self.b[axis], t)
    def plane(self, t):
        if self.pair:
            self.net.got(at(self.b["sib"], t), self.sems[t])
            add_to(at(self.b["acc"], t), at(self.b["sib"], t))
        done = ""
        for axis in self.order:
            if axis == "z": break
            k = self.exchange(axis, t, done)
            done += axis
            yield
            buf = self.inbox(axis, t, done)
            self.net.got(buf, k)
            add_to(self.view(t, done), buf)
        yield from self.flow(t, done)
        self.flows += 1
        if self.flows == self.nz:
            if self.order[-1] == "z": self.done = True
            else: self.agenda.add(job(self.name, 9), self.rest())
    def flow(self, t, done):
        nz, s, ks, recv = self.nz, self.s, (self.net.sem(), self.net.sem()), self.b["z"]
        far = max(t, nz - 1 - t)
        for h in range(far):
            if h: yield
            for way, total, here, dev in ((0, t, s.is_z[h], s.up), (1, nz - 1 - t, s.is_z[nz - 1 - h], s.down)):
                if h < total:
                    inc = at(recv, way, t)
                    if h:
                        self.net.got(inc, ks[way], here)
                        pl.when(here)(lambda inc=inc: add_to(self.view(t, done), inc))
                    self.net.send(self.view(t, done), inc, ks[way], dev, here)
        yield
        if t > 0: self.net.got(at(recv, 0, t), ks[0], s.is_z[t])
        if t < nz - 1: self.net.got(at(recv, 1, t), ks[1], s.is_z[t])
    def rest(self):
        s, i = self.s, self.order.index("z")
        done = self.order[:i + 1]
        own = self.view(s.z, done)
        for pred, way in ((s.has_below, 0), (s.has_above, 1)):
            pl.when(pred)(lambda way=way: add_to(own, at(self.b["z"], way, s.z)))
        for axis in self.order[i + 1:]:
            k = self.exchange(axis, s.z, done)
            done += axis
            yield
            buf = self.inbox(axis, s.z, done)
            self.net.got(buf, k)
            if axis != self.order[-1]: add_to(self.view(s.z, done), buf)
        self.done = True
    def total(self):
        assert self.done
        s, last = self.s, self.order[-1]
        sum_ = self.b["acc"][s.z, s.y, s.x if self.pair else 0].astype(F32)
        if last != "z": return sum_ + self.b[last][...].astype(F32).reshape(sum_.shape)
        for pred, way in ((s.has_below, 0), (s.has_above, 1)):
            sum_ = sum_ + jnp.where(pred, self.b["z"][way, s.z].astype(F32).reshape(sum_.shape), 0.0)
        return sum_

class Sums:
    def __init__(self, nz, net, agenda, bufs, outs, vin):
        self.nz, self.net, self.agenda, self.b, self.o, self.vin = nz, net, agenda, bufs, outs, vin
        self.d, self.f, self.z, self.y, self.x, self.c = place()
        d, f = self.d, self.f
        self.up, self.down = (d + 2, f), (d - 2, f)
        self.yp, self.xp, self.sp = (d ^ 1, f), (d, f ^ 2), (d, f ^ 1)
        self.turn = turns(nz)
        z = self.z
        self.is_z = [z == h for h in range(nz)]
        self.has_below, self.has_above, self.core0 = z > 0, z < nz - 1, self.c == 0
        self.D, self.W, self.Q = [[p.bind(bufs, self) for p in ps] for ps in pieces(nz)]
    def first(self, v): return jnp.where(self.core0, v[0], v[1])
    def second(self, v): return jnp.where(self.core0, v[1], v[0])
    def cols(self, ref, width, off, n, mine, rows=None):
        cc = self.c if mine else 1 - self.c
        return ref[slice(None) if rows is None else rows, pl.ds(pl.multiple_of(cc * width + off, 128), n)]

    def vectors(self):
        vb, vr = self.b["vb"], self.b["vr"]
        self.vin(vb)
        k = self.net.send_all(vb, vr, self.nz)
        vr[self.d * 4 + self.f] = vb[self.d * 4 + self.f]
        yield
        self.net.got_all(vr, k)
        total = vr[0]
        for n in range(1, self.nz * 8): total = total + vr[n]
        self.o["v"][...] = total

    def down_tile(self, t, g):
        g = g.reshape(2, 2, 2, 96, D)
        for p, (_, _, c0, c1) in zip(self.D, D_PIECES):
            for y in range(2):
                for x in range(2):
                    p.b["acc"][t, y, x] = self.first(g[y, x, :, :, c0:c1]).astype(BF)
                    p.b["stg"][t, y, x] = self.second(g[y, x, :, :, c0:c1]).astype(BF)
            p.start(t)
    def wide_piece(self, p, c0, c1, n2, du, og, da, gu, gw):
        for dst, mine in (("acc", True), ("stg", False)):
            if c0 < 384:
                n = min(c1, 384) - c0
                for j in range(4):
                    g = tn(og[j, :, 0:192], self.cols(da, 384, c0, n, mine)) + self.cols(gw, 384, c0, n, mine, pl.ds(j * 192, 192)).astype(F32)
                    p.b[dst][j * self.nz // 4:(j + 1) * self.nz // 4, :, :, :, 0:n] = g.astype(BF).reshape(self.nz // 4, 2, 2, 48, n)
            if c1 > 384:
                lo = max(c0, 384)
                g = tn(n2[...], self.cols(du, 1536, lo - 384, c1 - lo, mine)) + self.cols(gu, 1536, lo - 384, c1 - lo, mine).astype(F32)
                p.b[dst][:, :, :, :, lo - c0:c1 - c0] = g.astype(BF).reshape(self.nz, 2, 2, 48, c1 - lo)
        for t in self.turn: p.start(t)
    def q_piece(self, p, c0, c1, n1, dq, gq):
        for j in range(2):
            g = tn(n1[:, j * 384:(j + 1) * 384], dq[:, c0:c1]) + gq[j * 384:(j + 1) * 384, c0:c1].astype(F32)
            p.b["acc"][j * self.nz // 2:(j + 1) * self.nz // 2] = g.astype(BF).reshape(self.nz // 2, 2, 1, 96, c1 - c0)
        for t in self.turn: p.start(t)
    def ends(self):
        net, half, c, f, qf = self.net, self.b["half"], self.c, self.f, self.b["qf"]
        own = self.b["q_own"]
        for p, (_, _, c0, c1) in zip(self.Q, Q_PIECES):
            total = p.total()
            for j in range(4):
                own[j, :, c0:c1] = total[j * 24:(j + 1) * 24]
                qf[0, j, :, c0:c1] = total[j * 24:(j + 1) * 24].astype(BF)
        ks = [net.sem() for _ in range(4)]
        for k in (2, 3, 1):
            net.send(at(qf, 0, f ^ k), at(qf, 1, f), ks[k], (self.d, f ^ k))
        for p, (_, _, c0, c1) in zip(self.W, W_PIECES):
            total = p.total()
            half[0, :, c0:c1] = self.first((total[0:24], total[24:48]))
            half[1, :, c0:c1] = self.second((total[0:24], total[24:48]))
        kw = net.sem()
        net.send(at(half, 1), at(half, 2), kw, self.sp)
        self.o["qkv"][f] = own[f]
        for p, (_, _, c0, c1) in zip(self.D, D_PIECES):
            self.o["down"][:, c0:c1] = p.total()
        net.got(at(half, 2), kw)
        for cc, s in ((c, 0), (1 - c, 2)):
            self.o["outw"][:, pl.ds(pl.multiple_of(cc * 384, 128), 384)] = half[s, :, 0:384]
            self.o["up"][:, pl.ds(pl.multiple_of(cc * 1536, 128), 1536)] = half[s, :, 384:1920]
        for k in (1, 2, 3):
            net.got(at(qf, 1, f ^ k), ks[k])
            self.o["qkv"][f ^ k] = qf[1, f ^ k].astype(F32)

def pieces(nz):
    return ([Piece(n, o, 96, c1 - c0, nz) for n, o, c0, c1 in D_PIECES], [Piece(n, o, 48, c1 - c0, nz) for n, o, c0, c1 in W_PIECES],
            [Piece(n, o, 96, c1 - c0, nz, False) for n, o, c0, c1 in Q_PIECES])

def sum_buffers(nz):
    out = dict(rows24=((8, D), F32), rows96=((8, FF), F32), qf=((2, 4, 24, D), BF), q_own=((4, 24, D), F32), half=((3, 24, 1920), F32), vb=((nz * 8, 8, 128), F32), vr=((nz * 8, 8, 128), F32))
    for group in pieces(nz):
        for p in group: out.update(p.buffers())
    return out

def bwd_kernel(last, nz, names, *refs):
    r_ = dict(zip(names, refs))
    R = lambda *ns: [r_[n] for n in ns]
    lim, vec, g_h, x_h, wq_h, wou_h, wd_h, qkv_h, o_h, lse_h, r_h, gp_h = R("lim", "vec", "g", "x", "wq", "wou", "wd", "qkv", "o", "lse", "r", "gp")
    dos, dop, do, mine, part, inc, go, dr, dqkv, sums, bsum = R("dos", "dop", "do", "mine", "part", "inc", "go_v", "dr", "dqkv_v", "sums", "bsum")
    d = lax.axis_index("dp"); f = lax.axis_index("fsdp")
    ZERO[0] = f * 0
    mem = Copies(r_["lsem"])
    net = Links(r_["ssem"], r_["rsem"], (d, f ^ 1))
    agenda = Agenda(PLAN if last and nz == 4 else ())
    limit = lim[0]
    g0, g1, emb = vec[0:1, :], vec[1:2, :], vec[2:3, :] if last else vec[3:4, :]
    W = 768
    V, ws = pltpu.VMEM, wide_shapes(nz)
    if last:
        gs = Sums(nz, net, agenda, r_, dict(v=r_["v_o"], down=r_["down_o"], outw=r_["outw_o"], up=r_["up_o"], qkv=r_["qkv_o"]), None)
        sums1, bsum1 = r_["sums_1"], r_["bsum_1"]
        def all_sums(out):
            rows24, rows96 = r_["rows24"], r_["rows96"]
            rows24[...] = jnp.concatenate([jnp.zeros((1, D), F32), sums[0:2, :] + sums1[0:2, :], sums[2:3, :], sums1[2:3, :], jnp.zeros((3, D), F32)], axis=0)
            rows96[...] = jnp.concatenate([bsum[...] + bsum1[...], jnp.zeros((7, FF), F32)], axis=0)
            rows_to_slabs(rows24, rows96, nz * 8, out)
        gs.vin = all_sums
    g_in = mem.go(g_h, dr) if last else None
    sums[...] = jnp.zeros_like(sums)

    def phase1(du, dm, da):
        held = []
        def phase1a(wou, r, wd, gp):
            lw, lg = mem.go(wd_h, wd), mem.go(gp_h, gp)
            if last:
                full_barrier(nz, d * 4 + f)
                g_in.wait()
            else:
                group_barrier(d, f)
                ok = lax.lt(lax.broadcasted_iota(jnp.int32, (T, 1), 0) + f * T, lax.broadcast(limit, (T, 1)))
                dr[...] = jnp.where(ok, g_h[...].astype(F32), 0.0)
            dm[...] = dr[...].astype(BF)
            lw.wait(); lg.wait()
            held.append((mem.n, mem.go(wou_h, wou), mem.go(r_h, r)))
            for j in range(FF // W):
                cols = pl.ds(j * W, W)
                t = (nt(dm[...], wd[j * nz // 4:(j + 1) * nz // 4].reshape(W, D)) * gp[:, cols].astype(F32)).astype(BF)
                du[:, cols] = t
                bsum[:, cols] = jnp.sum(t.astype(F32), axis=0, keepdims=True)
                agenda.run()
        def phase1b(wou, r, a, gt, n2, og, gu, gw):
            la = mem.go(r_["a"], a)
            late = [mem.go(r_["n2"], n2), mem.go(r_["og"], og)]
            if last:
                tile = lambda n: mem.go(at(r_["gd_1"], pl.ds(gs.turn[n] * W, W)), at(gt, n % 2))
                tiles = [tile(0), tile(1)]
                late += [mem.go(r_["gu_1"], gu), mem.go(r_["gw_1"], gw)]
            mem.wait(held[0][0], wou_h, wou)
            mem.wait(held[0][0] + 1, r_h, r)
            for j in range(T // 128):
                rows = pl.ds(j * 128, 128)
                e = nt(du[rows, :], wou[:, :, :, :, D:].reshape(D, FF))
                xhat, scale = normed(r[rows, :])
                sums[1:2, :] += jnp.sum(e * xhat, axis=0, keepdims=True)
                t = dr[rows, :] + norm_back(xhat, scale, e, g1)
                dr[rows, :] = t
                da[rows, :] = t.astype(BF)
                agenda.run()
            for k in (3, 2, 1, 0):
                b = f ^ k
                piece = nt(da[...], wou[pl.ds(b * (nz // 4), nz // 4), :, :, :, 0:D].reshape(192, D)).astype(BF)
                piece = jnp.concatenate([piece, jnp.zeros((T, 64), BF)], axis=1)
                if k:
                    pack(piece, at(dos, k))
                    net.send(at(dos, k), at(dop, f), do_sems[k], (d, b))
                else: do[rows_at(f * T, T), :] = piece
            agenda.run()
            la.wait()
            def down_tiles():
                for n, t in enumerate(gs.turn):
                    tiles[n].wait()
                    gs.down_tile(t, tn(a[:, t * W:(t + 1) * W], dm[...]) + gt[n % 2].astype(F32))
                    if n + 2 < nz: tiles.append(tile(n + 2))
                    agenda.run()
            if last and not WIDE_FIRST: down_tiles()
            for c in late: c.wait()
            if last:
                for p, (_, _, c0, c1) in zip(gs.W, W_PIECES):
                    gs.wide_piece(p, c0, c1, n2, du, og, da, gu, gw)
                    agenda.run()
                if WIDE_FIRST: down_tiles()
            else:
                for j in range(FF // W):
                    rows = pl.ds(j * W, W)
                    r_["gd_v"][rows, :] = tn(a[:, rows], dm[...]).astype(BF)
                for j in range(FF // W):
                    cols = pl.ds(j * W, W)
                    r_["gu_v"][:, cols] = tn(n2[...], du[:, cols]).astype(BF)
                for j in range(4):
                    r_["gw_v"][j * 192:(j + 1) * 192, :] = tn(og[j, :, 0:192], da[...]).astype(BF)
        big, wide = [V((T, FF), BF)], [V((T, D), BF), V((4, T, 256), BF)]
        def with_wide(wou, r):
            pl.run_scoped(partial(phase1a, wou, r), V(*ws["wd"]), V((T, FF), BF))
            if last: pl.run_scoped(partial(phase1b, wou, r), *big, V((2, W, D), BF), *wide, V((D, FF), BF), V((D, D), BF))
            else: pl.run_scoped(lambda a, *v: phase1b(wou, r, a, None, *v, None, None), *big, *wide)
        pl.run_scoped(with_wide, V(*ws["wou"]), V((T, D), F32))
    do_sems = [net.sem() for _ in range(4)]
    pl.run_scoped(phase1, V((T, FF), BF), V((T, D), BF), V((T, D), BF))
    made = [] if last else [mem.go(r_[n + "_v"], r_[n + "_o"]) for n in ("gd", "gu", "gw")]

    def phase2(qkv, o, lse, qT, kT, doT, dqT, delta, dkv):
        loads = [mem.go(*p) for p in ((qkv_h, qkv), (o_h, o), (lse_h, lse))]
        dkv[...] = jnp.zeros_like(dkv)
        dqT[192:256, :] = jnp.zeros((64, S), F32)
        agenda.run()
        for c in loads: c.wait()
        qT[...] = (qkv[:, 0:256] * 0.125).astype(BF).T
        kT[...] = qkv[:, 256:512].T
        agenda.run(hold=True)
        for k in (1, 2, 3):
            net.got(at(dop, f ^ k), do_sems[k])
            do[rows_at((f ^ k) * T, T), :] = unpack(at(dop, f ^ k))
        doT[...] = do[...].T
        prod = (do[...].astype(F32) * o[...].astype(F32)).T
        for h in range(3):
            delta[h:h + 1, :] = jnp.sum(prod[h * 64:h * 64 + 64], axis=0, keepdims=True)
        for step in BWD_STEPS:
            for h in range(3):
                bwd_block(*step, h, qkv, do, lse, limit, qT, kT, doT, dqT, delta, dkv)
                agenda.run()
        dqkv[:, 0:256] = (dqT[...] * 0.125).astype(BF).T
        dqkv[:, 256:512] = (dkv[:, 0:256] * 0.125).astype(BF)
        dqkv[:, 512:768] = dkv[:, 256:512].astype(BF)
    two = (V((S, D), BF), V((S, 256), BF), V((8, S), F32), V((256, S), BF), V((256, S), BF), V((256, S), BF), V((256, S), F32), V((8, S), F32), V((S, 512), F32))

    def phase3(wq, x, n1, gq):
        lw, lx, late = mem.go(wq_h, wq), mem.go(x_h, x), [mem.go(r_["n1"], n1)]
        if last: late.append(mem.go(r_["gq_1"], gq))
        pl.run_scoped(phase2, *two)
        out = []
        lw.wait()
        def partial_rows(b, j):
            return nt(dqkv[rows_at(b * T + j * CH, CH), :], wq[...].reshape(D, D))
        k0, k1, k2 = [[net.sem() for _ in range(3)] for _ in range(3)]
        def for_sibling(j):
            rows = pl.ds(j * CH, CH)
            mine[0, rows, :] = partial_rows(f ^ 3, j).astype(BF)
            net.send(at(mine, 0, rows), at(part, 0, rows), k0[j], (d, f ^ 1))
        def for_chip(j):
            rows = pl.ds(j * CH, CH)
            t = partial_rows(f ^ 2, j)
            agenda.run(hold=True)
            net.got(at(part, 0, rows), k0[j])
            inc[rows, :] = (t + part[0, rows, :].astype(F32)).astype(BF)
            net.send(at(inc, rows), at(part, 2, rows), k2[j], (d, f ^ 2))
        for_sibling(0)
        for_sibling(1)
        for_chip(0)
        for_sibling(2)
        for_chip(1)
        for_chip(2)
        for c in late: c.wait()
        if last:
            agenda.run()
            for p, (_, _, c0, c1) in zip(gs.Q, Q_PIECES):
                gs.q_piece(p, c0, c1, n1, dqkv, gq)
                agenda.run()
        else:
            r_["gq_v"][...] = tn(n1[...], dqkv[...]).astype(BF)
        for j in range(3):
            rows = pl.ds(j * CH, CH)
            mine[1, rows, :] = partial_rows(f ^ 1, j).astype(BF)
            net.send(at(mine, 1, rows), at(part, 1, rows), k1[j], (d, f ^ 1))
        for j in range(3):
            rows = pl.ds(j * CH, CH)
            go[rows, :] = partial_rows(f, j)
        lx.wait()
        def finish_rows():
            for j in range(3):
                rows = pl.ds(j * CH, CH)
                net.got(at(part, 1, rows), k1[j])
                net.got(at(part, 2, rows), k2[j])
                e = go[rows, :] + part[1, rows, :].astype(F32) + part[2, rows, :].astype(F32)
                xhat, scale = normed(x[rows, :].astype(F32) + emb)
                sums[0:1, :] += jnp.sum(e * xhat, axis=0, keepdims=True)
                t = dr[rows, :] + norm_back(xhat, scale, e, g0)
                sums[2:3, :] += jnp.sum(t, axis=0, keepdims=True)
                go[rows, :] = t
                if j < 2: yield
            out.append(mem.go(go, r_["go_o"]))
            if last: agenda.add(job("V"), gs.vectors())
        agenda.add(job("G"), finish_rows())
        agenda.finish()
        if last:
            gs.ends()
        for c in out: c.wait()
    pl.run_scoped(phase3, V(*ws["wq"]), V((T, D), x_h.dtype), V((S, D), BF), V((D, D), BF) if last else V((16, 128), BF))
    if not last: made.append(mem.go(r_["gq_v"], r_["gq_o"]))
    for c in made: c.wait()
    net.close()

def bwd(lim, g, x, vec, wq, wou, wd, kept, cid, nz, last=None):
    n1, qkv, o, lse, og, r, n2, gp, a = [kept[n] for n in ("n1", "qkv", "o", "lse", "og", "r", "n2", "gp", "a")]
    n1 = n1.reshape(S, D)
    hbm = pl.BlockSpec(memory_space=pltpu.HBM); vm = pl.BlockSpec(memory_space=pltpu.VMEM); sm = pl.BlockSpec(memory_space=pltpu.SMEM)
    ins = dict(lim=lim, vec=vec, g=g, x=x, wq=wq, wou=wou, wd=wd, qkv=qkv, o=o, lse=lse, r=r, gp=gp, a=a, n2=n2, og=og, n1=n1)
    scratch = dict(dos=((4, T * 3 // 2, 128), BF), dop=((4, T * 3 // 2, 128), BF), do=((S, 256), BF), mine=((2, T, D), BF), part=((3, T, D), BF), inc=((T, D), BF), go_v=((T, D), F32), dr=((T, D), F32), dqkv_v=((S, D), BF))
    outs = dict(go_o=((T, D), F32), sums=((8, D), F32), bsum=((1, FF), F32))
    if last is None:
        for n, s in (("gd", (FF, D)), ("gu", (D, FF)), ("gw", (D, D)), ("gq", (D, D))):
            outs[n + "_o"] = scratch[n + "_v"] = (s, BF)
    else:
        ins.update(last)
        outs.update(down_o=((96, D), F32), outw_o=((24, D), F32), up_o=((24, FF), F32), qkv_o=((4, 24, D), F32), v_o=((8, 128), F32))
    if last is not None: scratch.update(sum_buffers(nz))
    sems = 320 if last is not None else 16
    names = list(ins) + list(outs) + list(scratch) + ["lsem", "ssem", "rsem"]
    place_of = lambda n: sm if n == "lim" else vm if (n == "g" and last is None) or n in ("vec", "sums", "bsum", "sums_1", "bsum_1", "down_o", "outw_o", "up_o", "qkv_o", "v_o") else hbm
    res = pl.pallas_call(partial(bwd_kernel, last is not None, nz, names),
        out_shape=[jax.ShapeDtypeStruct(*s) for s in outs.values()],
        in_specs=[place_of(n) for n in ins], out_specs=[place_of(n) for n in outs],
        scratch_shapes=[pltpu.VMEM(*s) for s in scratch.values()] + [pltpu.SemaphoreType.DMA((32,)), pltpu.SemaphoreType.DMA((sems,)), pltpu.SemaphoreType.DMA((sems,))],
        compiler_params=pltpu.CompilerParams(collective_id=cid, has_side_effects=True, vmem_limit_bytes=VMEM_LIMIT))(*ins.values())
    return dict(zip(outs, res))

class Spread:
    def __init__(self, name, ref, order, rows, cols, width, off, s, pair=True):
        self.name, self.ref, self.order, self.rows, self.cols, self.s = name, ref, order, rows, cols, s
        self.nx, self.sib = (2, True) if pair else (1, False)
        self.mine = pl.multiple_of(off + s.c * width, 128) if pair else off
        self.other = pl.multiple_of(off + (1 - s.c) * width, 128) if pair else off
        self.net, self.agenda, self.late, self.names = s.net, s.agenda, [], []
        self.zsem = {(i, k): s.net.sem() for i in range(1, s.nz) for k in (0, 1)}
    def view(self, t, done, other="", col=None):
        s = self.s
        ys = pl.ds(0, 2) if "y" in done else 1 - s.y if other == "y" else s.y
        xs = pl.ds(0, self.nx) if "x" in done or self.nx == 1 else 1 - s.x if other == "x" else s.x
        return at(self.ref, t, ys, xs, pl.ds(0, self.rows), pl.ds(self.mine if col is None else col, self.cols))
    def add(self, i, steps):
        self.names.append(job(self.name, i))
        self.agenda.add(self.names[-1], steps)
    def start(self): self.add(0, self.first())
    def planes(self, i):
        s = self.s
        return [(s.z, None, 0)] if i == 0 else [(s.z - i, s.ok[i, 0], 0), (s.z + i, s.ok[i, 1], 1)]
    def first(self):
        s, done = self.s, ""
        for axis in self.order:
            if axis == "z": break
            k = self.net.sem()
            self.net.send(self.view(s.z, done), self.view(s.z, done), k, s.xp if axis == "x" else s.yp)
            yield
            self.net.got(self.view(s.z, done, axis), k)
            done += axis
        for k, dev in ((0, s.up), (1, s.down)):
            self.net.send(self.view(s.z, done), self.view(s.z, done), self.zsem[1, k], dev, s.go_on[0, k])
        for i in range(1, s.nz): self.add(i, self.distance(i, done))
        yield from self.after(0, done + "z")
    def distance(self, i, done):
        s = self.s
        for t, ok, k in self.planes(i):
            self.net.got(self.view(t, done), self.zsem[i, k], ok)
            if i + 1 < s.nz:
                self.net.send(self.view(t, done), self.view(t, done), self.zsem[i + 1, k], (s.up, s.down)[k], s.go_on[i, k])
        yield from self.after(i, done + "z")
    def after(self, i, done):
        s = self.s
        for axis in self.order[self.order.index("z") + 1:]:
            ks = []
            for t, ok, _ in self.planes(i):
                ks.append(self.net.sem())
                self.net.send(self.view(t, done), self.view(t, done), ks[-1], s.xp if axis == "x" else s.yp, ok)
            yield
            for k, (t, ok, _) in zip(ks, self.planes(i)): self.net.got(self.view(t, done, axis), k, ok)
            done += axis
        if self.sib:
            for t, ok, _ in self.planes(i):
                k = self.net.sem()
                self.net.send(self.view(t, "xy"), self.view(t, "xy"), k, s.sp, ok)
                self.late.append((i, len(self.late), k))
    def wait(self):
        self.agenda.need(self.names)
        n = {}
        for i, _, k in self.late:
            t, ok, _ = self.planes(i)[n.setdefault(i, 0)]
            n[i] += 1
            self.net.got(self.view(t, "xy", col=self.other), k, ok)

class Spreads:
    def __init__(self, nz, net, agenda, wq, wou, wd):
        self.nz, self.net, self.agenda = nz, net, agenda
        self.d, self.f, self.z, self.y, self.x, self.c = place()
        d, f, z = self.d, self.f, self.z
        self.up, self.down = (d + 2, f), (d - 2, f)
        self.yp, self.xp, self.sp = (d ^ 1, f), (d, f ^ 2), (d, f ^ 1)
        self.ok = {(i, k): (z >= i if k == 0 else z + i < nz) for i in range(1, nz) for k in (0, 1)}
        self.go_on = {(0, 0): z < nz - 1, (0, 1): z > 0}
        for i in range(1, nz - 1):
            self.go_on[i, 0] = self.ok[i, 0] & (z < nz - 1)
            self.go_on[i, 1] = self.ok[i, 1] & (z > 0)
        self.Q = [Spread(n, wq, o, 96, c1 - c0, 0, c0, self, False) for n, o, c0, c1 in GQ]
        self.O = [Spread(n, wou, o, 48, c1 - c0, 384, c0, self) for n, o, c0, c1 in GO]
        self.U = [Spread(n, wou, o, 48, c1 - c0, 1536, D + c0, self) for n, o, c0, c1 in GU]
        self.D = [Spread(n, wd, o, 192, c1 - c0, 384, c0, self) for n, o, c0, c1 in GD]
    def pred_sets(self):
        nz = self.nz
        out = [(self.ok[i, k], [z for z in range(nz) if (z >= i if k == 0 else z + i < nz)]) for i, k in self.ok]
        return out + [(p, [z for z in range(nz) if (i == 0 or (z >= i if k == 0 else z + i < nz)) and (z < nz - 1 if k == 0 else z > 0)]) for (i, k), p in self.go_on.items()]

GQ = (("r", "zy", 0, 768),)
GO = (("o", "yxz", 0, 384),)
GU = (("u", "yxz", 0, 512), ("v", "zxy", 512, 1536))
GD = (("d", "zxy", 0, 256), ("e", "zyx", 256, 384))

def prepare(pidx, gains, table, ub, qw, slab, q4):
    rd = gains.shape[1]
    row = lax.broadcasted_iota(jnp.int32, table.shape, 0)
    slab[...] = jnp.zeros((8, 128), F32)
    slab[0:1, 0:4 * rd] = ub[...].astype(F32)
    slab[1:3, 0:rd] = gains[...].astype(F32)
    for n in range(2):
        slab[3 + n:4 + n, 0:rd] = jnp.sum(jnp.where(row == pidx[n], table[...].astype(F32), 0.0), axis=0, keepdims=True)
    w = qw[...].astype(F32)
    lane = lax.broadcasted_iota(jnp.int32, (rd, 256), 1)
    for k in range(4):
        for part in range(3):
            base = part * D + k * 192
            seg = w[:, base:base + 256] if base % 128 == 0 else pltpu.roll(w[:, base - 64:base + 192], 192, 1)
            q4[k, :, part * 256:(part + 1) * 256] = jnp.where(lane < 192, seg, 0.0).astype(BF)

def last_kernel(pidx, v, q, *refs):
    n = (len(refs) - 4) // 2
    qkv_o, gain_o, bias_o, table_o = refs[n:n + 4]
    rd = gain_o.shape[1]
    for src, dst in zip(refs[:n], refs[n + 4:]): dst[...] = src[...]
    lane = lax.broadcasted_iota(jnp.int32, (rd, 256), 1)
    for part in range(3):
        for pair in range(2):
            one, two = [jnp.where(lane < 192, q[2 * pair + i, :, part * 256:(part + 1) * 256], 0.0) for i in range(2)]
            col = part * D + pair * 384
            two = pltpu.roll(two, 64, 1)
            qkv_o[:, col:col + 128] = one[:, 0:128]
            qkv_o[:, col + 128:col + 256] = one[:, 128:256] + two[:, 0:128]
            qkv_o[:, col + 256:col + 384] = two[:, 128:256]
    bias_o[...] = v[0:1, 0:4 * rd]
    gain_o[...] = v[1:3, 0:rd]
    row = lax.broadcasted_iota(jnp.int32, table_o.shape, 0)
    table_o[...] = jnp.where(row == pidx[0], v[3:4, 0:rd], 0.0) + jnp.where(row == pidx[1], v[4:5, 0:rd], 0.0)

def finish(pidx, v, q, repeats, copied):
    rd = q.shape[1]
    vm = pl.BlockSpec(memory_space=pltpu.VMEM); sm = pl.BlockSpec(memory_space=pltpu.SMEM)
    outs = [jax.ShapeDtypeStruct(s, F32) for s in ((rd, 3 * D), (2, rd), (1, 4 * rd), (repeats, rd))] + [jax.ShapeDtypeStruct(a.shape, a.dtype) for a in copied]
    return pl.pallas_call(last_kernel, out_shape=outs, in_specs=[sm, vm, vm] + [vm] * len(copied), out_specs=[vm] * (4 + len(copied)),
        compiler_params=pltpu.CompilerParams(vmem_limit_bytes=VMEM_LIMIT))(pidx, v, q, *copied)

def everyone(nz):
    return [(b // 4, b % 4) for b in range(nz * 8)]

def full_barrier(nz, me):
    bar = pltpu.get_barrier_semaphore()
    for b, dev in enumerate(everyone(nz)):
        @pl.when(me != b)
        def _(): pl.semaphore_signal(bar, inc=1, device_id=dev, device_id_type=MESH)
    pl.semaphore_wait(bar, nz * 8 - 1)

def slabs_to_rows(slabs, count, width, out):
    lane = lax.broadcasted_iota(jnp.int32, (8, 128), 1)
    tiles = [None] * (count * width // 128)
    for b in range(count):
        tile, shift = b * width // 128, b * width % 128
        turned = pltpu.roll(slabs[b], shift, 1) if shift else slabs[b]
        parts = [(tile, turned)]
        if shift + width > 128:
            low = lax.lt(lane, lax.full_like(lane, shift))
            parts = [(tile, jnp.where(low, 0.0, turned)), (tile + 1, jnp.where(low, turned, 0.0))]
        for i, p in parts: tiles[i] = p if tiles[i] is None else tiles[i] + p
    for i, t in enumerate(tiles): out[:, i * 128:(i + 1) * 128] = t

def rows_to_slabs(rows24, rows96, count, out):
    lane = lax.broadcasted_iota(jnp.int32, (8, 128), 1)
    for b in range(count):
        total = None
        for rows, width in ((rows24, 24), (rows96, 96)):
            tile, shift = b * width // 128, b * width % 128
            part = rows[:, tile * 128:(tile + 1) * 128]
            if shift: part = pltpu.roll(part, 128 - shift, 1)
            if shift + width > 128:
                low = lax.lt(lane, lax.full_like(lane, 128 - shift))
                part = jnp.where(low, part, pltpu.roll(rows[:, (tile + 1) * 128:(tile + 2) * 128], 128 - shift, 1))
            part = jnp.where(lax.lt(lane, lax.full_like(lane, width)), part, 0.0)
            total = part if total is None else total + part
        out[b] = total

def fwd_head(i, h, qkv, limit, qT, vT, oT, lse):
    keys, cols = (i + 1) * QB, pl.ds(i * QB, QB)
    slot, hr = pl.ds((h // 2) * 128, 128), pl.ds(h * 64, 64)
    sT = dot(qkv[0:keys, 256 + (h // 2) * 128:384 + (h // 2) * 128], pick(qT[slot, cols], h))
    sT = mask_scores(sT, i, limit)
    m = jnp.max(sT, axis=0, keepdims=True)
    p = jnp.exp(sT - m)
    l = jnp.sum(p, axis=0, keepdims=True)
    oT[hr, cols] = dot(vT[hr, 0:keys], p.astype(BF)) * (1.0 / l)
    lse[h:h + 1, cols] = m + jnp.log(l)

def fwd_kernel(first, final, nz, names, *refs):
    r_ = dict(zip(names, refs))
    R = lambda *ns: [r_[n] for n in ns]
    lim, x, wq, wou, wd, n1, qkv, qT, vT, oT, o, lse, og, r, n2, gp, a, xo = R("lim", "x", "wq_v", "wou_v", "wd_v", "n1_v", "qkv_v", "qT", "vT", "oT", "o_v", "lse_v", "og_v", "r_v", "n2_v", "gp_v", "a_v", "xo_v")
    d = lax.axis_index("dp"); f = lax.axis_index("fsdp")
    ZERO[0] = f * 0
    mem = Copies(r_["lsem"])
    net = Links(r_["ssem"], r_["rsem"], (d, f ^ 1))
    agenda = Agenda(GATHER_PLAN if first and nz == 4 else ())
    limit = lim[0]
    stores = []
    def store(name): stores.append(mem.go(r_[name + "_v"], r_[name]))
    if first:
        me = d * 4 + f
        c = f % 2
        prepare(*R("pidx", "gains", "table", "ub", "qw", "slab", "q4"))
        vecs, bias, slabs, slab = r_["vecs"], r_["biasr"], r_["slabs"], r_["slab"]
        q4, ow, uw, dn, rq, ro, ru = R("q4", "ow", "uw", "dn", "rq", "ro", "ru")
        full_barrier(nz, me)
        sp = (d, f ^ 1)
        k_all = net.send_all(slab, slabs, nz)
        slabs[me] = slab[...]
        z, y, xx = d // 2, d % 2, f // 2
        k_o, k_u, k_d = net.sem(), net.sem(), net.sem()
        net.send(ow, ro, k_o, sp)
        net.send(uw, ru, k_u, sp)
        k_q = [net.sem() for _ in range(4)]
        for k in (1, 2, 3): net.send(q4.at[f ^ k], rq.at[f], k_q[k], (d, f ^ k))
        half = lambda cc: pl.ds(pl.multiple_of(cc * 384, 128), 384)
        net.send(dn.at[:, half(1 - c)], wd.at[z, y, xx, pl.ds(pl.multiple_of(c * 96, 16), 96), half(1 - c)], k_d, sp)
        own_d = pltpu.make_async_copy(dn.at[:, half(c)], wd.at[z, y, xx, pl.ds(pl.multiple_of(c * 96, 16), 96), half(c)], at(r_["lsem"], 31))
        own_d.start()
        rq[f] = q4[f]
        S_ = Spreads(nz, net, agenda, wq, wou, wd)
        first_core = c == 0
        def merge(own, other):
            m_, o_ = own[...].astype(F32), other[...].astype(F32)
            return jnp.concatenate([jnp.where(first_core, m_, o_), jnp.where(first_core, o_, m_)], axis=0).astype(BF)
        net.got(ro, k_o)
        r_["bo"][...] = merge(ow, ro)
        net.got(ru, k_u)
        r_["bu"][...] = merge(uw, ru)
        wide = lambda cc: pl.ds(pl.multiple_of(cc * 1536, 128), 1536)
        lo = [pltpu.make_async_copy(r_["bo"].at[:, half(c)], wou.at[z, y, xx, pl.ds(0, 48), half(c)], at(r_["lsem"], 30)),
              pltpu.make_async_copy(r_["bu"].at[:, wide(c)], wou.at[z, y, xx, pl.ds(0, 48), pl.ds(pl.multiple_of(D + c * 1536, 128), 1536)], at(r_["lsem"], 29))]
        for w in lo: w.start()
        for w in lo: w.wait()
        for p in S_.O + S_.U: p.start()
        agenda.run()
        own_d.wait()
        net.got(wd.at[z, y, xx, pl.ds(pl.multiple_of((1 - c) * 96, 16), 96), half(c)], k_d)
        for p in S_.D: p.start()
        for k in (1, 2, 3): net.got(rq.at[f ^ k], k_q[k])
        wq[z, y, 0] = jnp.concatenate([rq[k].astype(F32) for k in range(4)], axis=0).astype(BF)
        for p in S_.Q: p.start()
        agenda.run()
        net.got_all(slabs, k_all)
        slabs_to_rows(slabs, nz * 8, 24, r_["rows24"])
        slabs_to_rows(slabs, nz * 8, 96, r_["rows96"])
        vecs[0:4, :] = r_["rows24"][1:5, :]
        vecs[4:8, :] = jnp.zeros((4, D), F32)
        bias[...] = r_["rows96"][0:1, :]
        g0, g1, emb = vecs[0:1, :], vecs[1:2, :], vecs[2:3, :]
    else:
        loads = [mem.go(r_[n], r_[n + "_v"]) for n in ("wq", "wou", "wd")]
        vecs, bias = r_["vecs"], r_["biasr"]
        g0, g1, emb = vecs[0:1, :], vecs[1:2, :], vecs[3:4, :]
        group_barrier(d, f)
    k_n = [[net.sem() for _ in range(3)] for _ in range(3)]
    for j in range(T // CH):
        rows = pl.ds(j * CH, CH)
        xhat, _ = normed(x[rows, :].astype(F32) + emb)
        n1[f, rows, :] = (xhat * g0).astype(BF)
        reg = n1.at[f, rows, :]
        net.send(reg, reg, k_n[0][j], (d, f ^ 2))
        net.send(reg, reg, k_n[1][j], (d, f ^ 1))
    if first:
        for p in S_.Q:
            agenda.run(hold=True)
            p.wait()
        store("wq")
    else: loads[0].wait()
    def project(k):
        for j in range(2):
            rows = rows_at(j * 192, 192)
            qkv[rows_at(k * T + j * 192, 192), :] = dot(n1[k, rows, :], wq[...].reshape(D, D)).astype(BF)
    project(f)
    agenda.run()
    for j in range(3): net.got(n1.at[f ^ 1, pl.ds(j * CH, CH), :], k_n[1][j])
    project(f ^ 1)
    for j in range(3):
        agenda.run(hold=True)
        reg = n1.at[f ^ 2, pl.ds(j * CH, CH), :]
        net.got(reg, k_n[0][j])
        net.send(reg, reg, k_n[2][j], (d, f ^ 1))
    project(f ^ 2)
    agenda.run()
    for j in range(3): net.got(n1.at[f ^ 3, pl.ds(j * CH, CH), :], k_n[2][j])
    project(f ^ 3)
    store("n1"); store("qkv")
    qT[...] = (qkv[:, 0:256] * 0.125).astype(BF).T
    vT[...] = qkv[:, 512:768].T
    oT[192:256, :] = jnp.zeros((64, S), F32)
    lse[...] = jnp.zeros_like(lse)
    agenda.run()
    k_og = [net.sem() for _ in range(4)]
    def finish(b):
        rows = pl.ds(b * T, T)
        o[rows, :] = oT[:, rows].astype(BF).T
        @pl.when(f == b)
        def _(): og[b] = o[rows, :]
        pack(o[rows, :], r_["op"].at[b])
        for k in (1, 2, 3):
            net.send(r_["op"].at[b], r_["ogp"].at[f], k_og[k], (d, f ^ k), (f ^ k) == b)
    for i, ready in ((0, (0,)), (2, (3,)), (1, (1, 2))):
        for h in range(3):
            fwd_head(i, h, qkv, limit, qT, vT, oT, lse)
            agenda.run()
        for b in ready: finish(b)
    store("o"); store("lse")
    agenda.run(hold=True)
    for k in (1, 2, 3):
        net.got(r_["ogp"].at[f ^ k], k_og[k])
        og[f ^ k] = unpack(r_["ogp"].at[f ^ k])
    store("og")
    if first:
        for p in S_.O:
            agenda.run(hold=True)
            p.wait()
    else: loads[1].wait()
    for j in range(2):
        rows = rows_at(j * 192, 192)
        acc = x[rows, :].astype(F32) + emb
        for k in range(4):
            acc = acc + dot(og[k, rows, 0:192], wou[k * nz // 4:(k + 1) * nz // 4, :, :, :, 0:D].reshape(192, D))
        r[rows, :] = acc
        xhat, _ = normed(acc)
        n2[rows, :] = (xhat * g1).astype(BF)
        agenda.run()
    store("r"); store("n2")
    if first:
        for p in S_.U:
            agenda.run(hold=True)
            p.wait()
        store("wou")
    W = 768
    for j in range(FF // W):
        cols = pl.ds(j * W, W)
        u = dot(n2[...], wou[:, :, :, :, D + j * W:D + (j + 1) * W].reshape(D, W)) + bias[:, cols]
        sq = u * u
        t = jnp.tanh(0.7978845608028654 * u * (1.0 + 0.044715 * sq))
        half_ = 0.5 * (1.0 + t)
        a[:, cols] = (u * half_).astype(BF)
        gp[:, cols] = (half_ + 0.5 * u * (1.0 - t * t) * (0.7978845608028654 * (1.0 + 0.134145 * sq))).astype(BF)
        agenda.run()
    store("gp"); store("a")
    if first:
        for p in S_.D:
            agenda.run(hold=True)
            p.wait()
        store("wd")
    else: loads[2].wait()
    for j in range(D // 256):
        cols = pl.ds(j * 256, 256)
        xo[:, cols] = r[:, cols] + dot(a[...], wd[:, :, :, :, j * 256:(j + 1) * 256].reshape(FF, 256))
    if final:
        ok = lax.broadcasted_iota(jnp.int32, (T, 1), 0) + f * T < limit
        r_["out_v"][...] = jnp.where(ok, xo[...], 0.0).astype(BF)
        store("out")
    else: store("xo")
    agenda.finish()
    net.close()
    for w in stores: w.wait()

def wide_shapes(nz):
    rows = D // (nz * 4)
    return dict(wq=((nz, 2, 1, D // (nz * 2), D), BF), wou=((nz, 2, 2, rows, 3840), BF), wd=((nz, 2, 2, rows * 4, D), BF))

def fwd(lim, x, weights, cid, nz, first=False, final=False):
    hbm = pl.BlockSpec(memory_space=pltpu.HBM); vm = pl.BlockSpec(memory_space=pltpu.VMEM); sm = pl.BlockSpec(memory_space=pltpu.SMEM)
    ins = dict(lim=lim, x=x, **weights)
    ws = wide_shapes(nz)
    kept = dict(n1=((4, T, D), BF), qkv=((S, D), BF), o=((S, 256), BF), lse=((8, S), F32), og=((4, T, 256), BF), r=((T, D), F32), n2=((T, D), BF), gp=((T, FF), BF), a=((T, FF), BF))
    outs = dict(kept)
    if final: outs.update(out=((T, D), BF))
    else: outs.update(xo=((T, D), F32))
    if first: outs.update(ws, vecs=((8, D), F32), biasr=((1, FF), F32))
    scratch = {n + "_v": s for n, s in dict(kept, xo=((T, D), F32), **ws).items()}
    if final: scratch.update(out_v=((T, D), BF))
    scratch.update(op=((4, T * 3 // 2, 128), BF), ogp=((4, T * 3 // 2, 128), BF), qT=((256, S), BF), vT=((256, S), BF), oT=((256, S), F32))
    if first:
        scratch.update(slab=((8, 128), F32), q4=((4, 24, D), BF), slabs=((nz * 8, 8, 128), F32), rows24=((8, D), F32), rows96=((8, FF), F32), rq=((4, 24, D), BF), ro=((24, D), BF), ru=((24, FF), BF), bo=((48, D), BF), bu=((48, FF), BF))
    sems = 320 if first else 24
    names = list(ins) + list(outs) + list(scratch) + ["lsem", "ssem", "rsem"]
    inner = ("wq", "wou", "wd")
    place_of = lambda n: sm if n in ("lim", "pidx") else vm if n in ("x", "vecs", "biasr", "qw", "ow", "uw", "dn", "gains", "table", "ub") else hbm
    res = pl.pallas_call(partial(fwd_kernel, first, final, nz, names),
        out_shape=[jax.ShapeDtypeStruct(*s) for s in outs.values()],
        in_specs=[place_of(n) for n in ins], out_specs=[place_of(n) for n in outs],
        scratch_shapes=[pltpu.VMEM(*s) for s in scratch.values()] + [pltpu.SemaphoreType.DMA((32,)), pltpu.SemaphoreType.DMA((sems,)), pltpu.SemaphoreType.DMA((sems,))],
        compiler_params=pltpu.CompilerParams(collective_id=cid, has_side_effects=True, vmem_limit_bytes=VMEM_LIMIT))(*ins.values())
    return dict(zip(outs, res))

def gather_any(q4, ow, uw, dn, slab, nz):
    both = ("dp", "fsdp")
    wq = lax.dynamic_index_in_dim(lax.all_gather(q4, both, axis=0), lax.axis_index("fsdp"), 1, keepdims=False)
    slabs = lax.all_gather(slab, both, axis=0)
    rd = q4.shape[1]
    vecs = jnp.concatenate([slabs[:, 1:5, :rd].transpose(1, 0, 2).reshape(4, D), jnp.zeros((4, D), F32)], axis=0)
    wou = lax.all_gather(jnp.concatenate([ow, uw], axis=1), both, axis=0, tiled=True)
    shapes = wide_shapes(nz)
    return dict(wq=wq.reshape(shapes["wq"][0]), wou=wou.reshape(shapes["wou"][0]), wd=lax.all_gather(dn, both, axis=0, tiled=True).reshape(shapes["wd"][0]),
                vecs=vecs, biasr=slabs[:, 0, :4 * rd].reshape(1, FF))

def grads_any(own, vin, rd):
    both = ("dp", "fsdp")
    scatter = lambda v: lax.psum_scatter(v, both, scatter_dimension=0, tiled=True)
    down, out, up, q = own
    q = lax.dynamic_update_slice(jnp.zeros((4, D // rd, rd, D), F32), q.reshape(1, D // rd, rd, D), (lax.axis_index("fsdp"), 0, 0, 0))
    q_grad = lax.psum_scatter(q, both, scatter_dimension=1, tiled=True).reshape(4, rd, D)
    idx = lax.axis_index("dp") * 4 + lax.axis_index("fsdp")
    tot = lax.psum(vin, both)
    rows = lax.dynamic_slice_in_dim(tot[0:4], idx * rd, rd, 1)
    bias = lax.dynamic_slice_in_dim(tot[4:8].reshape(1, FF), idx * rd * 4, rd * 4, 1)
    slab = jnp.concatenate([jnp.pad(bias, ((0, 0), (0, 128 - rd * 4))), jnp.pad(rows, ((0, 3), (0, 128 - rd)))], axis=0)
    return scatter(down), scatter(out), scatter(up), q_grad, slab

def w_emb(w, n):
    return dict(w, vecs=jnp.concatenate([w["vecs"][0:3], w["vecs"][2 + n:3 + n], w["vecs"][4:8]], axis=0))

def body(tokens, qkv_weight, out_weight, up_weight, down_weight, norm_gains, up_bias, pass_table, pass_index, lengths, cotangent):
    rd = qkv_weight.shape[0]
    fast = rd == 24
    nz = lax.axis_size("dp") // 2 if fast else 4
    if fast:
        own = dict(pidx=pass_index, qw=qkv_weight, ow=out_weight, uw=up_weight, dn=down_weight, gains=norm_gains.T, table=pass_table.T, ub=up_bias.reshape(1, 4 * rd))
        k0 = fwd(lengths, tokens, own, 0, nz, first=True)
        w = {n: k0[n] for n in ("wq", "wou", "wd", "vecs", "biasr")}
    else:
        q4 = jnp.pad(qkv_weight.reshape(rd, 3, 4, 192), ((0, 0), (0, 0), (0, 0), (0, 64))).transpose(2, 0, 1, 3).reshape(4, rd, D)
        chooser = [(jnp.arange(pass_table.shape[1], dtype=jnp.int32) == pass_index[n]).astype(F32) for n in range(2)]
        emb = [jnp.sum(pass_table.astype(F32) * ch[None, :], axis=1) for ch in chooser]
        rows = jnp.stack([norm_gains[:, 0].astype(F32), norm_gains[:, 1].astype(F32)] + emb)
        slab = jnp.concatenate([jnp.pad(up_bias.astype(F32)[None, :], ((0, 0), (0, 128 - 4 * rd))), jnp.pad(rows, ((0, 3), (0, 128 - rd)))], axis=0)
        w = gather_any(q4, out_weight, up_weight, down_weight, slab, nz)
        k0 = fwd(lengths, tokens, w_emb(w, 0), 1, nz)
    k1 = fwd(lengths, k0["xo"], w, 1, nz, final=True)
    big = (w["wq"], w["wou"], w["wd"])
    b1 = bwd(lengths, cotangent, k0["xo"], w["vecs"], *big, k1, 2, nz)
    if fast:
        left = dict(gd_1=b1["gd_o"], gu_1=b1["gu_o"], gw_1=b1["gw_o"], gq_1=b1["gq_o"], sums_1=b1["sums"], bsum_1=b1["bsum"])
        b0 = bwd(lengths, b1["go_o"], tokens, w["vecs"], *big, k0, 3, nz, left)
        down_grad, out_grad, up_grad, q_grad, tot = b0["down_o"], b0["outw_o"], b0["up_o"], b0["qkv_o"], b0["v_o"]
    else:
        b0 = bwd(lengths, b1["go_o"], tokens, w_emb(w, 0)["vecs"], *big, k0, 2, nz)
        s0, s1 = b0["sums"], b1["sums"]
        vin = jnp.concatenate([s0[0:2] + s1[0:2], s0[2:3], s1[2:3], (b0["bsum"] + b1["bsum"]).reshape(4, D)], axis=0)
        down_grad, out_grad, up_grad, q_grad, tot = grads_any([b0[n].astype(F32) + b1[n].astype(F32) for n in ("gd_o", "gw_o", "gu_o", "gq_o")], vin, rd)
    qkv_grad, gains, bias_grad, table, block_out, input_grad, down_grad, out_grad, up_grad = finish(
        pass_index, tot, q_grad, pass_table.shape[1], (k1["out"], b0["go_o"], down_grad, out_grad, up_grad))
    return (block_out, input_grad, qkv_grad, out_grad, up_grad, down_grad, gains.T, bias_grad.reshape(4 * rd), table.T)

def solution(mesh):
    a = P(("dp", "fsdp"), None); b = P(("dp", "fsdp"))
    return jax.shard_map(body, mesh=mesh, in_specs=(a, a, a, a, a, a, b, a, P(), P("dp"), a), out_specs=(a, a, a, a, a, a, a, b, a), check_vma=False)
```
